32 devices in a mesh: dp: 16 (over z, y, core), fsdp: 2 (over x).
Axes of the slice: x: 2, y: 2, z: 4, core: 2. Of those that a mesh axis runs over, the one named last changes fastest.
Arguments:
- inputs: bfloat16 [32768, 768], P(('dp', 'fsdp')), may hold values from -6 to 6
- segment_ids: int32 [64, 512], P(('dp', 'fsdp')), may hold values from 0 to 7, never falling along the last dimension, each value on 1 to 128 neighbouring positions
- cotangent: bfloat16 [32768, 768], P(('dp', 'fsdp')), may hold values from -6 to 6
- w_query: bfloat16 [768, 768], P('fsdp'), may hold values from -0.21875 to 0.21875
- b_query: bfloat16 [768], P('fsdp'), may hold values from -3 to 3
- w_key: bfloat16 [768, 768], P('fsdp'), may hold values from -0.21875 to 0.21875
- b_key: bfloat16 [768], P('fsdp'), may hold values from -3 to 3
- w_value: bfloat16 [768, 768], P('fsdp'), may hold values from -0.21875 to 0.21875
- b_value: bfloat16 [768], P('fsdp'), may hold values from -3 to 3
- w_output: bfloat16 [768, 768], P('fsdp'), may hold values from -0.625 to 0.625
- b_output: bfloat16 [768], P('fsdp'), may hold values from -2 to 2
- gain_attn: bfloat16 [768], P('fsdp'), may hold values from 0.25 to 1.75
- bias_attn: bfloat16 [768], P('fsdp'), may hold values from -2 to 2
- w_up: bfloat16 [768, 3072], P('fsdp'), may hold values from -0.21875 to 0.21875
- b_up: bfloat16 [3072], P('fsdp'), may hold values from -3 to 3
- w_down: bfloat16 [3072, 768], P('fsdp'), may hold values from -0.15625 to 0.15625
- b_down: bfloat16 [768], P('fsdp'), may hold values from -2 to 2
- gain_ffn: bfloat16 [768], P('fsdp'), may hold values from 0.25 to 1.75
- bias_ffn: bfloat16 [768], P('fsdp'), may hold values from -2 to 2
Outputs:
- result: float32 [32768, 768], P(('dp', 'fsdp'))
- grad_inputs: float32 [32768, 768], P(('dp', 'fsdp'))
- grad_w_query: float32 [768, 768], P('fsdp')
- grad_b_query: float32 [768], P('fsdp')
- grad_w_key: float32 [768, 768], P('fsdp')
- grad_b_key: float32 [768], P('fsdp')
- grad_w_value: float32 [768, 768], P('fsdp')
- grad_b_value: float32 [768], P('fsdp')
- grad_w_output: float32 [768, 768], P('fsdp')
- grad_b_output: float32 [768], P('fsdp')
- grad_gain_attn: float32 [768], P('fsdp')
- grad_bias_attn: float32 [768], P('fsdp')
- grad_w_up: float32 [768, 3072], P('fsdp')
- grad_b_up: float32 [3072], P('fsdp')
- grad_w_down: float32 [3072, 768], P('fsdp')
- grad_b_down: float32 [768], P('fsdp')
- grad_gain_ffn: float32 [768], P('fsdp')
- grad_bias_ffn: float32 [768], P('fsdp')
The draws below stay inside these ranges and needn't reach their ends.
Inputs may be any that keep to these rules, and one draw needn't show every extreme that they name: `segment_ids`: ids within each row of 512 tokens start at 0, never fall, and rise by one at each document boundary; a document holds at most 128 tokens.
All inputs are finite; a program needn't handle non-finite values.
Results may differ from the reference program's by a relative error of at most 0.025.
Values may be sent and summed in bfloat16 or wider, within the bound.
No kernel may reach another device: no remote copies, remote signals or barrier semaphores. Data moves between devices by JAX's collectives and lax.ppermute only.
A program may use at most 256 MiB of HBM per device.

```python
import math
import jax
import jax.numpy as jnp
import numpy as np
from jax import lax

D = 768
HEAD = 64
FF = 3072
SEQ = 512
ROWS = 64
TOKENS = 32768


def steps_of(own_key, extent, cuts, smallest, high):
    def one(dim, blocks):
        steps = jax.random.uniform(jax.random.fold_in(jax.random.fold_in(own_key, 6), dim), (blocks,), jnp.float32, smallest / len(cuts), high / len(cuts))
        return jnp.repeat(jnp.exp(steps), extent[dim] // blocks).reshape((-1,) + (1,) * (len(extent) - dim - 1))

    level = one(*cuts[0])
    for cut in cuts[1:]:
        level = level * one(*cut)
    return level


def length_profile(count, total, most, skew):
    portions = [(1 << 20) // math.isqrt(grade ** skew) + 1 for grade in range(2, count + 1)]
    rest, counts = total - most - (count - 1), [1] * (count - 1)
    while rest > 0:
        movable = [i for i in range(count - 1) if counts[i] < most]
        mass, left = sum([portions[i] for i in movable]), rest
        for i in movable:
            extra = min(most - counts[i], max(1, left * portions[i] // mass), rest)
            counts[i] = counts[i] + extra
            rest = rest - extra
    return np.array([most] + counts)


def uneven_parts(rng, number_of, total, bound, skew):
    if number_of == 2:
        one = jax.random.randint(rng, (), max(1, total - bound), min(bound, total - 1) + 1)
        return jnp.stack([one, total - one])
    sizes = jnp.asarray(length_profile(number_of, total, bound, skew), jnp.int32)
    couples = (number_of - 1) // 2
    donor, sink = sizes[1:1 + 2 * couples:2], sizes[2:2 + 2 * couples:2]
    slack = jnp.minimum(donor - 1, bound - sink)
    passed = jax.random.randint(jax.random.fold_in(rng, 1), (couples,), 0, 1 << 20) % (slack + 1)
    sizes = sizes.at[1:1 + 2 * couples:2].set(donor - passed).at[2:2 + 2 * couples:2].set(sink + passed)
    return sizes[jax.random.permutation(jax.random.fold_in(rng, 2), number_of)]


def noise(stream_key, shape, scale, limit, shards=(), kind=jnp.bfloat16):
    values = jax.random.normal(stream_key, shape, jnp.float32) * scale
    if len(shards) > 0:
        values = steps_of(stream_key, shape, shards, -0.22, 0.18) * values
    return jnp.clip(values, min=-limit, max=limit).astype(kind)


def setup_inputs(seed: int = 0) -> dict:
    key_of = jax.random.split(jax.random.key(seed), 20)
    inputs = noise(key_of[0], (TOKENS, D), 1.0, 6.0, ((0, 32),))
    segment_ids = jax.vmap(lambda own: jnp.searchsorted(jnp.cumsum(uneven_parts(own, 8, SEQ, SEQ // 4, 2)), jnp.arange(SEQ), side="right"))(jax.random.split(key_of[1], ROWS)).reshape((ROWS, SEQ)).astype(jnp.int32)
    cotangent = noise(key_of[2], (TOKENS, D), 1.0, 6.0, ((0, 32),))
    w_query = noise(key_of[3], (D, D), D ** -0.5, 0.21875, ((0, 2),))
    b_query = noise(key_of[4], (D,), 0.5, 3.0, ((0, 2),))
    w_key = noise(key_of[5], (D, D), D ** -0.5, 0.21875, ((0, 2),))
    b_key = noise(key_of[6], (D,), 0.5, 3.0, ((0, 2),))
    w_value = noise(key_of[7], (D, D), D ** -0.5, 0.21875, ((0, 2),))
    b_value = noise(key_of[8], (D,), 0.5, 3.0, ((0, 2),))
    w_output = noise(key_of[9], (D, D), (D // 8) ** -0.5, 0.625, ((0, 2),))
    b_output = noise(key_of[10], (D,), 0.3, 2.0, ((0, 2),))
    gain_attn = jnp.clip(1.0 + 0.15 * jax.random.normal(key_of[11], (D,), jnp.float32), 0.25, 1.75).astype(jnp.bfloat16)
    bias_attn = noise(key_of[12], (D,), 0.3, 2.0, ((0, 2),))
    w_up = noise(key_of[13], (D, FF), D ** -0.5, 0.21875, ((0, 2),))
    b_up = noise(key_of[14], (FF,), 0.5, 3.0, ((0, 2),))
    w_down = noise(key_of[15], (FF, D), (FF // 2) ** -0.5, 0.15625, ((0, 2),))
    b_down = noise(key_of[16], (D,), 0.3, 2.0, ((0, 2),))
    gain_ffn = jnp.clip(1.0 + 0.15 * jax.random.normal(key_of[17], (D,), jnp.float32), 0.25, 1.75).astype(jnp.bfloat16)
    bias_ffn = noise(key_of[18], (D,), 0.3, 2.0, ((0, 2),))
    return {"inputs": inputs, "segment_ids": segment_ids, "cotangent": cotangent, "w_query": w_query, "b_query": b_query, "w_key": w_key, "b_key": b_key, "w_value": w_value, "b_value": b_value, "w_output": w_output, "b_output": b_output, "gain_attn": gain_attn, "bias_attn": bias_attn, "w_up": w_up, "b_up": b_up, "w_down": w_down, "b_down": b_down, "gain_ffn": gain_ffn, "bias_ffn": bias_ffn}


@jax.custom_vjp
def low(v):
    return lax.optimization_barrier(v.astype(jnp.bfloat16)).astype(jnp.float32)

@jax.custom_vjp
def low_back(v):
    return v

def low_keep(v):
    return (low(v), None)

def low_pass(kept, grad):
    return (grad,)

def back_keep(v):
    return (v, None)

def back_low(kept, grad):
    return (low(grad),)
low.defvjp(low_keep, low_pass)
low_back.defvjp(back_keep, back_low)
EPSILON = 1e-06
SCALE = 0.125
HIGH = lax.Precision.HIGHEST

def matmul_hi(left, right):
    return jnp.dot(left, right, precision=HIGH, preferred_element_type=jnp.float32)

def layer_norm(hidden, gain, shift):
    center = hidden - lax.optimization_barrier(jnp.mean(hidden, axis=-1, keepdims=True))
    spread = lax.optimization_barrier(jnp.mean(center * center, axis=-1, keepdims=True))
    return center * lax.rsqrt(spread + EPSILON) * gain + shift

def doc_places(segments):
    column = jnp.arange(segments.shape[1], dtype=jnp.int32)[None, :]
    starts = jnp.concatenate([jnp.ones((segments.shape[0], 1), dtype=jnp.bool_), segments[:, 1:] != segments[:, :-1]], axis=1)
    first = lax.cummax(jnp.where(starts, column, jnp.zeros_like(column)), axis=1)
    return (column - first).astype(jnp.float32)

def rotary_tables(segments, width):
    places = doc_places(segments).reshape(-1)
    column = jnp.arange(width, dtype=jnp.int32) % HEAD
    paired = (column // 2 * 2).astype(jnp.float32)
    freqs = jnp.exp(-jnp.log(10000.0) * paired / HEAD)
    angle = places[:, None] * freqs[None, :]
    return (jnp.cos(angle), jnp.sin(angle))

def pair_swap(values):
    ahead = jnp.roll(values, -1, axis=-1)
    behind = jnp.roll(values, 1, axis=-1)
    even = jnp.arange(values.shape[-1]) % 2 == 0
    return jnp.where(even, -ahead, behind)

def rotate(values, cosine, sine_tab):
    return values * cosine + pair_swap(values) * sine_tab

def block_forward(tokens, segments, params):
    w_query, b_query, w_key, b_key, w_value, b_value, w_output, b_output, gain_attn, bias_attn, w_up, b_up, w_down, b_down, gain_ffn, bias_ffn = params
    rows, length = segments.shape
    width = tokens.shape[1]
    heads = width // HEAD
    cosine, sine_tab = rotary_tables(segments, width)
    token_low = low(tokens)
    queries = low(rotate(low_back(matmul_hi(token_low, w_query) + b_query), cosine, sine_tab))
    key_rows = low(rotate(low_back(matmul_hi(token_low, w_key) + b_key), cosine, sine_tab))
    value_rows = low(low_back(matmul_hi(token_low, w_value) + b_value))
    shape_four = (rows, length, heads, HEAD)
    scores = jnp.einsum('nqhd,nkhd->nhqk', queries.reshape(shape_four), key_rows.reshape(shape_four), precision=HIGH) * SCALE
    scores = low_back(scores)
    same_doc = segments[:, None, :, None] == segments[:, None, None, :]
    masked = jnp.where(same_doc, scores, -1e+30)
    peak = lax.optimization_barrier(jnp.max(masked, axis=-1, keepdims=True))
    expo = jnp.exp(masked - peak)
    probs = low(expo / lax.optimization_barrier(jnp.sum(expo, axis=-1, keepdims=True)))
    context = jnp.einsum('nhqk,nkhd->nqhd', probs, value_rows.reshape(shape_four), precision=HIGH)
    context = low(low_back(context.reshape(rows * length, width)))
    attended = low_back(matmul_hi(context, w_output) + b_output)
    normed = layer_norm(tokens + attended, gain_attn, bias_attn)
    hidden = low_back(matmul_hi(low(normed), w_up) + b_up)
    active = low(jax.nn.gelu(hidden, approximate=False))
    down = low_back(matmul_hi(active, w_down) + b_down)
    return layer_norm(normed + down, gain_ffn, bias_ffn)

def reference(inputs, segment_ids, cotangent, w_query, b_query, w_key, b_key, w_value, b_value, w_output, b_output, gain_attn, bias_attn, w_up, b_up, w_down, b_down, gain_ffn, bias_ffn):
    params = tuple((item.astype(jnp.float32) for item in (w_query, b_query, w_key, b_key, w_value, b_value, w_output, b_output, gain_attn, bias_attn, w_up, b_up, w_down, b_down, gain_ffn, bias_ffn)))
    tokens = inputs.astype(jnp.float32)
    target = cotangent.astype(jnp.float32)
    rows, length = segment_ids.shape
    width = tokens.shape[1]
    group = math.gcd(rows, max(1, 4096 // length))
    count = rows // group
    grouped_ids = segment_ids.reshape(count, group, length)

    def forward(tokens_all, params_all):

        def one_group(pieces):
            return block_forward(pieces[0], pieces[1], params_all)
        outs = lax.map(jax.checkpoint(one_group), (tokens_all.reshape(count, group * length, width), grouped_ids))
        return outs.reshape(rows * length, width)
    result, pullback = jax.vjp(forward, tokens, params)
    grad_inputs, grads = pullback(target)
    g_wq, g_bq, g_wk, g_bk, g_wv, g_bv, g_wo, g_bo, g_ga, g_ba, g_wu, g_bu, g_wd, g_bd, g_gf, g_bf = grads
    return (result, grad_inputs, g_wq, g_bq, g_wk, g_bk, g_wv, g_bv, g_wo, g_bo, g_ga, g_ba, g_wu, g_bu, g_wd, g_bd, g_gf, g_bf)
```

```python
import functools
import jax
import jax.numpy as jnp
from jax import lax
from jax.experimental import pallas as pl
from jax.experimental.pallas import tpu as pltpu
from jax.sharding import PartitionSpec as P

HEAD = 64
EPSILON = 1e-06
LANES = 128
TILE = 256
WINDOW = 384
MASKED = -1e30
F32 = jnp.float32
BF16 = jnp.bfloat16
VMEM_BYTES = 60 * 1024 * 1024


def params(**kw):
    return pltpu.CompilerParams(vmem_limit_bytes=VMEM_BYTES, **kw)


def cost(flops, bytes_accessed, transcendentals=0):
    return pl.CostEstimate(
        flops=int(flops), bytes_accessed=int(bytes_accessed), transcendentals=int(transcendentals)
    )


def dot_nn(left, right):
    return lax.dot_general(left, right, (((1,), (0,)), ((), ())), preferred_element_type=F32)


def dot_nt(left, right):
    return lax.dot_general(left, right, (((1,), (1,)), ((), ())), preferred_element_type=F32)


def dot_tn(left, right):
    return lax.dot_general(left, right, (((0,), (0,)), ((), ())), preferred_element_type=F32)


def whole(*shape):
    return pl.BlockSpec(shape, lambda *_: (0,) * len(shape))


def piece_copies(pieces, starts, full, column, sems, first):
    copies = []
    for i, (piece, start) in enumerate(zip(pieces, starts)):
        target = full.at[
            pl.ds(pl.multiple_of(start, 16), piece.shape[0]), column : column + piece.shape[1]
        ]
        copies.append(pltpu.make_async_copy(piece, target, sems.at[first + i]))
    return copies


def joined_copies(own, pieces, rows, full, sems):
    copies, column = [], 0
    for i, shard in enumerate(own):
        copies += piece_copies([shard], [rows[0]], full, column, sems, i)
        column += shard.shape[1]
    starts = [rows[1 + i] for i in range(len(pieces))]
    return copies + piece_copies(pieces, starts, full, 0, sems, len(own))


def fetch_joined(own, pieces, rows, full, sems):
    copies = joined_copies(own, pieces, rows, full, sems)
    for copy in copies:
        copy.start()
    for copy in copies:
        copy.wait()


ANY = pl.BlockSpec(memory_space=pl.ANY)
SMEM = pl.BlockSpec(memory_space=pltpu.SMEM)


def tables_kernel(seg_row, seg_col, cos_ref, sin_ref):
    length = seg_row.shape[-1]
    key = lax.broadcasted_iota(jnp.int32, (length, length), 1)
    query = lax.broadcasted_iota(jnp.int32, (length, length), 0)
    earlier = (seg_col[...] == seg_row[0]) & (key < query)
    place = jnp.sum(earlier.astype(F32), axis=1, keepdims=True)
    lane = lax.broadcasted_iota(jnp.int32, (1, LANES), 1)
    paired = (lane % HEAD // 2 * 2).astype(F32)
    freqs = jnp.exp(-jnp.log(F32(10000.0)) * paired / HEAD)
    angle = place * freqs
    cos_ref[...] = jnp.cos(angle)
    sine = jnp.sin(angle)
    sin_ref[...] = jnp.where(lane % 2 == 0, -sine, sine)


def rotary_tables(segments):
    rows, length = segments.shape
    return pl.pallas_call(
        tables_kernel,
        grid=(rows,),
        in_specs=[
            pl.BlockSpec((1, 1, length), lambda r: (r, 0, 0)),
            pl.BlockSpec((length, 1), lambda r: (r, 0)),
        ],
        out_specs=[pl.BlockSpec((length, LANES), lambda r: (r, 0))] * 2,
        out_shape=[jax.ShapeDtypeStruct((rows * length, LANES), F32)] * 2,
        compiler_params=params(),
        cost_estimate=cost(rows * length * length * 4, rows * length * LANES * 8),
        name="rotary_tables",
    )(segments.reshape(rows, 1, length), segments.reshape(rows * length, 1))


def pair_swap(values):
    even = lax.broadcasted_iota(jnp.int32, values.shape, 1) % 2 == 0
    return jnp.where(
        even, pltpu.roll(values, LANES - 1, axis=1), pltpu.roll(values, 1, axis=1)
    )


def project_kernel(count, rows, x_ref, bias, cos_ref, sin_ref, *refs):
    own, pieces = refs[:3], refs[3 : 3 + count]
    q_ref, k_ref, v_ref, full, sems = refs[3 + count :]
    width = x_ref.shape[1]

    @pl.when(pl.program_id(0) == 0)
    def _():
        fetch_joined(own, pieces, rows, full, sems)

    x = x_ref[...]
    cosine, sine = cos_ref[...], sin_ref[...]
    step = 2 * LANES
    for i, out in enumerate((q_ref, k_ref, v_ref)):
        for c in range(0, width, step):
            lin = dot_nn(x, full[:, i * width + c : i * width + c + step])
            lin = lin + bias[i : i + 1, c : c + step]
            if i < 2:
                parts = []
                for d in range(0, step, LANES):
                    part = lin[:, d : d + LANES]
                    part = part * cosine + pair_swap(part) * sine
                    parts.append(part)
                lin = jnp.concatenate(parts, axis=1)
            if i == 0:
                out[:, c : c + step] = (lin.astype(BF16).astype(F32) * 0.125).astype(BF16)
            else:
                out[:, c : c + step] = lin.astype(BF16)


def project(x, weights, bias, cosine, sine):
    own, pieces, rows = weights
    tokens, width = x.shape
    tile = pl.BlockSpec((TILE, width), lambda t: (t, 0))
    table = pl.BlockSpec((TILE, LANES), lambda t: (t, 0))
    return pl.pallas_call(
        functools.partial(project_kernel, len(pieces)),
        grid=(tokens // TILE,),
        in_specs=[SMEM, tile, whole(*bias.shape), table, table] + [ANY] * (3 + len(pieces)),
        out_specs=[tile] * 3,
        out_shape=[jax.ShapeDtypeStruct((tokens, width), BF16)] * 3,
        scratch_shapes=[
            pltpu.VMEM((width, 3 * width), BF16),
            pltpu.SemaphoreType.DMA((3 + len(pieces),)),
        ],
        compiler_params=params(),
        cost_estimate=cost(6 * tokens * width * width, 8 * tokens * width + 6 * width * width),
        name="project",
    )(rows, x, bias, cosine, sine, *own, *pieces)


def attend_kernel(q_ref, k_ref, v_ref, seg_row, seg_col, ctx_ref, prob_ref, bias):
    length = q_ref.shape[0]
    blocks = length // TILE

    @pl.when(pl.program_id(1) == 0)
    def _():
        for b in range(blocks):
            first = min(max(b * TILE - LANES, 0), length - WINDOW)
            same = seg_col[first : first + WINDOW, :] == seg_row[0, :, b * TILE : (b + 1) * TILE]
            bias[b] = jnp.where(same, 0.0, MASKED)

    v_t = v_ref[...].T
    lane = lax.broadcasted_iota(jnp.int32, (1, LANES), 1)
    for b in range(blocks):
        first = min(max(b * TILE - LANES, 0), length - WINDOW)
        queries = q_ref[b * TILE : (b + 1) * TILE, :]
        keys = k_ref[first : first + WINDOW, :]
        parts = []
        for h in range(2):
            own = jnp.where(lane // HEAD == h, keys, jnp.zeros_like(keys))
            scores = dot_nt(own, queries) + bias[b]
            peak = jnp.max(scores, axis=0, keepdims=True)
            expo = jnp.exp(scores - peak)
            total = jnp.sum(expo, axis=0, keepdims=True)
            probs = (expo * (1.0 / total)).astype(BF16)
            prob_ref[0, 0, h, b] = probs
            parts.append(dot_nn(v_t[h * HEAD : (h + 1) * HEAD, first : first + WINDOW], probs))
        ctx_ref[b * TILE : (b + 1) * TILE, :] = jnp.concatenate(parts, axis=0).T.astype(BF16)


def attend(q, k, v, segments):
    rows, length = segments.shape
    tokens, width = q.shape
    pairs = width // LANES
    blocks = length // TILE
    head = pl.BlockSpec((length, LANES), lambda r, p: (r, p))
    return pl.pallas_call(
        attend_kernel,
        grid=(rows, pairs),
        in_specs=[head] * 3
        + [
            pl.BlockSpec((1, 1, length), lambda r, p: (r, 0, 0)),
            pl.BlockSpec((length, 1), lambda r, p: (r, 0)),
        ],
        out_specs=[
            head,
            pl.BlockSpec((1, 1, 2, blocks, WINDOW, TILE), lambda r, p: (r, p, 0, 0, 0, 0)),
        ],
        out_shape=[
            jax.ShapeDtypeStruct((tokens, width), BF16),
            jax.ShapeDtypeStruct((rows, pairs, 2, blocks, WINDOW, TILE), BF16),
        ],
        scratch_shapes=[pltpu.VMEM((blocks, WINDOW, TILE), F32)],
        compiler_params=params(),
        cost_estimate=cost(rows * pairs * blocks * 2 * WINDOW * TILE * LANES * 4, 16e6),
        name="attend",
    )(q, k, v, segments.reshape(rows, 1, length), segments.reshape(rows * length, 1))


def attend_back_kernel(
    q_ref, k_ref, v_ref, g_ref, prob_ref, cos_ref, sin_ref, gq_ref, gk_ref, gv_ref, acc_k, acc_v
):
    length = q_ref.shape[0]
    blocks = length // TILE
    lane = lax.broadcasted_iota(jnp.int32, (1, LANES), 1)
    k_t = k_ref[...].T
    acc_k[...] = jnp.zeros_like(acc_k)
    acc_v[...] = jnp.zeros_like(acc_v)

    def turn_back(grads, rows):
        return grads * cos_ref[rows, :] - pair_swap(grads) * sin_ref[rows, :]

    for b in range(blocks):
        first = min(max(b * TILE - LANES, 0), length - WINDOW)
        span = slice(first, first + WINDOW)
        own_rows = slice(b * TILE, (b + 1) * TILE)
        queries = q_ref[own_rows, :]
        grads = g_ref[own_rows, :]
        values = v_ref[span, :]
        gq_parts, gk_parts, gv_parts = [], [], []
        for h in range(2):
            probs_low = prob_ref[0, 0, h, b]
            probs = probs_low.astype(F32)
            own = jnp.where(lane // HEAD == h, values, jnp.zeros_like(values))
            grad_probs = dot_nt(own, grads)
            inner = jnp.sum(probs * grad_probs, axis=0, keepdims=True)
            grad_scores = (probs * (grad_probs - inner)).astype(BF16)
            gq_parts.append(dot_nn(k_t[h * HEAD : (h + 1) * HEAD, span], grad_scores))
            gk_parts.append(dot_nn(grad_scores, queries))
            gv_parts.append(dot_nn(probs_low, grads))
        gq = jnp.concatenate(gq_parts, axis=0).T * 0.125
        gq_ref[own_rows, :] = turn_back(gq, own_rows).astype(BF16)
        acc_k[span, :] += jnp.where(lane < HEAD, gk_parts[0], gk_parts[1])
        acc_v[span, :] += jnp.where(lane < HEAD, gv_parts[0], gv_parts[1])
    gk_ref[...] = turn_back(acc_k[...], slice(0, length)).astype(BF16)
    gv_ref[...] = acc_v[...].astype(BF16)


def attend_back(q, k, v, grad_context, probs, cosine, sine, rows):
    tokens, width = q.shape
    length = tokens // rows
    pairs = width // LANES
    blocks = length // TILE
    head = pl.BlockSpec((length, LANES), lambda r, p: (r, p))
    table = pl.BlockSpec((length, LANES), lambda r, p: (r, 0))
    return pl.pallas_call(
        attend_back_kernel,
        grid=(rows, pairs),
        in_specs=[head] * 4
        + [
            pl.BlockSpec((1, 1, 2, blocks, WINDOW, TILE), lambda r, p: (r, p, 0, 0, 0, 0)),
            table,
            table,
        ],
        out_specs=[head] * 3,
        out_shape=[jax.ShapeDtypeStruct((tokens, width), BF16)] * 3,
        scratch_shapes=[pltpu.VMEM((length, LANES), F32)] * 2,
        compiler_params=params(),
        cost_estimate=cost(rows * pairs * blocks * 2 * WINDOW * TILE * LANES * 8, 22e6),
        name="attend_back",
    )(q, k, v, grad_context, probs, cosine, sine)


def norm_parts(values):
    mean = jnp.mean(values, axis=-1, keepdims=True)
    center = values - mean
    spread = jnp.mean(center * center, axis=-1, keepdims=True)
    scale = lax.rsqrt(spread + EPSILON)
    return center * scale, scale


def norm_back(grads, gain, normal, scale):
    inner = grads * gain
    return scale * (
        inner
        - jnp.mean(inner, axis=-1, keepdims=True)
        - normal * jnp.mean(inner * normal, axis=-1, keepdims=True)
    )


def gelu_parts(values):
    size = jnp.abs(values)
    bell = jnp.exp(values * values * -0.5)
    t = 1.0 / (1.0 + (0.3275911 * 0.7071067811865476) * size)
    series = 1.061405429 * (0.5 * t) + (0.5 * -1.453152027)
    series = series * t + (0.5 * 1.421413741)
    series = series * t + (0.5 * -0.284496736)
    series = series * t + (0.5 * 0.254829592)
    tail = series * t * bell
    return jnp.where(values >= 0.0, 1.0 - tail, tail), bell * 0.3989422804014327


def fetch_feed(count, rows, refs, joined, wd, sems, sems_down):
    own, pieces = refs[:2], refs[2 : 2 + count]
    down = refs[2 + count : 3 + 2 * count]

    @pl.when(pl.program_id(0) == 0)
    def _():
        scale = wd.shape[0] // joined.shape[0]
        copies = joined_copies(own, pieces, rows, joined, sems)
        starts = [rows[i] * scale for i in range(len(down))]
        copies += piece_copies(down, starts, wd, 0, sems_down, 0)
        for copy in copies:
            copy.start()
        for copy in copies:
            copy.wait()


def feed_kernel(count, rows, ctx_ref, x_ref, cot_ref, vec, bu, *refs):
    (
        res_ref, normal_ref, scale_ref, low_ref, act_ref, slope_ref, gs_ref, gd_ref, small_ref,
        joined, wd, sems, sems_down,
    ) = refs[3 + 2 * count :]
    width = x_ref.shape[1]
    fetch_feed(count, rows, refs, joined, wd, sems, sems_down)
    wo, wu = joined.at[:, :width], joined.at[:, width:]
    bo, g1, s1, bd, g2, s2 = (vec[i : i + 1, :] for i in range(6))
    hidden_width = wu.shape[1]
    first_sum = x_ref[...].astype(F32) + (dot_nn(ctx_ref[...], wo[...]) + bo)
    normal, scale = norm_parts(first_sum)
    normal_ref[...] = normal
    scale_ref[...] = scale
    normed = normal * g1 + s1
    low = normed.astype(BF16)
    low_ref[...] = low
    down = None
    step = 512
    for c in range(0, hidden_width, step):
        hidden = dot_nn(low, wu[:, c : c + step]) + bu[:, c : c + step]
        share, density = gelu_parts(hidden)
        act = (hidden * share).astype(BF16)
        act_ref[:, c : c + step] = act
        slope_ref[:, c : c + step] = (share + hidden * density).astype(BF16)
        part = dot_nn(act, wd[c : c + step, :])
        down = part if down is None else down + part
    normal2, scale2 = norm_parts(normed + (down + bd))
    res_ref[...] = normal2 * g2 + s2
    cot = cot_ref[...].astype(F32)
    grad_second = norm_back(cot, g2, normal2, scale2)
    gs_ref[...] = grad_second
    grad_down = grad_second.astype(BF16)
    gd_ref[...] = grad_down

    @pl.when(pl.program_id(0) == 0)
    def _():
        small_ref[...] = jnp.zeros_like(small_ref)

    small_ref[0:1, :] += jnp.sum(cot * normal2, axis=0, keepdims=True)
    small_ref[1:2, :] += jnp.sum(cot, axis=0, keepdims=True)
    small_ref[2:3, :] += jnp.sum(grad_down.astype(F32), axis=0, keepdims=True)


def feed_scratch(width, hidden, count):
    return [
        pltpu.VMEM((width, width + hidden), BF16),
        pltpu.VMEM((hidden, width), BF16),
        pltpu.SemaphoreType.DMA((2 + count,)),
        pltpu.SemaphoreType.DMA((1 + count,)),
    ]


def feed(ctx, x, cot, joined, down, vec, bu):
    own, pieces, rows = joined
    count = len(pieces)
    tokens, width = x.shape
    hidden = bu.shape[1]
    tile = pl.BlockSpec((TILE, width), lambda t: (t, 0))
    wide = pl.BlockSpec((TILE, hidden), lambda t: (t, 0))
    line = pl.BlockSpec((TILE, 1), lambda t: (t, 0))
    shape = jax.ShapeDtypeStruct
    return pl.pallas_call(
        functools.partial(feed_kernel, count),
        grid=(tokens // TILE,),
        in_specs=[SMEM]
        + [tile] * 3
        + [whole(*vec.shape), whole(*bu.shape)]
        + [ANY] * (3 + 2 * count),
        out_specs=[tile, tile, line, tile, wide, wide, tile, tile, whole(8, width)],
        out_shape=[
            shape((tokens, width), F32),
            shape((tokens, width), F32),
            shape((tokens, 1), F32),
            shape((tokens, width), BF16),
            shape((tokens, hidden), BF16),
            shape((tokens, hidden), BF16),
            shape((tokens, width), F32),
            shape((tokens, width), BF16),
            shape((8, width), F32),
        ],
        scratch_shapes=feed_scratch(width, hidden, count),
        compiler_params=params(),
        cost_estimate=cost(2 * tokens * width * (width + 2 * hidden), 40e6, tokens * hidden),
        name="feed",
    )(rows, ctx, x, cot, vec, bu, *own, *pieces, *down)


def feed_back_kernel(
    count, rows, gd_ref, slope_ref, gs_ref, normal_ref, scale_ref, vec, *refs
):
    (
        gh_ref, gf_ref, ga_ref, gc_ref, small_ref, wide_ref, joined, wd, sems, sems_down
    ) = refs[3 + 2 * count :]
    width = gd_ref.shape[1]
    fetch_feed(count, rows, refs, joined, wd, sems, sems_down)
    wo, wu = joined.at[:, :width], joined.at[:, width:]
    hidden_width = wu.shape[1]
    grad_down = gd_ref[...]
    grad_normed = gs_ref[...]
    step = 512

    @pl.when(pl.program_id(0) == 0)
    def _():
        small_ref[...] = jnp.zeros_like(small_ref)
        wide_ref[...] = jnp.zeros_like(wide_ref)

    for c in range(0, hidden_width, step):
        grad_active = dot_nt(grad_down, wd[c : c + step, :])
        low = (grad_active * slope_ref[:, c : c + step].astype(F32)).astype(BF16)
        gh_ref[:, c : c + step] = low
        wide_ref[0:1, c : c + step] += jnp.sum(low.astype(F32), axis=0, keepdims=True)
        grad_normed = grad_normed + dot_nt(low, wu[:, c : c + step])
    normal = normal_ref[...]
    grad_first = norm_back(grad_normed, vec[1:2, :], normal, scale_ref[...])
    gf_ref[...] = grad_first
    low = grad_first.astype(BF16)
    ga_ref[...] = low
    gc_ref[...] = dot_nt(low, wo[...]).astype(BF16)
    small_ref[0:1, :] += jnp.sum(grad_normed * normal, axis=0, keepdims=True)
    small_ref[1:2, :] += jnp.sum(grad_normed, axis=0, keepdims=True)
    small_ref[2:3, :] += jnp.sum(low.astype(F32), axis=0, keepdims=True)


def feed_back(gd, slope, gs, normal, scale, joined, down, vec):
    own, pieces, rows = joined
    count = len(pieces)
    tokens, width = gd.shape
    hidden = slope.shape[1]
    tile = pl.BlockSpec((TILE, width), lambda t: (t, 0))
    wide = pl.BlockSpec((TILE, hidden), lambda t: (t, 0))
    line = pl.BlockSpec((TILE, 1), lambda t: (t, 0))
    shape = jax.ShapeDtypeStruct
    return pl.pallas_call(
        functools.partial(feed_back_kernel, count),
        grid=(tokens // TILE,),
        in_specs=[SMEM, tile, wide, tile, tile, line, whole(*vec.shape)]
        + [ANY] * (3 + 2 * count),
        out_specs=[wide, tile, tile, tile, whole(8, width), whole(8, hidden)],
        out_shape=[
            shape((tokens, hidden), BF16),
            shape((tokens, width), F32),
            shape((tokens, width), BF16),
            shape((tokens, width), BF16),
            shape((8, width), F32),
            shape((8, hidden), F32),
        ],
        scratch_shapes=feed_scratch(width, hidden, count),
        compiler_params=params(),
        cost_estimate=cost(2 * tokens * width * (width + 2 * hidden), 40e6),
        name="feed_back",
    )(rows, gd, slope, gs, normal, scale, vec, *own, *pieces, *down)


def outer_kernel(widths, where, *refs):
    count = len(widths)
    send_ref, keep_ref = refs[2 * count :]

    def put(out):
        column = 0
        for i, width in enumerate(widths):
            out[0, :, column : column + width] = dot_tn(
                refs[2 * i][...], refs[2 * i + 1][...]
            ).astype(BF16)
            column += width

    @pl.when(pl.program_id(0) == 0)
    def _():
        put(send_ref)

    @pl.when(pl.program_id(0) == 1)
    def _():
        put(keep_ref)


def outer(where, pairs, by_rows, name):
    tokens = pairs[0][0].shape[0]
    specs, arrays, widths = [], [], []
    for left, right in pairs:
        height, width = left.shape[1] // 2, right.shape[1]
        if by_rows:
            height = height // 2
            specs += [
                pl.BlockSpec(
                    (tokens, height), lambda c, h, at: (0, 2 * ((1 - h) ^ at[0]) + ((1 - c) ^ at[1]))
                ),
                pl.BlockSpec((tokens, width), lambda c, h, at: (0, 0)),
            ]
        else:
            width = width // 2
            specs += [
                pl.BlockSpec((tokens, height), lambda c, h, at: (0, (1 - h) ^ at[0])),
                pl.BlockSpec((tokens, width), lambda c, h, at: (0, (1 - c) ^ at[1])),
            ]
        arrays += [left, right]
        widths.append(width)
    total = sum(widths)
    return pl.pallas_call(
        functools.partial(outer_kernel, widths),
        grid_spec=pltpu.PrefetchScalarGridSpec(
            num_scalar_prefetch=1,
            grid=(2, 2),
            in_specs=specs,
            out_specs=[
                pl.BlockSpec((1, height, total), lambda c, h, at: (jnp.maximum(c, h), 0, 0)),
                pl.BlockSpec((1, height, total), lambda c, h, at: (c * h, 0, 0)),
            ],
        ),
        out_shape=[jax.ShapeDtypeStruct((2, height, total), BF16)] * 2,
        compiler_params=params(),
        cost_estimate=cost(8 * tokens * height * total, 8 * height * total + 8 * tokens * total),
        name=name,
    )(where, *arrays)


def inputs_back_kernel(count, rows, gq_ref, gk_ref, gv_ref, gf_ref, *refs):
    own, pieces = refs[:3], refs[3 : 3 + count]
    out_ref, small_ref, full, sems = refs[3 + count :]
    width = gq_ref.shape[1]
    total = gf_ref[...]

    @pl.when(pl.program_id(0) == 0)
    def _():
        small_ref[...] = jnp.zeros_like(small_ref)
        fetch_joined(own, pieces, rows, full, sems)

    for i, grad in enumerate((gq_ref, gk_ref, gv_ref)):
        low = grad[...]
        total = total + dot_nt(low, full[:, i * width : (i + 1) * width])
        small_ref[i : i + 1, :] += jnp.sum(low.astype(F32), axis=0, keepdims=True)
    out_ref[...] = total


def inputs_back(gq, gk, gv, gf, weights):
    own, pieces, rows = weights
    tokens, width = gq.shape
    tile = pl.BlockSpec((TILE, width), lambda t: (t, 0))
    return pl.pallas_call(
        functools.partial(inputs_back_kernel, len(pieces)),
        grid=(tokens // TILE,),
        in_specs=[SMEM] + [tile] * 4 + [ANY] * (3 + len(pieces)),
        out_specs=[tile, whole(8, width)],
        out_shape=[
            jax.ShapeDtypeStruct((tokens, width), F32),
            jax.ShapeDtypeStruct((8, width), F32),
        ],
        scratch_shapes=[
            pltpu.VMEM((width, 3 * width), BF16),
            pltpu.SemaphoreType.DMA((3 + len(pieces),)),
        ],
        compiler_params=params(),
        cost_estimate=cost(6 * tokens * width * width, 17e6),
        name="inputs_back",
    )(rows, gq, gk, gv, gf, *own, *pieces)


CORE, NEAR_Y, NEAR_Z, FAR_Z = 1, 2, 4, 8


def swap_dp(values, bit):
    size = lax.axis_size("dp")
    return lax.ppermute(values, "dp", [(i, i ^ bit) for i in range(size)])


def swap_fsdp(values):
    return lax.ppermute(values, "fsdp", [(0, 1), (1, 0)])


def rows_of(values, start, count):
    return lax.dynamic_slice_in_dim(values, start, count, axis=0)


def fetch_other(shards, place):
    half, core, y, z = place[:4]
    height = shards[0].shape[0]
    count = height // 8
    starts = (2 * y + core) * count, height // 2 + (2 * z + core) * count
    first = jnp.concatenate(
        [jnp.concatenate([rows_of(s, start, count) for s in shards], axis=1) for start in starts],
        axis=0,
    )
    first = swap_fsdp(first)
    along = first[:count], first[count:]
    along = along + (swap_dp(along[0], NEAR_Y), swap_dp(along[1], NEAR_Z))
    return along + tuple(swap_dp(part, CORE) for part in along)


def piece_rows(height, place):
    half, core, y, z = place[:4]
    count = height // 8
    base = (1 - half) * height
    rows = [half * height]
    for c in (core, 1 - core):
        rows += [
            base + (2 * y + c) * count,
            base + height // 2 + (2 * z + c) * count,
            base + (2 * (1 - y) + c) * count,
            base + height // 2 + (2 * (1 - z) + c) * count,
        ]
    return jnp.stack(rows).astype(jnp.int32)


def sum_chunk(send, keep, place, by_rows):
    half, core, y, z = place[:4]
    height = send.shape[1]
    near = swap_dp(send, CORE)
    across = swap_fsdp((keep[0].astype(F32) + near[0].astype(F32)).astype(BF16))

    def part(start, count):
        return (
            rows_of(keep[1], start, count).astype(F32)
            + rows_of(near[1], start, count).astype(F32)
            + rows_of(across, start, count).astype(F32)
        )

    two, four = height // 2, height // 4
    from_y = swap_dp(part((1 - y) * two, two).astype(BF16), NEAR_Y)

    def part_y(bit):
        return part(y * two + bit * four, four) + rows_of(from_y, bit * four, four).astype(F32)

    from_z = swap_dp(part_y(1 - z).astype(BF16), NEAR_Z)
    mine = (part_y(z) + from_z.astype(F32)).astype(BF16)
    mine = (mine.astype(F32) + swap_dp(mine, FAR_Z).astype(F32)).astype(BF16)

    def join(values, bit, axis, swap):
        other = swap_dp(values, swap)
        return jnp.where(
            bit == 0,
            jnp.concatenate([values, other], axis=axis),
            jnp.concatenate([other, values], axis=axis),
        )

    mine = join(mine, z, 0, NEAR_Z)
    mine = join(mine, y, 0, NEAR_Y)
    return mine, swap_dp(mine, CORE)


def widen(mine, other, core, axis):
    low = jnp.where(core == 0, mine, other).astype(F32)
    high = jnp.where(core == 0, other, mine).astype(F32)
    return jnp.concatenate([low, high], axis=axis)


def gather_all(values):
    return lax.all_gather(values, "fsdp", axis=0, tiled=True)


def sum_plain(left, right):
    whole_sum = jnp.einsum("ti,tj->ij", left, right, preferred_element_type=F32).astype(BF16)
    own = lax.psum_scatter(whole_sum, "fsdp", scatter_dimension=0, tiled=True)
    return lax.psum(own, "dp").astype(F32)


def local(
    inputs, segment_ids, cotangent, w_query, b_query, w_key, b_key, w_value, b_value,
    w_output, b_output, gain_attn, bias_attn, w_up, b_up, w_down, b_down, gain_ffn, bias_ffn,
):
    rows, length = segment_ids.shape
    width = inputs.shape[1]
    shards = lax.axis_size("fsdp")
    paired = shards == 2 and lax.axis_size("dp") == 16
    half = lax.axis_index("fsdp")
    dp = lax.axis_index("dp")
    place = (half, dp % 2, dp // 2 % 2, dp // 4 % 2)
    where = jnp.stack([half, dp % 2]).astype(jnp.int32)
    vectors = (b_query, b_key, b_value, b_output, gain_attn, bias_attn, b_down, gain_ffn, bias_ffn)
    height = w_query.shape[0]
    lines = jnp.concatenate(vectors + (b_up,)).reshape(-1, height)
    if paired:
        at = piece_rows(height, place)
        joined_qkv = ((w_query, w_key, w_value), fetch_other((w_query, w_key, w_value), place), at)
        other = swap_fsdp(lines)
        joined_up = ((w_output, w_up), fetch_other((w_output, w_up), place), at)
        down = (w_down,) + fetch_other((w_down,), place)
        lines = jnp.where(half == 0, jnp.stack([lines, other]), jnp.stack([other, lines]))
    else:
        at = jnp.zeros((1,), jnp.int32)
        joined_qkv = (tuple(gather_all(w) for w in (w_query, w_key, w_value)), (), at)
        joined_up = ((gather_all(w_output), gather_all(w_up)), (), at)
        down = (gather_all(w_down),)
        lines = lax.all_gather(lines, "fsdp", axis=0)
    lines = lines.astype(F32)
    vec = jnp.swapaxes(lines[:, :9], 0, 1).reshape(9, width)
    bias_up = lines[:, 9:].reshape(1, -1)

    cosine, sine = rotary_tables(segment_ids)
    q, k, v = project(inputs, joined_qkv, vec[:3], cosine, sine)
    context, probs = attend(q, k, v, segment_ids)
    vec = vec[3:]
    result, normal, scale, low, act, slope, grad_second, grad_down, small_ffn = feed(
        context, inputs, cotangent, joined_up, down, vec, bias_up
    )
    if paired:
        sent_down = outer(where, [(act, grad_down)], True, "outer_down")
        sum_down = sum_chunk(*sent_down, place, True)
    grad_hidden, grad_first, grad_attended, grad_context, small_attn, small_up = feed_back(
        grad_down, slope, grad_second, normal, scale, joined_up, down, vec
    )
    if paired:
        sent_up = outer(where, [(low, grad_hidden), (context, grad_attended)], False, "outer_up")
        sum_up = sum_chunk(*sent_up, place, False)
    gq, gk, gv = attend_back(q, k, v, grad_context, probs, cosine, sine, rows)
    if paired:
        sent_qkv = outer(where, [(inputs, gq), (inputs, gk), (inputs, gv)], False, "outer_qkv")
        sum_qkv = sum_chunk(*sent_qkv, place, False)
    grad_inputs, small_qkv = inputs_back(gq, gk, gv, grad_first, joined_qkv)

    early = jnp.concatenate(
        [small_attn[2], small_attn[0], small_attn[1], small_ffn[2], small_ffn[0], small_ffn[1]]
        + [small_up[0]]
    )
    early = lax.psum(early, ("dp", "fsdp"))
    late = lax.psum(small_qkv[:3].reshape(-1), ("dp", "fsdp"))

    def own(values, index, count):
        start = index * width + half * (count // shards)
        return lax.dynamic_slice_in_dim(values, start, count // shards, axis=0)

    smalls = [own(late, i, width) for i in range(3)] + [own(early, i, width) for i in range(6)]
    small_up = own(early, 6, b_up.shape[0] * shards)
    gbq, gbk, gbv, gbo, gga, gba, gbd, ggf, gbf = smalls
    if paired:
        core = place[1]
        gwd = widen(*sum_down, core, 0)
        cut = (w_up.shape[1] + width) // 2 - width // 2
        gwu = widen(sum_up[0][:, :cut], sum_up[1][:, :cut], core, 1)
        gwo = widen(sum_up[0][:, cut:], sum_up[1][:, cut:], core, 1)
        part = width // 2
        gwq, gwk, gwv = (
            widen(
                sum_qkv[0][:, i * part : (i + 1) * part],
                sum_qkv[1][:, i * part : (i + 1) * part],
                core,
                1,
            )
            for i in range(3)
        )
    else:
        gwd = sum_plain(act, grad_down)
        gwu, gwo = sum_plain(low, grad_hidden), sum_plain(context, grad_attended)
        gwq, gwk, gwv = (sum_plain(inputs, g) for g in (gq, gk, gv))
    return (
        result, grad_inputs, gwq, gbq, gwk, gbk, gwv, gbv, gwo, gbo, gga, gba,
        gwu, small_up, gwd, gbd, ggf, gbf,
    )


def solution(mesh):
    tokens, matrix, vector = P(("dp", "fsdp"), None), P("fsdp", None), P("fsdp")
    weights = (
        matrix, vector, matrix, vector, matrix, vector, matrix, vector, vector, vector,
        matrix, vector, matrix, vector, vector, vector,
    )
    return jax.shard_map(
        local,
        mesh=mesh,
        in_specs=(tokens,) * 3 + weights,
        out_specs=(tokens,) * 2 + weights,
        check_vma=False,
    )
```

```python
import functools
import jax
import jax.numpy as jnp
from jax import lax
from jax.experimental import pallas as pl
from jax.experimental.pallas import tpu as pltpu
from jax.sharding import PartitionSpec as P

HEAD = 64
EPSILON = 1e-06
LANES = 128
TILE = 256
LARGE = 512
CHUNK = 512
MASKED = -1e30
F32 = jnp.float32
BF16 = jnp.bfloat16


def params(mebibytes):
    return pltpu.CompilerParams(vmem_limit_bytes=mebibytes * 1024 * 1024)


LIGHT = pl.CostEstimate(flops=1000, bytes_accessed=1000, transcendentals=0)


def dot_nn(left, right):
    return lax.dot_general(left, right, (((1,), (0,)), ((), ())), preferred_element_type=F32)


def dot_nt(left, right):
    return lax.dot_general(left, right, (((1,), (1,)), ((), ())), preferred_element_type=F32)


def dot_tn(left, right):
    return lax.dot_general(left, right, (((0,), (0,)), ((), ())), preferred_element_type=F32)


def whole(*shape):
    return pl.BlockSpec(shape, lambda *_: (0,) * len(shape))


def piece_copies(pieces, starts, full, column, sems, first):
    copies = []
    for i, (piece, start) in enumerate(zip(pieces, starts)):
        target = full.at[
            pl.ds(pl.multiple_of(start, 16), piece.shape[0]), column : column + piece.shape[1]
        ]
        copies.append(pltpu.make_async_copy(piece, target, sems.at[first + i]))
    return copies


def joined_copies(own, pieces, rows, full, sems):
    copies, column = [], 0
    for i, shard in enumerate(own):
        copies += piece_copies([shard], [rows[0]], full, column, sems, i)
        column += shard.shape[1]
    starts = [rows[1 + i] for i in range(len(pieces))]
    return copies + piece_copies(pieces, starts, full, 0, sems, len(own))


def fetch_joined(own, pieces, rows, full, sems):
    copies = joined_copies(own, pieces, rows, full, sems)
    for copy in copies:
        copy.start()
    for copy in copies:
        copy.wait()


ANY = pl.BlockSpec(memory_space=pl.ANY)
SMEM = pl.BlockSpec(memory_space=pltpu.SMEM)


def tables_kernel(seg_row, seg_col, x_ref, cos_ref, sin_ref, turned_ref):
    length = seg_row.shape[-1]
    key = lax.broadcasted_iota(jnp.int32, (length, length), 1)
    query = lax.broadcasted_iota(jnp.int32, (length, length), 0)
    earlier = (seg_col[...] == seg_row[0]) & (key < query)
    place = jnp.sum(earlier.astype(F32), axis=1, keepdims=True)
    lane = lax.broadcasted_iota(jnp.int32, (1, LANES), 1)
    paired = (lane % HEAD // 2 * 2).astype(F32)
    freqs = jnp.exp(-jnp.log(F32(10000.0)) * paired / HEAD)
    angle = place * freqs
    cos_ref[...] = jnp.cos(angle)
    sine = jnp.sin(angle)
    sin_ref[...] = jnp.where(lane % 2 == 0, -sine, sine)
    turned_ref[...] = x_ref[...].T


def rotary_tables(segments, x):
    rows, length = segments.shape
    width = x.shape[1]
    return pl.pallas_call(
        tables_kernel,
        grid=(rows,),
        in_specs=[
            pl.BlockSpec((1, 1, length), lambda r: (r, 0, 0)),
            pl.BlockSpec((length, 1), lambda r: (r, 0)),
            pl.BlockSpec((length, width), lambda r: (r, 0)),
        ],
        out_specs=[pl.BlockSpec((length, LANES), lambda r: (r, 0))] * 2
        + [pl.BlockSpec((width, length), lambda r: (0, r))],
        out_shape=[jax.ShapeDtypeStruct((rows * length, LANES), F32)] * 2
        + [jax.ShapeDtypeStruct((width, rows * length), BF16)],
        compiler_params=params(60),
        cost_estimate=LIGHT,
        name="rotary_tables",
    )(segments.reshape(rows, 1, length), segments.reshape(rows * length, 1), x)


def pair_swap(values):
    even = lax.broadcasted_iota(jnp.int32, values.shape, 1) % 2 == 0
    return jnp.where(
        even, pltpu.roll(values, LANES - 1, axis=1), pltpu.roll(values, 1, axis=1)
    )


def project_kernel(count, rows, x_ref, bias, cos_ref, sin_ref, *refs):
    own, pieces = refs[:3], refs[3 : 3 + count]
    q_ref, k_ref, v_ref, full, sems = refs[3 + count :]
    width = x_ref.shape[1]

    @pl.when(pl.program_id(0) == 0)
    def _():
        fetch_joined(own, pieces, rows, full, sems)

    x = x_ref[...]
    cosine, sine = cos_ref[...], sin_ref[...]
    step = 2 * LANES
    for i, out in enumerate((q_ref, k_ref, v_ref)):
        for c in range(0, width, step):
            lin = dot_nn(x, full[:, i * width + c : i * width + c + step])
            lin = lin + bias[i : i + 1, c : c + step]
            if i < 2:
                parts = []
                for d in range(0, step, LANES):
                    part = lin[:, d : d + LANES]
                    part = part * cosine + pair_swap(part) * sine
                    parts.append(part)
                lin = jnp.concatenate(parts, axis=1)
            if i == 0:
                out[:, c : c + step] = (lin.astype(BF16).astype(F32) * 0.125).astype(BF16)
            else:
                out[:, c : c + step] = lin.astype(BF16)


def project(x, weights, bias, cosine, sine):
    own, pieces, rows = weights
    tokens, width = x.shape
    tile = pl.BlockSpec((TILE, width), lambda t: (t, 0))
    table = pl.BlockSpec((TILE, LANES), lambda t: (t, 0))
    return pl.pallas_call(
        functools.partial(project_kernel, len(pieces)),
        grid=(tokens // TILE,),
        in_specs=[SMEM, tile, whole(*bias.shape), table, table] + [ANY] * (3 + len(pieces)),
        out_specs=[tile] * 3,
        out_shape=[jax.ShapeDtypeStruct((tokens, width), BF16)] * 3,
        scratch_shapes=[
            pltpu.VMEM((width, 3 * width), BF16),
            pltpu.SemaphoreType.DMA((3 + len(pieces),)),
        ],
        compiler_params=params(60),
        cost_estimate=LIGHT,
        name="project",
    )(rows, x, bias, cosine, sine, *own, *pieces)


def spans(length):
    found, offset = [], 0
    for first in range(0, length, LANES):
        low, high = max(first - LANES, 0), min(first + 2 * LANES, length)
        found.append((slice(first, first + LANES), slice(low, high), slice(offset, offset + high - low)))
        offset += high - low
    return found, offset


def split_heads(values):
    lane = lax.broadcasted_iota(jnp.int32, (1, LANES), 1)
    return [jnp.where(lane // HEAD == h, values, jnp.zeros_like(values)) for h in range(2)]


def stack_heads(heads, rows):
    return jnp.concatenate([head[rows, :] for head in heads], axis=0)


def merge_heads(stacked):
    lane = lax.broadcasted_iota(jnp.int32, (1, LANES), 1)
    half = stacked.shape[0] // 2
    return jnp.where(lane < HEAD, stacked[:half], stacked[half:])


def attend_kernel(q_ref, k_ref, v_ref, seg_row, seg_col, *refs):
    ctx_ref, prob_ref, bias = refs[-3:]
    blocks, _ = spans(q_ref.shape[0])

    @pl.when(pl.program_id(0) == 0)
    def _():
        for own, span, at in blocks:
            bias[at, :] = jnp.where(seg_col[span, :] == seg_row[0, :, own], 0.0, MASKED)

    queries = split_heads(q_ref[...])
    scores = [dot_nt(k_ref[span, :], stack_heads(queries, own)) for own, span, _ in blocks]
    probs = []
    for (own, span, at), pair in zip(blocks, scores):
        heads = []
        for h in range(2):
            masked = pair[:, h * LANES : (h + 1) * LANES] + bias[at, :]
            peak = jnp.max(masked, axis=0, keepdims=True)
            expo = jnp.exp(masked - peak)
            total = jnp.sum(expo, axis=0, keepdims=True)
            heads.append((expo * (1.0 / total)).astype(BF16))
        probs.append(jnp.concatenate(heads, axis=1))
    for (own, span, at), prob in zip(blocks, probs):
        prob_ref[0, 0, at, :] = prob
        ctx_ref[own, :] = merge_heads(dot_tn(prob, v_ref[span, :])).astype(BF16)


def attend(q, k, v, segments, row, made=()):
    length = segments.shape[1]
    rows = segments.shape[0]
    tokens, width = q.shape
    pairs = width // LANES
    _, depth = spans(length)
    head = pl.BlockSpec((length, LANES), lambda p: (row, p))
    return pl.pallas_call(
        attend_kernel,
        grid=(pairs,),
        in_specs=[head] * 3
        + [
            pl.BlockSpec((1, 1, length), lambda p: (row, 0, 0)),
            pl.BlockSpec((length, 1), lambda p: (row, 0)),
        ]
        + [ANY] * len(made),
        out_specs=[
            head,
            pl.BlockSpec((1, 1, depth, 2 * LANES), lambda p: (row, p, 0, 0)),
        ],
        out_shape=[
            jax.ShapeDtypeStruct((tokens, width), BF16),
            jax.ShapeDtypeStruct((rows, pairs, depth, 2 * LANES), BF16),
        ],
        input_output_aliases={5 + i: i for i in range(len(made))},
        scratch_shapes=[pltpu.VMEM((depth, LANES), F32)],
        compiler_params=params(60),
        cost_estimate=LIGHT,
        name="attend",
    )(q, k, v, segments.reshape(rows, 1, length), segments.reshape(tokens, 1), *made)


def block_of(where, step):
    core = jnp.where(step < 2, 1 - where[1], where[1])
    half = jnp.where(step % 2 == 0, 1 - where[0], where[0])
    return half, core


def send_spec(height, width, first):
    return pl.BlockSpec((1, height, width), lambda s, *_: (jnp.clip(s - first, 0, 1), 0, 0))


def keep_spec(height, width, first):
    return pl.BlockSpec((1, height, width), lambda s, *_: (jnp.clip(s - first - 2, 0, 1), 0, 0))


def put_block(send_ref, keep_ref, step, columns, value):
    @pl.when(step < 2)
    def _():
        send_ref[0, :, columns] = value

    @pl.when(step >= 2)
    def _():
        keep_ref[0, :, columns] = value


def attend_back_kernel(
    where, q_ref, k_ref, v_ref, g_ref, prob_ref, cos_ref, sin_ref, turned_ref,
    gq_ref, gk_ref, gv_ref, small_ref, send_ref, keep_ref, acc_k, acc_v, grads_all,
):
    step = pl.program_id(0)
    length = q_ref.shape[0]
    pairs = gq_ref.shape[1] // LANES
    rows = gq_ref.shape[0] // length

    @pl.when(step == 0)
    def _():
        small_ref[...] = jnp.zeros_like(small_ref)

    @pl.when(step < pairs * rows)
    def _():
        blocks, _ = spans(length)
        queries, grads = split_heads(q_ref[...]), split_heads(g_ref[...])
        k_t = k_ref[...].T
        acc_k[...] = jnp.zeros_like(acc_k)
        acc_v[...] = jnp.zeros_like(acc_v)

        def turn_back(values, rows):
            return values * cos_ref[rows, :] - pair_swap(values) * sin_ref[rows, :]

        grad_probs = [dot_nt(v_ref[span, :], stack_heads(grads, own)) for own, span, _ in blocks]
        grad_scores = []
        for (own, span, at), pair in zip(blocks, grad_probs):
            heads = []
            for h in range(2):
                columns = slice(h * LANES, (h + 1) * LANES)
                probs = prob_ref[0, 0, at, columns].astype(F32)
                inner = jnp.sum(probs * pair[:, columns], axis=0, keepdims=True)
                heads.append((probs * (pair[:, columns] - inner)).astype(BF16))
            grad_scores.append(jnp.concatenate(heads, axis=1))
        turned = []
        for (own, span, at), low in zip(blocks, grad_scores):
            acc_k[span, :] += dot_nn(low, stack_heads(queries, own))
            acc_v[span, :] += dot_nn(prob_ref[0, 0, at, :], stack_heads(grads, own))
            product = dot_nn(k_t[:, span], low)
            both = jnp.concatenate([product[:HEAD, :LANES], product[HEAD:, LANES:]], axis=0)
            turned.append(both.T)
        gq = jnp.concatenate(
            [turn_back(part * 0.125, own).astype(BF16) for (own, _, _), part in zip(blocks, turned)],
            axis=0,
        )
        gk = turn_back(acc_k[...], slice(0, length)).astype(BF16)
        gv = acc_v[...].astype(BF16)
        row, pair = step // pairs, step % pairs
        at_rows = pl.ds(pl.multiple_of(row * length, length), length)
        at_lanes = pl.ds(pl.multiple_of(pair * LANES, LANES), LANES)
        for i, (grad, out) in enumerate(((gq, gq_ref), (gk, gk_ref), (gv, gv_ref))):
            out[at_rows, at_lanes] = grad
            grads_all[at_rows, pl.ds(pl.multiple_of((i * pairs + pair) * LANES, LANES), LANES)] = grad
            small_ref[i : i + 1, at_lanes] += jnp.sum(grad.astype(F32), axis=0, keepdims=True)

    @pl.when(step >= pairs * rows)
    def _():
        product_step = step - pairs * rows
        height = send_ref.shape[1]
        half, core = block_of(where, product_step)
        at_left = pl.ds(pl.multiple_of((2 * half + core) * height, 16), height)
        value = dot_nn(turned_ref[at_left, :], grads_all[...]).astype(BF16)
        put_block(send_ref, keep_ref, product_step, slice(None), value)


def attend_back(where, q, k, v, grad_context, probs, cosine, sine, turned, first, pairs):
    tokens, width = q.shape
    rows, _, depth = probs.shape[:3]
    length = tokens // rows
    units = rows * pairs
    height = width // 4

    def at(s):
        s = jnp.minimum(s, units - 1)
        return s // pairs, first + s % pairs

    head = pl.BlockSpec((length, LANES), lambda s, *_: at(s))
    table = pl.BlockSpec((length, LANES), lambda s, *_: (at(s)[0], 0))
    out = whole(tokens, pairs * LANES)
    shape = jax.ShapeDtypeStruct
    return pl.pallas_call(
        attend_back_kernel,
        grid_spec=pltpu.PrefetchScalarGridSpec(
            num_scalar_prefetch=1,
            grid=(units + 4,),
            in_specs=[head] * 4
            + [
                pl.BlockSpec((1, 1, depth, 2 * LANES), lambda s, *_: at(s) + (0, 0)),
                table,
                table,
                whole(width, tokens),
            ],
            out_specs=[out] * 3
            + [
                whole(8, pairs * LANES),
                send_spec(height, 3 * pairs * LANES, units),
                keep_spec(height, 3 * pairs * LANES, units),
            ],
            scratch_shapes=[pltpu.VMEM((length, LANES), F32)] * 2
            + [pltpu.VMEM((tokens, 3 * pairs * LANES), BF16)],
        ),
        out_shape=[shape((tokens, pairs * LANES), BF16)] * 3
        + [shape((8, pairs * LANES), F32)]
        + [shape((2, height, 3 * pairs * LANES), BF16)] * 2,
        compiler_params=params(60),
        cost_estimate=LIGHT,
        name="attend_back",
    )(where, q, k, v, grad_context, probs, cosine, sine, turned)


def norm_parts(values):
    mean = jnp.mean(values, axis=-1, keepdims=True)
    center = values - mean
    spread = jnp.mean(center * center, axis=-1, keepdims=True)
    scale = lax.rsqrt(spread + EPSILON)
    return center * scale, scale


def norm_back(grads, gain, normal, scale):
    inner = grads * gain
    return scale * (
        inner
        - jnp.mean(inner, axis=-1, keepdims=True)
        - normal * jnp.mean(inner * normal, axis=-1, keepdims=True)
    )


def gelu_parts(values):
    share = 0.5 + 0.5 * lax.erf(values * 0.7071067811865476)
    return share, jnp.exp(values * values * -0.5) * 0.3989422804014327


def down_copies(down, rows, wd, sems):
    scale = wd.shape[0] // wd.shape[1]
    starts = [rows[i] * scale for i in range(len(down))]
    return piece_copies(down, starts, wd, 0, sems, 0)


def feed_up_kernel(count, rows, ctx_ref, x_ref, vec, bu, *refs):
    own, pieces = refs[:2], refs[2 : 2 + count]
    normal_ref, scale_ref, low_ref, act_ref, slope_ref, joined, sems = refs[2 + count :]
    width = x_ref.shape[1]

    @pl.when(pl.program_id(0) == 0)
    def _():
        fetch_joined(own, pieces, rows, joined, sems)

    bo, g1, s1 = (vec[i : i + 1, :] for i in range(3))
    subs = [slice(r, r + TILE) for r in range(0, x_ref.shape[0], TILE)]
    attended = [dot_nn(ctx_ref[s, :], joined[:, :width]) for s in subs]
    lows = []
    for s, value in zip(subs, attended):
        normal, scale = norm_parts(x_ref[s, :].astype(F32) + (value + bo))
        normal_ref[s, :] = normal
        scale_ref[s, :] = scale
        lows.append((normal * g1 + s1).astype(BF16))
        low_ref[s, :] = lows[-1]

    def product(i, c):
        return dot_nn(lows[i], joined[:, width + c : width + c + CHUNK])

    items = [(i, c) for i in range(len(subs)) for c in range(0, bu.shape[1], CHUNK)]
    ahead = product(*items[0])
    for n, (i, c) in enumerate(items):
        hidden = ahead + bu[:, c : c + CHUNK]
        if n + 1 < len(items):
            ahead = product(*items[n + 1])
        share, density = gelu_parts(hidden)
        act_ref[subs[i], c : c + CHUNK] = (hidden * share).astype(BF16)
        slope_ref[subs[i], c : c + CHUNK] = (share + hidden * density).astype(BF16)


def feed_up(ctx, x, joined, vec, bu):
    own, pieces, rows = joined
    count = len(pieces)
    tokens, width = x.shape
    hidden = bu.shape[1]
    tile = pl.BlockSpec((LARGE, width), lambda t: (t, 0))
    wide = pl.BlockSpec((LARGE, hidden), lambda t: (t, 0))
    line = pl.BlockSpec((LARGE, 1), lambda t: (t, 0))
    shape = jax.ShapeDtypeStruct
    return pl.pallas_call(
        functools.partial(feed_up_kernel, count),
        grid=(tokens // LARGE,),
        in_specs=[SMEM, tile, tile, whole(*vec.shape), whole(*bu.shape)] + [ANY] * (2 + count),
        out_specs=[tile, line, tile, wide, wide],
        out_shape=[
            shape((tokens, width), F32),
            shape((tokens, 1), F32),
            shape((tokens, width), BF16),
            shape((tokens, hidden), BF16),
            shape((tokens, hidden), BF16),
        ],
        scratch_shapes=[
            pltpu.VMEM((width, width + hidden), BF16),
            pltpu.SemaphoreType.DMA((2 + count,)),
        ],
        compiler_params=params(60),
        cost_estimate=LIGHT,
        name="feed_up",
    )(rows, ctx, x, vec, bu, *own, *pieces)


def feed_down_kernel(count, steps, where, rows, normal_ref, cot_ref, vec, act_any, *refs):
    down = refs[:count]
    res_ref, gs_ref, gd_ref, small_ref, send_ref, keep_ref = refs[count : count + 6]
    wd, act, grads_all, sems, sems_act = refs[count + 6 :]
    step = pl.program_id(0)
    tile = cot_ref.shape[0]
    g1, s1, bd, g2, s2 = (vec[i : i + 1, :] for i in range(1, 6))
    loads = [
        pltpu.make_async_copy(
            act_any.at[pl.ds(i * tile, tile), :], act.at[pl.ds(i * tile, tile), :], sems_act.at[i]
        )
        for i in range(steps)
    ]

    @pl.when(step == 0)
    def _():
        small_ref[...] = jnp.zeros_like(small_ref)
        copies = down_copies(down, rows, wd, sems) + loads
        for copy in copies:
            copy.start()
        for copy in copies[: len(down)]:
            copy.wait()

    for i in range(steps):

        @pl.when(step == i)
        def _():
            loads[i].wait()
            subs = [slice(r, r + LANES) for r in range(0, tile, LANES)]
            products = [
                dot_nn(act[i * tile + s.start : i * tile + s.stop, :], wd[...]) for s in subs
            ]
            for s, value in zip(subs, products):
                normal2, scale2 = norm_parts(normal_ref[s, :] * g1 + s1 + (value + bd))
                res_ref[s, :] = normal2 * g2 + s2
                cot = cot_ref[s, :].astype(F32)
                grad_second = norm_back(cot, g2, normal2, scale2)
                gs_ref[s, :] = grad_second
                low = grad_second.astype(BF16)
                gd_ref[s, :] = low
                grads_all[i * tile + s.start : i * tile + s.stop, :] = low
                small_ref[0:1, :] += jnp.sum(cot * normal2, axis=0, keepdims=True)
                small_ref[1:2, :] += jnp.sum(cot, axis=0, keepdims=True)
                small_ref[2:3, :] += jnp.sum(low.astype(F32), axis=0, keepdims=True)

    @pl.when(step >= steps)
    def _():
        height = send_ref.shape[1]
        half, core = block_of(where, step - steps)
        at_left = pl.ds(pl.multiple_of((2 * half + core) * height, LANES), height)
        value = dot_tn(act[:, at_left], grads_all[...]).astype(BF16)
        put_block(send_ref, keep_ref, step - steps, slice(None), value)


def feed_down(where, act, normal, cot, down, rows, vec):
    count = len(down)
    tokens, width = cot.shape
    hidden = act.shape[1]
    steps = tokens // LARGE
    height = hidden // 4
    tile = pl.BlockSpec((LARGE, width), lambda s, *_: (jnp.minimum(s, steps - 1), 0))
    shape = jax.ShapeDtypeStruct
    return pl.pallas_call(
        functools.partial(feed_down_kernel, count, steps),
        grid_spec=pltpu.PrefetchScalarGridSpec(
            num_scalar_prefetch=1,
            grid=(steps + 4,),
            in_specs=[SMEM, tile, tile, whole(*vec.shape)] + [ANY] * (1 + count),
            out_specs=[tile, tile, tile, whole(8, width)]
            + [send_spec(height, width, steps), keep_spec(height, width, steps)],
            scratch_shapes=[
                pltpu.VMEM((hidden, width), BF16),
                pltpu.VMEM((tokens, hidden), BF16),
                pltpu.VMEM((tokens, width), BF16),
                pltpu.SemaphoreType.DMA((count,)),
                pltpu.SemaphoreType.DMA((steps,)),
            ],
        ),
        out_shape=[
            shape((tokens, width), F32),
            shape((tokens, width), F32),
            shape((tokens, width), BF16),
            shape((8, width), F32),
        ]
        + [shape((2, height, width), BF16)] * 2,
        compiler_params=params(60),
        cost_estimate=LIGHT,
        name="feed_down",
    )(where, rows, normal, cot, vec, act, *down)


def feed_back_kernel(
    count, steps, where, rows, gd_ref, slope_ref, gs_ref, normal_ref, scale_ref, vec,
    low_ref, ctx_ref, *refs
):
    own, pieces = refs[:2], refs[2 : 2 + count]
    down = refs[2 + count : 3 + 2 * count]
    gf_ref, gc_ref, small_ref, wide_ref, send_ref, keep_ref = refs[3 + 2 * count : 9 + 2 * count]
    joined, wd, hidden_all, attended_all, sems, sems_down = refs[9 + 2 * count :]
    width = gd_ref.shape[1]
    step = pl.program_id(0)

    @pl.when(step == 0)
    def _():
        small_ref[...] = jnp.zeros_like(small_ref)
        wide_ref[...] = jnp.zeros_like(wide_ref)
        copies = down_copies(down, rows, wd, sems_down)
        copies += joined_copies(own, pieces, rows, joined, sems)
        for copy in copies:
            copy.start()
        for copy in copies:
            copy.wait()

    @pl.when(step < steps)
    def _():
        base = pl.multiple_of(step * gd_ref.shape[0], gd_ref.shape[0])
        feed_back_tile(
            base, gd_ref, slope_ref, gs_ref, normal_ref, scale_ref, vec, joined, wd,
            gf_ref, gc_ref, small_ref, wide_ref, hidden_all, attended_all,
        )

    @pl.when(step >= steps)
    def _():
        half, core = block_of(where, step - steps)
        height, cut = width // 2, hidden_all.shape[1] // 2
        at_left = pl.ds(pl.multiple_of(half * height, LANES), height)
        at_wide = pl.ds(pl.multiple_of(core * cut, LANES), cut)
        at_narrow = pl.ds(pl.multiple_of(core * height, LANES), height)
        value = dot_tn(low_ref[:, at_left], hidden_all[:, at_wide]).astype(BF16)
        put_block(send_ref, keep_ref, step - steps, slice(0, cut), value)
        value = dot_tn(ctx_ref[:, at_left], attended_all[:, at_narrow]).astype(BF16)
        put_block(send_ref, keep_ref, step - steps, slice(cut, cut + height), value)


def feed_back_tile(
    base, gd_ref, slope_ref, gs_ref, normal_ref, scale_ref, vec, joined, wd,
    gf_ref, gc_ref, small_ref, wide_ref, hidden_all, attended_all,
):
    width = gd_ref.shape[1]
    subs = [slice(r, r + TILE) for r in range(0, gd_ref.shape[0], TILE)]
    items = [(i, c) for i in range(len(subs)) for c in range(0, slope_ref.shape[1], CHUNK)]

    def product(i, c):
        return dot_nt(gd_ref[subs[i], :], wd[c : c + CHUNK, :])

    def norm_step(i, grad_normed):
        s = subs[i]
        normal = normal_ref[s, :]
        grad_first = norm_back(grad_normed, vec[1:2, :], normal, scale_ref[s, :])
        gf_ref[s, :] = grad_first
        low = grad_first.astype(BF16)
        attended_all[pl.ds(base + s.start, TILE), :] = low
        small_ref[0:1, :] += jnp.sum(grad_normed * normal, axis=0, keepdims=True)
        small_ref[1:2, :] += jnp.sum(grad_normed, axis=0, keepdims=True)
        small_ref[2:3, :] += jnp.sum(low.astype(F32), axis=0, keepdims=True)
        gc_ref[s, :] = dot_nt(low, joined[:, :width]).astype(BF16)

    ahead = product(*items[0])
    pending, grad_normed = None, None
    for n, (i, c) in enumerate(items):
        grad_active = ahead
        if n + 1 < len(items):
            ahead = product(*items[n + 1])
        low = (grad_active * slope_ref[subs[i], c : c + CHUNK].astype(F32)).astype(BF16)
        hidden_all[pl.ds(base + subs[i].start, TILE), c : c + CHUNK] = low
        wide_ref[0:1, c : c + CHUNK] += jnp.sum(low.astype(F32), axis=0, keepdims=True)
        part = dot_nt(low, joined[:, width + c : width + c + CHUNK])
        grad_normed = (gs_ref[subs[i], :] if c == 0 else grad_normed) + part
        if pending is not None:
            norm_step(*pending)
            pending = None
        if c + CHUNK >= slope_ref.shape[1]:
            pending = (i, grad_normed)
    norm_step(*pending)


def feed_back(where, gd, slope, gs, normal, scale, joined, down, vec, low, context):
    own, pieces, rows = joined
    count = len(pieces)
    tokens, width = gd.shape
    hidden = slope.shape[1]
    steps = tokens // LARGE
    total = (hidden + width) // 2

    def tiled(columns):
        return pl.BlockSpec((LARGE, columns), lambda s, *_: (jnp.minimum(s, steps - 1), 0))

    tile = tiled(width)
    shape = jax.ShapeDtypeStruct
    return pl.pallas_call(
        functools.partial(feed_back_kernel, count, steps),
        grid_spec=pltpu.PrefetchScalarGridSpec(
            num_scalar_prefetch=1,
            grid=(steps + 4,),
            in_specs=[SMEM, tile, tiled(hidden), tile, tile, tiled(1), whole(*vec.shape)]
            + [whole(tokens, width)] * 2
            + [ANY] * (3 + 2 * count),
            out_specs=[tile, tile, whole(8, width), whole(8, hidden)]
            + [send_spec(width // 2, total, steps), keep_spec(width // 2, total, steps)],
            scratch_shapes=[
                pltpu.VMEM((width, width + hidden), BF16),
                pltpu.VMEM((hidden, width), BF16),
                pltpu.VMEM((tokens, hidden), BF16),
                pltpu.VMEM((tokens, width), BF16),
                pltpu.SemaphoreType.DMA((2 + count,)),
                pltpu.SemaphoreType.DMA((1 + count,)),
            ],
        ),
        out_shape=[
            shape((tokens, width), F32),
            shape((tokens, width), BF16),
            shape((8, width), F32),
            shape((8, hidden), F32),
        ]
        + [shape((2, width // 2, total), BF16)] * 2,
        compiler_params=params(60),
        cost_estimate=LIGHT,
        name="feed_back",
    )(where, rows, gd, slope, gs, normal, scale, vec, low, context, *own, *pieces, *down)


def inputs_back_kernel(count, parts, rows, gf_ref, *refs):
    grads, refs = refs[: 3 * parts], refs[3 * parts :]
    own, pieces = refs[:3], refs[3 : 3 + count]
    out_ref, full, sems = refs[3 + count :]
    width = gf_ref.shape[1]
    part = width // parts

    @pl.when(pl.program_id(0) == 0)
    def _():
        fetch_joined(own, pieces, rows, full, sems)

    low = [jnp.concatenate([grads[3 * j + i][...] for j in range(parts)], axis=1) for i in range(3)]
    total = gf_ref[...]
    for i in range(3):
        total = total + dot_nt(low[i], full[:, i * width : (i + 1) * width])
    out_ref[...] = total


def inputs_back(grads, gf, weights):
    own, pieces, rows = weights
    tokens, width = gf.shape
    parts = len(grads) // 3
    tile = pl.BlockSpec((TILE, width), lambda t: (t, 0))
    narrow = pl.BlockSpec((TILE, width // parts), lambda t: (t, 0))
    return pl.pallas_call(
        functools.partial(inputs_back_kernel, len(pieces), parts),
        grid=(tokens // TILE,),
        in_specs=[SMEM, tile] + [narrow] * len(grads) + [ANY] * (3 + len(pieces)),
        out_specs=tile,
        out_shape=jax.ShapeDtypeStruct((tokens, width), F32),
        scratch_shapes=[
            pltpu.VMEM((width, 3 * width), BF16),
            pltpu.SemaphoreType.DMA((3 + len(pieces),)),
        ],
        compiler_params=params(60),
        cost_estimate=LIGHT,
        name="inputs_back",
    )(rows, gf, *grads, *own, *pieces)


CORE, NEAR_Y, NEAR_Z, FAR_Z = 1, 2, 4, 8


def after(value, *others):
    return lax.optimization_barrier((value,) + others)[0]


def swap_dp(values, bit):
    size = lax.axis_size("dp")
    return lax.ppermute(values, "dp", [(i, i ^ bit) for i in range(size)])


def swap_fsdp(values):
    return lax.ppermute(values, "fsdp", [(0, 1), (1, 0)])


def swap_both(values):
    size = lax.axis_size("dp")
    pairs = [(2 * i + h, 2 * (i ^ NEAR_Y) + 1 - h) for i in range(size) for h in range(2)]
    return lax.ppermute(values, ("dp", "fsdp"), pairs)


def rows_of(values, start, count):
    return lax.dynamic_slice_in_dim(values, start, count, axis=0)


def own_part(shards, place):
    half, core, y, z = place
    height = shards[0].shape[0]
    count = height // 8
    starts = (2 * y + core) * count, height // 2 + (2 * z + core) * count
    return jnp.concatenate(
        [jnp.concatenate([rows_of(s, start, count) for s in shards], axis=1) for start in starts],
        axis=0,
    )


def pass_on(first):
    count = first.shape[0] // 2
    return (
        first[:count],
        first[count:],
        swap_dp(first[:count], NEAR_Y),
        swap_dp(first[count:], NEAR_Z),
    )


def with_core(parts):
    return tuple(parts) + tuple(swap_dp(part, CORE) for part in parts)


def piece_rows(height, place):
    half, core, y, z = place
    count = height // 8
    base = (1 - half) * height
    rows = [half * height]
    for c in (core, 1 - core):
        rows += [
            base + (2 * y + c) * count,
            base + height // 2 + (2 * z + c) * count,
            base + (2 * (1 - y) + c) * count,
            base + height // 2 + (2 * (1 - z) + c) * count,
        ]
    return jnp.stack(rows).astype(jnp.int32)


class Part:
    def __init__(self, terms, place):
        self.bits = {0: 1, 1: place[2], 2: place[3]}
        self.swaps = {
            0: swap_fsdp,
            1: lambda v: swap_dp(v, NEAR_Y),
            2: lambda v: swap_dp(v, NEAR_Z),
            3: lambda v: swap_dp(v, FAR_Z),
        }
        self.terms = [t.reshape(2, 2, 2, t.shape[1] // 4, t.shape[2]) for t in terms]
        self.flight, self.joined = [], None

    def total(self, terms):
        value = terms[0].astype(F32)
        for term in terms[1:]:
            value = value + term.astype(F32)
        return value.astype(BF16)

    def pick(self, terms, axis, index):
        return [lax.dynamic_slice_in_dim(t, index, 1, axis) for t in terms]

    def halve(self, axis):
        sent = self.total(self.pick(self.terms, axis, 1 - self.bits[axis]))
        self.terms = self.pick(self.terms, axis, self.bits[axis])
        self.flight, self.route = [sent], [self.swaps[axis]]

    def both(self):
        across, along = self.swaps[0], self.swaps[1]
        other = self.pick(self.terms, 0, 0)
        own = self.pick(self.terms, 0, 1)
        bit = self.bits[1]
        self.flight = [
            self.total(self.pick(other, 1, bit)),
            self.total(self.pick(own, 1, 1 - bit)),
            self.total(self.pick(other, 1, 1 - bit)),
        ]
        self.route = [across, along, swap_both]
        self.terms = self.pick(own, 1, bit)

    def merge(self, other):
        self.terms = [
            jnp.concatenate([self.total(self.terms), self.total(other.terms)], axis=-1)
        ]

    def far(self):
        sent = self.total(self.terms)
        self.terms = []
        self.flight, self.route = [sent], [lambda v: (v, self.swaps[3](v))]

    def join(self, axis):
        self.flight, self.route = [self.total(self.terms)], [lambda v: (v, self.swaps[axis](v))]
        self.terms, self.joined = [], axis

    def land(self):
        for sent, route in zip(self.flight, self.route):
            got = route(sent)
            self.terms += list(got) if isinstance(got, tuple) else [got]
        self.flight = []

    def settle(self):
        if self.joined is None:
            return
        mine, other = self.terms
        axis, self.joined = self.joined, None
        value = jnp.where(
            self.bits[axis] == 0,
            jnp.concatenate([mine, other], axis=axis),
            jnp.concatenate([other, mine], axis=axis),
        )
        self.terms = [value]

    def finish(self):
        value = self.terms[0].reshape(-1, self.terms[0].shape[-1])
        self.flight, self.route = [value], [lambda v: (v, swap_dp(v, CORE))]
        self.terms = []


def fence(parts, *arrays):
    counts = [(len(p.terms), len(p.flight)) for p in parts]
    flat = [a for p in parts for a in p.terms + p.flight] + list(arrays)
    flat = list(lax.optimization_barrier(tuple(flat)))
    for part, (terms, flight) in zip(parts, counts):
        part.terms, flat = flat[:terms], flat[terms:]
        part.flight, flat = flat[:flight], flat[flight:]
    return flat


def widen(mine, other, core, axis):
    low = jnp.where(core == 0, mine, other).astype(F32)
    high = jnp.where(core == 0, other, mine).astype(F32)
    return jnp.concatenate([low, high], axis=axis)


def gather_all(values):
    return lax.all_gather(values, "fsdp", axis=0, tiled=True)


def sum_plain(send, keep, by_rows):
    blocks = [[keep[1], send[1]], [keep[0], send[0]]]
    axis = 0 if by_rows else 1
    value = jnp.concatenate([jnp.concatenate(pair, axis=axis) for pair in blocks], axis=0)
    own = lax.psum_scatter(value, "fsdp", scatter_dimension=0, tiled=True)
    return lax.psum(own, "dp").astype(F32)


def local(
    inputs, segment_ids, cotangent, w_query, b_query, w_key, b_key, w_value, b_value,
    w_output, b_output, gain_attn, bias_attn, w_up, b_up, w_down, b_down, gain_ffn, bias_ffn,
):
    rows, length = segment_ids.shape
    width = inputs.shape[1]
    shards = lax.axis_size("fsdp")
    paired = shards == 2 and lax.axis_size("dp") == 16
    half = lax.axis_index("fsdp")
    dp = lax.axis_index("dp")
    place = (half, dp % 2, dp // 2 % 2, dp // 4 % 2)
    core = place[1]
    vectors = (b_query, b_key, b_value, b_output, gain_attn, bias_attn, b_down, gain_ffn, bias_ffn)
    height = w_query.shape[0]
    cosine, sine, turned = rotary_tables(segment_ids, inputs)
    if paired:
        where = jnp.stack([half, core]).astype(jnp.int32)
        part_qkv = own_part((w_query, w_key, w_value), place)
        part_up = after(own_part((w_output, w_up), place), part_qkv)
        part_down = own_part((w_down,), place)
        here_qkv = swap_fsdp(part_qkv)
        lines = jnp.concatenate(vectors + (b_up,)).reshape(-1, height)
        other = swap_fsdp(after(lines, part_qkv))
        here_up = swap_fsdp(part_up)
        here_down = swap_fsdp(after(part_down, part_up, here_qkv))
        at = piece_rows(height, place)
        joined_qkv = ((w_query, w_key, w_value), with_core(pass_on(here_qkv)), at)
        lines = jnp.where(half == 0, jnp.stack([lines, other]), jnp.stack([other, lines]))
    else:
        where = jnp.zeros((2,), jnp.int32)
        at = jnp.zeros((1,), jnp.int32)
        joined_qkv = (tuple(gather_all(w) for w in (w_query, w_key, w_value)), (), at)
        joined_up = ((gather_all(w_output), gather_all(w_up)), (), at)
        down = (gather_all(w_down),)
        lines = jnp.concatenate(vectors + (b_up,)).reshape(-1, height)
        lines = lax.all_gather(lines, "fsdp", axis=0)
    lines = lines.astype(F32)
    vec = jnp.swapaxes(lines[:, :9], 0, 1).reshape(9, width)
    bias_up = lines[:, 9:].reshape(1, -1)

    q, k, v = project(inputs, joined_qkv, vec[:3], cosine, sine)
    vec = vec[3:]
    if paired:
        here_up = after(here_up, q)
        q = after(q, here_up)
        parts_up = pass_on(here_up)
    made = attend(q, k, v, segment_ids, 0)
    if paired:
        here_down = after(here_down, made[0])
        parts_up = [after(part, made[0]) for part in parts_up]
        made = (after(made[0], here_down, *parts_up), made[1])
        joined_up = ((w_output, w_up), with_core(parts_up), at)
        parts_down = pass_on(here_down)
    for row in range(1, rows):
        made = attend(q, k, v, segment_ids, row, made)
    context, probs = made
    if paired:
        parts_down = [after(part, context) for part in parts_down]
        context = after(context, *parts_down)
        down = (w_down,) + with_core(parts_down)
    normal, scale, low, act, slope = feed_up(context, inputs, joined_up, vec, bias_up)
    result, grad_second, grad_down, small_ffn, send, keep = feed_down(
        where, act, normal, cotangent, down, at, vec
    )
    sent = [(send, keep)]
    if paired:
        sum_d = Part([keep, swap_dp(send, CORE)], place)
        sum_d.both()
        (grad_down,) = fence([sum_d], grad_down)
    outs = feed_back(
        where, grad_down, slope, grad_second, normal, scale, joined_up, down, vec, low, context
    )
    if paired:
        sum_d.land()
        outs = fence([sum_d], *outs)
    grad_first, grad_context, small_attn, small_up, send, keep = outs
    sent.append((send, keep))
    if paired:
        near = swap_dp(send, CORE)
        cut = keep.shape[2] // 2 // LANES * LANES
        sum_u = Part([keep[..., :cut], near[..., :cut]], place)
        sum_v = Part([keep[..., cut:], near[..., cut:]], place)
        sum_d.halve(2)
        sum_u.halve(0)
        sum_v.halve(1)
        parts = [sum_d, sum_u, sum_v]
        (grad_context,) = fence(parts, grad_context)
    pairs = width // LANES // 2
    grads, smalls = [], []
    for part in range(2):
        outs = attend_back(
            where, q, k, v, grad_context, probs, cosine, sine, turned, part * pairs, pairs
        )
        if paired:
            for p in parts:
                p.land()
            outs = fence(parts, *outs)
        *three, small, send, keep = outs
        grads += three
        smalls.append(small)
        sent.append((send, keep))
        if paired:
            near = swap_dp(send, CORE)
            if part == 0:
                cut = keep.shape[2] // 2 // LANES * LANES
                sum_q = Part([keep[..., :cut], near[..., :cut]], place)
                sum_r = Part([keep[..., cut:], near[..., cut:]], place)
                sum_q.halve(0)
                sum_r.halve(1)
                sum_d.far()
                sum_u.halve(1)
                sum_v.halve(0)
                parts += [sum_q, sum_r]
                (grad_context,) = fence(parts, grad_context)
            else:
                sum_s = Part([keep, near], place)
                sum_s.both()
                sum_d.join(2)
                sum_u.merge(sum_v)
                sum_u.halve(2)
                sum_q.halve(1)
                sum_r.halve(0)
                parts = [sum_d, sum_u, sum_q, sum_r, sum_s]
    small = jnp.concatenate(
        [small_attn[2], small_attn[0], small_attn[1], small_ffn[2], small_ffn[0], small_ffn[1]]
        + [small_up[0]]
        + [smalls[j][i] for i in range(3) for j in range(2)]
    ).reshape(-1, width)
    if paired:
        grad_first, small = fence(parts, grad_first, small)
    grad_inputs = inputs_back(grads, grad_first, joined_qkv)
    if paired:
        for p in parts:
            p.land()
        grad_inputs, small, other = fence(parts, grad_inputs, small, swap_dp(small, CORE))
        small = small + other
        sum_q.merge(sum_r)
        sum_q.merge(sum_s)
        parts = [sum_d, sum_u, sum_q]
        rounds = (
            (("join", 1), ("far",), ("halve", 2)),
            (("finish",), ("join", 2), ("far",)),
            ((), ("join", 1), ("join", 2)),
            ((), ("finish",), ("join", 1)),
            ((), (), ("finish",)),
        )
        routes = (
            swap_fsdp,
            lambda v: swap_dp(v, NEAR_Y),
            lambda v: swap_dp(v, NEAR_Z),
            lambda v: swap_dp(v, FAR_Z),
        )
        for n, moves in enumerate(rounds):
            moving = [(p, move) for p, move in zip(parts, moves) if move]
            for p, (name, *axis) in moving:
                p.settle()
                getattr(p, name)(*axis)
            moving = [p for p, _ in moving]
            (small,) = fence(moving, small)
            other = routes[n](small) if n < len(routes) else None
            for p in moving:
                p.land()
            if other is not None:
                small, other = fence(moving, small, other)
                small = small + other
            else:
                fence(moving)
        small = small.reshape(-1)
    else:
        small = lax.psum(small.reshape(-1), ("dp", "fsdp"))

    def own(index, count):
        start = index * width + half * (count // shards)
        return lax.dynamic_slice_in_dim(small, start, count // shards, axis=0)

    wide = b_up.shape[0] * shards
    gbo, gga, gba, gbd, ggf, gbf = (own(i, width) for i in range(6))
    gbu = own(6, wide)
    gbq, gbk, gbv = (own(6 + wide // width + i, width) for i in range(3))
    if paired:
        gwd = widen(*sum_d.terms, core, 0)
        cut = wide // 2
        mine, other = sum_u.terms
        gwu = widen(mine[:, :cut], other[:, :cut], core, 1)
        gwo = widen(mine[:, cut:], other[:, cut:], core, 1)
        part = width // 2
        gwq, gwk, gwv = (
            jnp.concatenate(
                [
                    widen(*(end[:, i * part : (i + 1) * part] for end in sum_q.terms), core, 0)
                    for i in (j, j + 3)
                ],
                axis=1,
            )
            for j in range(3)
        )
    else:
        gwd = sum_plain(*sent[0], True)
        both = sum_plain(*sent[1], False).reshape(height, 2, -1)
        cut = wide // 2
        gwu = both[..., :cut].reshape(height, -1)
        gwo = both[..., cut:].reshape(height, -1)
        both = [sum_plain(*pair, True).reshape(height, 3, -1) for pair in sent[2:]]
        gwq, gwk, gwv = (jnp.concatenate([b[:, i] for b in both], axis=1) for i in range(3))
    return (
        result, grad_inputs, gwq, gbq, gwk, gbk, gwv, gbv, gwo, gbo, gga, gba,
        gwu, gbu, gwd, gbd, ggf, gbf,
    )


def solution(mesh):
    tokens, matrix, vector = P(("dp", "fsdp"), None), P("fsdp", None), P("fsdp")
    weights = (
        matrix, vector, matrix, vector, matrix, vector, matrix, vector, vector, vector,
        matrix, vector, matrix, vector, vector, vector,
    )
    return jax.shard_map(
        local,
        mesh=mesh,
        in_specs=(tokens,) * 3 + weights,
        out_specs=(tokens,) * 2 + weights,
        check_vma=False,
    )
```

```python
import functools
import jax
import jax.numpy as jnp
from jax import lax
from jax.experimental import pallas as pl
from jax.experimental.pallas import tpu as pltpu
from jax.sharding import PartitionSpec as P

HEAD = 64
EPSILON = 1e-06
LANES = 128
TILE = 256
CHUNK = 512
MASKED = -1e30
SUM_FFN, SUM_ATTN, SUM_UP, SUM_QKV, SUM_ROWS = 0, 3, 6, 10, 16
F32 = jnp.float32
BF16 = jnp.bfloat16


def params(mebibytes):
    return pltpu.CompilerParams(vmem_limit_bytes=mebibytes * 1024 * 1024)


LIGHT = pl.CostEstimate(flops=1000, bytes_accessed=1000, transcendentals=0)


def dot_nn(left, right):
    return lax.dot_general(left, right, (((1,), (0,)), ((), ())), preferred_element_type=F32)


def dot_nt(left, right):
    return lax.dot_general(left, right, (((1,), (1,)), ((), ())), preferred_element_type=F32)


def dot_tn(left, right):
    return lax.dot_general(left, right, (((0,), (0,)), ((), ())), preferred_element_type=F32)


def whole(*shape):
    return pl.BlockSpec(shape, lambda *_: (0,) * len(shape))


SPLITS = 4


def piece_copies(pieces, starts, full, column, sems, first):
    copies = []
    for i, (piece, start) in enumerate(zip(pieces, starts)):
        height, width = piece.shape
        splits = SPLITS if height * width >= 500_000 and height % (16 * SPLITS) == 0 else 1
        count = height // splits
        for j in range(splits):
            row = pl.multiple_of(start + j * count, 16)
            copies.append(
                pltpu.make_async_copy(
                    piece.at[pl.ds(j * count, count), :],
                    full.at[pl.ds(row, count), column : column + width],
                    sems.at[SPLITS * (first + i) + j],
                )
            )
    return copies


def joined_copies(own, pieces, rows, full, sems, cut=None):
    shards, column = [], 0
    for i, shard in enumerate(own):
        shards.append(piece_copies([shard], [rows[0]], full, column, sems, i))
        column += shard.shape[1]
    starts = [rows[1 + i] for i in range(len(pieces))]
    first = len(own)
    if cut is None:
        return sum(shards, []) + piece_copies(pieces, starts, full, 0, sems, first)
    left = [piece.at[:, :cut] for piece in pieces]
    right = [piece.at[:, cut:] for piece in pieces]
    return (
        shards[0] + piece_copies(left, starts, full, 0, sems, first),
        sum(shards[1:], []) + piece_copies(right, starts, full, cut, sems, first + len(pieces)),
    )


def fetch_joined(own, pieces, rows, full, sems):
    copies = joined_copies(own, pieces, rows, full, sems)
    for copy in copies:
        copy.start()
    for copy in copies:
        copy.wait()


ANY = pl.BlockSpec(memory_space=pl.ANY)
SMEM = pl.BlockSpec(memory_space=pltpu.SMEM)


def tables_kernel(seg_row, seg_col, x_ref, cos_ref, sin_ref, turned_ref):
    length = seg_row.shape[-1]
    key = lax.broadcasted_iota(jnp.int32, (length, length), 1)
    query = lax.broadcasted_iota(jnp.int32, (length, length), 0)
    earlier = (seg_col[...] == seg_row[0]) & (key < query)
    place = jnp.sum(earlier.astype(F32), axis=1, keepdims=True)
    lane = lax.broadcasted_iota(jnp.int32, (1, LANES), 1)
    paired = (lane % HEAD // 2 * 2).astype(F32)
    freqs = jnp.exp(-jnp.log(F32(10000.0)) * paired / HEAD)
    angle = place * freqs
    cos_ref[...] = jnp.cos(angle)
    sine = jnp.sin(angle)
    sin_ref[...] = jnp.where(lane % 2 == 0, -sine, sine)
    turned_ref[...] = x_ref[...].T


def rotary_tables(segments, x):
    rows, length = segments.shape
    width = x.shape[1]
    return pl.pallas_call(
        tables_kernel,
        grid=(rows,),
        in_specs=[
            pl.BlockSpec((1, 1, length), lambda r: (r, 0, 0)),
            pl.BlockSpec((length, 1), lambda r: (r, 0)),
            pl.BlockSpec((length, width), lambda r: (r, 0)),
        ],
        out_specs=[pl.BlockSpec((length, LANES), lambda r: (r, 0))] * 2
        + [pl.BlockSpec((width, length), lambda r: (0, r))],
        out_shape=[jax.ShapeDtypeStruct((rows * length, LANES), F32)] * 2
        + [jax.ShapeDtypeStruct((width, rows * length), BF16)],
        compiler_params=params(60),
        cost_estimate=LIGHT,
        name="rotary_tables",
    )(segments.reshape(rows, 1, length), segments.reshape(rows * length, 1), x)


def pair_swap(values):
    even = lax.broadcasted_iota(jnp.int32, values.shape, 1) % 2 == 0
    return jnp.where(
        even, pltpu.roll(values, LANES - 1, axis=1), pltpu.roll(values, 1, axis=1)
    )


def project_kernel(count, rows, x_ref, bias, cos_ref, sin_ref, *refs):
    own, pieces = refs[:3], refs[3 : 3 + count]
    q_ref, k_ref, v_ref, full, sems = refs[3 + count :]
    width = x_ref.shape[1]

    @pl.when(pl.program_id(0) == 0)
    def _():
        fetch_joined(own, pieces, rows, full, sems)

    x = x_ref[...]
    cosine, sine = cos_ref[...], sin_ref[...]
    step = 2 * LANES
    for i, out in enumerate((q_ref, k_ref, v_ref)):
        for c in range(0, width, step):
            lin = dot_nn(x, full[:, i * width + c : i * width + c + step])
            lin = lin + bias[i : i + 1, c : c + step]
            if i < 2:
                parts = []
                for d in range(0, step, LANES):
                    part = lin[:, d : d + LANES]
                    part = part * cosine + pair_swap(part) * sine
                    parts.append(part)
                lin = jnp.concatenate(parts, axis=1)
            if i == 0:
                out[:, c : c + step] = (lin.astype(BF16).astype(F32) * 0.125).astype(BF16)
            else:
                out[:, c : c + step] = lin.astype(BF16)


def project(x, weights, bias, cosine, sine):
    own, pieces, rows = weights
    tokens, width = x.shape
    tile = pl.BlockSpec((TILE, width), lambda t: (t, 0))
    table = pl.BlockSpec((TILE, LANES), lambda t: (t, 0))
    return pl.pallas_call(
        functools.partial(project_kernel, len(pieces)),
        grid=(tokens // TILE,),
        in_specs=[SMEM, tile, whole(*bias.shape), table, table] + [ANY] * (3 + len(pieces)),
        out_specs=[tile] * 3,
        out_shape=[jax.ShapeDtypeStruct((tokens, width), BF16)] * 3,
        scratch_shapes=[
            pltpu.VMEM((width, 3 * width), BF16),
            pltpu.SemaphoreType.DMA((SPLITS * (3 + len(pieces)),)),
        ],
        compiler_params=params(60),
        cost_estimate=LIGHT,
        name="project",
    )(rows, x, bias, cosine, sine, *own, *pieces)


def spans(length):
    found, offset = [], 0
    for first in range(0, length, LANES):
        low, high = max(first - LANES, 0), min(first + 2 * LANES, length)
        found.append((slice(first, first + LANES), slice(low, high), slice(offset, offset + high - low)))
        offset += high - low
    return found, offset


def split_heads(values):
    lane = lax.broadcasted_iota(jnp.int32, (1, LANES), 1)
    return [jnp.where(lane // HEAD == h, values, jnp.zeros_like(values)) for h in range(2)]


def stack_heads(heads, rows):
    return jnp.concatenate([head[rows, :] for head in heads], axis=0)


def merge_heads(stacked):
    lane = lax.broadcasted_iota(jnp.int32, (1, LANES), 1)
    half = stacked.shape[0] // 2
    return jnp.where(lane < HEAD, stacked[:half], stacked[half:])


def attend_kernel(q_ref, k_ref, v_ref, seg_row, seg_col, ctx_ref, prob_ref, bias):
    blocks, _ = spans(q_ref.shape[0])

    @pl.when(pl.program_id(1) == 0)
    def _():
        for own, span, at in blocks:
            bias[at, :] = jnp.where(seg_col[span, :] == seg_row[0, :, own], 0.0, MASKED)

    queries = split_heads(q_ref[...])
    scores = [dot_nt(k_ref[span, :], stack_heads(queries, own)) for own, span, _ in blocks]
    probs = []
    for (own, span, at), pair in zip(blocks, scores):
        heads = []
        for h in range(2):
            masked = pair[:, h * LANES : (h + 1) * LANES] + bias[at, :]
            peak = jnp.max(masked, axis=0, keepdims=True)
            expo = jnp.exp(masked - peak)
            total = jnp.sum(expo, axis=0, keepdims=True)
            heads.append((expo * (1.0 / total)).astype(BF16))
        probs.append(jnp.concatenate(heads, axis=1))
    for (own, span, at), prob in zip(blocks, probs):
        prob_ref[0, 0, at, :] = prob
        ctx_ref[own, :] = merge_heads(dot_tn(prob, v_ref[span, :])).astype(BF16)


def attend(q, k, v, segments):
    rows, length = segments.shape
    tokens, width = q.shape
    pairs = width // LANES
    _, depth = spans(length)
    head = pl.BlockSpec((length, LANES), lambda r, p: (r, p))
    return pl.pallas_call(
        attend_kernel,
        grid=(rows, pairs),
        in_specs=[head] * 3
        + [
            pl.BlockSpec((1, 1, length), lambda r, p: (r, 0, 0)),
            pl.BlockSpec((length, 1), lambda r, p: (r, 0)),
        ],
        out_specs=[
            head,
            pl.BlockSpec((1, 1, depth, 2 * LANES), lambda r, p: (r, p, 0, 0)),
        ],
        out_shape=[
            jax.ShapeDtypeStruct((tokens, width), BF16),
            jax.ShapeDtypeStruct((rows, pairs, depth, 2 * LANES), BF16),
        ],
        scratch_shapes=[pltpu.VMEM((depth, LANES), F32)],
        compiler_params=params(60),
        cost_estimate=LIGHT,
        name="attend",
    )(q, k, v, segments.reshape(rows, 1, length), segments.reshape(tokens, 1))


def send_spec(steps, height, width, first):
    return pl.BlockSpec(
        (2 // steps, height, width), lambda s, *_: (jnp.clip(s - first, 0, steps - 1), 0, 0)
    )


def keep_spec(steps, height, width, first):
    return pl.BlockSpec(
        (2 // steps, height, width), lambda s, *_: (jnp.clip(s - first - steps, 0, steps - 1), 0, 0)
    )


def put_blocks(send_ref, keep_ref, sending, slots, columns, values):
    @pl.when(sending)
    def _():
        for slot, value in zip(slots, values):
            send_ref[slot, :, columns] = value

    @pl.when(jnp.logical_not(sending))
    def _():
        for slot, value in zip(slots, values):
            keep_ref[slot, :, columns] = value


def attend_back_kernel(
    rows, where, q_ref, k_ref, v_ref, g_ref, prob_ref, cos_ref, sin_ref, sums_ref, turned_any,
    small_ref, send_ref, keep_ref, out_any, acc_k, acc_v, grads_all, turned, sems,
):
    step = pl.program_id(0)
    length = q_ref.shape[0]
    width = turned.shape[0]
    pairs = width // LANES
    units = rows * pairs
    fetch = pltpu.make_async_copy(turned_any, turned, sems.at[0])
    hand_on = pltpu.make_async_copy(grads_all, out_any, sems.at[1])

    @pl.when(step == 0)
    def _():
        fetch.start()
        small_ref[...] = sums_ref[...]

    @pl.when(step < units)
    def _():
        blocks, _ = spans(length)
        queries, grads = split_heads(q_ref[...]), split_heads(g_ref[...])
        k_t = k_ref[...].T
        acc_k[...] = jnp.zeros_like(acc_k)
        acc_v[...] = jnp.zeros_like(acc_v)

        def turn_back(values, rows):
            return values * cos_ref[rows, :] - pair_swap(values) * sin_ref[rows, :]

        grad_probs = [dot_nt(v_ref[span, :], stack_heads(grads, own)) for own, span, _ in blocks]
        grad_scores = []
        for (own, span, at), pair in zip(blocks, grad_probs):
            heads = []
            for h in range(2):
                columns = slice(h * LANES, (h + 1) * LANES)
                probs = prob_ref[0, 0, at, columns].astype(F32)
                inner = jnp.sum(probs * pair[:, columns], axis=0, keepdims=True)
                heads.append((probs * (pair[:, columns] - inner)).astype(BF16))
            grad_scores.append(jnp.concatenate(heads, axis=1))
        turned_parts = []
        for (own, span, at), low in zip(blocks, grad_scores):
            acc_k[span, :] += dot_nn(low, stack_heads(queries, own))
            acc_v[span, :] += dot_nn(prob_ref[0, 0, at, :], stack_heads(grads, own))
            product = dot_nn(k_t[:, span], low)
            both = jnp.concatenate([product[:HEAD, :LANES], product[HEAD:, LANES:]], axis=0)
            turned_parts.append(both.T)
        gq = jnp.concatenate(
            [
                turn_back(part * 0.125, own).astype(BF16)
                for (own, _, _), part in zip(blocks, turned_parts)
            ],
            axis=0,
        )
        gk = turn_back(acc_k[...], slice(0, length)).astype(BF16)
        gv = acc_v[...].astype(BF16)
        row, pair = step // pairs, step % pairs
        at_rows = pl.ds(pl.multiple_of(row * length, length), length)
        at_lanes = pl.ds(pl.multiple_of(pair * LANES, LANES), LANES)
        for i, grad in enumerate((gq, gk, gv)):
            at_grad = pl.ds(pl.multiple_of((i * pairs + pair) * LANES, LANES), LANES)
            grads_all[at_rows, at_grad] = grad
            line = SUM_QKV + i
            small_ref[line : line + 1, at_lanes] += jnp.sum(
                grad.astype(F32), axis=0, keepdims=True
            )

    @pl.when(step == units)
    def _():
        hand_on.start()
        fetch.wait()

    @pl.when(step >= units)
    def _():
        sending = step == units
        height = send_ref.shape[1]
        core = jnp.where(sending, 1 - where[1], where[1])
        left = [
            turned[pl.ds(pl.multiple_of((2 * half + core) * height, 16), height), :]
            for half in (1 - where[0], where[0])
        ]
        value = dot_nn(jnp.concatenate(left, axis=0), grads_all[...]).astype(BF16)
        put_blocks(
            send_ref, keep_ref, sending, (0, 1), slice(None), (value[:height], value[height:])
        )

    @pl.when(step == units + 1)
    def _():
        hand_on.wait()


def attend_back(where, q, k, v, grad_context, probs, cosine, sine, turned, sums):
    tokens, width = q.shape
    rows, pairs, depth = probs.shape[:3]
    length = tokens // rows
    units = rows * pairs
    height = width // 4

    def at(s):
        s = jnp.minimum(s, units - 1)
        return s // pairs, s % pairs

    head = pl.BlockSpec((length, LANES), lambda s, *_: at(s))
    table = pl.BlockSpec((length, LANES), lambda s, *_: (at(s)[0], 0))
    shape = jax.ShapeDtypeStruct
    return pl.pallas_call(
        functools.partial(attend_back_kernel, rows),
        grid_spec=pltpu.PrefetchScalarGridSpec(
            num_scalar_prefetch=1,
            grid=(units + 2,),
            in_specs=[head] * 4
            + [
                pl.BlockSpec((1, 1, depth, 2 * LANES), lambda s, *_: at(s) + (0, 0)),
                table,
                table,
                whole(*sums.shape),
                ANY,
            ],
            out_specs=[
                whole(*sums.shape),
                send_spec(1, height, 3 * width, units),
                keep_spec(1, height, 3 * width, units),
                ANY,
            ],
            scratch_shapes=[pltpu.VMEM((length, LANES), F32)] * 2
            + [
                pltpu.VMEM((tokens, 3 * width), BF16),
                pltpu.VMEM((width, tokens), BF16),
                pltpu.SemaphoreType.DMA((2,)),
            ],
        ),
        out_shape=[shape(sums.shape, F32)]
        + [shape((2, height, 3 * width), BF16)] * 2
        + [shape((tokens, 3 * width), BF16)],
        compiler_params=params(60),
        cost_estimate=LIGHT,
        name="attend_back",
    )(where, q, k, v, grad_context, probs, cosine, sine, sums, turned)


def norm_parts(values):
    mean = jnp.mean(values, axis=-1, keepdims=True)
    center = values - mean
    spread = jnp.mean(center * center, axis=-1, keepdims=True)
    scale = lax.rsqrt(spread + EPSILON)
    return center * scale, scale


def norm_back(grads, gain, normal, scale):
    inner = grads * gain
    return scale * (
        inner
        - jnp.mean(inner, axis=-1, keepdims=True)
        - normal * jnp.mean(inner * normal, axis=-1, keepdims=True)
    )


def gelu_parts(values):
    share = 0.5 + 0.5 * lax.erf(values * 0.7071067811865476)
    return share, jnp.exp(values * values * -0.5) * 0.3989422804014327


def down_copies(down, rows, wd, sems):
    scale = wd.shape[0] // wd.shape[1]
    starts = [rows[i] * scale for i in range(len(down))]
    return piece_copies(down, starts, wd, 0, sems, 0)


def feed_up_kernel(count, rows, ctx_ref, x_ref, vec, bu, *refs):
    own, pieces = refs[:2], refs[2 : 2 + count]
    normal_ref, scale_ref, act_ref, slope_ref, joined, lows, sems = refs[2 + count :]
    width = x_ref.shape[1]
    step, last = pl.program_id(0), pl.num_programs(0) - 1

    def norm_stage():
        bo, g1, s1 = (vec[i : i + 1, :] for i in range(3))
        attended = dot_nn(ctx_ref[...], joined[:, :width]) + bo
        normal, scale = norm_parts(x_ref[...].astype(F32) + attended)
        normal = normal.astype(BF16)
        normal_ref[...] = normal
        scale_ref[...] = scale
        lows[pl.ds(step % 2, 1)] = (normal.astype(F32) * g1 + s1).astype(BF16)[None]

    def wide_stage(between):
        low = lows[pl.ds((step + 1) % 2, 1)][0]
        chunks = list(range(0, bu.shape[1], CHUNK))

        def product(c):
            return dot_nn(low, joined[:, width + c : width + c + CHUNK])

        ahead = product(0)
        for n, c in enumerate(chunks):
            hidden = ahead + bu[:, c : c + CHUNK]
            if n + 1 < len(chunks):
                ahead = product(chunks[n + 1])
            share, density = gelu_parts(hidden)
            act_ref[:, c : c + CHUNK] = (hidden * share).astype(BF16)
            slope_ref[:, c : c + CHUNK] = (share + hidden * density).astype(BF16)
            if n == 1:
                between()

    @pl.when(step == 0)
    def _():
        sooner, later = joined_copies(own, pieces, rows, joined, sems, width)
        for copy in sooner + later:
            copy.start()
        for copy in sooner:
            copy.wait()
        norm_stage()
        for copy in later:
            copy.wait()

    @pl.when((step > 0) & (step < last))
    def _():
        wide_stage(norm_stage)

    @pl.when(step == last)
    def _():
        wide_stage(lambda: None)


def feed_up(ctx, x, joined, vec, bu):
    own, pieces, rows = joined
    count = len(pieces)
    tokens, width = x.shape
    hidden = bu.shape[1]
    steps = tokens // TILE

    def now(columns):
        return pl.BlockSpec((TILE, columns), lambda s: (jnp.minimum(s, steps - 1), 0))

    def late(columns):
        return pl.BlockSpec((TILE, columns), lambda s: (jnp.maximum(s - 1, 0), 0))

    shape = jax.ShapeDtypeStruct
    return pl.pallas_call(
        functools.partial(feed_up_kernel, count),
        grid=(steps + 1,),
        in_specs=[SMEM, now(width), now(width), whole(*vec.shape), whole(*bu.shape)]
        + [ANY] * (2 + count),
        out_specs=[now(width), now(1), late(hidden), late(hidden)],
        out_shape=[
            shape((tokens, width), BF16),
            shape((tokens, 1), F32),
            shape((tokens, hidden), BF16),
            shape((tokens, hidden), BF16),
        ],
        scratch_shapes=[
            pltpu.VMEM((width, width + hidden), BF16),
            pltpu.VMEM((2, TILE, width), BF16),
            pltpu.SemaphoreType.DMA((SPLITS * (2 + 2 * count),)),
        ],
        compiler_params=params(60),
        cost_estimate=LIGHT,
        name="feed_up",
    )(rows, ctx, x, vec, bu, *own, *pieces)


def feed_down_kernel(count, steps, where, rows, normal_ref, cot_ref, vec, act_any, *refs):
    down = refs[:count]
    small_ref, send_ref, keep_ref, res_any, gd_any = refs[count : count + 5]
    wd, act, products, res, grads_all, sems, sems_act, sems_out = refs[count + 5 :]
    step = pl.program_id(0)
    tile = cot_ref.shape[0]

    def stores(i):
        span = pl.ds(i * tile, tile)
        return [
            pltpu.make_async_copy(s.at[span, :], d.at[span, :], sems_out.at[j * steps + i])
            for j, (s, d) in enumerate(((res, res_any), (grads_all, gd_any)))
        ]

    def load(i):
        span = pl.ds(i * tile, tile)
        return pltpu.make_async_copy(act_any.at[span, :], act.at[span, :], sems_act.at[i])

    def product_stage(i):
        products[i % 2] = dot_nn(act[i * tile : (i + 1) * tile, :], wd[...])

    def norm_stage(i):
        span = slice(i * tile, (i + 1) * tile)
        g1, s1, bd, g2, s2 = (vec[j : j + 1, :] for j in range(1, 6))
        normed = normal_ref[...].astype(F32) * g1 + s1
        normal2, scale2 = norm_parts(normed + (products[i % 2] + bd))
        res[span, :] = normal2 * g2 + s2
        cot = cot_ref[...].astype(F32)
        low = norm_back(cot, g2, normal2, scale2).astype(BF16)
        grads_all[span, :] = low
        for j, value in enumerate((cot * normal2, cot, low.astype(F32))):
            line = SUM_FFN + j
            small_ref[line : line + 1, :] += jnp.sum(value, axis=0, keepdims=True)

    for i in range(steps + 1):

        @pl.when(step == i)
        def _():
            if i == 0:
                small_ref[...] = jnp.zeros_like(small_ref)
                copies = down_copies(down, rows, wd, sems)
                for copy in [load(0)] + copies + [load(j) for j in range(1, steps)]:
                    copy.start()
                for copy in copies:
                    copy.wait()
            if i < steps:
                load(i).wait()
                product_stage(i)
            if i > 0:
                norm_stage(i - 1)
                for copy in stores(i - 1):
                    copy.start()

    @pl.when(step > steps)
    def _():
        product_step = step - steps - 1
        height = send_ref.shape[1]
        sending = product_step < 2
        core = jnp.where(sending, 1 - where[1], where[1])
        half = jnp.where(product_step % 2 == 0, 1 - where[0], where[0])
        at_left = pl.ds(pl.multiple_of((2 * half + core) * height, LANES), height)
        value = dot_tn(act[:, at_left], grads_all[...]).astype(BF16)
        put_blocks(send_ref, keep_ref, sending, (0,), slice(None), (value,))

    @pl.when(step == steps + 4)
    def _():
        for i in range(steps):
            for copy in stores(i):
                copy.wait()


def feed_down(where, act, normal, cot, down, rows, vec):
    count = len(down)
    tokens, width = cot.shape
    wide = act.shape[1]
    steps = tokens // TILE
    height = wide // 4
    late = pl.BlockSpec((TILE, width), lambda s, *_: (jnp.clip(s - 1, 0, steps - 1), 0))
    shape = jax.ShapeDtypeStruct
    return pl.pallas_call(
        functools.partial(feed_down_kernel, count, steps),
        grid_spec=pltpu.PrefetchScalarGridSpec(
            num_scalar_prefetch=1,
            grid=(steps + 5,),
            in_specs=[SMEM, late, late, whole(*vec.shape)] + [ANY] * (1 + count),
            out_specs=[whole(SUM_ROWS, width)]
            + [send_spec(2, height, width, steps + 1), keep_spec(2, height, width, steps + 1)]
            + [ANY] * 2,
            scratch_shapes=[
                pltpu.VMEM((wide, width), BF16),
                pltpu.VMEM((tokens, wide), BF16),
                pltpu.VMEM((2, TILE, width), F32),
                pltpu.VMEM((tokens, width), F32),
                pltpu.VMEM((tokens, width), BF16),
                pltpu.SemaphoreType.DMA((SPLITS * count,)),
                pltpu.SemaphoreType.DMA((steps,)),
                pltpu.SemaphoreType.DMA((2 * steps,)),
            ],
        ),
        out_shape=[shape((SUM_ROWS, width), F32)]
        + [shape((2, height, width), BF16)] * 2
        + [shape((tokens, width), F32), shape((tokens, width), BF16)],
        compiler_params=params(60),
        cost_estimate=LIGHT,
        name="feed_down",
    )(where, rows, normal, cot, vec, act, *down)


def feed_back_kernel(
    count, steps, where, rows, gd_ref, slope_ref, normal_ref, scale_ref, vec, sums_ref, ctx_any,
    *refs,
):
    own, pieces = refs[:2], refs[2 : 2 + count]
    down = refs[2 + count : 3 + 2 * count]
    small_ref, send_ref, keep_ref, ga_any, gc_any = refs[3 + 2 * count : 8 + 2 * count]
    (
        joined, wd, low, ctx, hidden_all, attended_all, grad_sums, gc, wide,
        sems, sems_down, sem_ctx, sems_out,
    ) = refs[8 + 2 * count :]
    tile, width = gd_ref.shape
    hidden = wide.shape[1]
    step = pl.program_id(0)
    load_ctx = pltpu.make_async_copy(ctx_any, ctx, sem_ctx.at[0])

    def stores(i):
        span = pl.ds(i * tile, tile)
        return [
            pltpu.make_async_copy(s.at[span, :], d.at[span, :], sems_out.at[j * steps + i])
            for j, (s, d) in enumerate(((attended_all, ga_any), (gc, gc_any)))
        ]

    def norm_stage(i):
        span = slice(i * tile, (i + 1) * tile)
        grad_normed, normal = grad_sums[i % 2], normal_ref[...].astype(F32)
        low[span, :] = (normal * vec[1:2, :] + vec[2:3, :]).astype(BF16)
        rounded = norm_back(grad_normed, vec[1:2, :], normal, scale_ref[...]).astype(BF16)
        attended_all[span, :] = rounded
        for j, value in enumerate((grad_normed * normal, grad_normed, rounded.astype(F32))):
            line = SUM_ATTN + j
            small_ref[line : line + 1, :] += jnp.sum(value, axis=0, keepdims=True)
        gc[span, :] = dot_nt(rounded, joined[:, :width]).astype(BF16)

    def wide_stage(i, between):
        span = slice(i * tile, (i + 1) * tile)
        chunks = list(range(0, hidden, CHUNK))

        def product(c):
            return dot_nt(gd_ref[...], wd[c : c + CHUNK, :])

        ahead = product(0)
        if i == 0:
            for copy in joined_copies(own, pieces, rows, joined, sems):
                copy.wait()
        total = gd_ref[...].astype(F32)
        for n, c in enumerate(chunks):
            grad_active = ahead
            if n + 1 < len(chunks):
                ahead = product(chunks[n + 1])
            rounded = (grad_active * slope_ref[:, c : c + CHUNK].astype(F32)).astype(BF16)
            hidden_all[span, c : c + CHUNK] = rounded
            wide[0:1, c : c + CHUNK] += jnp.sum(rounded.astype(F32), axis=0, keepdims=True)
            total = total + dot_nt(rounded, joined[:, width + c : width + c + CHUNK])
            if n == 1:
                between()
        grad_sums[i % 2] = total

    for i in range(steps + 1):

        @pl.when(step == i)
        def _():
            if i == 0:
                copies = down_copies(down, rows, wd, sems_down)
                for copy in copies + joined_copies(own, pieces, rows, joined, sems) + [load_ctx]:
                    copy.start()
                small_ref[...] = sums_ref[...]
                wide[...] = jnp.zeros_like(wide)
                for copy in copies:
                    copy.wait()
            if i == steps:
                norm_stage(i - 1)
                for j in range(hidden // width):
                    line = SUM_UP + j
                    small_ref[line : line + 1, :] = wide[0:1, j * width : (j + 1) * width]
                load_ctx.wait()
            else:
                wide_stage(i, (lambda: norm_stage(i - 1)) if i > 0 else (lambda: None))
            if i > 0:
                for copy in stores(i - 1):
                    copy.start()

    @pl.when(step > steps)
    def _():
        sending = step == steps + 1
        core = jnp.where(sending, 1 - where[1], where[1])
        height, cut = width // 2, hidden // 2
        at_wide = pl.ds(pl.multiple_of(core * cut, LANES), cut)
        at_narrow = pl.ds(pl.multiple_of(core * height, LANES), height)
        slots = (jnp.where(where[0] == 0, 1, 0), jnp.where(where[0] == 0, 0, 1))
        value = dot_tn(low[...], hidden_all[:, at_wide]).astype(BF16)
        put_blocks(
            send_ref, keep_ref, sending, slots, slice(0, cut), (value[:height], value[height:])
        )
        value = dot_tn(ctx[...], attended_all[:, at_narrow]).astype(BF16)
        put_blocks(
            send_ref, keep_ref, sending, slots, slice(cut, cut + height),
            (value[:height], value[height:]),
        )

    @pl.when(step == steps + 2)
    def _():
        for i in range(steps):
            for copy in stores(i):
                copy.wait()


def feed_back(where, gd, slope, normal, scale, joined, down, vec, context, sums):
    own, pieces, rows = joined
    count = len(pieces)
    tokens, width = gd.shape
    wide = slope.shape[1]
    steps = tokens // TILE
    total = (wide + width) // 2

    def now(columns):
        return pl.BlockSpec((TILE, columns), lambda s, *_: (jnp.minimum(s, steps - 1), 0))

    def late(columns):
        return pl.BlockSpec((TILE, columns), lambda s, *_: (jnp.clip(s - 1, 0, steps - 1), 0))

    shape = jax.ShapeDtypeStruct
    return pl.pallas_call(
        functools.partial(feed_back_kernel, count, steps),
        grid_spec=pltpu.PrefetchScalarGridSpec(
            num_scalar_prefetch=1,
            grid=(steps + 3,),
            in_specs=[SMEM, now(width), now(wide), late(width), late(1)]
            + [whole(*vec.shape), whole(*sums.shape)]
            + [ANY] * (4 + 2 * count),
            out_specs=[whole(*sums.shape)]
            + [send_spec(1, width // 2, total, steps + 1)]
            + [keep_spec(1, width // 2, total, steps + 1)]
            + [ANY] * 2,
            scratch_shapes=[
                pltpu.VMEM((width, width + wide), BF16),
                pltpu.VMEM((wide, width), BF16),
                pltpu.VMEM((tokens, width), BF16),
                pltpu.VMEM((tokens, width), BF16),
                pltpu.VMEM((tokens, wide), BF16),
                pltpu.VMEM((tokens, width), BF16),
                pltpu.VMEM((2, TILE, width), F32),
                pltpu.VMEM((tokens, width), BF16),
                pltpu.VMEM((8, wide), F32),
                pltpu.SemaphoreType.DMA((SPLITS * (2 + count),)),
                pltpu.SemaphoreType.DMA((SPLITS * (1 + count),)),
                pltpu.SemaphoreType.DMA((1,)),
                pltpu.SemaphoreType.DMA((2 * steps,)),
            ],
        ),
        out_shape=[shape(sums.shape, F32)]
        + [shape((2, width // 2, total), BF16)] * 2
        + [shape((tokens, width), BF16)] * 2,
        compiler_params=params(60),
        cost_estimate=LIGHT,
        name="feed_back",
    )(where, rows, gd, slope, normal, scale, vec, sums, context, *own, *pieces, *down)


def inputs_back_kernel(count, rows, ga_ref, grads, *refs):
    own, pieces = refs[:3], refs[3 : 3 + count]
    out_ref, full, sems = refs[3 + count :]

    @pl.when(pl.program_id(0) == 0)
    def _():
        fetch_joined(own, pieces, rows, full, sems)

    out_ref[...] = ga_ref[...].astype(F32) + dot_nt(grads[...], full[...])


def inputs_back(grads, ga, weights):
    own, pieces, rows = weights
    tokens, width = ga.shape
    tile = pl.BlockSpec((TILE, width), lambda t: (t, 0))
    return pl.pallas_call(
        functools.partial(inputs_back_kernel, len(pieces)),
        grid=(tokens // TILE,),
        in_specs=[SMEM, tile, pl.BlockSpec((TILE, 3 * width), lambda t: (t, 0))]
        + [ANY] * (3 + len(pieces)),
        out_specs=tile,
        out_shape=jax.ShapeDtypeStruct((tokens, width), F32),
        scratch_shapes=[
            pltpu.VMEM((width, 3 * width), BF16),
            pltpu.SemaphoreType.DMA((SPLITS * (3 + len(pieces)),)),
        ],
        compiler_params=params(60),
        cost_estimate=LIGHT,
        name="inputs_back",
    )(rows, ga, grads, *own, *pieces)


CORE, NEAR_Y, NEAR_Z, FAR_Z = 1, 2, 4, 8


def after(value, *others):
    return lax.optimization_barrier((value,) + others)[0]


def swap_dp(values, bit):
    size = lax.axis_size("dp")
    return lax.ppermute(values, "dp", [(i, i ^ bit) for i in range(size)])


def swap_fsdp(values):
    return lax.ppermute(values, "fsdp", [(0, 1), (1, 0)])


def swap_both(values):
    size = lax.axis_size("dp")
    pairs = [(2 * i + h, 2 * (i ^ NEAR_Y) + 1 - h) for i in range(size) for h in range(2)]
    return lax.ppermute(values, ("dp", "fsdp"), pairs)


def rows_of(values, start, count):
    return lax.dynamic_slice_in_dim(values, start, count, axis=0)


def own_part(shards, place):
    half, core, y, z = place
    height = shards[0].shape[0]
    count = height // 8
    starts = (2 * y + core) * count, height // 2 + (2 * z + core) * count
    return jnp.concatenate(
        [jnp.concatenate([rows_of(s, start, count) for s in shards], axis=1) for start in starts],
        axis=0,
    )


def pass_on(first):
    count = first.shape[0] // 2
    return (
        first[:count],
        first[count:],
        swap_dp(first[:count], NEAR_Y),
        swap_dp(first[count:], NEAR_Z),
    )


def with_core(parts):
    return tuple(parts) + tuple(swap_dp(part, CORE) for part in parts)


def far_parts(first):
    count = first.shape[0] // 2
    left, right = first[:count], first[count:]
    return (
        swap_dp(left, NEAR_Y),
        swap_dp(right, NEAR_Z),
        swap_dp(left, NEAR_Y | CORE),
        swap_dp(right, NEAR_Z | CORE),
    )


def all_parts(first, far):
    count = first.shape[0] // 2
    other = swap_dp(first, CORE)
    return (first[:count], first[count:]) + far[:2] + (other[:count], other[count:]) + far[2:]


def piece_rows(height, place):
    half, core, y, z = place
    count = height // 8
    base = (1 - half) * height
    rows = [half * height]
    for c in (core, 1 - core):
        rows += [
            base + (2 * y + c) * count,
            base + height // 2 + (2 * z + c) * count,
            base + (2 * (1 - y) + c) * count,
            base + height // 2 + (2 * (1 - z) + c) * count,
        ]
    return jnp.stack(rows).astype(jnp.int32)


class Part:
    def __init__(self, terms, place, columns=None):
        self.bits = {0: 1, 1: place[2], 2: place[3]}
        self.swaps = {
            0: swap_fsdp,
            1: lambda v: swap_dp(v, NEAR_Y),
            2: lambda v: swap_dp(v, NEAR_Z),
            3: lambda v: swap_dp(v, FAR_Z),
        }
        self.terms = [t.reshape(2, 2, 2, t.shape[1] // 4, t.shape[2]) for t in terms]
        self.views = [(columns, ())] * len(terms)
        self.flight, self.joined = [], None

    def total(self, *picks):
        value = None
        for term, (columns, before) in zip(self.terms, self.views):
            if columns is not None:
                term = term[..., columns[0] : columns[1]]
            for axis, index in before + picks:
                term = lax.dynamic_slice_in_dim(term, index, 1, axis)
            term = term.astype(F32)
            value = term if value is None else value + term
        return value.astype(BF16)

    def cut(self, *picks):
        self.views = [(columns, before + picks) for columns, before in self.views]

    def halve(self, axis):
        bit = self.bits[axis]
        self.flight, self.route = [self.total((axis, 1 - bit))], [self.swaps[axis]]
        self.cut((axis, bit))

    def both(self):
        bit = self.bits[1]
        self.flight = [
            self.total((0, 0), (1, bit)),
            self.total((0, 1), (1, 1 - bit)),
            self.total((0, 0), (1, 1 - bit)),
        ]
        self.route = [self.swaps[0], self.swaps[1], swap_both]
        self.cut((0, 1), (1, bit))

    def merge(self, *others):
        value = jnp.concatenate([part.total() for part in (self,) + others], axis=-1)
        self.terms, self.views = [value], [(None, ())]

    def send_whole(self, swap, reshape=None):
        value = self.total() if len(self.terms) > 1 else self.terms[0]
        if reshape:
            value = value.reshape(-1, value.shape[-1])
        self.flight, self.route = [value], [lambda v: (v, swap(v))]
        self.terms, self.views = [], []

    def far(self):
        self.send_whole(self.swaps[3])

    def spread(self):
        near = (NEAR_Y, NEAR_Z, NEAR_Y | NEAR_Z)
        value = self.total() if len(self.terms) > 1 else self.terms[0]
        self.flight = [value]
        self.route = [lambda v: (v,) + tuple(swap_dp(v, bit) for bit in near)]
        self.terms, self.views, self.joined = [], [], (1, 2)

    def finish(self):
        self.send_whole(lambda v: swap_dp(v, CORE), True)

    def land(self):
        for sent, route in zip(self.flight, self.route):
            got = route(sent)
            self.terms += list(got) if isinstance(got, tuple) else [got]
        self.views = self.views + [(None, ())] * (len(self.terms) - len(self.views))
        self.flight = []

    def settle(self):
        if self.joined is None:
            return
        def order(mine, other, axis):
            return jnp.where(
                self.bits[axis] == 0,
                jnp.concatenate([mine, other], axis=axis),
                jnp.concatenate([other, mine], axis=axis),
            )

        mine, along, up, both = self.terms
        value = order(order(mine, up, 2), order(along, both, 2), 1)
        self.joined = None
        self.terms, self.views = [value], [(None, ())]


def fence(parts, *arrays):
    counts = [(len(p.terms), len(p.flight)) for p in parts]
    flat = [a for p in parts for a in p.terms + p.flight] + list(arrays)
    flat = list(lax.optimization_barrier(tuple(flat)))
    for part, (terms, flight) in zip(parts, counts):
        part.terms, flat = flat[:terms], flat[terms:]
        part.flight, flat = flat[:flight], flat[flight:]
    return flat


def widen(mine, other, core, axis):
    low = jnp.where(core == 0, mine, other).astype(F32)
    high = jnp.where(core == 0, other, mine).astype(F32)
    return jnp.concatenate([low, high], axis=axis)


def gather_all(values):
    return lax.all_gather(values, "fsdp", axis=0, tiled=True)


def sum_plain(send, keep, by_rows):
    blocks = [[keep[1], send[1]], [keep[0], send[0]]]
    axis = 0 if by_rows else 1
    value = jnp.concatenate([jnp.concatenate(pair, axis=axis) for pair in blocks], axis=0)
    own = lax.psum_scatter(value, "fsdp", scatter_dimension=0, tiled=True)
    return lax.psum(own, "dp").astype(F32)


def local(
    inputs, segment_ids, cotangent, w_query, b_query, w_key, b_key, w_value, b_value,
    w_output, b_output, gain_attn, bias_attn, w_up, b_up, w_down, b_down, gain_ffn, bias_ffn,
):
    rows, length = segment_ids.shape
    width = inputs.shape[1]
    shards = lax.axis_size("fsdp")
    paired = shards == 2 and lax.axis_size("dp") == 16
    half = lax.axis_index("fsdp")
    dp = lax.axis_index("dp")
    place = (half, dp % 2, dp // 2 % 2, dp // 4 % 2)
    core = place[1]
    vectors = (b_query, b_key, b_value, b_output, gain_attn, bias_attn, b_down, gain_ffn, bias_ffn)
    height = w_query.shape[0]
    cosine, sine, turned = rotary_tables(segment_ids, inputs)
    if paired:
        where = jnp.stack([half, core]).astype(jnp.int32)
        part_qkv = own_part((w_query, w_key, w_value), place)
        part_up = own_part((w_output, w_up), place)
        part_down = own_part((w_down,), place)
        here_qkv = swap_fsdp(part_qkv)
        lines = jnp.concatenate(vectors + (b_up,)).reshape(-1, height)
        other = swap_fsdp(after(lines, part_qkv))
        here_up = swap_fsdp(after(part_up, here_qkv))
        at = piece_rows(height, place)
        joined_qkv = ((w_query, w_key, w_value), with_core(pass_on(here_qkv)), at)
        lines = jnp.where(half == 0, jnp.stack([lines, other]), jnp.stack([other, lines]))
    else:
        where = jnp.zeros((2,), jnp.int32)
        at = jnp.zeros((1,), jnp.int32)
        joined_qkv = (tuple(gather_all(w) for w in (w_query, w_key, w_value)), (), at)
        joined_up = ((gather_all(w_output), gather_all(w_up)), (), at)
        down = (gather_all(w_down),)
        lines = jnp.concatenate(vectors + (b_up,)).reshape(-1, height)
        lines = lax.all_gather(lines, "fsdp", axis=0)
    lines = lines.astype(F32)
    vec = jnp.swapaxes(lines[:, :9], 0, 1).reshape(9, width)
    bias_up = lines[:, 9:].reshape(1, -1)

    q, k, v = project(inputs, joined_qkv, vec[:3], cosine, sine)
    vec = vec[3:]
    if paired:
        q, here_up, part_down = lax.optimization_barrier((q, here_up, part_down))
        here_down = swap_fsdp(part_down)
        far_up = far_parts(here_up)
    context, probs = attend(q, k, v, segment_ids)
    if paired:
        context, probs, here_up, here_down, far_up = lax.optimization_barrier(
            (context, probs, here_up, here_down, far_up)
        )
        joined_up = ((w_output, w_up), all_parts(here_up, far_up), at)
        context, joined_up, here_down = lax.optimization_barrier((context, joined_up, here_down))
        far_down = far_parts(here_down)
    normal, scale, act, slope = feed_up(context, inputs, joined_up, vec, bias_up)
    if paired:
        act, slope, here_down, far_down = lax.optimization_barrier(
            (act, slope, here_down, far_down)
        )
        down = (w_down,) + all_parts(here_down, far_down)
    sums, send, keep, result, grad_down = feed_down(
        where, act, normal, cotangent, down, at, vec
    )
    sent = [(send, keep)]
    if paired:
        sum_d = Part([keep, swap_dp(send, CORE)], place)
        sum_d.both()
        (grad_down,) = fence([sum_d], grad_down)
    outs = feed_back(
        where, grad_down, slope, normal, scale, joined_up, down, vec, context, sums
    )
    if paired:
        sum_d.land()
        outs = fence([sum_d], *outs)
    sums, send, keep, grad_attended, grad_context = outs
    sent.append((send, keep))
    if paired:
        sum_u = Part([keep, swap_dp(send, CORE)], place)
        sum_d.halve(2)
        sum_u.both()
        parts = [sum_d, sum_u]
        (grad_context,) = fence(parts, grad_context)
    outs = attend_back(where, q, k, v, grad_context, probs, cosine, sine, turned, sums)
    if paired:
        for p in parts:
            p.land()
        outs = fence(parts, *outs)
    sums, send, keep, grads = outs
    sent.append((send, keep))
    if paired:
        sum_q = Part([keep, swap_dp(send, CORE)], place)
        sum_d.far()
        sum_u.halve(2)
        sum_q.both()
        parts = [sum_d, sum_u, sum_q]
        grad_attended, sums = fence(parts, grad_attended, sums)
    grad_inputs = inputs_back(grads, grad_attended, joined_qkv)
    if paired:
        for p in parts:
            p.land()
        grad_inputs, sums, other = fence(parts, grad_inputs, sums, swap_dp(sums, CORE))
        sums = sums + other
        rounds = (
            (("spread",), ("far",), ("halve", 2)),
            (("finish",), ("spread",), ("far",)),
            ((), ("finish",), ("spread",)),
            ((), (), ("finish",)),
        )
        routes = (
            swap_fsdp,
            lambda v: swap_dp(v, NEAR_Y),
            lambda v: swap_dp(v, NEAR_Z),
            lambda v: swap_dp(v, FAR_Z),
        )
        for n, moves in enumerate(rounds):
            moving = [(p, move) for p, move in zip(parts, moves) if move]
            for p, (name, *axis) in moving:
                p.settle()
                getattr(p, name)(*axis)
            moving = [p for p, _ in moving]
            if n < len(routes):
                (sums,) = fence(moving, sums)
                other = routes[n](sums)
                for p in moving:
                    p.land()
                sums, other = fence(moving, sums, other)
                sums = sums + other
            else:
                fence(moving)
                for p in moving:
                    p.land()
                fence(moving)
    else:
        sums = lax.psum(sums, ("dp", "fsdp"))

    def own(line, count=1):
        line = line * width + half * (count * width // shards)
        return lax.dynamic_slice_in_dim(sums.reshape(-1), line, count * width // shards, axis=0)

    wide = b_up.shape[0] * shards
    ggf, gbf, gbd = (own(SUM_FFN + i) for i in range(3))
    gga, gba, gbo = (own(SUM_ATTN + i) for i in range(3))
    gbq, gbk, gbv = (own(SUM_QKV + i) for i in range(3))
    gbu = own(SUM_UP, wide // width)
    if paired:
        gwd = widen(*sum_d.terms, core, 0)
        cut = wide // 2
        mine, other = sum_u.terms
        gwu = widen(mine[:, :cut], other[:, :cut], core, 1)
        gwo = widen(mine[:, cut:], other[:, cut:], core, 1)
        gwq, gwk, gwv = (
            widen(*(end[:, i * width : (i + 1) * width] for end in sum_q.terms), core, 0)
            for i in range(3)
        )
    else:
        gwd = sum_plain(*sent[0], True)
        both = sum_plain(*sent[1], False).reshape(height, 2, -1)
        cut = wide // 2
        gwu = both[..., :cut].reshape(height, -1)
        gwo = both[..., cut:].reshape(height, -1)
        both = sum_plain(*sent[2], True)
        gwq, gwk, gwv = (both[:, i * width : (i + 1) * width] for i in range(3))
    return (
        result, grad_inputs, gwq, gbq, gwk, gbk, gwv, gbv, gwo, gbo, gga, gba,
        gwu, gbu, gwd, gbd, ggf, gbf,
    )


def solution(mesh):
    tokens, matrix, vector = P(("dp", "fsdp"), None), P("fsdp", None), P("fsdp")
    weights = (
        matrix, vector, matrix, vector, matrix, vector, matrix, vector, vector, vector,
        matrix, vector, matrix, vector, vector, vector,
    )
    return jax.shard_map(
        local,
        mesh=mesh,
        in_specs=(tokens,) * 3 + weights,
        out_specs=(tokens,) * 2 + weights,
        check_vma=False,
    )
```

```python
import copy
import functools
import jax
import jax.numpy as jnp
from jax import lax
from jax.experimental import pallas as pl
from jax.experimental.pallas import tpu as pltpu
from jax.sharding import PartitionSpec as P

HEAD = 64
EPSILON = 1e-06
LANES = 128
TILE = 256
CHUNK = 512
MASKED = -1e30
SUM_FFN, SUM_ATTN, SUM_UP, SUM_QKV, SUM_ROWS = 0, 3, 6, 10, 16
F32 = jnp.float32
BF16 = jnp.bfloat16


def params(mebibytes):
    return pltpu.CompilerParams(vmem_limit_bytes=mebibytes * 1024 * 1024)


LIGHT = pl.CostEstimate(flops=1000, bytes_accessed=1000, transcendentals=0)


def dot_nn(left, right):
    return lax.dot_general(left, right, (((1,), (0,)), ((), ())), preferred_element_type=F32)


def dot_nt(left, right):
    return lax.dot_general(left, right, (((1,), (1,)), ((), ())), preferred_element_type=F32)


def dot_tn(left, right):
    return lax.dot_general(left, right, (((0,), (0,)), ((), ())), preferred_element_type=F32)


def whole(*shape):
    return pl.BlockSpec(shape, lambda *_: (0,) * len(shape))


SPLITS = 4


def piece_copies(pieces, starts, full, column, sems, first):
    copies = []
    for i, (piece, start) in enumerate(zip(pieces, starts)):
        height, width = piece.shape
        splits = SPLITS if height * width >= 500_000 and height % (16 * SPLITS) == 0 else 1
        count = height // splits
        for j in range(splits):
            row = pl.multiple_of(start + j * count, 16)
            copies.append(
                pltpu.make_async_copy(
                    piece.at[pl.ds(j * count, count), :],
                    full.at[pl.ds(row, count), column : column + width],
                    sems.at[SPLITS * (first + i) + j],
                )
            )
    return copies


def joined_copies(own, pieces, rows, full, sems, cut=None):
    shards, column = [], 0
    for i, shard in enumerate(own):
        shards.append(piece_copies([shard], [rows[0]], full, column, sems, i))
        column += shard.shape[1]
    starts = [rows[1 + i] for i in range(len(pieces))]
    first = len(own)
    if cut is None:
        return sum(shards, []) + piece_copies(pieces, starts, full, 0, sems, first)
    left = [piece.at[:, :cut] for piece in pieces]
    right = [piece.at[:, cut:] for piece in pieces]
    return (
        shards[0] + piece_copies(left, starts, full, 0, sems, first),
        sum(shards[1:], []) + piece_copies(right, starts, full, cut, sems, first + len(pieces)),
    )


def fetch_joined(own, pieces, rows, full, sems):
    copies = joined_copies(own, pieces, rows, full, sems)
    for copy in copies:
        copy.start()
    for copy in copies:
        copy.wait()


ANY = pl.BlockSpec(memory_space=pl.ANY)
SMEM = pl.BlockSpec(memory_space=pltpu.SMEM)


def tables_kernel(seg_row, seg_col, x_ref, cos_ref, sin_ref, turned_ref):
    length = seg_row.shape[-1]
    key = lax.broadcasted_iota(jnp.int32, (length, length), 1)
    query = lax.broadcasted_iota(jnp.int32, (length, length), 0)
    earlier = (seg_col[...] == seg_row[0]) & (key < query)
    place = jnp.sum(earlier.astype(F32), axis=1, keepdims=True)
    lane = lax.broadcasted_iota(jnp.int32, (1, LANES), 1)
    paired = (lane % HEAD // 2 * 2).astype(F32)
    freqs = jnp.exp(-jnp.log(F32(10000.0)) * paired / HEAD)
    angle = place * freqs
    cos_ref[...] = jnp.cos(angle)
    sine = jnp.sin(angle)
    sin_ref[...] = jnp.where(lane % 2 == 0, -sine, sine)
    turned_ref[...] = x_ref[...].T


def rotary_tables(segments, x):
    rows, length = segments.shape
    width = x.shape[1]
    return pl.pallas_call(
        tables_kernel,
        grid=(rows,),
        in_specs=[
            pl.BlockSpec((1, 1, length), lambda r: (r, 0, 0)),
            pl.BlockSpec((length, 1), lambda r: (r, 0)),
            pl.BlockSpec((length, width), lambda r: (r, 0)),
        ],
        out_specs=[pl.BlockSpec((length, LANES), lambda r: (r, 0))] * 2
        + [pl.BlockSpec((width, length), lambda r: (0, r))],
        out_shape=[jax.ShapeDtypeStruct((rows * length, LANES), F32)] * 2
        + [jax.ShapeDtypeStruct((width, rows * length), BF16)],
        compiler_params=params(60),
        cost_estimate=LIGHT,
        name="rotary_tables",
    )(segments.reshape(rows, 1, length), segments.reshape(rows * length, 1), x)


def pair_swap(values):
    even = lax.broadcasted_iota(jnp.int32, values.shape, 1) % 2 == 0
    return jnp.where(
        even, pltpu.roll(values, LANES - 1, axis=1), pltpu.roll(values, 1, axis=1)
    )


def project_kernel(count, rows, x_ref, bias, cos_ref, sin_ref, *refs):
    own, pieces = refs[:3], refs[3 : 3 + count]
    q_ref, k_ref, v_ref, full, sems = refs[3 + count :]
    width = x_ref.shape[1]

    @pl.when(pl.program_id(0) == 0)
    def _():
        fetch_joined(own, pieces, rows, full, sems)

    x = x_ref[...]
    cosine, sine = cos_ref[...], sin_ref[...]
    step = 2 * LANES
    for i, out in enumerate((q_ref, k_ref, v_ref)):
        for c in range(0, width, step):
            lin = dot_nn(x, full[:, i * width + c : i * width + c + step])
            lin = lin + bias[i : i + 1, c : c + step]
            if i < 2:
                parts = []
                for d in range(0, step, LANES):
                    part = lin[:, d : d + LANES]
                    part = part * cosine + pair_swap(part) * sine
                    parts.append(part)
                lin = jnp.concatenate(parts, axis=1)
            if i == 0:
                out[:, c : c + step] = (lin.astype(BF16).astype(F32) * 0.125).astype(BF16)
            else:
                out[:, c : c + step] = lin.astype(BF16)


def project(x, weights, bias, cosine, sine):
    own, pieces, rows = weights
    tokens, width = x.shape
    tile = pl.BlockSpec((TILE, width), lambda t: (t, 0))
    table = pl.BlockSpec((TILE, LANES), lambda t: (t, 0))
    return pl.pallas_call(
        functools.partial(project_kernel, len(pieces)),
        grid=(tokens // TILE,),
        in_specs=[SMEM, tile, whole(*bias.shape), table, table] + [ANY] * (3 + len(pieces)),
        out_specs=[tile] * 3,
        out_shape=[jax.ShapeDtypeStruct((tokens, width), BF16)] * 3,
        scratch_shapes=[
            pltpu.VMEM((width, 3 * width), BF16),
            pltpu.SemaphoreType.DMA((SPLITS * (3 + len(pieces)),)),
        ],
        compiler_params=params(60),
        cost_estimate=LIGHT,
        name="project",
    )(rows, x, bias, cosine, sine, *own, *pieces)


def spans(length):
    found, offset = [], 0
    for first in range(0, length, LANES):
        low, high = max(first - LANES, 0), min(first + 2 * LANES, length)
        found.append((slice(first, first + LANES), slice(low, high), slice(offset, offset + high - low)))
        offset += high - low
    return found, offset


def split_heads(values):
    lane = lax.broadcasted_iota(jnp.int32, (1, LANES), 1)
    return [jnp.where(lane // HEAD == h, values, jnp.zeros_like(values)) for h in range(2)]


def stack_heads(heads, rows):
    return jnp.concatenate([head[rows, :] for head in heads], axis=0)


def merge_heads(stacked):
    lane = lax.broadcasted_iota(jnp.int32, (1, LANES), 1)
    half = stacked.shape[0] // 2
    return jnp.where(lane < HEAD, stacked[:half], stacked[half:])


def attend_kernel(q_ref, k_ref, v_ref, seg_row, seg_col, ctx_ref, prob_ref, bias):
    blocks, _ = spans(q_ref.shape[0])

    @pl.when(pl.program_id(1) == 0)
    def _():
        for own, span, at in blocks:
            bias[at, :] = jnp.where(seg_col[span, :] == seg_row[0, :, own], 0.0, MASKED)

    queries = split_heads(q_ref[...])
    scores = [dot_nt(k_ref[span, :], stack_heads(queries, own)) for own, span, _ in blocks]
    probs = []
    for (own, span, at), pair in zip(blocks, scores):
        heads = []
        for h in range(2):
            masked = pair[:, h * LANES : (h + 1) * LANES] + bias[at, :]
            peak = jnp.max(masked, axis=0, keepdims=True)
            expo = jnp.exp(masked - peak)
            total = jnp.sum(expo, axis=0, keepdims=True)
            heads.append((expo * (1.0 / total)).astype(BF16))
        probs.append(jnp.concatenate(heads, axis=1))
    for (own, span, at), prob in zip(blocks, probs):
        prob_ref[0, 0, at, :] = prob
        ctx_ref[own, :] = merge_heads(dot_tn(prob, v_ref[span, :])).astype(BF16)


def attend(q, k, v, segments):
    rows, length = segments.shape
    tokens, width = q.shape
    pairs = width // LANES
    _, depth = spans(length)
    head = pl.BlockSpec((length, LANES), lambda r, p: (r, p))
    return pl.pallas_call(
        attend_kernel,
        grid=(rows, pairs),
        in_specs=[head] * 3
        + [
            pl.BlockSpec((1, 1, length), lambda r, p: (r, 0, 0)),
            pl.BlockSpec((length, 1), lambda r, p: (r, 0)),
        ],
        out_specs=[
            head,
            pl.BlockSpec((1, 1, depth, 2 * LANES), lambda r, p: (r, p, 0, 0)),
        ],
        out_shape=[
            jax.ShapeDtypeStruct((tokens, width), BF16),
            jax.ShapeDtypeStruct((rows, pairs, depth, 2 * LANES), BF16),
        ],
        scratch_shapes=[pltpu.VMEM((depth, LANES), F32)],
        compiler_params=params(60),
        cost_estimate=LIGHT,
        name="attend",
    )(q, k, v, segments.reshape(rows, 1, length), segments.reshape(tokens, 1))


def send_spec(steps, height, width, first):
    return pl.BlockSpec(
        (2 // steps, height, width), lambda s, *_: (jnp.clip(s - first, 0, steps - 1), 0, 0)
    )


def keep_spec(steps, height, width, first):
    return pl.BlockSpec(
        (2 // steps, height, width), lambda s, *_: (jnp.clip(s - first - steps, 0, steps - 1), 0, 0)
    )


def put_blocks(send_ref, keep_ref, sending, slots, columns, values):
    @pl.when(sending)
    def _():
        for slot, value in zip(slots, values):
            send_ref[slot, :, columns] = value

    @pl.when(jnp.logical_not(sending))
    def _():
        for slot, value in zip(slots, values):
            keep_ref[slot, :, columns] = value


LINES = (SUM_FFN, SUM_FFN + 1, SUM_FFN + 2, SUM_ATTN, SUM_ATTN + 1, SUM_ATTN + 2) + (
    SUM_QKV, SUM_QKV + 1, SUM_QKV + 2,
)


def pack_vectors(small_ref, packed, half):
    width = small_ref.shape[1]
    part = width // 2 // LANES
    packed[...] = jnp.zeros_like(packed)
    for i, line in enumerate(LINES):
        for j in range(part):
            lanes = pl.ds(pl.multiple_of(half * (width // 2) + j * LANES, LANES), LANES)
            packed[i * part + j : i * part + j + 1, :] = small_ref[line : line + 1, lanes]
    base, count = len(LINES) * part, width // LANES
    lines = (SUM_QKV - SUM_UP) // 2
    for i in range(lines):
        for j in range(count):
            row = base + i * count + j
            lanes = slice(j * LANES, (j + 1) * LANES)
            low, high = (small_ref[SUM_UP + n : SUM_UP + n + 1, lanes] for n in (i, lines + i))
            packed[row : row + 1, :] = jnp.where(half == 0, low, high)


def attend_back_kernel(
    rows, where, q_ref, k_ref, v_ref, g_ref, prob_ref, cos_ref, sin_ref, sums_ref, turned_any,
    small_ref, send_ref, keep_ref, out_any, acc_k, acc_v, grads_all, turned, packed, sems,
):
    step = pl.program_id(0)
    length = q_ref.shape[0]
    width = turned.shape[0]
    pairs = width // LANES
    units = rows * pairs
    fetch = pltpu.make_async_copy(turned_any, turned, sems.at[0])
    hand_on = pltpu.make_async_copy(grads_all, out_any, sems.at[1])

    @pl.when(step == 0)
    def _():
        fetch.start()
        small_ref[...] = sums_ref[...]

    @pl.when(step < units)
    def _():
        blocks, _ = spans(length)
        queries, grads = split_heads(q_ref[...]), split_heads(g_ref[...])
        k_t = k_ref[...].T
        acc_k[...] = jnp.zeros_like(acc_k)
        acc_v[...] = jnp.zeros_like(acc_v)

        def turn_back(values, rows):
            return values * cos_ref[rows, :] - pair_swap(values) * sin_ref[rows, :]

        grad_probs = [dot_nt(v_ref[span, :], stack_heads(grads, own)) for own, span, _ in blocks]
        grad_scores = []
        for (own, span, at), pair in zip(blocks, grad_probs):
            heads = []
            for h in range(2):
                columns = slice(h * LANES, (h + 1) * LANES)
                probs = prob_ref[0, 0, at, columns].astype(F32)
                inner = jnp.sum(probs * pair[:, columns], axis=0, keepdims=True)
                heads.append((probs * (pair[:, columns] - inner)).astype(BF16))
            grad_scores.append(jnp.concatenate(heads, axis=1))
        turned_parts = []
        for (own, span, at), low in zip(blocks, grad_scores):
            acc_k[span, :] += dot_nn(low, stack_heads(queries, own))
            acc_v[span, :] += dot_nn(prob_ref[0, 0, at, :], stack_heads(grads, own))
            product = dot_nn(k_t[:, span], low)
            both = jnp.concatenate([product[:HEAD, :LANES], product[HEAD:, LANES:]], axis=0)
            turned_parts.append(both.T)
        gq = jnp.concatenate(
            [
                turn_back(part * 0.125, own).astype(BF16)
                for (own, _, _), part in zip(blocks, turned_parts)
            ],
            axis=0,
        )
        gk = turn_back(acc_k[...], slice(0, length)).astype(BF16)
        gv = acc_v[...].astype(BF16)
        row, pair = step // pairs, step % pairs
        at_rows = pl.ds(pl.multiple_of(row * length, length), length)
        at_lanes = pl.ds(pl.multiple_of(pair * LANES, LANES), LANES)
        for i, grad in enumerate((gq, gk, gv)):
            at_grad = pl.ds(pl.multiple_of((i * pairs + pair) * LANES, LANES), LANES)
            grads_all[at_rows, at_grad] = grad
            line = SUM_QKV + i
            small_ref[line : line + 1, at_lanes] += jnp.sum(
                grad.astype(F32), axis=0, keepdims=True
            )

    @pl.when(step == units)
    def _():
        hand_on.start()
        fetch.wait()

    @pl.when(step >= units)
    def _():
        sending = step == units
        height = send_ref.shape[1]
        core = jnp.where(sending, 1 - where[1], where[1])
        left = [
            turned[pl.ds(pl.multiple_of((2 * half + core) * height, 16), height), :]
            for half in (1 - where[0], where[0])
        ]
        value = dot_nn(jnp.concatenate(left, axis=0), grads_all[...]).astype(BF16)
        put_blocks(
            send_ref, keep_ref, sending, (0, 1), slice(0, 3 * width), (value[:height], value[height:])
        )
        for slot, half in enumerate((1 - where[0], where[0])):
            pack_vectors(small_ref, packed, half)
            vectors = jnp.where(core == 0, packed[...], 0.0).astype(BF16)
            put_blocks(
                send_ref, keep_ref, sending, (slot,), slice(3 * width, 3 * width + LANES), (vectors,)
            )

    @pl.when(step == units + 1)
    def _():
        hand_on.wait()


def attend_back(where, q, k, v, grad_context, probs, cosine, sine, turned, sums):
    tokens, width = q.shape
    rows, pairs, depth = probs.shape[:3]
    length = tokens // rows
    units = rows * pairs
    height = width // 4

    def at(s):
        s = jnp.minimum(s, units - 1)
        return s // pairs, s % pairs

    head = pl.BlockSpec((length, LANES), lambda s, *_: at(s))
    table = pl.BlockSpec((length, LANES), lambda s, *_: (at(s)[0], 0))
    shape = jax.ShapeDtypeStruct
    return pl.pallas_call(
        functools.partial(attend_back_kernel, rows),
        grid_spec=pltpu.PrefetchScalarGridSpec(
            num_scalar_prefetch=1,
            grid=(units + 2,),
            in_specs=[head] * 4
            + [
                pl.BlockSpec((1, 1, depth, 2 * LANES), lambda s, *_: at(s) + (0, 0)),
                table,
                table,
                whole(*sums.shape),
                ANY,
            ],
            out_specs=[
                whole(*sums.shape),
                send_spec(1, height, 3 * width + LANES, units),
                keep_spec(1, height, 3 * width + LANES, units),
                ANY,
            ],
            scratch_shapes=[pltpu.VMEM((length, LANES), F32)] * 2
            + [
                pltpu.VMEM((tokens, 3 * width), BF16),
                pltpu.VMEM((width, tokens), BF16),
                pltpu.VMEM((height, LANES), F32),
                pltpu.SemaphoreType.DMA((2,)),
            ],
        ),
        out_shape=[shape(sums.shape, F32)]
        + [shape((2, height, 3 * width + LANES), BF16)] * 2
        + [shape((tokens, 3 * width), BF16)],
        compiler_params=params(60),
        cost_estimate=LIGHT,
        name="attend_back",
    )(where, q, k, v, grad_context, probs, cosine, sine, sums, turned)


def norm_parts(values):
    mean = jnp.mean(values, axis=-1, keepdims=True)
    center = values - mean
    spread = jnp.mean(center * center, axis=-1, keepdims=True)
    scale = lax.rsqrt(spread + EPSILON)
    return center * scale, scale


def norm_back(grads, gain, normal, scale):
    inner = grads * gain
    return scale * (
        inner
        - jnp.mean(inner, axis=-1, keepdims=True)
        - normal * jnp.mean(inner * normal, axis=-1, keepdims=True)
    )


def gelu_parts(values):
    share = 0.5 + 0.5 * lax.erf(values * 0.7071067811865476)
    return share, jnp.exp(values * values * -0.5) * 0.3989422804014327


def down_copies(down, rows, wd, sems):
    scale = wd.shape[0] // wd.shape[1]
    starts = [rows[i] * scale for i in range(len(down))]
    return piece_copies(down, starts, wd, 0, sems, 0)


def feed_up_kernel(count, rows, ctx_ref, x_ref, vec, bu, *refs):
    own, pieces = refs[:2], refs[2 : 2 + count]
    normal_ref, scale_ref, act_ref, slope_ref, joined, lows, sems = refs[2 + count :]
    width = x_ref.shape[1]
    step, last = pl.program_id(0), pl.num_programs(0) - 1

    def norm_stage():
        bo, g1, s1 = (vec[i : i + 1, :] for i in range(3))
        attended = dot_nn(ctx_ref[...], joined[:, :width]) + bo
        normal, scale = norm_parts(x_ref[...].astype(F32) + attended)
        normal = normal.astype(BF16)
        normal_ref[...] = normal
        scale_ref[...] = scale
        lows[pl.ds(step % 2, 1)] = (normal.astype(F32) * g1 + s1).astype(BF16)[None]

    def wide_stage(between):
        low = lows[pl.ds((step + 1) % 2, 1)][0]
        chunks = list(range(0, bu.shape[1], CHUNK))

        def product(c):
            return dot_nn(low, joined[:, width + c : width + c + CHUNK])

        ahead = product(0)
        for n, c in enumerate(chunks):
            hidden = ahead + bu[:, c : c + CHUNK]
            if n + 1 < len(chunks):
                ahead = product(chunks[n + 1])
            share, density = gelu_parts(hidden)
            act_ref[:, c : c + CHUNK] = (hidden * share).astype(BF16)
            slope_ref[:, c : c + CHUNK] = (share + hidden * density).astype(BF16)
            if n == 1:
                between()

    @pl.when(step == 0)
    def _():
        sooner, later = joined_copies(own, pieces, rows, joined, sems, width)
        for copy in sooner + later:
            copy.start()
        for copy in sooner:
            copy.wait()
        norm_stage()
        for copy in later:
            copy.wait()

    @pl.when((step > 0) & (step < last))
    def _():
        wide_stage(norm_stage)

    @pl.when(step == last)
    def _():
        wide_stage(lambda: None)


def feed_up(ctx, x, joined, vec, bu):
    own, pieces, rows = joined
    count = len(pieces)
    tokens, width = x.shape
    hidden = bu.shape[1]
    steps = tokens // TILE

    def now(columns):
        return pl.BlockSpec((TILE, columns), lambda s: (jnp.minimum(s, steps - 1), 0))

    def late(columns):
        return pl.BlockSpec((TILE, columns), lambda s: (jnp.maximum(s - 1, 0), 0))

    shape = jax.ShapeDtypeStruct
    return pl.pallas_call(
        functools.partial(feed_up_kernel, count),
        grid=(steps + 1,),
        in_specs=[SMEM, now(width), now(width), whole(*vec.shape), whole(*bu.shape)]
        + [ANY] * (2 + count),
        out_specs=[now(width), now(1), late(hidden), late(hidden)],
        out_shape=[
            shape((tokens, width), BF16),
            shape((tokens, 1), F32),
            shape((tokens, hidden), BF16),
            shape((tokens, hidden), BF16),
        ],
        scratch_shapes=[
            pltpu.VMEM((width, width + hidden), BF16),
            pltpu.VMEM((2, TILE, width), BF16),
            pltpu.SemaphoreType.DMA((SPLITS * (2 + 2 * count),)),
        ],
        compiler_params=params(60),
        cost_estimate=LIGHT,
        name="feed_up",
    )(rows, ctx, x, vec, bu, *own, *pieces)


def feed_down_kernel(count, steps, where, rows, normal_ref, cot_ref, vec, act_any, *refs):
    down = refs[:count]
    small_ref, send_ref, keep_ref, res_any, gd_any = refs[count : count + 5]
    wd, act, products, res, grads_all, sems, sems_act, sems_out = refs[count + 5 :]
    step = pl.program_id(0)
    tile = cot_ref.shape[0]

    def rows_at(i):
        return pl.ds(pl.multiple_of(i * tile, tile), tile)

    def stores(i):
        span = rows_at(i)
        return [
            pltpu.make_async_copy(s.at[span, :], d.at[span, :], sems_out.at[j * steps + i])
            for j, (s, d) in enumerate(((res, res_any), (grads_all, gd_any)))
        ]

    def load(i):
        span = rows_at(i)
        return pltpu.make_async_copy(act_any.at[span, :], act.at[span, :], sems_act.at[i])

    def product_stage():
        load(step).wait()
        products[pl.ds(step % 2, 1)] = dot_nn(act[rows_at(step), :], wd[...])[None]

    def norm_stage():
        span = rows_at(step - 1)
        g1, s1, bd, g2, s2 = (vec[j : j + 1, :] for j in range(1, 6))
        normed = normal_ref[...].astype(F32) * g1 + s1
        product = products[pl.ds((step + 1) % 2, 1)][0]
        normal2, scale2 = norm_parts(normed + (product + bd))
        res[span, :] = normal2 * g2 + s2
        cot = cot_ref[...].astype(F32)
        low = norm_back(cot, g2, normal2, scale2).astype(BF16)
        grads_all[span, :] = low
        for j, value in enumerate((cot * normal2, cot, low.astype(F32))):
            line = SUM_FFN + j
            small_ref[line : line + 1, :] += jnp.sum(value, axis=0, keepdims=True)
        for copy in stores(step - 1):
            copy.start()

    @pl.when(step == 0)
    def _():
        small_ref[...] = jnp.zeros_like(small_ref)
        copies = down_copies(down, rows, wd, sems)
        for copy in [load(0)] + copies + [load(j) for j in range(1, steps)]:
            copy.start()
        for copy in copies:
            copy.wait()
        product_stage()

    @pl.when((step > 0) & (step < steps))
    def _():
        product_stage()
        norm_stage()

    @pl.when(step == steps)
    def _():
        norm_stage()

    @pl.when(step > steps)
    def _():
        product_step = step - steps - 1
        height = send_ref.shape[1]
        sending = product_step < 2
        core = jnp.where(sending, 1 - where[1], where[1])
        half = jnp.where(product_step % 2 == 0, 1 - where[0], where[0])
        at_left = pl.ds(pl.multiple_of((2 * half + core) * height, LANES), height)
        value = dot_tn(act[:, at_left], grads_all[...]).astype(BF16)
        put_blocks(send_ref, keep_ref, sending, (0,), slice(None), (value,))

    @pl.when(step == steps + 4)
    def _():
        for i in range(steps):
            for copy in stores(i):
                copy.wait()


def feed_down(where, act, normal, cot, down, rows, vec):
    count = len(down)
    tokens, width = cot.shape
    wide = act.shape[1]
    steps = tokens // TILE
    height = wide // 4
    late = pl.BlockSpec((TILE, width), lambda s, *_: (jnp.clip(s - 1, 0, steps - 1), 0))
    shape = jax.ShapeDtypeStruct
    return pl.pallas_call(
        functools.partial(feed_down_kernel, count, steps),
        grid_spec=pltpu.PrefetchScalarGridSpec(
            num_scalar_prefetch=1,
            grid=(steps + 5,),
            in_specs=[SMEM, late, late, whole(*vec.shape)] + [ANY] * (1 + count),
            out_specs=[whole(SUM_ROWS, width)]
            + [send_spec(2, height, width, steps + 1), keep_spec(2, height, width, steps + 1)]
            + [ANY] * 2,
            scratch_shapes=[
                pltpu.VMEM((wide, width), BF16),
                pltpu.VMEM((tokens, wide), BF16),
                pltpu.VMEM((2, TILE, width), F32),
                pltpu.VMEM((tokens, width), F32),
                pltpu.VMEM((tokens, width), BF16),
                pltpu.SemaphoreType.DMA((SPLITS * count,)),
                pltpu.SemaphoreType.DMA((steps,)),
                pltpu.SemaphoreType.DMA((2 * steps,)),
            ],
        ),
        out_shape=[shape((SUM_ROWS, width), F32)]
        + [shape((2, height, width), BF16)] * 2
        + [shape((tokens, width), F32), shape((tokens, width), BF16)],
        compiler_params=params(60),
        cost_estimate=LIGHT,
        name="feed_down",
    )(where, rows, normal, cot, vec, act, *down)


def feed_back_kernel(
    count, steps, where, rows, gd_ref, slope_ref, normal_ref, scale_ref, vec, sums_ref, ctx_any,
    *refs,
):
    own, pieces = refs[:2], refs[2 : 2 + count]
    down = refs[2 + count : 3 + 2 * count]
    small_ref, send_ref, keep_ref, ga_any, gc_any = refs[3 + 2 * count : 8 + 2 * count]
    (
        joined, wd, low, ctx, hidden_all, attended_all, grad_sums, gc, wide,
        sems, sems_down, sem_ctx, sems_out,
    ) = refs[8 + 2 * count :]
    tile, width = gd_ref.shape
    hidden = wide.shape[1]
    step = pl.program_id(0)
    load_ctx = pltpu.make_async_copy(ctx_any, ctx, sem_ctx.at[0])

    def rows_at(i):
        return pl.ds(pl.multiple_of(i * tile, tile), tile)

    def stores(i):
        span = rows_at(i)
        return [
            pltpu.make_async_copy(s.at[span, :], d.at[span, :], sems_out.at[j * steps + i])
            for j, (s, d) in enumerate(((attended_all, ga_any), (gc, gc_any)))
        ]

    def norm_stage():
        span = rows_at(step - 1)
        grad_normed = grad_sums[pl.ds((step + 1) % 2, 1)][0]
        normal = normal_ref[...].astype(F32)
        low[span, :] = (normal * vec[1:2, :] + vec[2:3, :]).astype(BF16)
        rounded = norm_back(grad_normed, vec[1:2, :], normal, scale_ref[...]).astype(BF16)
        attended_all[span, :] = rounded
        for j, value in enumerate((grad_normed * normal, grad_normed, rounded.astype(F32))):
            line = SUM_ATTN + j
            small_ref[line : line + 1, :] += jnp.sum(value, axis=0, keepdims=True)
        gc[span, :] = dot_nt(rounded, joined[:, :width]).astype(BF16)

    def wide_stage(waiting, between):
        span = rows_at(step)
        chunks = list(range(0, hidden, CHUNK))

        def product(c):
            return dot_nt(gd_ref[...], wd[c : c + CHUNK, :])

        ahead = product(0)
        for copy in waiting:
            copy.wait()
        total = gd_ref[...].astype(F32)
        for n, c in enumerate(chunks):
            grad_active = ahead
            if n + 1 < len(chunks):
                ahead = product(chunks[n + 1])
            rounded = (grad_active * slope_ref[:, c : c + CHUNK].astype(F32)).astype(BF16)
            hidden_all[span, c : c + CHUNK] = rounded
            wide[0:1, c : c + CHUNK] += jnp.sum(rounded.astype(F32), axis=0, keepdims=True)
            total = total + dot_nt(rounded, joined[:, width + c : width + c + CHUNK])
            if n == 1:
                between()
        grad_sums[pl.ds(step % 2, 1)] = total[None]

    @pl.when(step == 0)
    def _():
        copies = down_copies(down, rows, wd, sems_down)
        later = joined_copies(own, pieces, rows, joined, sems)
        for copy in copies + later + [load_ctx]:
            copy.start()
        small_ref[...] = sums_ref[...]
        wide[...] = jnp.zeros_like(wide)
        for copy in copies:
            copy.wait()
        wide_stage(later, lambda: None)

    @pl.when((step > 0) & (step < steps))
    def _():
        wide_stage([], norm_stage)

    @pl.when(step == steps)
    def _():
        norm_stage()
        for j in range(hidden // width):
            line = SUM_UP + j
            small_ref[line : line + 1, :] = wide[0:1, j * width : (j + 1) * width]
        load_ctx.wait()

    @pl.when((step > 0) & (step <= steps))
    def _():
        for copy in stores(step - 1):
            copy.start()

    @pl.when(step > steps)
    def _():
        sending = step == steps + 1
        core = jnp.where(sending, 1 - where[1], where[1])
        height, cut = width // 2, hidden // 2
        at_wide = pl.ds(pl.multiple_of(core * cut, LANES), cut)
        at_narrow = pl.ds(pl.multiple_of(core * height, LANES), height)
        slots = (jnp.where(where[0] == 0, 1, 0), jnp.where(where[0] == 0, 0, 1))
        value = dot_tn(low[...], hidden_all[:, at_wide]).astype(BF16)
        put_blocks(
            send_ref, keep_ref, sending, slots, slice(0, cut), (value[:height], value[height:])
        )
        value = dot_tn(ctx[...], attended_all[:, at_narrow]).astype(BF16)
        put_blocks(
            send_ref, keep_ref, sending, slots, slice(cut, cut + height),
            (value[:height], value[height:]),
        )

    @pl.when(step == steps + 2)
    def _():
        for i in range(steps):
            for copy in stores(i):
                copy.wait()


def feed_back(where, gd, slope, normal, scale, joined, down, vec, context, sums):
    own, pieces, rows = joined
    count = len(pieces)
    tokens, width = gd.shape
    wide = slope.shape[1]
    steps = tokens // TILE
    total = (wide + width) // 2

    def now(columns):
        return pl.BlockSpec((TILE, columns), lambda s, *_: (jnp.minimum(s, steps - 1), 0))

    def late(columns):
        return pl.BlockSpec((TILE, columns), lambda s, *_: (jnp.clip(s - 1, 0, steps - 1), 0))

    shape = jax.ShapeDtypeStruct
    return pl.pallas_call(
        functools.partial(feed_back_kernel, count, steps),
        grid_spec=pltpu.PrefetchScalarGridSpec(
            num_scalar_prefetch=1,
            grid=(steps + 3,),
            in_specs=[SMEM, now(width), now(wide), late(width), late(1)]
            + [whole(*vec.shape), whole(*sums.shape)]
            + [ANY] * (4 + 2 * count),
            out_specs=[whole(*sums.shape)]
            + [send_spec(1, width // 2, total, steps + 1)]
            + [keep_spec(1, width // 2, total, steps + 1)]
            + [ANY] * 2,
            scratch_shapes=[
                pltpu.VMEM((width, width + wide), BF16),
                pltpu.VMEM((wide, width), BF16),
                pltpu.VMEM((tokens, width), BF16),
                pltpu.VMEM((tokens, width), BF16),
                pltpu.VMEM((tokens, wide), BF16),
                pltpu.VMEM((tokens, width), BF16),
                pltpu.VMEM((2, TILE, width), F32),
                pltpu.VMEM((tokens, width), BF16),
                pltpu.VMEM((8, wide), F32),
                pltpu.SemaphoreType.DMA((SPLITS * (2 + count),)),
                pltpu.SemaphoreType.DMA((SPLITS * (1 + count),)),
                pltpu.SemaphoreType.DMA((1,)),
                pltpu.SemaphoreType.DMA((2 * steps,)),
            ],
        ),
        out_shape=[shape(sums.shape, F32)]
        + [shape((2, width // 2, total), BF16)] * 2
        + [shape((tokens, width), BF16)] * 2,
        compiler_params=params(60),
        cost_estimate=LIGHT,
        name="feed_back",
    )(where, rows, gd, slope, normal, scale, vec, sums, context, *own, *pieces, *down)


def inputs_back_kernel(count, rows, ga_ref, grads, *refs):
    own, pieces = refs[:3], refs[3 : 3 + count]
    out_ref, full, sems = refs[3 + count :]

    @pl.when(pl.program_id(0) == 0)
    def _():
        fetch_joined(own, pieces, rows, full, sems)

    out_ref[...] = ga_ref[...].astype(F32) + dot_nt(grads[...], full[...])


def inputs_back(grads, ga, weights):
    own, pieces, rows = weights
    tokens, width = ga.shape
    tile = pl.BlockSpec((TILE, width), lambda t: (t, 0))
    return pl.pallas_call(
        functools.partial(inputs_back_kernel, len(pieces)),
        grid=(tokens // TILE,),
        in_specs=[SMEM, tile, pl.BlockSpec((TILE, 3 * width), lambda t: (t, 0))]
        + [ANY] * (3 + len(pieces)),
        out_specs=tile,
        out_shape=jax.ShapeDtypeStruct((tokens, width), F32),
        scratch_shapes=[
            pltpu.VMEM((width, 3 * width), BF16),
            pltpu.SemaphoreType.DMA((SPLITS * (3 + len(pieces)),)),
        ],
        compiler_params=params(60),
        cost_estimate=LIGHT,
        name="inputs_back",
    )(rows, ga, grads, *own, *pieces)


CORE, NEAR_Y, NEAR_Z, FAR_Z = 1, 2, 4, 8


def after(value, *others):
    return lax.optimization_barrier((value,) + others)[0]


def swap_dp(values, bit):
    size = lax.axis_size("dp")
    return lax.ppermute(values, "dp", [(i, i ^ bit) for i in range(size)])


def swap_fsdp(values):
    return lax.ppermute(values, "fsdp", [(0, 1), (1, 0)])


def swap_both(values):
    size = lax.axis_size("dp")
    pairs = [(2 * i + h, 2 * (i ^ NEAR_Y) + 1 - h) for i in range(size) for h in range(2)]
    return lax.ppermute(values, ("dp", "fsdp"), pairs)


def rows_of(values, start, count):
    return lax.dynamic_slice_in_dim(values, start, count, axis=0)


def own_part(shards, place):
    half, core, y, z = place
    height = shards[0].shape[0]
    count = height // 8
    starts = (2 * y + core) * count, height // 2 + (2 * z + core) * count
    return jnp.concatenate(
        [jnp.concatenate([rows_of(s, start, count) for s in shards], axis=1) for start in starts],
        axis=0,
    )


def pass_on(first):
    count = first.shape[0] // 2
    return (
        first[:count],
        first[count:],
        swap_dp(first[:count], NEAR_Y),
        swap_dp(first[count:], NEAR_Z),
    )


def with_core(parts):
    return tuple(parts) + tuple(swap_dp(part, CORE) for part in parts)


def far_parts(first):
    count = first.shape[0] // 2
    left, right = first[:count], first[count:]
    return (
        swap_dp(left, NEAR_Y),
        swap_dp(right, NEAR_Z),
        swap_dp(left, NEAR_Y | CORE),
        swap_dp(right, NEAR_Z | CORE),
    )


def all_parts(first, far):
    count = first.shape[0] // 2
    other = swap_dp(first, CORE)
    return (first[:count], first[count:]) + far[:2] + (other[:count], other[count:]) + far[2:]


def piece_rows(height, place):
    half, core, y, z = place
    count = height // 8
    base = (1 - half) * height
    rows = [half * height]
    for c in (core, 1 - core):
        rows += [
            base + (2 * y + c) * count,
            base + height // 2 + (2 * z + c) * count,
            base + (2 * (1 - y) + c) * count,
            base + height // 2 + (2 * (1 - z) + c) * count,
        ]
    return jnp.stack(rows).astype(jnp.int32)


class Part:
    def __init__(self, terms, place, columns=None):
        self.bits = {0: 1, 1: place[2], 2: place[3]}
        self.swaps = {
            0: swap_fsdp,
            1: lambda v: swap_dp(v, NEAR_Y),
            2: lambda v: swap_dp(v, NEAR_Z),
            3: lambda v: swap_dp(v, FAR_Z),
        }
        self.terms = [t.reshape(2, 2, 2, t.shape[1] // 4, t.shape[2]) for t in terms]
        self.views = [(columns, ())] * len(terms)
        self.flight, self.joined = [], None

    def total(self, *picks):
        value = None
        for term, (columns, before) in zip(self.terms, self.views):
            if columns is not None:
                term = term[..., columns[0] : columns[1]]
            for axis, index in before + picks:
                term = lax.dynamic_slice_in_dim(term, index, 1, axis)
            term = term.astype(F32)
            value = term if value is None else value + term
        return value.astype(BF16)

    def cut(self, *picks):
        self.views = [(columns, before + picks) for columns, before in self.views]

    def halve(self, axis):
        bit = self.bits[axis]
        self.flight, self.route = [self.total((axis, 1 - bit))], [self.swaps[axis]]
        self.cut((axis, bit))

    def both(self):
        bit = self.bits[1]
        self.flight = [
            self.total((0, 0), (1, bit)),
            self.total((0, 1), (1, 1 - bit)),
            self.total((0, 0), (1, 1 - bit)),
        ]
        self.route = [self.swaps[0], self.swaps[1], swap_both]
        self.cut((0, 1), (1, bit))

    def merge(self, *others):
        value = jnp.concatenate([part.total() for part in (self,) + others], axis=-1)
        self.terms, self.views = [value], [(None, ())]

    def split(self, cut):
        other = copy.copy(self)
        end = self.terms[0].shape[-1]
        self.views = [((0, cut), before) for _, before in self.views]
        other.views = [((cut, end), before) for _, before in other.views]
        return other

    def send_whole(self, swap, reshape=None):
        value = self.terms[0]
        if len(self.terms) > 1 or self.views[0][0] is not None:
            value = self.total()
        if reshape:
            value = value.reshape(-1, value.shape[-1])
        self.flight, self.route = [value], [lambda v: (v, swap(v))]
        self.terms, self.views = [], []

    def far(self):
        self.send_whole(self.swaps[3])

    def join(self, axis):
        self.send_whole(self.swaps[axis])
        self.joined = axis

    def finish(self):
        self.send_whole(lambda v: swap_dp(v, CORE), True)

    def land(self):
        for sent, route in zip(self.flight, self.route):
            got = route(sent)
            self.terms += list(got) if isinstance(got, tuple) else [got]
        self.views = self.views + [(None, ())] * (len(self.terms) - len(self.views))
        self.flight = []

    def settle(self):
        if self.joined is None:
            return
        mine, other = self.terms
        axis, self.joined = self.joined, None
        value = jnp.where(
            self.bits[axis] == 0,
            jnp.concatenate([mine, other], axis=axis),
            jnp.concatenate([other, mine], axis=axis),
        )
        self.terms, self.views = [value], [(None, ())]


def fence(parts, *arrays):
    counts = [(len(p.terms), len(p.flight)) for p in parts]
    flat = [a for p in parts for a in p.terms + p.flight] + list(arrays)
    flat = list(lax.optimization_barrier(tuple(flat)))
    for part, (terms, flight) in zip(parts, counts):
        part.terms, flat = flat[:terms], flat[terms:]
        part.flight, flat = flat[:flight], flat[flight:]
    return flat


def widen(mine, other, core, axis):
    low = jnp.where(core == 0, mine, other).astype(F32)
    high = jnp.where(core == 0, other, mine).astype(F32)
    return jnp.concatenate([low, high], axis=axis)


def gather_all(values):
    return lax.all_gather(values, "fsdp", axis=0, tiled=True)


def sum_plain(send, keep, by_rows):
    blocks = [[keep[1], send[1]], [keep[0], send[0]]]
    axis = 0 if by_rows else 1
    value = jnp.concatenate([jnp.concatenate(pair, axis=axis) for pair in blocks], axis=0)
    own = lax.psum_scatter(value, "fsdp", scatter_dimension=0, tiled=True)
    return lax.psum(own, "dp").astype(F32)


def local(
    inputs, segment_ids, cotangent, w_query, b_query, w_key, b_key, w_value, b_value,
    w_output, b_output, gain_attn, bias_attn, w_up, b_up, w_down, b_down, gain_ffn, bias_ffn,
):
    rows, length = segment_ids.shape
    width = inputs.shape[1]
    shards = lax.axis_size("fsdp")
    paired = shards == 2 and lax.axis_size("dp") == 16
    half = lax.axis_index("fsdp")
    dp = lax.axis_index("dp")
    place = (half, dp % 2, dp // 2 % 2, dp // 4 % 2)
    core = place[1]
    vectors = (b_query, b_key, b_value, b_output, gain_attn, bias_attn, b_down, gain_ffn, bias_ffn)
    height = w_query.shape[0]
    cosine, sine, turned = rotary_tables(segment_ids, inputs)
    if paired:
        where = jnp.stack([half, core]).astype(jnp.int32)
        part_qkv = own_part((w_query, w_key, w_value), place)
        part_up = own_part((w_output, w_up), place)
        part_down = own_part((w_down,), place)
        here_qkv = swap_fsdp(part_qkv)
        lines = jnp.concatenate(vectors + (b_up,)).reshape(-1, height)
        other = swap_fsdp(after(lines, part_qkv))
        here_up = swap_fsdp(after(part_up, here_qkv))
        at = piece_rows(height, place)
        joined_qkv = ((w_query, w_key, w_value), with_core(pass_on(here_qkv)), at)
        lines = jnp.where(half == 0, jnp.stack([lines, other]), jnp.stack([other, lines]))
    else:
        where = jnp.zeros((2,), jnp.int32)
        at = jnp.zeros((1,), jnp.int32)
        joined_qkv = (tuple(gather_all(w) for w in (w_query, w_key, w_value)), (), at)
        joined_up = ((gather_all(w_output), gather_all(w_up)), (), at)
        down = (gather_all(w_down),)
        lines = jnp.concatenate(vectors + (b_up,)).reshape(-1, height)
        lines = lax.all_gather(lines, "fsdp", axis=0)
    lines = lines.astype(F32)
    vec = jnp.swapaxes(lines[:, :9], 0, 1).reshape(9, width)
    bias_up = lines[:, 9:].reshape(1, -1)

    q, k, v = project(inputs, joined_qkv, vec[:3], cosine, sine)
    vec = vec[3:]
    if paired:
        q, here_up, part_down = lax.optimization_barrier((q, here_up, part_down))
        here_down = swap_fsdp(part_down)
        far_up = far_parts(here_up)
    context, probs = attend(q, k, v, segment_ids)
    if paired:
        context, probs, here_up, here_down, far_up = lax.optimization_barrier(
            (context, probs, here_up, here_down, far_up)
        )
        joined_up = ((w_output, w_up), all_parts(here_up, far_up), at)
        context, joined_up, here_down = lax.optimization_barrier((context, joined_up, here_down))
        far_down = far_parts(here_down)
    normal, scale, act, slope = feed_up(context, inputs, joined_up, vec, bias_up)
    if paired:
        act, slope, here_down, far_down = lax.optimization_barrier(
            (act, slope, here_down, far_down)
        )
        down = (w_down,) + all_parts(here_down, far_down)
    sums, send, keep, result, grad_down = feed_down(
        where, act, normal, cotangent, down, at, vec
    )
    sent = [(send, keep)]
    if paired:
        sum_d = Part([keep, swap_dp(send, CORE)], place)
        sum_d.both()
        (grad_down,) = fence([sum_d], grad_down)
    outs = feed_back(
        where, grad_down, slope, normal, scale, joined_up, down, vec, context, sums
    )
    sent.append(outs[1:3])
    if paired:
        sum_d.land()
        outs = fence([sum_d], *outs)
    sums, send, keep, grad_attended, grad_context = outs
    if paired:
        sum_u = Part([keep, swap_dp(send, CORE)], place)
        sum_d.halve(2)
        sum_u.both()
        parts = [sum_d, sum_u]
        (grad_context,) = fence(parts, grad_context)
    outs = attend_back(where, q, k, v, grad_context, probs, cosine, sine, turned, sums)
    sent.append(outs[1:3])
    if paired:
        for p in parts:
            p.land()
        outs = fence(parts, *outs)
    sums, send, keep, grads = outs
    if paired:
        sum_q = Part([keep, swap_dp(send, CORE)], place)
        sum_d.far()
        sum_u.halve(2)
        sum_q.both()
        parts = [sum_d, sum_u, sum_q]
        (grad_attended,) = fence(parts, grad_attended)
    grad_inputs = inputs_back(grads, grad_attended, joined_qkv)
    if paired:
        for p in parts:
            p.land()
        (grad_inputs,) = fence(parts, grad_inputs)
        value = sum_d.total().reshape(sum_d.terms[-1].shape[-2:])
        groups = [[8 * i + j for j in range(8)] for i in range(2)]
        whole_d = lax.all_gather(value, "dp", axis_index_groups=groups)
        last = value

        def step(part, name, *axis):
            nonlocal last
            (last,) = fence([part], last)
            part.settle()
            getattr(part, name)(*axis)
            (last,) = fence([part], last)
            last = part.flight[0]
            part.land()

        step(sum_u, "far")
        step(sum_q, "halve", 2)
        step(sum_q, "far")
        cut_u, cut_q = ((p.terms[0].shape[-1] // 2 + 64) // LANES * LANES for p in (sum_u, sum_q))
        (last,) = fence([sum_u], last)
        sum_v = sum_u.split(cut_u)
        step(sum_u, "join", 2)
        step(sum_v, "join", 1)
        (last,) = fence([sum_q], last)
        sum_r = sum_q.split(cut_q)
        step(sum_q, "join", 2)
        step(sum_r, "join", 1)
        step(sum_u, "join", 1)
        step(sum_v, "join", 2)
        step(sum_q, "join", 1)
        step(sum_r, "join", 2)
        whole_d = after(whole_d, last).reshape((2, 2, 2) + value.shape).astype(F32)
        gwd = jnp.transpose(whole_d, (2, 1, 0, 3, 4)).reshape(-1, width)
        step(sum_u, "finish")
        step(sum_v, "finish")
        last = after(last, gwd)
        step(sum_q, "finish")
        step(sum_r, "finish")
    else:
        sums = lax.psum(sums, ("dp", "fsdp"))

    wide = b_up.shape[0] * shards
    if paired:
        mine, other = (
            jnp.concatenate([a, b], axis=1) for a, b in zip(sum_u.terms, sum_v.terms)
        )
        cut = wide // 2
        gwu = widen(mine[:, :cut], other[:, :cut], core, 1)
        gwo = widen(mine[:, cut:], other[:, cut:], core, 1)
        mine, other = (
            jnp.concatenate([a, b], axis=1) for a, b in zip(sum_q.terms, sum_r.terms)
        )
        gwq, gwk, gwv = (
            widen(*(end[:, i * width : (i + 1) * width] for end in (mine, other)), core, 0)
            for i in range(3)
        )
        count = height // LANES
        packed = jnp.where(core == 0, mine[:, 3 * width :], other[:, 3 * width :])
        packed = packed[: len(LINES) * count + wide // 2 // LANES].astype(F32)
        vectors = [packed[i * count : (i + 1) * count].reshape(-1) for i in range(len(LINES))]
        gbu = packed[len(LINES) * count :].reshape(-1)
        ggf, gbf, gbd, gga, gba, gbo, gbq, gbk, gbv = vectors
    else:

        def own(line, count=1):
            start = line * width + half * (count * width // shards)
            return lax.dynamic_slice_in_dim(
                sums.reshape(-1), start, count * width // shards, axis=0
            )

        ggf, gbf, gbd, gga, gba, gbo, gbq, gbk, gbv = (own(line) for line in LINES)
        gbu = own(SUM_UP, wide // width)
        gwd = sum_plain(*sent[0], True)
        both = sum_plain(*sent[1], False).reshape(height, 2, -1)
        cut = wide // 2
        gwu = both[..., :cut].reshape(height, -1)
        gwo = both[..., cut:].reshape(height, -1)
        both = sum_plain(*sent[2], True)
        gwq, gwk, gwv = (both[:, i * width : (i + 1) * width] for i in range(3))
    return (
        result, grad_inputs, gwq, gbq, gwk, gbk, gwv, gbv, gwo, gbo, gga, gba,
        gwu, gbu, gwd, gbd, ggf, gbf,
    )


def solution(mesh):
    tokens, matrix, vector = P(("dp", "fsdp"), None), P("fsdp", None), P("fsdp")
    weights = (
        matrix, vector, matrix, vector, matrix, vector, matrix, vector, vector, vector,
        matrix, vector, matrix, vector, vector, vector,
    )
    return jax.shard_map(
        local,
        mesh=mesh,
        in_specs=(tokens,) * 3 + weights,
        out_specs=(tokens,) * 2 + weights,
        check_vma=False,
    )
```

```python
import copy
import functools
import jax
import jax.numpy as jnp
from jax import lax
from jax.experimental import pallas as pl
from jax.experimental.pallas import tpu as pltpu
from jax.sharding import PartitionSpec as P

HEAD = 64
GROUP = 3
EPSILON = 1e-06
LANES = 128
TILE = 256
CHUNK = 512
MASKED = -1e30
SUM_FFN, SUM_ATTN, SUM_UP, SUM_QKV, SUM_ROWS = 0, 3, 6, 10, 16
F32 = jnp.float32
BF16 = jnp.bfloat16


def params(mebibytes):
    return pltpu.CompilerParams(vmem_limit_bytes=mebibytes * 1024 * 1024)


LIGHT = pl.CostEstimate(flops=1000, bytes_accessed=1000, transcendentals=0)


def dot_nn(left, right):
    return lax.dot_general(left, right, (((1,), (0,)), ((), ())), preferred_element_type=F32)


def dot_nt(left, right):
    return lax.dot_general(left, right, (((1,), (1,)), ((), ())), preferred_element_type=F32)


def dot_tn(left, right):
    return lax.dot_general(left, right, (((0,), (0,)), ((), ())), preferred_element_type=F32)


def whole(*shape):
    return pl.BlockSpec(shape, lambda *_: (0,) * len(shape))


SPLITS = 4


def piece_copies(pieces, starts, full, column, sems, first):
    copies = []
    assert len(pieces) == len(starts)
    for i, (piece, start) in enumerate(zip(pieces, starts)):
        height, width = piece.shape
        splits = SPLITS if height * width >= 500_000 and height % (16 * SPLITS) == 0 else 1
        count = height // splits
        for j in range(splits):
            row = pl.multiple_of(start + j * count, 16)
            copies.append(
                pltpu.make_async_copy(
                    piece.at[pl.ds(j * count, count), :],
                    full.at[pl.ds(row, count), column : column + width],
                    sems.at[SPLITS * (first + i) + j],
                )
            )
    return copies


def cut_pieces(pieces):
    cut = []
    for i, piece in enumerate(pieces):
        count = piece.shape[0] // 2
        cut += [piece.at[:count, :], piece.at[count:, :]] if i % 3 == 0 else [piece]
    return cut


def joined_copies(own, pieces, rows, full, sems, cut=None):
    pieces = cut_pieces(pieces)
    shards, column = [], 0
    for i, shard in enumerate(own):
        shards.append(piece_copies([shard], [rows[0]], full, column, sems, i))
        column += shard.shape[1]
    starts = [rows[1 + i] for i in range(len(pieces))]
    first = len(own)
    if cut is None:
        return sum(shards, []) + piece_copies(pieces, starts, full, 0, sems, first)
    left = [piece.at[:, :cut] for piece in pieces]
    right = [piece.at[:, cut:] for piece in pieces]
    return (
        shards[0] + piece_copies(left, starts, full, 0, sems, first),
        sum(shards[1:], []) + piece_copies(right, starts, full, cut, sems, first + len(pieces)),
    )


def fetch_joined(own, pieces, rows, full, sems):
    copies = joined_copies(own, pieces, rows, full, sems)
    for copy in copies:
        copy.start()
    for copy in copies:
        copy.wait()


ANY = pl.BlockSpec(memory_space=pl.ANY)
SMEM = pl.BlockSpec(memory_space=pltpu.SMEM)


def tables_kernel(seg_row, seg_col, x_ref, cos_ref, sin_ref, turned_ref):
    length = seg_row.shape[-1]
    key = lax.broadcasted_iota(jnp.int32, (length, length), 1)
    query = lax.broadcasted_iota(jnp.int32, (length, length), 0)
    earlier = (seg_col[...] == seg_row[0]) & (key < query)
    place = jnp.sum(earlier.astype(F32), axis=1, keepdims=True)
    lane = lax.broadcasted_iota(jnp.int32, (1, LANES), 1)
    paired = (lane % HEAD // 2 * 2).astype(F32)
    freqs = jnp.exp(-jnp.log(F32(10000.0)) * paired / HEAD)
    angle = place * freqs
    cos_ref[...] = jnp.cos(angle)
    sine = jnp.sin(angle)
    sin_ref[...] = jnp.where(lane % 2 == 0, -sine, sine)
    turned_ref[...] = x_ref[...].T


def rotary_tables(segments, x):
    rows, length = segments.shape
    width = x.shape[1]
    return pl.pallas_call(
        tables_kernel,
        grid=(rows,),
        in_specs=[
            pl.BlockSpec((1, 1, length), lambda r: (r, 0, 0)),
            pl.BlockSpec((length, 1), lambda r: (r, 0)),
            pl.BlockSpec((length, width), lambda r: (r, 0)),
        ],
        out_specs=[pl.BlockSpec((length, LANES), lambda r: (r, 0))] * 2
        + [pl.BlockSpec((width, length), lambda r: (0, r))],
        out_shape=[jax.ShapeDtypeStruct((rows * length, LANES), F32)] * 2
        + [jax.ShapeDtypeStruct((width, rows * length), BF16)],
        compiler_params=params(60),
        cost_estimate=LIGHT,
        name="rotary_tables",
    )(segments.reshape(rows, 1, length), segments.reshape(rows * length, 1), x)


def pair_swap(values):
    even = lax.broadcasted_iota(jnp.int32, values.shape, 1) % 2 == 0
    return jnp.where(
        even, pltpu.roll(values, LANES - 1, axis=1), pltpu.roll(values, 1, axis=1)
    )


def project_kernel(count, rows, x_ref, bias, cos_ref, sin_ref, *refs):
    own, pieces = refs[:3], refs[3 : 3 + count]
    q_ref, k_ref, v_ref, full, sems = refs[3 + count :]
    width = x_ref.shape[1]

    @pl.when(pl.program_id(0) == 0)
    def _():
        fetch_joined(own, pieces, rows, full, sems)

    x = x_ref[...]
    cosine, sine = cos_ref[...], sin_ref[...]
    step = 2 * LANES
    for i, out in enumerate((q_ref, k_ref, v_ref)):
        for c in range(0, width, step):
            lin = dot_nn(x, full[:, i * width + c : i * width + c + step])
            lin = lin + bias[i : i + 1, c : c + step]
            if i < 2:
                parts = []
                for d in range(0, step, LANES):
                    part = lin[:, d : d + LANES]
                    part = part * cosine + pair_swap(part) * sine
                    parts.append(part)
                lin = jnp.concatenate(parts, axis=1)
            if i == 0:
                out[:, c : c + step] = (lin.astype(BF16).astype(F32) * 0.125).astype(BF16)
            else:
                out[:, c : c + step] = lin.astype(BF16)


def project(x, weights, bias, cosine, sine):
    own, pieces, rows = weights
    tokens, width = x.shape
    tile = pl.BlockSpec((TILE, width), lambda t: (t, 0))
    table = pl.BlockSpec((TILE, LANES), lambda t: (t, 0))
    return pl.pallas_call(
        functools.partial(project_kernel, len(pieces)),
        grid=(tokens // TILE,),
        in_specs=[SMEM, tile, whole(*bias.shape), table, table] + [ANY] * (3 + len(pieces)),
        out_specs=[tile] * 3,
        out_shape=[jax.ShapeDtypeStruct((tokens, width), BF16)] * 3,
        scratch_shapes=[
            pltpu.VMEM((width, 3 * width), BF16),
            pltpu.SemaphoreType.DMA((SPLITS * (3 + 2 * len(pieces)),)),
        ],
        compiler_params=params(60),
        cost_estimate=LIGHT,
        name="project",
    )(rows, x, bias, cosine, sine, *own, *pieces)


def spans(length):
    found, offset = [], 0
    for first in range(0, length, LANES):
        low, high = max(first - LANES, 0), min(first + 2 * LANES, length)
        found.append((slice(first, first + LANES), slice(low, high), slice(offset, offset + high - low)))
        offset += high - low
    return found, offset


def split_heads(values):
    lane = lax.broadcasted_iota(jnp.int32, (1, LANES), 1)
    return [jnp.where(lane // HEAD == h, values, jnp.zeros_like(values)) for h in range(2)]


def stack_heads(heads, rows):
    return jnp.concatenate([head[rows, :] for head in heads], axis=0)


def merge_heads(stacked):
    lane = lax.broadcasted_iota(jnp.int32, (1, LANES), 1)
    half = stacked.shape[0] // 2
    return jnp.where(lane < HEAD, stacked[:half], stacked[half:])


def attend_kernel(q_ref, k_ref, v_ref, seg_row, seg_col, ctx_ref, prob_ref, bias):
    blocks, _ = spans(q_ref.shape[0])

    @pl.when(pl.program_id(1) == 0)
    def _():
        for own, span, at in blocks:
            bias[at, :] = jnp.where(seg_col[span, :] == seg_row[0, :, own], 0.0, MASKED)

    pairs = [slice(p * LANES, (p + 1) * LANES) for p in range(GROUP)]
    units = [(p, lanes) + block for p, lanes in enumerate(pairs) for block in blocks]
    queries = [split_heads(q_ref[:, lanes]) for lanes in pairs]

    def product(unit):
        p, lanes, own, span, _ = unit
        return dot_nt(k_ref[span, lanes], stack_heads(queries[p], own))

    def soften(unit, scores):
        at = unit[-1]
        heads = []
        for h in range(2):
            masked = scores[:, h * LANES : (h + 1) * LANES] + bias[at, :]
            peak = jnp.max(masked, axis=0, keepdims=True)
            expo = jnp.exp(masked - peak)
            total = jnp.sum(expo, axis=0, keepdims=True)
            heads.append((expo * (1.0 / total)).astype(BF16))
        return jnp.concatenate(heads, axis=1)

    def finish(unit, probs):
        p, lanes, own, span, at = unit
        prob_ref[0, p, at, :] = probs
        ctx_ref[own, lanes] = merge_heads(dot_tn(probs, v_ref[span, lanes])).astype(BF16)

    count = len(blocks)
    scores = [product(unit) for unit in units[:count]]
    waiting = []
    for p in range(GROUP):
        now = units[p * count : (p + 1) * count]
        probs = [soften(unit, value) for unit, value in zip(now, scores)]
        scores = [product(unit) for unit in units[(p + 1) * count : (p + 2) * count]]
        for unit, value in waiting:
            finish(unit, value)
        waiting = list(zip(now, probs))
    for unit, value in waiting:
        finish(unit, value)


def attend(q, k, v, segments):
    rows, length = segments.shape
    tokens, width = q.shape
    pairs = width // LANES
    wide = GROUP * LANES
    _, depth = spans(length)
    head = pl.BlockSpec((length, wide), lambda r, p: (r, p))
    return pl.pallas_call(
        attend_kernel,
        grid=(rows, pairs // GROUP),
        in_specs=[head] * 3
        + [
            pl.BlockSpec((1, 1, length), lambda r, p: (r, 0, 0)),
            pl.BlockSpec((length, 1), lambda r, p: (r, 0)),
        ],
        out_specs=[
            head,
            pl.BlockSpec((1, GROUP, depth, 2 * LANES), lambda r, p: (r, p, 0, 0)),
        ],
        out_shape=[
            jax.ShapeDtypeStruct((tokens, width), BF16),
            jax.ShapeDtypeStruct((rows, pairs, depth, 2 * LANES), BF16),
        ],
        scratch_shapes=[pltpu.VMEM((depth, LANES), F32)],
        compiler_params=params(60),
        cost_estimate=LIGHT,
        name="attend",
    )(q, k, v, segments.reshape(rows, 1, length), segments.reshape(tokens, 1))


def send_spec(steps, height, width, first):
    return pl.BlockSpec(
        (2 // steps, height, width), lambda s, *_: (jnp.clip(s - first, 0, steps - 1), 0, 0)
    )


def keep_spec(steps, height, width, first):
    return pl.BlockSpec(
        (2 // steps, height, width), lambda s, *_: (jnp.clip(s - first - steps, 0, steps - 1), 0, 0)
    )


def put_blocks(send_ref, keep_ref, sending, slots, columns, values):
    @pl.when(sending)
    def _():
        for slot, value in zip(slots, values):
            send_ref[slot, :, columns] = value

    @pl.when(jnp.logical_not(sending))
    def _():
        for slot, value in zip(slots, values):
            keep_ref[slot, :, columns] = value


LINES = (SUM_FFN, SUM_FFN + 1, SUM_FFN + 2, SUM_ATTN, SUM_ATTN + 1, SUM_ATTN + 2) + (
    SUM_QKV, SUM_QKV + 1, SUM_QKV + 2,
)


def pack_vectors(small_ref, packed, half):
    width = small_ref.shape[1]
    part = width // 2 // LANES
    packed[...] = jnp.zeros_like(packed)
    for i, line in enumerate(LINES):
        for j in range(part):
            lanes = pl.ds(pl.multiple_of(half * (width // 2) + j * LANES, LANES), LANES)
            packed[i * part + j : i * part + j + 1, :] = small_ref[line : line + 1, lanes]
    base, count = len(LINES) * part, width // LANES
    lines = (SUM_QKV - SUM_UP) // 2
    for i in range(lines):
        for j in range(count):
            row = base + i * count + j
            lanes = slice(j * LANES, (j + 1) * LANES)
            low, high = (small_ref[SUM_UP + n : SUM_UP + n + 1, lanes] for n in (i, lines + i))
            packed[row : row + 1, :] = jnp.where(half == 0, low, high)


def attend_back_kernel(
    rows, where, q_ref, k_ref, v_ref, g_ref, prob_ref, cos_ref, sin_ref, sums_ref, turned_any,
    small_ref, send_ref, keep_ref, out_any, acc_k, acc_v, grads_all, turned, packed, sems,
):
    step = pl.program_id(0)
    length = q_ref.shape[0]
    width = turned.shape[0]
    pairs = width // LANES
    units = rows * pairs // GROUP
    fetch = pltpu.make_async_copy(turned_any, turned, sems.at[0])
    hand_on = pltpu.make_async_copy(grads_all, out_any, sems.at[1])

    @pl.when(step == 0)
    def _():
        fetch.start()
        small_ref[...] = sums_ref[...]

    @pl.when(step < units)
    def _():
        blocks, _ = spans(length)
        groups = pairs // GROUP
        row, group = step // groups, step % groups
        at_rows = pl.ds(pl.multiple_of(row * length, length), length)
        lanes_of = [slice(p * LANES, (p + 1) * LANES) for p in range(GROUP)]

        def turn_back(values, rows):
            return values * cos_ref[rows, :] - pair_swap(values) * sin_ref[rows, :]

        def first(p):
            grads = split_heads(g_ref[:, lanes_of[p]])
            return [
                dot_nt(v_ref[span, lanes_of[p]], stack_heads(grads, own)) for own, span, _ in blocks
            ]

        def second(p, grad_probs):
            made = []
            for (own, span, at), pair in zip(blocks, grad_probs):
                heads = []
                for h in range(2):
                    columns = slice(h * LANES, (h + 1) * LANES)
                    probs = prob_ref[0, p, at, columns].astype(F32)
                    inner = jnp.sum(probs * pair[:, columns], axis=0, keepdims=True)
                    heads.append((probs * (pair[:, columns] - inner)).astype(BF16))
                made.append(jnp.concatenate(heads, axis=1))
            return made

        def third(p, grad_scores):
            lanes = lanes_of[p]
            queries, grads = split_heads(q_ref[:, lanes]), split_heads(g_ref[:, lanes])
            k_t = k_ref[:, lanes].T
            acc_k[p] = jnp.zeros_like(acc_k[p])
            acc_v[p] = jnp.zeros_like(acc_v[p])
            turned_parts = []
            for (own, span, at), low in zip(blocks, grad_scores):
                acc_k[p, span, :] += dot_nn(low, stack_heads(queries, own))
                acc_v[p, span, :] += dot_nn(prob_ref[0, p, at, :], stack_heads(grads, own))
                product = dot_nn(k_t[:, span], low)
                both = jnp.concatenate([product[:HEAD, :LANES], product[HEAD:, LANES:]], axis=0)
                turned_parts.append(both.T)
            return turned_parts

        def fourth(p, turned_parts):
            gq = jnp.concatenate(
                [
                    turn_back(part * 0.125, own).astype(BF16)
                    for (own, _, _), part in zip(blocks, turned_parts)
                ],
                axis=0,
            )
            gk = turn_back(acc_k[p], slice(0, length)).astype(BF16)
            gv = acc_v[p].astype(BF16)
            pair = group * GROUP + p
            at_lanes = pl.ds(pl.multiple_of(pair * LANES, LANES), LANES)
            for i, grad in enumerate((gq, gk, gv)):
                at_grad = pl.ds(pl.multiple_of((i * pairs + pair) * LANES, LANES), LANES)
                grads_all[at_rows, at_grad] = grad
                line = SUM_QKV + i
                small_ref[line : line + 1, at_lanes] += jnp.sum(
                    grad.astype(F32), axis=0, keepdims=True
                )

        grad_probs = first(0)
        waiting = None
        for p in range(GROUP):
            grad_scores = second(p, grad_probs)
            if p + 1 < GROUP:
                grad_probs = first(p + 1)
            turned_parts = third(p, grad_scores)
            if waiting is not None:
                fourth(*waiting)
            waiting = (p, turned_parts)
        fourth(*waiting)

    @pl.when(step == units)
    def _():
        hand_on.start()
        fetch.wait()

    @pl.when(step >= units)
    def _():
        sending = step == units
        height = send_ref.shape[1]
        core = jnp.where(sending, 1 - where[1], where[1])
        left = [
            turned[pl.ds(pl.multiple_of((2 * half + core) * height, 16), height), :]
            for half in (1 - where[0], where[0])
        ]
        value = dot_nn(jnp.concatenate(left, axis=0), grads_all[...]).astype(BF16)
        put_blocks(
            send_ref, keep_ref, sending, (0, 1), slice(0, 3 * width), (value[:height], value[height:])
        )
        for slot, half in enumerate((1 - where[0], where[0])):
            pack_vectors(small_ref, packed, half)
            vectors = jnp.where(core == 0, packed[...], 0.0).astype(BF16)
            put_blocks(
                send_ref, keep_ref, sending, (slot,), slice(3 * width, 3 * width + LANES), (vectors,)
            )

    @pl.when(step == units + 1)
    def _():
        hand_on.wait()


def attend_back(where, q, k, v, grad_context, probs, cosine, sine, turned, sums):
    tokens, width = q.shape
    rows, pairs, depth = probs.shape[:3]
    length = tokens // rows
    units = rows * pairs // GROUP
    height = width // 4

    def at(s):
        s = jnp.minimum(s, units - 1)
        return s // (pairs // GROUP), s % (pairs // GROUP)

    head = pl.BlockSpec((length, GROUP * LANES), lambda s, *_: at(s))
    table = pl.BlockSpec((length, LANES), lambda s, *_: (at(s)[0], 0))
    shape = jax.ShapeDtypeStruct
    return pl.pallas_call(
        functools.partial(attend_back_kernel, rows),
        grid_spec=pltpu.PrefetchScalarGridSpec(
            num_scalar_prefetch=1,
            grid=(units + 2,),
            in_specs=[head] * 4
            + [
                pl.BlockSpec((1, GROUP, depth, 2 * LANES), lambda s, *_: at(s) + (0, 0)),
                table,
                table,
                whole(*sums.shape),
                ANY,
            ],
            out_specs=[
                whole(*sums.shape),
                send_spec(1, height, 3 * width + LANES, units),
                keep_spec(1, height, 3 * width + LANES, units),
                ANY,
            ],
            scratch_shapes=[pltpu.VMEM((GROUP, length, LANES), F32)] * 2
            + [
                pltpu.VMEM((tokens, 3 * width), BF16),
                pltpu.VMEM((width, tokens), BF16),
                pltpu.VMEM((height, LANES), F32),
                pltpu.SemaphoreType.DMA((2,)),
            ],
        ),
        out_shape=[shape(sums.shape, F32)]
        + [shape((2, height, 3 * width + LANES), BF16)] * 2
        + [shape((tokens, 3 * width), BF16)],
        compiler_params=params(60),
        cost_estimate=LIGHT,
        name="attend_back",
    )(where, q, k, v, grad_context, probs, cosine, sine, sums, turned)


def norm_parts(values):
    mean = jnp.mean(values, axis=-1, keepdims=True)
    center = values - mean
    spread = jnp.mean(center * center, axis=-1, keepdims=True)
    scale = lax.rsqrt(spread + EPSILON)
    return center * scale, scale


def norm_back(grads, gain, normal, scale):
    inner = grads * gain
    return scale * (
        inner
        - jnp.mean(inner, axis=-1, keepdims=True)
        - normal * jnp.mean(inner * normal, axis=-1, keepdims=True)
    )


def gelu_parts(values):
    share = 0.5 + 0.5 * lax.erf(values * 0.7071067811865476)
    return share, jnp.exp(values * values * -0.5) * 0.3989422804014327


def down_copies(down, rows, wd, sems):
    scale = wd.shape[0] // wd.shape[1]
    pieces = list(down[:1]) + cut_pieces(down[1:])
    starts = [rows[i] * scale for i in range(len(pieces))]
    return piece_copies(pieces, starts, wd, 0, sems, 0)


def feed_up_kernel(count, rows, ctx_ref, x_ref, vec, bu, *refs):
    own, pieces = refs[:2], refs[2 : 2 + count]
    normal_ref, scale_ref, act_ref, slope_ref, joined, lows, sems = refs[2 + count :]
    width = x_ref.shape[1]
    step, last = pl.program_id(0), pl.num_programs(0) - 1

    def norm_stage():
        bo, g1, s1 = (vec[i : i + 1, :] for i in range(3))
        attended = dot_nn(ctx_ref[...], joined[:, :width]) + bo
        normal, scale = norm_parts(x_ref[...].astype(F32) + attended)
        normal = normal.astype(BF16)
        normal_ref[...] = normal
        scale_ref[...] = scale
        lows[pl.ds(step % 2, 1)] = (normal.astype(F32) * g1 + s1).astype(BF16)[None]

    def wide_stage(between):
        low = lows[pl.ds((step + 1) % 2, 1)][0]
        chunks = list(range(0, bu.shape[1], CHUNK))

        def product(c):
            return dot_nn(low, joined[:, width + c : width + c + CHUNK])

        ahead = product(0)
        for n, c in enumerate(chunks):
            hidden = ahead + bu[:, c : c + CHUNK]
            if n + 1 < len(chunks):
                ahead = product(chunks[n + 1])
            share, density = gelu_parts(hidden)
            act_ref[:, c : c + CHUNK] = (hidden * share).astype(BF16)
            slope_ref[:, c : c + CHUNK] = (share + hidden * density).astype(BF16)
            if n == 1:
                between()

    @pl.when(step == 0)
    def _():
        sooner, later = joined_copies(own, pieces, rows, joined, sems, width)
        for copy in sooner + later:
            copy.start()
        for copy in sooner:
            copy.wait()
        norm_stage()
        for copy in later:
            copy.wait()

    @pl.when((step > 0) & (step < last))
    def _():
        wide_stage(norm_stage)

    @pl.when(step == last)
    def _():
        wide_stage(lambda: None)


def feed_up(ctx, x, joined, vec, bu):
    own, pieces, rows = joined
    count = len(pieces)
    tokens, width = x.shape
    hidden = bu.shape[1]
    steps = tokens // TILE

    def now(columns):
        return pl.BlockSpec((TILE, columns), lambda s: (jnp.minimum(s, steps - 1), 0))

    def late(columns):
        return pl.BlockSpec((TILE, columns), lambda s: (jnp.maximum(s - 1, 0), 0))

    shape = jax.ShapeDtypeStruct
    return pl.pallas_call(
        functools.partial(feed_up_kernel, count),
        grid=(steps + 1,),
        in_specs=[SMEM, now(width), now(width), whole(*vec.shape), whole(*bu.shape)]
        + [ANY] * (2 + count),
        out_specs=[now(width), now(1), late(hidden), late(hidden)],
        out_shape=[
            shape((tokens, width), BF16),
            shape((tokens, 1), F32),
            shape((tokens, hidden), BF16),
            shape((tokens, hidden), BF16),
        ],
        scratch_shapes=[
            pltpu.VMEM((width, width + hidden), BF16),
            pltpu.VMEM((2, TILE, width), BF16),
            pltpu.SemaphoreType.DMA((SPLITS * (2 + 4 * count),)),
        ],
        compiler_params=params(60),
        cost_estimate=LIGHT,
        name="feed_up",
    )(rows, ctx, x, vec, bu, *own, *pieces)


def feed_down_kernel(count, steps, where, rows, normal_ref, cot_ref, vec, act_any, *refs):
    down = refs[:count]
    small_ref, send_ref, keep_ref, res_any, gd_any = refs[count : count + 5]
    wd, act, products, res, grads_all, sems, sems_act, sems_out = refs[count + 5 :]
    step = pl.program_id(0)
    tile = cot_ref.shape[0]

    def rows_at(i):
        return pl.ds(pl.multiple_of(i * tile, tile), tile)

    def stores(i):
        span = rows_at(i)
        return [
            pltpu.make_async_copy(s.at[span, :], d.at[span, :], sems_out.at[j * steps + i])
            for j, (s, d) in enumerate(((res, res_any), (grads_all, gd_any)))
        ]

    def load(i):
        span = rows_at(i)
        return pltpu.make_async_copy(act_any.at[span, :], act.at[span, :], sems_act.at[i])

    def product_stage():
        load(step).wait()
        products[pl.ds(step % 2, 1)] = dot_nn(act[rows_at(step), :], wd[...])[None]

    def norm_stage():
        span = rows_at(step - 1)
        g1, s1, bd, g2, s2 = (vec[j : j + 1, :] for j in range(1, 6))
        normed = normal_ref[...].astype(F32) * g1 + s1
        product = products[pl.ds((step + 1) % 2, 1)][0]
        normal2, scale2 = norm_parts(normed + (product + bd))
        res[span, :] = normal2 * g2 + s2
        cot = cot_ref[...].astype(F32)
        low = norm_back(cot, g2, normal2, scale2).astype(BF16)
        grads_all[span, :] = low
        for j, value in enumerate((cot * normal2, cot, low.astype(F32))):
            line = SUM_FFN + j
            small_ref[line : line + 1, :] += jnp.sum(value, axis=0, keepdims=True)
        for copy in stores(step - 1):
            copy.start()

    @pl.when(step == 0)
    def _():
        small_ref[...] = jnp.zeros_like(small_ref)
        copies = down_copies(down, rows, wd, sems)
        for copy in [load(0)] + copies + [load(j) for j in range(1, steps)]:
            copy.start()
        for copy in copies:
            copy.wait()
        product_stage()

    @pl.when((step > 0) & (step < steps))
    def _():
        product_stage()
        norm_stage()

    @pl.when(step == steps)
    def _():
        norm_stage()

    @pl.when(step > steps)
    def _():
        product_step = step - steps - 1
        height = send_ref.shape[1]
        sending = product_step < 2
        core = jnp.where(sending, 1 - where[1], where[1])
        half = jnp.where(product_step % 2 == 0, 1 - where[0], where[0])
        at_left = pl.ds(pl.multiple_of((2 * half + core) * height, LANES), height)
        value = dot_tn(act[:, at_left], grads_all[...]).astype(BF16)
        put_blocks(send_ref, keep_ref, sending, (0,), slice(None), (value,))

    @pl.when(step == steps + 4)
    def _():
        for i in range(steps):
            for copy in stores(i):
                copy.wait()


def feed_down(where, act, normal, cot, down, rows, vec):
    count = len(down)
    tokens, width = cot.shape
    wide = act.shape[1]
    steps = tokens // TILE
    height = wide // 4
    late = pl.BlockSpec((TILE, width), lambda s, *_: (jnp.clip(s - 1, 0, steps - 1), 0))
    shape = jax.ShapeDtypeStruct
    return pl.pallas_call(
        functools.partial(feed_down_kernel, count, steps),
        grid_spec=pltpu.PrefetchScalarGridSpec(
            num_scalar_prefetch=1,
            grid=(steps + 5,),
            in_specs=[SMEM, late, late, whole(*vec.shape)] + [ANY] * (1 + count),
            out_specs=[whole(SUM_ROWS, width)]
            + [send_spec(2, height, width, steps + 1), keep_spec(2, height, width, steps + 1)]
            + [ANY] * 2,
            scratch_shapes=[
                pltpu.VMEM((wide, width), BF16),
                pltpu.VMEM((tokens, wide), BF16),
                pltpu.VMEM((2, TILE, width), F32),
                pltpu.VMEM((tokens, width), F32),
                pltpu.VMEM((tokens, width), BF16),
                pltpu.SemaphoreType.DMA((SPLITS * (2 * count + 1),)),
                pltpu.SemaphoreType.DMA((steps,)),
                pltpu.SemaphoreType.DMA((2 * steps,)),
            ],
        ),
        out_shape=[shape((SUM_ROWS, width), F32)]
        + [shape((2, height, width), BF16)] * 2
        + [shape((tokens, width), F32), shape((tokens, width), BF16)],
        compiler_params=params(60),
        cost_estimate=LIGHT,
        name="feed_down",
    )(where, rows, normal, cot, vec, act, *down)


def feed_back_kernel(
    count, steps, where, rows, gd_ref, slope_ref, normal_ref, scale_ref, vec, sums_ref, ctx_any,
    *refs,
):
    own, pieces = refs[:2], refs[2 : 2 + count]
    down = refs[2 + count : 3 + 2 * count]
    small_ref, send_ref, keep_ref, ga_any, gc_any = refs[3 + 2 * count : 8 + 2 * count]
    (
        joined, wd, low, ctx, hidden_all, attended_all, grad_sums, gc, wide,
        sems, sems_down, sem_ctx, sems_out,
    ) = refs[8 + 2 * count :]
    tile, width = gd_ref.shape
    hidden = wide.shape[1]
    step = pl.program_id(0)
    load_ctx = pltpu.make_async_copy(ctx_any, ctx, sem_ctx.at[0])

    def rows_at(i):
        return pl.ds(pl.multiple_of(i * tile, tile), tile)

    def stores(i):
        span = rows_at(i)
        return [
            pltpu.make_async_copy(s.at[span, :], d.at[span, :], sems_out.at[j * steps + i])
            for j, (s, d) in enumerate(((attended_all, ga_any), (gc, gc_any)))
        ]

    def norm_stage():
        span = rows_at(step - 1)
        grad_normed = grad_sums[pl.ds((step + 1) % 2, 1)][0]
        normal = normal_ref[...].astype(F32)
        low[span, :] = (normal * vec[1:2, :] + vec[2:3, :]).astype(BF16)
        rounded = norm_back(grad_normed, vec[1:2, :], normal, scale_ref[...]).astype(BF16)
        attended_all[span, :] = rounded
        for j, value in enumerate((grad_normed * normal, grad_normed, rounded.astype(F32))):
            line = SUM_ATTN + j
            small_ref[line : line + 1, :] += jnp.sum(value, axis=0, keepdims=True)
        gc[span, :] = dot_nt(rounded, joined[:, :width]).astype(BF16)

    def wide_stage(waiting, between):
        span = rows_at(step)
        chunks = list(range(0, hidden, CHUNK))

        def product(c):
            return dot_nt(gd_ref[...], wd[c : c + CHUNK, :])

        ahead = product(0)
        for copy in waiting:
            copy.wait()
        total = gd_ref[...].astype(F32)
        for n, c in enumerate(chunks):
            grad_active = ahead
            if n + 1 < len(chunks):
                ahead = product(chunks[n + 1])
            rounded = (grad_active * slope_ref[:, c : c + CHUNK].astype(F32)).astype(BF16)
            hidden_all[span, c : c + CHUNK] = rounded
            wide[0:1, c : c + CHUNK] += jnp.sum(rounded.astype(F32), axis=0, keepdims=True)
            total = total + dot_nt(rounded, joined[:, width + c : width + c + CHUNK])
            if n == 1:
                between()
        grad_sums[pl.ds(step % 2, 1)] = total[None]

    @pl.when(step == 0)
    def _():
        copies = down_copies(down, rows, wd, sems_down)
        later = joined_copies(own, pieces, rows, joined, sems)
        for copy in copies + later + [load_ctx]:
            copy.start()
        small_ref[...] = sums_ref[...]
        wide[...] = jnp.zeros_like(wide)
        for copy in copies:
            copy.wait()
        wide_stage(later, lambda: None)

    @pl.when((step > 0) & (step < steps))
    def _():
        wide_stage([], norm_stage)

    @pl.when(step == steps)
    def _():
        norm_stage()
        for j in range(hidden // width):
            line = SUM_UP + j
            small_ref[line : line + 1, :] = wide[0:1, j * width : (j + 1) * width]
        load_ctx.wait()

    @pl.when((step > 0) & (step <= steps))
    def _():
        for copy in stores(step - 1):
            copy.start()

    @pl.when(step > steps)
    def _():
        sending = step == steps + 1
        core = jnp.where(sending, 1 - where[1], where[1])
        height, cut = width // 2, hidden // 2
        at_wide = pl.ds(pl.multiple_of(core * cut, LANES), cut)
        at_narrow = pl.ds(pl.multiple_of(core * height, LANES), height)
        slots = (jnp.where(where[0] == 0, 1, 0), jnp.where(where[0] == 0, 0, 1))
        value = dot_tn(low[...], hidden_all[:, at_wide]).astype(BF16)
        put_blocks(
            send_ref, keep_ref, sending, slots, slice(0, cut), (value[:height], value[height:])
        )
        value = dot_tn(ctx[...], attended_all[:, at_narrow]).astype(BF16)
        put_blocks(
            send_ref, keep_ref, sending, slots, slice(cut, cut + height),
            (value[:height], value[height:]),
        )

    @pl.when(step == steps + 2)
    def _():
        for i in range(steps):
            for copy in stores(i):
                copy.wait()


def feed_back(where, gd, slope, normal, scale, joined, down, vec, context, sums):
    own, pieces, rows = joined
    count = len(pieces)
    tokens, width = gd.shape
    wide = slope.shape[1]
    steps = tokens // TILE
    total = (wide + width) // 2

    def now(columns):
        return pl.BlockSpec((TILE, columns), lambda s, *_: (jnp.minimum(s, steps - 1), 0))

    def late(columns):
        return pl.BlockSpec((TILE, columns), lambda s, *_: (jnp.clip(s - 1, 0, steps - 1), 0))

    shape = jax.ShapeDtypeStruct
    return pl.pallas_call(
        functools.partial(feed_back_kernel, count, steps),
        grid_spec=pltpu.PrefetchScalarGridSpec(
            num_scalar_prefetch=1,
            grid=(steps + 3,),
            in_specs=[SMEM, now(width), now(wide), late(width), late(1)]
            + [whole(*vec.shape), whole(*sums.shape)]
            + [ANY] * (4 + 2 * count),
            out_specs=[whole(*sums.shape)]
            + [send_spec(1, width // 2, total, steps + 1)]
            + [keep_spec(1, width // 2, total, steps + 1)]
            + [ANY] * 2,
            scratch_shapes=[
                pltpu.VMEM((width, width + wide), BF16),
                pltpu.VMEM((wide, width), BF16),
                pltpu.VMEM((tokens, width), BF16),
                pltpu.VMEM((tokens, width), BF16),
                pltpu.VMEM((tokens, wide), BF16),
                pltpu.VMEM((tokens, width), BF16),
                pltpu.VMEM((2, TILE, width), F32),
                pltpu.VMEM((tokens, width), BF16),
                pltpu.VMEM((8, wide), F32),
                pltpu.SemaphoreType.DMA((SPLITS * (2 + 2 * count),)),
                pltpu.SemaphoreType.DMA((SPLITS * (1 + 2 * count),)),
                pltpu.SemaphoreType.DMA((1,)),
                pltpu.SemaphoreType.DMA((2 * steps,)),
            ],
        ),
        out_shape=[shape(sums.shape, F32)]
        + [shape((2, width // 2, total), BF16)] * 2
        + [shape((tokens, width), BF16)] * 2,
        compiler_params=params(60),
        cost_estimate=LIGHT,
        name="feed_back",
    )(where, rows, gd, slope, normal, scale, vec, sums, context, *own, *pieces, *down)


def inputs_back_kernel(count, rows, ga_ref, grads, *refs):
    own, pieces = refs[:3], refs[3 : 3 + count]
    out_ref, full, sems = refs[3 + count :]

    @pl.when(pl.program_id(0) == 0)
    def _():
        fetch_joined(own, pieces, rows, full, sems)

    out_ref[...] = ga_ref[...].astype(F32) + dot_nt(grads[...], full[...])


def inputs_back(grads, ga, weights):
    own, pieces, rows = weights
    tokens, width = ga.shape
    tile = pl.BlockSpec((TILE, width), lambda t: (t, 0))
    return pl.pallas_call(
        functools.partial(inputs_back_kernel, len(pieces)),
        grid=(tokens // TILE,),
        in_specs=[SMEM, tile, pl.BlockSpec((TILE, 3 * width), lambda t: (t, 0))]
        + [ANY] * (3 + len(pieces)),
        out_specs=tile,
        out_shape=jax.ShapeDtypeStruct((tokens, width), F32),
        scratch_shapes=[
            pltpu.VMEM((width, 3 * width), BF16),
            pltpu.SemaphoreType.DMA((SPLITS * (3 + 2 * len(pieces)),)),
        ],
        compiler_params=params(60),
        cost_estimate=LIGHT,
        name="inputs_back",
    )(rows, ga, grads, *own, *pieces)


CORE, NEAR_Y, NEAR_Z, FAR_Z = 1, 2, 4, 8


def after(value, *others):
    return lax.optimization_barrier((value,) + others)[0]


def swap_dp(values, bit):
    size = lax.axis_size("dp")
    return lax.ppermute(values, "dp", [(i, i ^ bit) for i in range(size)])


def swap_fsdp(values):
    return lax.ppermute(values, "fsdp", [(0, 1), (1, 0)])


def swap_both(values):
    size = lax.axis_size("dp")
    pairs = [(2 * i + h, 2 * (i ^ NEAR_Y) + 1 - h) for i in range(size) for h in range(2)]
    return lax.ppermute(values, ("dp", "fsdp"), pairs)


def rows_of(values, start, count):
    return lax.dynamic_slice_in_dim(values, start, count, axis=0)


def own_part(shards, place):
    half, core, y, z = place
    height = shards[0].shape[0]
    count = height // 8
    starts = (2 * y + core) * count, height // 2 + (2 * z + core) * count
    return jnp.concatenate(
        [jnp.concatenate([rows_of(s, start, count) for s in shards], axis=1) for start in starts],
        axis=0,
    )


def pass_on(first):
    count = first.shape[0] // 2
    along, up = swap_dp(first[:count], NEAR_Y), swap_dp(first[count:], NEAR_Z)
    return (first, along, up) + tuple(swap_dp(part, CORE) for part in (first, along, up))


def far_parts(first):
    count = first.shape[0] // 2
    left, right = first[:count], first[count:]
    return (
        swap_dp(left, NEAR_Y),
        swap_dp(right, NEAR_Z),
        swap_dp(left, NEAR_Y | CORE),
        swap_dp(right, NEAR_Z | CORE),
    )


def all_parts(first, far):
    return (first,) + far[:2] + (swap_dp(first, CORE),) + far[2:]


def piece_rows(height, place):
    half, core, y, z = place
    count = height // 8
    base = (1 - half) * height
    rows = [half * height]
    for c in (core, 1 - core):
        rows += [
            base + (2 * y + c) * count,
            base + height // 2 + (2 * z + c) * count,
            base + (2 * (1 - y) + c) * count,
            base + height // 2 + (2 * (1 - z) + c) * count,
        ]
    return jnp.stack(rows).astype(jnp.int32)


class Part:
    def __init__(self, terms, place, columns=None):
        self.bits = {0: 1, 1: place[2], 2: place[3]}
        self.swaps = {
            0: swap_fsdp,
            1: lambda v: swap_dp(v, NEAR_Y),
            2: lambda v: swap_dp(v, NEAR_Z),
            3: lambda v: swap_dp(v, FAR_Z),
        }
        self.terms = [t.reshape(2, 2, 2, t.shape[1] // 4, t.shape[2]) for t in terms]
        self.views = [(columns, ())] * len(terms)
        self.flight, self.joined = [], None

    def total(self, *picks):
        value = None
        for term, (columns, before) in zip(self.terms, self.views):
            if columns is not None:
                term = term[..., columns[0] : columns[1]]
            for axis, index in before + picks:
                term = lax.dynamic_slice_in_dim(term, index, 1, axis)
            term = term.astype(F32)
            value = term if value is None else value + term
        return value.astype(BF16)

    def cut(self, *picks):
        self.views = [(columns, before + picks) for columns, before in self.views]

    def halve(self, axis):
        bit = self.bits[axis]
        self.flight, self.route = [self.total((axis, 1 - bit))], [self.swaps[axis]]
        self.cut((axis, bit))

    def both(self):
        bit = self.bits[1]
        self.flight = [
            self.total((0, 0), (1, bit)),
            self.total((0, 1), (1, 1 - bit)),
            self.total((0, 0), (1, 1 - bit)),
        ]
        self.route = [self.swaps[0], self.swaps[1], swap_both]
        self.cut((0, 1), (1, bit))

    def merge(self, *others):
        value = jnp.concatenate([part.total() for part in (self,) + others], axis=-1)
        self.terms, self.views = [value], [(None, ())]

    def split(self, cut):
        other = copy.copy(self)
        end = self.terms[0].shape[-1]
        self.views = [((0, cut), before) for _, before in self.views]
        other.views = [((cut, end), before) for _, before in other.views]
        return other

    def send_whole(self, swap, reshape=None):
        value = self.terms[0]
        if len(self.terms) > 1 or self.views[0][0] is not None:
            value = self.total()
        if reshape:
            value = value.reshape(-1, value.shape[-1])
        self.flight, self.route = [value], [lambda v: (v, swap(v))]
        self.terms, self.views = [], []

    def far(self):
        self.send_whole(self.swaps[3])

    def join(self, axis):
        self.send_whole(self.swaps[axis])
        self.joined = axis

    def finish(self):
        self.send_whole(lambda v: swap_dp(v, CORE), True)

    def land(self):
        for sent, route in zip(self.flight, self.route):
            got = route(sent)
            self.terms += list(got) if isinstance(got, tuple) else [got]
        self.views = self.views + [(None, ())] * (len(self.terms) - len(self.views))
        self.flight = []

    def settle(self):
        if self.joined is None:
            return
        mine, other = self.terms
        axis, self.joined = self.joined, None
        value = jnp.where(
            self.bits[axis] == 0,
            jnp.concatenate([mine, other], axis=axis),
            jnp.concatenate([other, mine], axis=axis),
        )
        self.terms, self.views = [value], [(None, ())]


def fence(parts, *arrays):
    counts = [(len(p.terms), len(p.flight)) for p in parts]
    flat = [a for p in parts for a in p.terms + p.flight] + list(arrays)
    flat = list(lax.optimization_barrier(tuple(flat)))
    for part, (terms, flight) in zip(parts, counts):
        part.terms, flat = flat[:terms], flat[terms:]
        part.flight, flat = flat[:flight], flat[flight:]
    return flat


def widen(mine, other, core, axis):
    low = jnp.where(core == 0, mine, other).astype(F32)
    high = jnp.where(core == 0, other, mine).astype(F32)
    return jnp.concatenate([low, high], axis=axis)


def gather_all(values):
    return lax.all_gather(values, "fsdp", axis=0, tiled=True)


def sum_plain(send, keep, by_rows):
    blocks = [[keep[1], send[1]], [keep[0], send[0]]]
    axis = 0 if by_rows else 1
    value = jnp.concatenate([jnp.concatenate(pair, axis=axis) for pair in blocks], axis=0)
    own = lax.psum_scatter(value, "fsdp", scatter_dimension=0, tiled=True)
    return lax.psum(own, "dp").astype(F32)


def local(
    inputs, segment_ids, cotangent, w_query, b_query, w_key, b_key, w_value, b_value,
    w_output, b_output, gain_attn, bias_attn, w_up, b_up, w_down, b_down, gain_ffn, bias_ffn,
):
    rows, length = segment_ids.shape
    width = inputs.shape[1]
    shards = lax.axis_size("fsdp")
    paired = shards == 2 and lax.axis_size("dp") == 16
    half = lax.axis_index("fsdp")
    dp = lax.axis_index("dp")
    place = (half, dp % 2, dp // 2 % 2, dp // 4 % 2)
    core = place[1]
    vectors = (b_query, b_key, b_value, b_output, gain_attn, bias_attn, b_down, gain_ffn, bias_ffn)
    height = w_query.shape[0]
    cosine, sine, turned = rotary_tables(segment_ids, inputs)
    if paired:
        where = jnp.stack([half, core]).astype(jnp.int32)
        part_qkv = own_part((w_query, w_key, w_value), place)
        part_up = own_part((w_output, w_up), place)
        part_down = own_part((w_down,), place)
        here_qkv = after(swap_fsdp(part_qkv), cosine)
        lines = jnp.concatenate(vectors + (b_up,)).reshape(-1, height)
        other = swap_fsdp(after(lines, part_qkv))
        here_up = swap_fsdp(after(part_up, here_qkv))
        at = piece_rows(height, place)
        joined_qkv = ((w_query, w_key, w_value), pass_on(here_qkv), at)
        lines = jnp.where(half == 0, jnp.stack([lines, other]), jnp.stack([other, lines]))
    else:
        where = jnp.zeros((2,), jnp.int32)
        at = jnp.zeros((1,), jnp.int32)
        joined_qkv = (tuple(gather_all(w) for w in (w_query, w_key, w_value)), (), at)
        joined_up = ((gather_all(w_output), gather_all(w_up)), (), at)
        down = (gather_all(w_down),)
        lines = jnp.concatenate(vectors + (b_up,)).reshape(-1, height)
        lines = lax.all_gather(lines, "fsdp", axis=0)
    lines = lines.astype(F32)
    vec = jnp.swapaxes(lines[:, :9], 0, 1).reshape(9, width)
    bias_up = lines[:, 9:].reshape(1, -1)

    q, k, v = project(inputs, joined_qkv, vec[:3], cosine, sine)
    vec = vec[3:]
    if paired:
        q, here_up, part_down, vec, bias_up = lax.optimization_barrier(
            (q, here_up, part_down, vec, bias_up)
        )
        here_down = swap_fsdp(part_down)
        far_up = far_parts(here_up)
    context, probs = attend(q, k, v, segment_ids)
    if paired:
        context, probs, here_up, here_down, far_up = lax.optimization_barrier(
            (context, probs, here_up, here_down, far_up)
        )
        joined_up = ((w_output, w_up), all_parts(here_up, far_up), at)
        far_down = far_parts(here_down)
    normal, scale, act, slope = feed_up(context, inputs, joined_up, vec, bias_up)
    if paired:
        act, slope, here_down, far_down = lax.optimization_barrier(
            (act, slope, here_down, far_down)
        )
        down = (w_down,) + all_parts(here_down, far_down)
    sums, send, keep, result, grad_down = feed_down(
        where, act, normal, cotangent, down, at, vec
    )
    sent = [(send, keep)]
    if paired:
        sum_d = Part([keep, swap_dp(send, CORE)], place)
        sum_d.both()
        (grad_down,) = fence([sum_d], grad_down)
    outs = feed_back(
        where, grad_down, slope, normal, scale, joined_up, down, vec, context, sums
    )
    sent.append(outs[1:3])
    if paired:
        sum_d.land()
        outs = fence([sum_d], *outs)
    sums, send, keep, grad_attended, grad_context = outs
    if paired:
        sum_d.merge()
        sum_u = Part([keep, swap_dp(send, CORE)], place)
        sum_d.halve(2)
        sum_u.both()
        parts = [sum_d, sum_u]
        (grad_context,) = fence(parts, grad_context)
    outs = attend_back(where, q, k, v, grad_context, probs, cosine, sine, turned, sums)
    sent.append(outs[1:3])
    if paired:
        for p in parts:
            p.land()
        outs = fence(parts, *outs)
    sums, send, keep, grads = outs
    if paired:
        sum_q = Part([keep, swap_dp(send, CORE)], place)
        sum_u.merge()
        sum_d.far()
        sum_u.halve(2)
        sum_q.both()
        parts = [sum_d, sum_u, sum_q]
        (grad_attended,) = fence(parts, grad_attended)
    grad_inputs = inputs_back(grads, grad_attended, joined_qkv)
    if paired:
        for p in parts:
            p.land()
        (grad_inputs,) = fence(parts, grad_inputs)
        last = grad_inputs

        def step(part, name, *axis):
            nonlocal last
            (last,) = fence([part], last)
            part.settle()
            getattr(part, name)(*axis)
            (last,) = fence([part], last)
            last = part.flight[0]
            part.land()

        step(sum_d, "join", 2)
        sum_q.merge()
        step(sum_q, "halve", 2)
        step(sum_u, "far")
        step(sum_d, "join", 1)
        step(sum_q, "far")
        cut_u, cut_q = ((p.terms[0].shape[-1] // 2 + 64) // LANES * LANES for p in (sum_u, sum_q))
        (last,) = fence([sum_u], last)
        sum_v = sum_u.split(cut_u)
        step(sum_u, "join", 2)
        step(sum_v, "join", 1)
        step(sum_d, "finish")
        gwd = widen(*sum_d.terms, core, 0)
        (last,) = fence([sum_q], last)
        sum_r = sum_q.split(cut_q)
        step(sum_q, "join", 2)
        step(sum_r, "join", 1)
        step(sum_u, "join", 1)
        step(sum_v, "join", 2)
        (gwd,) = fence([sum_q, sum_r], gwd)
        step(sum_q, "join", 1)
        step(sum_r, "join", 2)
        step(sum_u, "finish")
        step(sum_v, "finish")
        fence([sum_u, sum_v, sum_q, sum_r])
        step(sum_q, "finish")
        step(sum_r, "finish")
    else:
        sums = lax.psum(sums, ("dp", "fsdp"))

    wide = b_up.shape[0] * shards
    if paired:
        mine, other = (
            jnp.concatenate([a, b], axis=1) for a, b in zip(sum_u.terms, sum_v.terms)
        )
        cut = wide // 2
        gwu = widen(mine[:, :cut], other[:, :cut], core, 1)
        gwo = widen(mine[:, cut:], other[:, cut:], core, 1)
        mine, other = (
            jnp.concatenate([a, b], axis=1) for a, b in zip(sum_q.terms, sum_r.terms)
        )
        gwq, gwk, gwv = (
            widen(*(end[:, i * width : (i + 1) * width] for end in (mine, other)), core, 0)
            for i in range(3)
        )
        count = height // LANES
        packed = jnp.where(core == 0, mine[:, 3 * width :], other[:, 3 * width :])
        packed = packed[: len(LINES) * count + wide // 2 // LANES].astype(F32)
        vectors = [packed[i * count : (i + 1) * count].reshape(-1) for i in range(len(LINES))]
        gbu = packed[len(LINES) * count :].reshape(-1)
        ggf, gbf, gbd, gga, gba, gbo, gbq, gbk, gbv = vectors
    else:

        def own(line, count=1):
            start = line * width + half * (count * width // shards)
            return lax.dynamic_slice_in_dim(
                sums.reshape(-1), start, count * width // shards, axis=0
            )

        ggf, gbf, gbd, gga, gba, gbo, gbq, gbk, gbv = (own(line) for line in LINES)
        gbu = own(SUM_UP, wide // width)
        gwd = sum_plain(*sent[0], True)
        both = sum_plain(*sent[1], False).reshape(height, 2, -1)
        cut = wide // 2
        gwu = both[..., :cut].reshape(height, -1)
        gwo = both[..., cut:].reshape(height, -1)
        both = sum_plain(*sent[2], True)
        gwq, gwk, gwv = (both[:, i * width : (i + 1) * width] for i in range(3))
    return (
        result, grad_inputs, gwq, gbq, gwk, gbk, gwv, gbv, gwo, gbo, gga, gba,
        gwu, gbu, gwd, gbd, ggf, gbf,
    )


def solution(mesh):
    tokens, matrix, vector = P(("dp", "fsdp"), None), P("fsdp", None), P("fsdp")
    weights = (
        matrix, vector, matrix, vector, matrix, vector, matrix, vector, vector, vector,
        matrix, vector, matrix, vector, vector, vector,
    )
    return jax.shard_map(
        local,
        mesh=mesh,
        in_specs=(tokens,) * 3 + weights,
        out_specs=(tokens,) * 2 + weights,
        check_vma=False,
    )
```

```python
import copy
import functools
import jax
import jax.numpy as jnp
from jax import lax
from jax.experimental import pallas as pl
from jax.experimental.pallas import tpu as pltpu
from jax.sharding import PartitionSpec as P

HEAD = 64
GROUP = 3
EPSILON = 1e-06
LANES = 128
TILE = 256
CHUNK = 512
MASKED = -1e30
SUM_FFN, SUM_ATTN, SUM_UP, SUM_QKV, SUM_ROWS = 0, 3, 6, 10, 16
F32 = jnp.float32
BF16 = jnp.bfloat16


def params(mebibytes):
    return pltpu.CompilerParams(vmem_limit_bytes=mebibytes * 1024 * 1024)


LIGHT = pl.CostEstimate(flops=1000, bytes_accessed=1000, transcendentals=0)


def dot_nn(left, right):
    return lax.dot_general(left, right, (((1,), (0,)), ((), ())), preferred_element_type=F32)


def dot_nt(left, right):
    return lax.dot_general(left, right, (((1,), (1,)), ((), ())), preferred_element_type=F32)


def dot_tn(left, right):
    return lax.dot_general(left, right, (((0,), (0,)), ((), ())), preferred_element_type=F32)


def whole(*shape):
    return pl.BlockSpec(shape, lambda *_: (0,) * len(shape))


SPLITS = 4


def piece_copies(pieces, starts, full, column, sems, first):
    copies = []
    assert len(pieces) == len(starts)
    for i, (piece, start) in enumerate(zip(pieces, starts)):
        height, width = piece.shape
        splits = SPLITS if height * width >= 500_000 and height % (16 * SPLITS) == 0 else 1
        count = height // splits
        for j in range(splits):
            row = pl.multiple_of(start + j * count, 16)
            copies.append(
                pltpu.make_async_copy(
                    piece.at[pl.ds(j * count, count), :],
                    full.at[pl.ds(row, count), column : column + width],
                    sems.at[SPLITS * (first + i) + j],
                )
            )
    return copies


def cut_pieces(pieces):
    cut = []
    for i, piece in enumerate(pieces):
        count = piece.shape[0] // 2
        cut += [piece.at[:count, :], piece.at[count:, :]] if i % 3 == 0 else [piece]
    return cut


def joined_copies(own, pieces, rows, full, sems, cut=None):
    pieces = cut_pieces(pieces)
    shards, column = [], 0
    for i, shard in enumerate(own):
        shards.append(piece_copies([shard], [rows[0]], full, column, sems, i))
        column += shard.shape[1]
    starts = [rows[1 + i] for i in range(len(pieces))]
    first = len(own)
    if cut is None:
        return sum(shards, []) + piece_copies(pieces, starts, full, 0, sems, first)
    left = [piece.at[:, :cut] for piece in pieces]
    right = [piece.at[:, cut:] for piece in pieces]
    return (
        shards[0] + piece_copies(left, starts, full, 0, sems, first),
        sum(shards[1:], []) + piece_copies(right, starts, full, cut, sems, first + len(pieces)),
    )


def fetch_joined(own, pieces, rows, full, sems):
    copies = joined_copies(own, pieces, rows, full, sems)
    for copy in copies:
        copy.start()
    for copy in copies:
        copy.wait()


ANY = pl.BlockSpec(memory_space=pl.ANY)
SMEM = pl.BlockSpec(memory_space=pltpu.SMEM)


def tables_kernel(seg_row, seg_col, x_ref, cos_ref, sin_ref, turned_ref):
    length = seg_row.shape[-1]
    key = lax.broadcasted_iota(jnp.int32, (length, length), 1)
    query = lax.broadcasted_iota(jnp.int32, (length, length), 0)
    earlier = (seg_col[...] == seg_row[0]) & (key < query)
    place = jnp.sum(earlier.astype(F32), axis=1, keepdims=True)
    lane = lax.broadcasted_iota(jnp.int32, (1, LANES), 1)
    paired = (lane % HEAD // 2 * 2).astype(F32)
    freqs = jnp.exp(-jnp.log(F32(10000.0)) * paired / HEAD)
    angle = place * freqs
    cos_ref[...] = jnp.cos(angle)
    sine = jnp.sin(angle)
    sin_ref[...] = jnp.where(lane % 2 == 0, -sine, sine)
    turned_ref[...] = x_ref[...].T


def rotary_tables(segments, x):
    rows, length = segments.shape
    width = x.shape[1]
    return pl.pallas_call(
        tables_kernel,
        grid=(rows,),
        in_specs=[
            pl.BlockSpec((1, 1, length), lambda r: (r, 0, 0)),
            pl.BlockSpec((length, 1), lambda r: (r, 0)),
            pl.BlockSpec((length, width), lambda r: (r, 0)),
        ],
        out_specs=[pl.BlockSpec((length, LANES), lambda r: (r, 0))] * 2
        + [pl.BlockSpec((width, length), lambda r: (0, r))],
        out_shape=[jax.ShapeDtypeStruct((rows * length, LANES), F32)] * 2
        + [jax.ShapeDtypeStruct((width, rows * length), BF16)],
        compiler_params=params(60),
        cost_estimate=LIGHT,
        name="rotary_tables",
    )(segments.reshape(rows, 1, length), segments.reshape(rows * length, 1), x)


def pair_swap(values):
    even = lax.broadcasted_iota(jnp.int32, values.shape, 1) % 2 == 0
    return jnp.where(
        even, pltpu.roll(values, LANES - 1, axis=1), pltpu.roll(values, 1, axis=1)
    )


def project_kernel(count, rows, x_ref, bias, cos_ref, sin_ref, *refs):
    own, pieces = refs[:3], refs[3 : 3 + count]
    q_ref, k_ref, v_ref, full, sems = refs[3 + count :]
    width = x_ref.shape[1]

    @pl.when(pl.program_id(0) == 0)
    def _():
        fetch_joined(own, pieces, rows, full, sems)

    x = x_ref[...]
    cosine, sine = cos_ref[...], sin_ref[...]
    step = 2 * LANES
    for i, out in enumerate((q_ref, k_ref, v_ref)):
        for c in range(0, width, step):
            lin = dot_nn(x, full[:, i * width + c : i * width + c + step])
            lin = lin + bias[i : i + 1, c : c + step]
            if i < 2:
                parts = []
                for d in range(0, step, LANES):
                    part = lin[:, d : d + LANES]
                    part = part * cosine + pair_swap(part) * sine
                    parts.append(part)
                lin = jnp.concatenate(parts, axis=1)
            if i == 0:
                out[:, c : c + step] = (lin.astype(BF16).astype(F32) * 0.125).astype(BF16)
            else:
                out[:, c : c + step] = lin.astype(BF16)


def project(x, weights, bias, cosine, sine):
    own, pieces, rows = weights
    tokens, width = x.shape
    tile = pl.BlockSpec((TILE, width), lambda t: (t, 0))
    table = pl.BlockSpec((TILE, LANES), lambda t: (t, 0))
    return pl.pallas_call(
        functools.partial(project_kernel, len(pieces)),
        grid=(tokens // TILE,),
        in_specs=[SMEM, tile, whole(*bias.shape), table, table] + [ANY] * (3 + len(pieces)),
        out_specs=[tile] * 3,
        out_shape=[jax.ShapeDtypeStruct((tokens, width), BF16)] * 3,
        scratch_shapes=[
            pltpu.VMEM((width, 3 * width), BF16),
            pltpu.SemaphoreType.DMA((SPLITS * (3 + 2 * len(pieces)),)),
        ],
        compiler_params=params(60),
        cost_estimate=LIGHT,
        name="project",
    )(rows, x, bias, cosine, sine, *own, *pieces)


def spans(length):
    found, offset = [], 0
    for first in range(0, length, LANES):
        low, high = max(first - LANES, 0), min(first + 2 * LANES, length)
        found.append((slice(first, first + LANES), slice(low, high), slice(offset, offset + high - low)))
        offset += high - low
    return found, offset


def split_heads(values):
    lane = lax.broadcasted_iota(jnp.int32, (1, LANES), 1)
    return [jnp.where(lane // HEAD == h, values, jnp.zeros_like(values)) for h in range(2)]


def stack_heads(heads, rows):
    return jnp.concatenate([head[rows, :] for head in heads], axis=0)


def merge_heads(stacked):
    lane = lax.broadcasted_iota(jnp.int32, (1, LANES), 1)
    half = stacked.shape[0] // 2
    return jnp.where(lane < HEAD, stacked[:half], stacked[half:])


def attend_kernel(q_ref, k_ref, v_ref, seg_row, seg_col, ctx_ref, prob_ref, bias):
    blocks, _ = spans(q_ref.shape[0])

    @pl.when(pl.program_id(1) == 0)
    def _():
        for own, span, at in blocks:
            bias[at, :] = jnp.where(seg_col[span, :] == seg_row[0, :, own], 0.0, MASKED)

    pairs = [slice(p * LANES, (p + 1) * LANES) for p in range(GROUP)]
    units = [(p, lanes) + block for p, lanes in enumerate(pairs) for block in blocks]
    queries = [split_heads(q_ref[:, lanes]) for lanes in pairs]

    def product(unit):
        p, lanes, own, span, _ = unit
        return dot_nt(k_ref[span, lanes], stack_heads(queries[p], own))

    def soften(unit, scores):
        at = unit[-1]
        heads = []
        for h in range(2):
            masked = scores[:, h * LANES : (h + 1) * LANES] + bias[at, :]
            peak = jnp.max(masked, axis=0, keepdims=True)
            expo = jnp.exp(masked - peak)
            total = jnp.sum(expo, axis=0, keepdims=True)
            heads.append((expo * (1.0 / total)).astype(BF16))
        return jnp.concatenate(heads, axis=1)

    def finish(unit, probs):
        p, lanes, own, span, at = unit
        prob_ref[0, p, at, :] = probs
        ctx_ref[own, lanes] = merge_heads(dot_tn(probs, v_ref[span, lanes])).astype(BF16)

    count = len(blocks)
    scores = [product(unit) for unit in units[:count]]
    waiting = []
    for p in range(GROUP):
        now = units[p * count : (p + 1) * count]
        probs = [soften(unit, value) for unit, value in zip(now, scores)]
        scores = [product(unit) for unit in units[(p + 1) * count : (p + 2) * count]]
        for unit, value in waiting:
            finish(unit, value)
        waiting = list(zip(now, probs))
    for unit, value in waiting:
        finish(unit, value)


def attend(q, k, v, segments):
    rows, length = segments.shape
    tokens, width = q.shape
    pairs = width // LANES
    wide = GROUP * LANES
    _, depth = spans(length)
    head = pl.BlockSpec((length, wide), lambda r, p: (r, p))
    return pl.pallas_call(
        attend_kernel,
        grid=(rows, pairs // GROUP),
        in_specs=[head] * 3
        + [
            pl.BlockSpec((1, 1, length), lambda r, p: (r, 0, 0)),
            pl.BlockSpec((length, 1), lambda r, p: (r, 0)),
        ],
        out_specs=[
            head,
            pl.BlockSpec((1, GROUP, depth, 2 * LANES), lambda r, p: (r, p, 0, 0)),
        ],
        out_shape=[
            jax.ShapeDtypeStruct((tokens, width), BF16),
            jax.ShapeDtypeStruct((rows, pairs, depth, 2 * LANES), BF16),
        ],
        scratch_shapes=[pltpu.VMEM((depth, LANES), F32)],
        compiler_params=params(60),
        cost_estimate=LIGHT,
        name="attend",
    )(q, k, v, segments.reshape(rows, 1, length), segments.reshape(tokens, 1))


def send_spec(steps, height, width, first):
    return pl.BlockSpec(
        (2 // steps, height, width), lambda s, *_: (jnp.clip(s - first, 0, steps - 1), 0, 0)
    )


def keep_spec(steps, height, width, first):
    return pl.BlockSpec(
        (2 // steps, height, width), lambda s, *_: (jnp.clip(s - first - steps, 0, steps - 1), 0, 0)
    )


def put_blocks(send_ref, keep_ref, sending, slots, columns, values):
    @pl.when(sending)
    def _():
        for slot, value in zip(slots, values):
            send_ref[slot, :, columns] = value

    @pl.when(jnp.logical_not(sending))
    def _():
        for slot, value in zip(slots, values):
            keep_ref[slot, :, columns] = value


LINES = (SUM_FFN, SUM_FFN + 1, SUM_FFN + 2, SUM_ATTN, SUM_ATTN + 1, SUM_ATTN + 2) + (
    SUM_QKV, SUM_QKV + 1, SUM_QKV + 2,
)


def pack_vectors(small_ref, packed, half):
    width = small_ref.shape[1]
    part = width // 2 // LANES
    packed[...] = jnp.zeros_like(packed)
    for i, line in enumerate(LINES):
        for j in range(part):
            lanes = pl.ds(pl.multiple_of(half * (width // 2) + j * LANES, LANES), LANES)
            packed[i * part + j : i * part + j + 1, :] = small_ref[line : line + 1, lanes]
    base, count = len(LINES) * part, width // LANES
    lines = (SUM_QKV - SUM_UP) // 2
    for i in range(lines):
        for j in range(count):
            row = base + i * count + j
            lanes = slice(j * LANES, (j + 1) * LANES)
            low, high = (small_ref[SUM_UP + n : SUM_UP + n + 1, lanes] for n in (i, lines + i))
            packed[row : row + 1, :] = jnp.where(half == 0, low, high)


def attend_back_kernel(
    rows, before, last, where, q_ref, k_ref, v_ref, g_ref, prob_ref, cos_ref, sin_ref, sums_ref,
    *refs,
):
    if last:
        (
            turned_any, *made_any, small_ref, send_ref, keep_ref, out_any,
            acc_k, acc_v, grads_all, turned, packed, sems,
        ) = refs
    else:
        small_ref, out_any, acc_k, acc_v, grads_all, sems = refs
    step = pl.program_id(0)
    length, width = q_ref.shape[0], small_ref.shape[1]
    pairs = width // LANES
    units = rows * pairs // GROUP
    hand_on = pltpu.make_async_copy(grads_all, out_any, sems.at[0])
    loads = []
    if last:
        loads.append(pltpu.make_async_copy(turned_any, turned, sems.at[1]))
        if before:
            target = grads_all.at[pl.ds(0, before * length), :]
            loads.append(pltpu.make_async_copy(made_any[0], target, sems.at[2]))

    @pl.when(step == 0)
    def _():
        for load in loads:
            load.start()
        small_ref[...] = sums_ref[...]

    @pl.when(step < units)
    def _():
        blocks, _ = spans(length)
        groups = pairs // GROUP
        row, group = before * last + step // groups, step % groups
        at_rows = pl.ds(pl.multiple_of(row * length, length), length)
        lanes_of = [slice(p * LANES, (p + 1) * LANES) for p in range(GROUP)]

        def turn_back(values, rows):
            return values * cos_ref[rows, :] - pair_swap(values) * sin_ref[rows, :]

        def first(p):
            grads = split_heads(g_ref[:, lanes_of[p]])
            return [
                dot_nt(v_ref[span, lanes_of[p]], stack_heads(grads, own)) for own, span, _ in blocks
            ]

        def second(p, grad_probs):
            made = []
            for (own, span, at), pair in zip(blocks, grad_probs):
                heads = []
                for h in range(2):
                    columns = slice(h * LANES, (h + 1) * LANES)
                    probs = prob_ref[0, p, at, columns].astype(F32)
                    inner = jnp.sum(probs * pair[:, columns], axis=0, keepdims=True)
                    heads.append((probs * (pair[:, columns] - inner)).astype(BF16))
                made.append(jnp.concatenate(heads, axis=1))
            return made

        def third(p, grad_scores):
            lanes = lanes_of[p]
            queries, grads = split_heads(q_ref[:, lanes]), split_heads(g_ref[:, lanes])
            k_t = k_ref[:, lanes].T
            acc_k[p] = jnp.zeros_like(acc_k[p])
            acc_v[p] = jnp.zeros_like(acc_v[p])
            turned_parts = []
            for (own, span, at), low in zip(blocks, grad_scores):
                acc_k[p, span, :] += dot_nn(low, stack_heads(queries, own))
                acc_v[p, span, :] += dot_nn(prob_ref[0, p, at, :], stack_heads(grads, own))
                product = dot_nn(k_t[:, span], low)
                both = jnp.concatenate([product[:HEAD, :LANES], product[HEAD:, LANES:]], axis=0)
                turned_parts.append(both.T)
            return turned_parts

        def fourth(p, turned_parts):
            gq = jnp.concatenate(
                [
                    turn_back(part * 0.125, own).astype(BF16)
                    for (own, _, _), part in zip(blocks, turned_parts)
                ],
                axis=0,
            )
            gk = turn_back(acc_k[p], slice(0, length)).astype(BF16)
            gv = acc_v[p].astype(BF16)
            pair = group * GROUP + p
            at_lanes = pl.ds(pl.multiple_of(pair * LANES, LANES), LANES)
            for i, grad in enumerate((gq, gk, gv)):
                at_grad = pl.ds(pl.multiple_of((i * pairs + pair) * LANES, LANES), LANES)
                grads_all[at_rows, at_grad] = grad
                line = SUM_QKV + i
                small_ref[line : line + 1, at_lanes] += jnp.sum(
                    grad.astype(F32), axis=0, keepdims=True
                )

        grad_probs = first(0)
        waiting = None
        for p in range(GROUP):
            grad_scores = second(p, grad_probs)
            if p + 1 < GROUP:
                grad_probs = first(p + 1)
            turned_parts = third(p, grad_scores)
            if waiting is not None:
                fourth(*waiting)
            waiting = (p, turned_parts)
        fourth(*waiting)

    if not last:

        @pl.when(step == units - 1)
        def _():
            hand_on.start()
            hand_on.wait()

        return

    @pl.when(step == units)
    def _():
        for load in loads:
            load.wait()
        hand_on.start()

    @pl.when(step >= units)
    def _():
        sending = step == units
        height = send_ref.shape[1]
        core = jnp.where(sending, 1 - where[1], where[1])
        left = [
            turned[pl.ds(pl.multiple_of((2 * half + core) * height, 16), height), :]
            for half in (1 - where[0], where[0])
        ]
        value = dot_nn(jnp.concatenate(left, axis=0), grads_all[...]).astype(BF16)
        put_blocks(
            send_ref, keep_ref, sending, (0, 1), slice(0, 3 * width), (value[:height], value[height:])
        )
        for slot, half in enumerate((1 - where[0], where[0])):
            pack_vectors(small_ref, packed, half)
            vectors = jnp.where(core == 0, packed[...], 0.0).astype(BF16)
            put_blocks(
                send_ref, keep_ref, sending, (slot,), slice(3 * width, 3 * width + LANES), (vectors,)
            )

    @pl.when(step == units + 1)
    def _():
        hand_on.wait()


def attend_back(where, q, k, v, grad_context, probs, cosine, sine, turned, sums, row, made=None):
    tokens, width = q.shape
    total, pairs, depth = probs.shape[:3]
    length = tokens // total
    last = row == total - 1
    rows = 1 if last else total - 1
    units = rows * pairs // GROUP
    height = width // 4
    here = tokens if last else rows * length

    def at(s):
        s = jnp.minimum(s, units - 1)
        return row + s // (pairs // GROUP), s % (pairs // GROUP)

    head = pl.BlockSpec((length, GROUP * LANES), lambda s, *_: at(s))
    table = pl.BlockSpec((length, LANES), lambda s, *_: (at(s)[0], 0))
    shape = jax.ShapeDtypeStruct
    out_specs = [whole(*sums.shape)]
    out_shape = [shape(sums.shape, F32)]
    scratch = [pltpu.VMEM((GROUP, length, LANES), F32)] * 2
    scratch += [pltpu.VMEM((here, 3 * width), BF16)]
    extra = ()
    if last:
        extra = (turned,) if made is None else (turned, made)
        out_specs += [
            send_spec(1, height, 3 * width + LANES, units),
            keep_spec(1, height, 3 * width + LANES, units),
        ]
        out_shape += [shape((2, height, 3 * width + LANES), BF16)] * 2
        scratch += [pltpu.VMEM((width, tokens), BF16), pltpu.VMEM((height, LANES), F32)]
    return pl.pallas_call(
        functools.partial(attend_back_kernel, rows, row, last),
        grid_spec=pltpu.PrefetchScalarGridSpec(
            num_scalar_prefetch=1,
            grid=(units + 2 * last,),
            in_specs=[head] * 4
            + [
                pl.BlockSpec((1, GROUP, depth, 2 * LANES), lambda s, *_: at(s) + (0, 0)),
                table,
                table,
                whole(*sums.shape),
            ]
            + [ANY] * len(extra),
            out_specs=out_specs + [ANY],
            scratch_shapes=scratch + [pltpu.SemaphoreType.DMA((3,))],
        ),
        out_shape=out_shape + [shape((here, 3 * width), BF16)],
        compiler_params=params(60),
        cost_estimate=LIGHT,
        name="attend_back",
    )(where, q, k, v, grad_context, probs, cosine, sine, sums, *extra)


def norm_parts(values):
    mean = jnp.mean(values, axis=-1, keepdims=True)
    center = values - mean
    spread = jnp.mean(center * center, axis=-1, keepdims=True)
    scale = lax.rsqrt(spread + EPSILON)
    return center * scale, scale


def norm_back(grads, gain, normal, scale):
    inner = grads * gain
    return scale * (
        inner
        - jnp.mean(inner, axis=-1, keepdims=True)
        - normal * jnp.mean(inner * normal, axis=-1, keepdims=True)
    )


def gelu_parts(values):
    share = 0.5 + 0.5 * lax.erf(values * 0.7071067811865476)
    return share, jnp.exp(values * values * -0.5) * 0.3989422804014327


def down_copies(down, rows, wd, sems):
    scale = wd.shape[0] // wd.shape[1]
    pieces = list(down[:1]) + cut_pieces(down[1:])
    starts = [rows[i] * scale for i in range(len(pieces))]
    return piece_copies(pieces, starts, wd, 0, sems, 0)


def feed_up_kernel(count, rows, ctx_ref, x_ref, vec, bu, *refs):
    own, pieces = refs[:2], refs[2 : 2 + count]
    normal_ref, scale_ref, act_ref, slope_ref, joined, lows, sems = refs[2 + count :]
    width = x_ref.shape[1]
    step, last = pl.program_id(0), pl.num_programs(0) - 1

    def norm_stage():
        bo, g1, s1 = (vec[i : i + 1, :] for i in range(3))
        attended = dot_nn(ctx_ref[...], joined[:, :width]) + bo
        normal, scale = norm_parts(x_ref[...].astype(F32) + attended)
        normal = normal.astype(BF16)
        normal_ref[...] = normal
        scale_ref[...] = scale
        lows[pl.ds(step % 2, 1)] = (normal.astype(F32) * g1 + s1).astype(BF16)[None]

    def wide_stage(between):
        low = lows[pl.ds((step + 1) % 2, 1)][0]
        chunks = list(range(0, bu.shape[1], CHUNK))

        def product(c):
            return dot_nn(low, joined[:, width + c : width + c + CHUNK])

        ahead = product(0)
        for n, c in enumerate(chunks):
            hidden = ahead + bu[:, c : c + CHUNK]
            if n + 1 < len(chunks):
                ahead = product(chunks[n + 1])
            share, density = gelu_parts(hidden)
            act_ref[:, c : c + CHUNK] = (hidden * share).astype(BF16)
            slope_ref[:, c : c + CHUNK] = (share + hidden * density).astype(BF16)
            if n == 1:
                between()

    @pl.when(step == 0)
    def _():
        sooner, later = joined_copies(own, pieces, rows, joined, sems, width)
        for copy in sooner + later:
            copy.start()
        for copy in sooner:
            copy.wait()
        norm_stage()
        for copy in later:
            copy.wait()

    @pl.when((step > 0) & (step < last))
    def _():
        wide_stage(norm_stage)

    @pl.when(step == last)
    def _():
        wide_stage(lambda: None)


def feed_up(ctx, x, joined, vec, bu):
    own, pieces, rows = joined
    count = len(pieces)
    tokens, width = x.shape
    hidden = bu.shape[1]
    steps = tokens // TILE

    def now(columns):
        return pl.BlockSpec((TILE, columns), lambda s: (jnp.minimum(s, steps - 1), 0))

    def late(columns):
        return pl.BlockSpec((TILE, columns), lambda s: (jnp.maximum(s - 1, 0), 0))

    shape = jax.ShapeDtypeStruct
    return pl.pallas_call(
        functools.partial(feed_up_kernel, count),
        grid=(steps + 1,),
        in_specs=[SMEM, now(width), now(width), whole(*vec.shape), whole(*bu.shape)]
        + [ANY] * (2 + count),
        out_specs=[now(width), now(1), late(hidden), late(hidden)],
        out_shape=[
            shape((tokens, width), BF16),
            shape((tokens, 1), F32),
            shape((tokens, hidden), BF16),
            shape((tokens, hidden), BF16),
        ],
        scratch_shapes=[
            pltpu.VMEM((width, width + hidden), BF16),
            pltpu.VMEM((2, TILE, width), BF16),
            pltpu.SemaphoreType.DMA((SPLITS * (2 + 4 * count),)),
        ],
        compiler_params=params(60),
        cost_estimate=LIGHT,
        name="feed_up",
    )(rows, ctx, x, vec, bu, *own, *pieces)


def feed_down_kernel(count, steps, where, rows, normal_ref, cot_ref, vec, act_any, *refs):
    down = refs[:count]
    small_ref, send_ref, keep_ref, res_any, gd_any = refs[count : count + 5]
    wd, act, products, res, grads_all, sems, sems_act, sems_out = refs[count + 5 :]
    step = pl.program_id(0)
    tile = cot_ref.shape[0]

    def rows_at(i):
        return pl.ds(pl.multiple_of(i * tile, tile), tile)

    def stores(i):
        span = rows_at(i)
        return [
            pltpu.make_async_copy(s.at[span, :], d.at[span, :], sems_out.at[j * steps + i])
            for j, (s, d) in enumerate(((res, res_any), (grads_all, gd_any)))
        ]

    def load(i):
        span = rows_at(i)
        return pltpu.make_async_copy(act_any.at[span, :], act.at[span, :], sems_act.at[i])

    def product_stage():
        load(step).wait()
        products[pl.ds(step % 2, 1)] = dot_nn(act[rows_at(step), :], wd[...])[None]

    def norm_stage():
        span = rows_at(step - 1)
        g1, s1, bd, g2, s2 = (vec[j : j + 1, :] for j in range(1, 6))
        normed = normal_ref[...].astype(F32) * g1 + s1
        product = products[pl.ds((step + 1) % 2, 1)][0]
        normal2, scale2 = norm_parts(normed + (product + bd))
        res[span, :] = normal2 * g2 + s2
        cot = cot_ref[...].astype(F32)
        low = norm_back(cot, g2, normal2, scale2).astype(BF16)
        grads_all[span, :] = low
        for j, value in enumerate((cot * normal2, cot, low.astype(F32))):
            line = SUM_FFN + j
            small_ref[line : line + 1, :] += jnp.sum(value, axis=0, keepdims=True)
        for copy in stores(step - 1):
            copy.start()

    @pl.when(step == 0)
    def _():
        small_ref[...] = jnp.zeros_like(small_ref)
        copies = down_copies(down, rows, wd, sems)
        for copy in [load(0)] + copies + [load(j) for j in range(1, steps)]:
            copy.start()
        for copy in copies:
            copy.wait()
        product_stage()

    @pl.when((step > 0) & (step < steps))
    def _():
        product_stage()
        norm_stage()

    @pl.when(step == steps)
    def _():
        norm_stage()

    @pl.when(step > steps)
    def _():
        product_step = step - steps - 1
        height = send_ref.shape[1]
        sending = product_step < 2
        core = jnp.where(sending, 1 - where[1], where[1])
        half = jnp.where(product_step % 2 == 0, 1 - where[0], where[0])
        at_left = pl.ds(pl.multiple_of((2 * half + core) * height, LANES), height)
        value = dot_tn(act[:, at_left], grads_all[...]).astype(BF16)
        put_blocks(send_ref, keep_ref, sending, (0,), slice(None), (value,))

    @pl.when(step == steps + 4)
    def _():
        for i in range(steps):
            for copy in stores(i):
                copy.wait()


def feed_down(where, act, normal, cot, down, rows, vec):
    count = len(down)
    tokens, width = cot.shape
    wide = act.shape[1]
    steps = tokens // TILE
    height = wide // 4
    late = pl.BlockSpec((TILE, width), lambda s, *_: (jnp.clip(s - 1, 0, steps - 1), 0))
    shape = jax.ShapeDtypeStruct
    return pl.pallas_call(
        functools.partial(feed_down_kernel, count, steps),
        grid_spec=pltpu.PrefetchScalarGridSpec(
            num_scalar_prefetch=1,
            grid=(steps + 5,),
            in_specs=[SMEM, late, late, whole(*vec.shape)] + [ANY] * (1 + count),
            out_specs=[whole(SUM_ROWS, width)]
            + [send_spec(2, height, width, steps + 1), keep_spec(2, height, width, steps + 1)]
            + [ANY] * 2,
            scratch_shapes=[
                pltpu.VMEM((wide, width), BF16),
                pltpu.VMEM((tokens, wide), BF16),
                pltpu.VMEM((2, TILE, width), F32),
                pltpu.VMEM((tokens, width), F32),
                pltpu.VMEM((tokens, width), BF16),
                pltpu.SemaphoreType.DMA((SPLITS * (2 * count + 1),)),
                pltpu.SemaphoreType.DMA((steps,)),
                pltpu.SemaphoreType.DMA((2 * steps,)),
            ],
        ),
        out_shape=[shape((SUM_ROWS, width), F32)]
        + [shape((2, height, width), BF16)] * 2
        + [shape((tokens, width), F32), shape((tokens, width), BF16)],
        compiler_params=params(60),
        cost_estimate=LIGHT,
        name="feed_down",
    )(where, rows, normal, cot, vec, act, *down)


def feed_back_kernel(
    count, steps, where, rows, gd_ref, slope_ref, normal_ref, scale_ref, vec, sums_ref, ctx_any,
    *refs,
):
    own, pieces = refs[:2], refs[2 : 2 + count]
    down = refs[2 + count : 3 + 2 * count]
    small_ref, send_ref, keep_ref, ga_any, gc_any = refs[3 + 2 * count : 8 + 2 * count]
    (
        joined, wd, low, ctx, hidden_all, attended_all, grad_sums, gc, wide,
        sems, sems_down, sem_ctx, sems_out,
    ) = refs[8 + 2 * count :]
    tile, width = gd_ref.shape
    hidden = wide.shape[1]
    step = pl.program_id(0)
    load_ctx = pltpu.make_async_copy(ctx_any, ctx, sem_ctx.at[0])

    def rows_at(i):
        return pl.ds(pl.multiple_of(i * tile, tile), tile)

    def stores(i):
        span = rows_at(i)
        return [
            pltpu.make_async_copy(s.at[span, :], d.at[span, :], sems_out.at[j * steps + i])
            for j, (s, d) in enumerate(((attended_all, ga_any), (gc, gc_any)))
        ]

    def norm_stage():
        span = rows_at(step - 1)
        grad_normed = grad_sums[pl.ds((step + 1) % 2, 1)][0]
        normal = normal_ref[...].astype(F32)
        low[span, :] = (normal * vec[1:2, :] + vec[2:3, :]).astype(BF16)
        rounded = norm_back(grad_normed, vec[1:2, :], normal, scale_ref[...]).astype(BF16)
        attended_all[span, :] = rounded
        for j, value in enumerate((grad_normed * normal, grad_normed, rounded.astype(F32))):
            line = SUM_ATTN + j
            small_ref[line : line + 1, :] += jnp.sum(value, axis=0, keepdims=True)
        gc[span, :] = dot_nt(rounded, joined[:, :width]).astype(BF16)

    def wide_stage(waiting, between):
        span = rows_at(step)
        chunks = list(range(0, hidden, CHUNK))

        def product(c):
            return dot_nt(gd_ref[...], wd[c : c + CHUNK, :])

        ahead = product(0)
        for copy in waiting:
            copy.wait()
        total = gd_ref[...].astype(F32)
        for n, c in enumerate(chunks):
            grad_active = ahead
            if n + 1 < len(chunks):
                ahead = product(chunks[n + 1])
            rounded = (grad_active * slope_ref[:, c : c + CHUNK].astype(F32)).astype(BF16)
            hidden_all[span, c : c + CHUNK] = rounded
            wide[0:1, c : c + CHUNK] += jnp.sum(rounded.astype(F32), axis=0, keepdims=True)
            total = total + dot_nt(rounded, joined[:, width + c : width + c + CHUNK])
            if n == 1:
                between()
        grad_sums[pl.ds(step % 2, 1)] = total[None]

    @pl.when(step == 0)
    def _():
        copies = down_copies(down, rows, wd, sems_down)
        later = joined_copies(own, pieces, rows, joined, sems)
        for copy in copies + later + [load_ctx]:
            copy.start()
        small_ref[...] = sums_ref[...]
        wide[...] = jnp.zeros_like(wide)
        for copy in copies:
            copy.wait()
        wide_stage(later, lambda: None)

    @pl.when((step > 0) & (step < steps))
    def _():
        wide_stage([], norm_stage)

    @pl.when(step == steps)
    def _():
        norm_stage()
        for j in range(hidden // width):
            line = SUM_UP + j
            small_ref[line : line + 1, :] = wide[0:1, j * width : (j + 1) * width]
        load_ctx.wait()

    @pl.when((step > 0) & (step <= steps))
    def _():
        for copy in stores(step - 1):
            copy.start()

    @pl.when(step > steps)
    def _():
        sending = step == steps + 1
        core = jnp.where(sending, 1 - where[1], where[1])
        height, cut = width // 2, hidden // 2
        at_wide = pl.ds(pl.multiple_of(core * cut, LANES), cut)
        at_narrow = pl.ds(pl.multiple_of(core * height, LANES), height)
        slots = (jnp.where(where[0] == 0, 1, 0), jnp.where(where[0] == 0, 0, 1))
        value = dot_tn(low[...], hidden_all[:, at_wide]).astype(BF16)
        put_blocks(
            send_ref, keep_ref, sending, slots, slice(0, cut), (value[:height], value[height:])
        )
        value = dot_tn(ctx[...], attended_all[:, at_narrow]).astype(BF16)
        put_blocks(
            send_ref, keep_ref, sending, slots, slice(cut, cut + height),
            (value[:height], value[height:]),
        )

    @pl.when(step == steps + 2)
    def _():
        for i in range(steps):
            for copy in stores(i):
                copy.wait()


def feed_back(where, gd, slope, normal, scale, joined, down, vec, context, sums):
    own, pieces, rows = joined
    count = len(pieces)
    tokens, width = gd.shape
    wide = slope.shape[1]
    steps = tokens // TILE
    total = (wide + width) // 2

    def now(columns):
        return pl.BlockSpec((TILE, columns), lambda s, *_: (jnp.minimum(s, steps - 1), 0))

    def late(columns):
        return pl.BlockSpec((TILE, columns), lambda s, *_: (jnp.clip(s - 1, 0, steps - 1), 0))

    shape = jax.ShapeDtypeStruct
    return pl.pallas_call(
        functools.partial(feed_back_kernel, count, steps),
        grid_spec=pltpu.PrefetchScalarGridSpec(
            num_scalar_prefetch=1,
            grid=(steps + 3,),
            in_specs=[SMEM, now(width), now(wide), late(width), late(1)]
            + [whole(*vec.shape), whole(*sums.shape)]
            + [ANY] * (4 + 2 * count),
            out_specs=[whole(*sums.shape)]
            + [send_spec(1, width // 2, total, steps + 1)]
            + [keep_spec(1, width // 2, total, steps + 1)]
            + [ANY] * 2,
            scratch_shapes=[
                pltpu.VMEM((width, width + wide), BF16),
                pltpu.VMEM((wide, width), BF16),
                pltpu.VMEM((tokens, width), BF16),
                pltpu.VMEM((tokens, width), BF16),
                pltpu.VMEM((tokens, wide), BF16),
                pltpu.VMEM((tokens, width), BF16),
                pltpu.VMEM((2, TILE, width), F32),
                pltpu.VMEM((tokens, width), BF16),
                pltpu.VMEM((8, wide), F32),
                pltpu.SemaphoreType.DMA((SPLITS * (2 + 2 * count),)),
                pltpu.SemaphoreType.DMA((SPLITS * (1 + 2 * count),)),
                pltpu.SemaphoreType.DMA((1,)),
                pltpu.SemaphoreType.DMA((2 * steps,)),
            ],
        ),
        out_shape=[shape(sums.shape, F32)]
        + [shape((2, width // 2, total), BF16)] * 2
        + [shape((tokens, width), BF16)] * 2,
        compiler_params=params(60),
        cost_estimate=LIGHT,
        name="feed_back",
    )(where, rows, gd, slope, normal, scale, vec, sums, context, *own, *pieces, *down)


def inputs_back_kernel(count, rows, ga_ref, grads, *refs):
    own, pieces = refs[:3], refs[3 : 3 + count]
    out_ref, full, sems = refs[3 + count :]

    @pl.when(pl.program_id(0) == 0)
    def _():
        fetch_joined(own, pieces, rows, full, sems)

    out_ref[...] = ga_ref[...].astype(F32) + dot_nt(grads[...], full[...])


def inputs_back(grads, ga, weights):
    own, pieces, rows = weights
    tokens, width = ga.shape
    tile = pl.BlockSpec((TILE, width), lambda t: (t, 0))
    return pl.pallas_call(
        functools.partial(inputs_back_kernel, len(pieces)),
        grid=(tokens // TILE,),
        in_specs=[SMEM, tile, pl.BlockSpec((TILE, 3 * width), lambda t: (t, 0))]
        + [ANY] * (3 + len(pieces)),
        out_specs=tile,
        out_shape=jax.ShapeDtypeStruct((tokens, width), F32),
        scratch_shapes=[
            pltpu.VMEM((width, 3 * width), BF16),
            pltpu.SemaphoreType.DMA((SPLITS * (3 + 2 * len(pieces)),)),
        ],
        compiler_params=params(60),
        cost_estimate=LIGHT,
        name="inputs_back",
    )(rows, ga, grads, *own, *pieces)


CORE, NEAR_Y, NEAR_Z, FAR_Z = 1, 2, 4, 8


def after(value, *others):
    return lax.optimization_barrier((value,) + others)[0]


def swap_dp(values, bit):
    size = lax.axis_size("dp")
    return lax.ppermute(values, "dp", [(i, i ^ bit) for i in range(size)])


def swap_fsdp(values):
    return lax.ppermute(values, "fsdp", [(0, 1), (1, 0)])


def swap_both(values):
    size = lax.axis_size("dp")
    pairs = [(2 * i + h, 2 * (i ^ NEAR_Y) + 1 - h) for i in range(size) for h in range(2)]
    return lax.ppermute(values, ("dp", "fsdp"), pairs)


def rows_of(values, start, count):
    return lax.dynamic_slice_in_dim(values, start, count, axis=0)


def own_part(shards, place):
    half, core, y, z = place
    height = shards[0].shape[0]
    count = height // 8
    starts = (2 * y + core) * count, height // 2 + (2 * z + core) * count
    return jnp.concatenate(
        [jnp.concatenate([rows_of(s, start, count) for s in shards], axis=1) for start in starts],
        axis=0,
    )


def pass_on(first):
    count = first.shape[0] // 2
    along, up = swap_dp(first[:count], NEAR_Y), swap_dp(first[count:], NEAR_Z)
    return (first, along, up) + tuple(swap_dp(part, CORE) for part in (first, along, up))


def far_parts(first):
    count = first.shape[0] // 2
    left, right = first[:count], first[count:]
    return (
        swap_dp(left, NEAR_Y),
        swap_dp(right, NEAR_Z),
        swap_dp(left, NEAR_Y | CORE),
        swap_dp(right, NEAR_Z | CORE),
    )


def all_parts(first, far):
    return (first,) + far[:2] + (swap_dp(first, CORE),) + far[2:]


def piece_rows(height, place):
    half, core, y, z = place
    count = height // 8
    base = (1 - half) * height
    rows = [half * height]
    for c in (core, 1 - core):
        rows += [
            base + (2 * y + c) * count,
            base + height // 2 + (2 * z + c) * count,
            base + (2 * (1 - y) + c) * count,
            base + height // 2 + (2 * (1 - z) + c) * count,
        ]
    return jnp.stack(rows).astype(jnp.int32)


class Part:
    def __init__(self, terms, place, columns=None):
        self.bits = {0: 1, 1: place[2], 2: place[3]}
        self.swaps = {
            0: swap_fsdp,
            1: lambda v: swap_dp(v, NEAR_Y),
            2: lambda v: swap_dp(v, NEAR_Z),
            3: lambda v: swap_dp(v, FAR_Z),
        }
        self.terms = [t.reshape(2, 2, 2, t.shape[1] // 4, t.shape[2]) for t in terms]
        self.views = [(columns, ())] * len(terms)
        self.flight, self.joined = [], None

    def total(self, *picks):
        value = None
        for term, (columns, before) in zip(self.terms, self.views):
            if columns is not None:
                term = term[..., columns[0] : columns[1]]
            for axis, index in before + picks:
                term = lax.dynamic_slice_in_dim(term, index, 1, axis)
            term = term.astype(F32)
            value = term if value is None else value + term
        return value.astype(BF16)

    def cut(self, *picks):
        self.views = [(columns, before + picks) for columns, before in self.views]

    def halve(self, axis):
        bit = self.bits[axis]
        self.flight, self.route = [self.total((axis, 1 - bit))], [self.swaps[axis]]
        self.cut((axis, bit))

    def both(self):
        bit = self.bits[1]
        self.flight = [
            self.total((0, 0), (1, bit)),
            self.total((0, 1), (1, 1 - bit)),
            self.total((0, 0), (1, 1 - bit)),
        ]
        self.route = [self.swaps[0], self.swaps[1], swap_both]
        self.cut((0, 1), (1, bit))

    def merge(self, *others):
        value = jnp.concatenate([part.total() for part in (self,) + others], axis=-1)
        self.terms, self.views = [value], [(None, ())]

    def split(self, cut):
        other = copy.copy(self)
        end = self.terms[0].shape[-1]
        self.views = [((0, cut), before) for _, before in self.views]
        other.views = [((cut, end), before) for _, before in other.views]
        return other

    def send_whole(self, swap, reshape=None):
        value = self.terms[0]
        if len(self.terms) > 1 or self.views[0][0] is not None:
            value = self.total()
        if reshape:
            value = value.reshape(-1, value.shape[-1])
        self.flight, self.route = [value], [lambda v: (v, swap(v))]
        self.terms, self.views = [], []

    def far(self):
        self.send_whole(self.swaps[3])

    def join(self, axis):
        self.send_whole(self.swaps[axis])
        self.joined = axis

    def finish(self):
        self.send_whole(lambda v: swap_dp(v, CORE), True)

    def land(self):
        for sent, route in zip(self.flight, self.route):
            got = route(sent)
            self.terms += list(got) if isinstance(got, tuple) else [got]
        self.views = self.views + [(None, ())] * (len(self.terms) - len(self.views))
        self.flight = []

    def settle(self):
        if self.joined is None:
            return
        mine, other = self.terms
        axis, self.joined = self.joined, None
        value = jnp.where(
            self.bits[axis] == 0,
            jnp.concatenate([mine, other], axis=axis),
            jnp.concatenate([other, mine], axis=axis),
        )
        self.terms, self.views = [value], [(None, ())]


def fence(parts, *arrays):
    counts = [(len(p.terms), len(p.flight)) for p in parts]
    flat = [a for p in parts for a in p.terms + p.flight] + list(arrays)
    flat = list(lax.optimization_barrier(tuple(flat)))
    for part, (terms, flight) in zip(parts, counts):
        part.terms, flat = flat[:terms], flat[terms:]
        part.flight, flat = flat[:flight], flat[flight:]
    return flat


def widen(mine, other, core, axis):
    low = jnp.where(core == 0, mine, other).astype(F32)
    high = jnp.where(core == 0, other, mine).astype(F32)
    return jnp.concatenate([low, high], axis=axis)


def gather_all(values):
    return lax.all_gather(values, "fsdp", axis=0, tiled=True)


def sum_plain(send, keep, by_rows):
    blocks = [[keep[1], send[1]], [keep[0], send[0]]]
    axis = 0 if by_rows else 1
    value = jnp.concatenate([jnp.concatenate(pair, axis=axis) for pair in blocks], axis=0)
    own = lax.psum_scatter(value, "fsdp", scatter_dimension=0, tiled=True)
    return lax.psum(own, "dp").astype(F32)


def local(
    inputs, segment_ids, cotangent, w_query, b_query, w_key, b_key, w_value, b_value,
    w_output, b_output, gain_attn, bias_attn, w_up, b_up, w_down, b_down, gain_ffn, bias_ffn,
):
    rows, length = segment_ids.shape
    width = inputs.shape[1]
    shards = lax.axis_size("fsdp")
    paired = shards == 2 and lax.axis_size("dp") == 16
    half = lax.axis_index("fsdp")
    dp = lax.axis_index("dp")
    place = (half, dp % 2, dp // 2 % 2, dp // 4 % 2)
    core = place[1]
    vectors = (b_query, b_key, b_value, b_output, gain_attn, bias_attn, b_down, gain_ffn, bias_ffn)
    height = w_query.shape[0]
    cosine, sine, turned = rotary_tables(segment_ids, inputs)
    if paired:
        where = jnp.stack([half, core]).astype(jnp.int32)
        part_qkv = own_part((w_query, w_key, w_value), place)
        part_up = own_part((w_output, w_up), place)
        part_down = own_part((w_down,), place)
        here_qkv = after(swap_fsdp(part_qkv), cosine)
        lines = jnp.concatenate(vectors + (b_up,)).reshape(-1, height)
        other = swap_fsdp(after(lines, part_qkv))
        here_up = swap_fsdp(after(part_up, here_qkv))
        at = piece_rows(height, place)
        joined_qkv = ((w_query, w_key, w_value), pass_on(here_qkv), at)
        lines = jnp.where(half == 0, jnp.stack([lines, other]), jnp.stack([other, lines]))
    else:
        where = jnp.zeros((2,), jnp.int32)
        at = jnp.zeros((1,), jnp.int32)
        joined_qkv = (tuple(gather_all(w) for w in (w_query, w_key, w_value)), (), at)
        joined_up = ((gather_all(w_output), gather_all(w_up)), (), at)
        down = (gather_all(w_down),)
        lines = jnp.concatenate(vectors + (b_up,)).reshape(-1, height)
        lines = lax.all_gather(lines, "fsdp", axis=0)
    lines = lines.astype(F32)
    vec = jnp.swapaxes(lines[:, :9], 0, 1).reshape(9, width)
    bias_up = lines[:, 9:].reshape(1, -1)

    q, k, v = project(inputs, joined_qkv, vec[:3], cosine, sine)
    vec = vec[3:]
    if paired:
        q, here_up, part_down, vec, bias_up = lax.optimization_barrier(
            (q, here_up, part_down, vec, bias_up)
        )
        here_down = swap_fsdp(part_down)
        far_up = far_parts(here_up)
    context, probs = attend(q, k, v, segment_ids)
    if paired:
        context, probs, here_up, here_down, far_up = lax.optimization_barrier(
            (context, probs, here_up, here_down, far_up)
        )
        joined_up = ((w_output, w_up), all_parts(here_up, far_up), at)
        far_down = far_parts(here_down)
    normal, scale, act, slope = feed_up(context, inputs, joined_up, vec, bias_up)
    if paired:
        act, slope, here_down, far_down = lax.optimization_barrier(
            (act, slope, here_down, far_down)
        )
        down = (w_down,) + all_parts(here_down, far_down)
    sums, send, keep, result, grad_down = feed_down(
        where, act, normal, cotangent, down, at, vec
    )
    sent = [(send, keep)]
    if paired:
        sum_d = Part([keep, swap_dp(send, CORE)], place)
        sum_d.both()
        (grad_down,) = fence([sum_d], grad_down)
    outs = feed_back(
        where, grad_down, slope, normal, scale, joined_up, down, vec, context, sums
    )
    sent.append(outs[1:3])
    if paired:
        sum_d.land()
        outs = fence([sum_d], *outs)
    sums, send, keep, grad_attended, grad_context = outs
    if paired:
        sum_d.merge()
        sum_u = Part([keep, swap_dp(send, CORE)], place)
        sum_d.halve(2)
        sum_u.both()
        parts = [sum_d, sum_u]
        (grad_context,) = fence(parts, grad_context)
    tables = (probs, cosine, sine, turned)
    made = None
    if rows > 1:
        sums, made = attend_back(where, q, k, v, grad_context, *tables, sums, 0)
        if paired:
            sum_d.land()
            sums, made, grad_context = fence([sum_d], sums, made, grad_context)
            sum_d.far()
            sums, grad_context = fence([sum_d], sums, grad_context)
    outs = attend_back(where, q, k, v, grad_context, *tables, sums, rows - 1, made)
    sent.append(outs[1:3])
    if paired:
        for p in parts:
            p.land()
        outs = fence(parts, *outs)
    sums, send, keep, grads = outs
    if paired:
        sum_q = Part([keep, swap_dp(send, CORE)], place)
        sum_u.merge()
        sum_d.join(2) if rows > 1 else sum_d.far()
        sum_u.halve(2)
        sum_q.both()
        parts = [sum_d, sum_u, sum_q]
        (grad_attended,) = fence(parts, grad_attended)
    grad_inputs = inputs_back(grads, grad_attended, joined_qkv)
    if paired:
        for p in parts:
            p.land()
        (grad_inputs,) = fence(parts, grad_inputs)
        last = grad_inputs

        def step(part, name, *axis):
            nonlocal last
            (last,) = fence([part], last)
            part.settle()
            getattr(part, name)(*axis)
            (last,) = fence([part], last)
            last = part.flight[0]
            part.land()

        if rows == 1:
            step(sum_d, "join", 2)
        step(sum_u, "far")
        sum_q.merge()
        step(sum_q, "halve", 2)
        step(sum_d, "join", 1)
        step(sum_q, "far")
        cut_u, cut_q = ((p.terms[0].shape[-1] // 2 + 64) // LANES * LANES for p in (sum_u, sum_q))
        (last,) = fence([sum_u], last)
        sum_v = sum_u.split(cut_u)
        step(sum_u, "join", 2)
        step(sum_v, "join", 1)
        step(sum_d, "finish")
        gwd = widen(*sum_d.terms, core, 0)
        (last,) = fence([sum_q], last)
        sum_r = sum_q.split(cut_q)
        step(sum_q, "join", 2)
        step(sum_r, "join", 1)
        step(sum_u, "join", 1)
        step(sum_v, "join", 2)
        (gwd,) = fence([sum_q, sum_r], gwd)
        step(sum_q, "join", 1)
        step(sum_r, "join", 2)
        for part in (sum_u, sum_v):
            part.settle()
            part.finish()
        fence([sum_u, sum_v, sum_q, sum_r])
        sum_u.land()
        sum_v.land()
        for part in (sum_q, sum_r):
            part.settle()
            part.finish()
            part.land()
    else:
        sums = lax.psum(sums, ("dp", "fsdp"))

    wide = b_up.shape[0] * shards
    if paired:
        mine, other = (
            jnp.concatenate([a, b], axis=1) for a, b in zip(sum_u.terms, sum_v.terms)
        )
        cut = wide // 2
        gwu = widen(mine[:, :cut], other[:, :cut], core, 1)
        gwo = widen(mine[:, cut:], other[:, cut:], core, 1)
        mine, other = (
            jnp.concatenate([a, b], axis=1) for a, b in zip(sum_q.terms, sum_r.terms)
        )
        gwq, gwk, gwv = (
            widen(*(end[:, i * width : (i + 1) * width] for end in (mine, other)), core, 0)
            for i in range(3)
        )
        count = height // LANES
        packed = jnp.where(core == 0, mine[:, 3 * width :], other[:, 3 * width :])
        packed = packed[: len(LINES) * count + wide // 2 // LANES].astype(F32)
        vectors = [packed[i * count : (i + 1) * count].reshape(-1) for i in range(len(LINES))]
        gbu = packed[len(LINES) * count :].reshape(-1)
        ggf, gbf, gbd, gga, gba, gbo, gbq, gbk, gbv = vectors
    else:

        def own(line, count=1):
            start = line * width + half * (count * width // shards)
            return lax.dynamic_slice_in_dim(
                sums.reshape(-1), start, count * width // shards, axis=0
            )

        ggf, gbf, gbd, gga, gba, gbo, gbq, gbk, gbv = (own(line) for line in LINES)
        gbu = own(SUM_UP, wide // width)
        gwd = sum_plain(*sent[0], True)
        both = sum_plain(*sent[1], False).reshape(height, 2, -1)
        cut = wide // 2
        gwu = both[..., :cut].reshape(height, -1)
        gwo = both[..., cut:].reshape(height, -1)
        both = sum_plain(*sent[2], True)
        gwq, gwk, gwv = (both[:, i * width : (i + 1) * width] for i in range(3))
    return (
        result, grad_inputs, gwq, gbq, gwk, gbk, gwv, gbv, gwo, gbo, gga, gba,
        gwu, gbu, gwd, gbd, ggf, gbf,
    )


def solution(mesh):
    tokens, matrix, vector = P(("dp", "fsdp"), None), P("fsdp", None), P("fsdp")
    weights = (
        matrix, vector, matrix, vector, matrix, vector, matrix, vector, vector, vector,
        matrix, vector, matrix, vector, vector, vector,
    )
    return jax.shard_map(
        local,
        mesh=mesh,
        in_specs=(tokens,) * 3 + weights,
        out_specs=(tokens,) * 2 + weights,
        check_vma=False,
    )
```

```python
import copy
import functools
import jax
import jax.numpy as jnp
from jax import lax
from jax.experimental import pallas as pl
from jax.experimental.pallas import tpu as pltpu
from jax.sharding import PartitionSpec as P

HEAD = 64
GROUP = 3
EPSILON = 1e-06
LANES = 128
TILE = 256
CHUNK = 512
MASKED = -1e30
SUM_FFN, SUM_ATTN, SUM_UP, SUM_QKV, SUM_ROWS = 0, 3, 6, 10, 16
F32 = jnp.float32
BF16 = jnp.bfloat16


def params(mebibytes):
    return pltpu.CompilerParams(vmem_limit_bytes=mebibytes * 1024 * 1024)


LIGHT = pl.CostEstimate(flops=1000, bytes_accessed=1000, transcendentals=0)


def dot_nn(left, right):
    return lax.dot_general(left, right, (((1,), (0,)), ((), ())), preferred_element_type=F32)


def dot_nt(left, right):
    return lax.dot_general(left, right, (((1,), (1,)), ((), ())), preferred_element_type=F32)


def dot_tn(left, right):
    return lax.dot_general(left, right, (((0,), (0,)), ((), ())), preferred_element_type=F32)


def whole(*shape):
    return pl.BlockSpec(shape, lambda *_: (0,) * len(shape))


SPLITS = 4


def piece_copies(pieces, starts, full, column, sems, first):
    copies = []
    assert len(pieces) == len(starts)
    for i, (piece, start) in enumerate(zip(pieces, starts)):
        height, width = piece.shape
        splits = SPLITS if height * width >= 500_000 and height % (16 * SPLITS) == 0 else 1
        count = height // splits
        for j in range(splits):
            row = pl.multiple_of(start + j * count, 16)
            copies.append(
                pltpu.make_async_copy(
                    piece.at[pl.ds(j * count, count), :],
                    full.at[pl.ds(row, count), column : column + width],
                    sems.at[SPLITS * (first + i) + j],
                )
            )
    return copies


def cut_pieces(pieces):
    cut = []
    for i, piece in enumerate(pieces):
        count = piece.shape[0] // 2
        cut += [piece.at[:count, :], piece.at[count:, :]] if i % 3 == 0 else [piece]
    return cut


def joined_copies(own, pieces, rows, full, sems, cut=None):
    pieces = cut_pieces(pieces)
    shards, column = [], 0
    for i, shard in enumerate(own):
        shards.append(piece_copies([shard], [rows[0]], full, column, sems, i))
        column += shard.shape[1]
    starts = [rows[1 + i] for i in range(len(pieces))]
    first = len(own)
    if cut is None:
        return sum(shards, []) + piece_copies(pieces, starts, full, 0, sems, first)
    left = [piece.at[:, :cut] for piece in pieces]
    right = [piece.at[:, cut:] for piece in pieces]
    return (
        shards[0] + piece_copies(left, starts, full, 0, sems, first),
        sum(shards[1:], []) + piece_copies(right, starts, full, cut, sems, first + len(pieces)),
    )


def fetch_joined(own, pieces, rows, full, sems):
    copies = joined_copies(own, pieces, rows, full, sems)
    for copy in copies:
        copy.start()
    for copy in copies:
        copy.wait()


ANY = pl.BlockSpec(memory_space=pl.ANY)
SMEM = pl.BlockSpec(memory_space=pltpu.SMEM)


def tables_kernel(seg_row, seg_col, x_ref, cos_ref, sin_ref, turned_ref):
    length = seg_row.shape[-1]
    key = lax.broadcasted_iota(jnp.int32, (length, length), 1)
    query = lax.broadcasted_iota(jnp.int32, (length, length), 0)
    earlier = (seg_col[...] == seg_row[0]) & (key < query)
    place = jnp.sum(earlier.astype(F32), axis=1, keepdims=True)
    lane = lax.broadcasted_iota(jnp.int32, (1, LANES), 1)
    paired = (lane % HEAD // 2 * 2).astype(F32)
    freqs = jnp.exp(-jnp.log(F32(10000.0)) * paired / HEAD)
    angle = place * freqs
    cos_ref[...] = jnp.cos(angle)
    sine = jnp.sin(angle)
    sin_ref[...] = jnp.where(lane % 2 == 0, -sine, sine)
    turned_ref[...] = x_ref[...].T


def rotary_tables(segments, x):
    rows, length = segments.shape
    width = x.shape[1]
    return pl.pallas_call(
        tables_kernel,
        grid=(rows,),
        in_specs=[
            pl.BlockSpec((1, 1, length), lambda r: (r, 0, 0)),
            pl.BlockSpec((length, 1), lambda r: (r, 0)),
            pl.BlockSpec((length, width), lambda r: (r, 0)),
        ],
        out_specs=[pl.BlockSpec((length, LANES), lambda r: (r, 0))] * 2
        + [pl.BlockSpec((width, length), lambda r: (0, r))],
        out_shape=[jax.ShapeDtypeStruct((rows * length, LANES), F32)] * 2
        + [jax.ShapeDtypeStruct((width, rows * length), BF16)],
        compiler_params=params(60),
        cost_estimate=LIGHT,
        name="rotary_tables",
    )(segments.reshape(rows, 1, length), segments.reshape(rows * length, 1), x)


def pair_swap(values):
    even = lax.broadcasted_iota(jnp.int32, values.shape, 1) % 2 == 0
    return jnp.where(
        even, pltpu.roll(values, LANES - 1, axis=1), pltpu.roll(values, 1, axis=1)
    )


def project_kernel(count, rows, x_ref, bias, cos_ref, sin_ref, *refs):
    own, pieces = refs[:3], refs[3 : 3 + count]
    q_ref, k_ref, v_ref, full, sems = refs[3 + count :]
    width = x_ref.shape[1]

    @pl.when(pl.program_id(0) == 0)
    def _():
        fetch_joined(own, pieces, rows, full, sems)

    x = x_ref[...]
    cosine, sine = cos_ref[...], sin_ref[...]
    step = 2 * LANES
    for i, out in enumerate((q_ref, k_ref, v_ref)):
        for c in range(0, width, step):
            lin = dot_nn(x, full[:, i * width + c : i * width + c + step])
            lin = lin + bias[i : i + 1, c : c + step]
            if i < 2:
                parts = []
                for d in range(0, step, LANES):
                    part = lin[:, d : d + LANES]
                    part = part * cosine + pair_swap(part) * sine
                    parts.append(part)
                lin = jnp.concatenate(parts, axis=1)
            if i == 0:
                out[:, c : c + step] = (lin.astype(BF16).astype(F32) * 0.125).astype(BF16)
            else:
                out[:, c : c + step] = lin.astype(BF16)


def project(x, weights, bias, cosine, sine):
    own, pieces, rows = weights
    tokens, width = x.shape
    tile = pl.BlockSpec((TILE, width), lambda t: (t, 0))
    table = pl.BlockSpec((TILE, LANES), lambda t: (t, 0))
    return pl.pallas_call(
        functools.partial(project_kernel, len(pieces)),
        grid=(tokens // TILE,),
        in_specs=[SMEM, tile, whole(*bias.shape), table, table] + [ANY] * (3 + len(pieces)),
        out_specs=[tile] * 3,
        out_shape=[jax.ShapeDtypeStruct((tokens, width), BF16)] * 3,
        scratch_shapes=[
            pltpu.VMEM((width, 3 * width), BF16),
            pltpu.SemaphoreType.DMA((SPLITS * (3 + 2 * len(pieces)),)),
        ],
        compiler_params=params(60),
        cost_estimate=LIGHT,
        name="project",
    )(rows, x, bias, cosine, sine, *own, *pieces)


def spans(length):
    found, offset = [], 0
    for first in range(0, length, LANES):
        low, high = max(first - LANES, 0), min(first + 2 * LANES, length)
        found.append((slice(first, first + LANES), slice(low, high), slice(offset, offset + high - low)))
        offset += high - low
    return found, offset


def split_heads(values):
    lane = lax.broadcasted_iota(jnp.int32, (1, LANES), 1)
    return [jnp.where(lane // HEAD == h, values, jnp.zeros_like(values)) for h in range(2)]


def stack_heads(heads, rows):
    return jnp.concatenate([head[rows, :] for head in heads], axis=0)


def merge_heads(stacked):
    lane = lax.broadcasted_iota(jnp.int32, (1, LANES), 1)
    half = stacked.shape[0] // 2
    return jnp.where(lane < HEAD, stacked[:half], stacked[half:])


def attend_kernel(q_ref, k_ref, v_ref, seg_row, seg_col, ctx_ref, prob_ref, bias):
    blocks, _ = spans(q_ref.shape[0])

    @pl.when(pl.program_id(1) == 0)
    def _():
        for own, span, at in blocks:
            bias[at, :] = jnp.where(seg_col[span, :] == seg_row[0, :, own], 0.0, MASKED)

    pairs = [slice(p * LANES, (p + 1) * LANES) for p in range(GROUP)]
    units = [(p, lanes) + block for p, lanes in enumerate(pairs) for block in blocks]
    queries = [split_heads(q_ref[:, lanes]) for lanes in pairs]

    def product(unit):
        p, lanes, own, span, _ = unit
        return dot_nt(k_ref[span, lanes], stack_heads(queries[p], own))

    def soften(unit, scores):
        at = unit[-1]
        heads = []
        for h in range(2):
            masked = scores[:, h * LANES : (h + 1) * LANES] + bias[at, :]
            peak = jnp.max(masked, axis=0, keepdims=True)
            expo = jnp.exp(masked - peak)
            total = jnp.sum(expo, axis=0, keepdims=True)
            heads.append((expo * (1.0 / total)).astype(BF16))
        return jnp.concatenate(heads, axis=1)

    def finish(unit, probs):
        p, lanes, own, span, at = unit
        prob_ref[0, p, at, :] = probs
        ctx_ref[own, lanes] = merge_heads(dot_tn(probs, v_ref[span, lanes])).astype(BF16)

    count = len(blocks)
    scores = [product(unit) for unit in units[:count]]
    waiting = []
    for p in range(GROUP):
        now = units[p * count : (p + 1) * count]
        probs = [soften(unit, value) for unit, value in zip(now, scores)]
        scores = [product(unit) for unit in units[(p + 1) * count : (p + 2) * count]]
        for unit, value in waiting:
            finish(unit, value)
        waiting = list(zip(now, probs))
    for unit, value in waiting:
        finish(unit, value)


def attend(q, k, v, segments):
    rows, length = segments.shape
    tokens, width = q.shape
    pairs = width // LANES
    wide = GROUP * LANES
    _, depth = spans(length)
    head = pl.BlockSpec((length, wide), lambda r, p: (r, p))
    return pl.pallas_call(
        attend_kernel,
        grid=(rows, pairs // GROUP),
        in_specs=[head] * 3
        + [
            pl.BlockSpec((1, 1, length), lambda r, p: (r, 0, 0)),
            pl.BlockSpec((length, 1), lambda r, p: (r, 0)),
        ],
        out_specs=[
            head,
            pl.BlockSpec((1, GROUP, depth, 2 * LANES), lambda r, p: (r, p, 0, 0)),
        ],
        out_shape=[
            jax.ShapeDtypeStruct((tokens, width), BF16),
            jax.ShapeDtypeStruct((rows, pairs, depth, 2 * LANES), BF16),
        ],
        scratch_shapes=[pltpu.VMEM((depth, LANES), F32)],
        compiler_params=params(60),
        cost_estimate=LIGHT,
        name="attend",
    )(q, k, v, segments.reshape(rows, 1, length), segments.reshape(tokens, 1))


def send_spec(steps, height, width, first):
    return pl.BlockSpec(
        (2 // steps, height, width), lambda s, *_: (jnp.clip(s - first, 0, steps - 1), 0, 0)
    )


def keep_spec(steps, height, width, first):
    return pl.BlockSpec(
        (2 // steps, height, width), lambda s, *_: (jnp.clip(s - first - steps, 0, steps - 1), 0, 0)
    )


def put_blocks(send_ref, keep_ref, sending, slots, columns, values):
    @pl.when(sending)
    def _():
        for slot, value in zip(slots, values):
            send_ref[slot, :, columns] = value

    @pl.when(jnp.logical_not(sending))
    def _():
        for slot, value in zip(slots, values):
            keep_ref[slot, :, columns] = value


LINES = (SUM_FFN, SUM_FFN + 1, SUM_FFN + 2, SUM_ATTN, SUM_ATTN + 1, SUM_ATTN + 2) + (
    SUM_QKV, SUM_QKV + 1, SUM_QKV + 2,
)


def pack_vectors(small_ref, packed, half):
    width = small_ref.shape[1]
    part = width // 2 // LANES
    packed[...] = jnp.zeros_like(packed)
    for i, line in enumerate(LINES):
        for j in range(part):
            lanes = pl.ds(pl.multiple_of(half * (width // 2) + j * LANES, LANES), LANES)
            packed[i * part + j : i * part + j + 1, :] = small_ref[line : line + 1, lanes]
    base, count = len(LINES) * part, width // LANES
    lines = (SUM_QKV - SUM_UP) // 2
    for i in range(lines):
        for j in range(count):
            row = base + i * count + j
            lanes = slice(j * LANES, (j + 1) * LANES)
            low, high = (small_ref[SUM_UP + n : SUM_UP + n + 1, lanes] for n in (i, lines + i))
            packed[row : row + 1, :] = jnp.where(half == 0, low, high)


def attend_back_kernel(
    rows, before, last, where, q_ref, k_ref, v_ref, g_ref, prob_ref, cos_ref, sin_ref, sums_ref,
    *refs,
):
    if last:
        (
            turned_any, *made_any, small_ref, send_ref, keep_ref, out_any,
            acc_k, acc_v, grads_all, turned, packed, sems,
        ) = refs
    else:
        small_ref, out_any, acc_k, acc_v, grads_all, sems = refs
    step = pl.program_id(0)
    length, width = q_ref.shape[0], small_ref.shape[1]
    pairs = width // LANES
    units = rows * pairs // GROUP
    hand_on = pltpu.make_async_copy(grads_all, out_any, sems.at[0])
    loads = []
    if last:
        loads.append(pltpu.make_async_copy(turned_any, turned, sems.at[1]))
        if before:
            target = grads_all.at[pl.ds(0, before * length), :]
            loads.append(pltpu.make_async_copy(made_any[0], target, sems.at[2]))

    @pl.when(step == 0)
    def _():
        for load in loads:
            load.start()
        small_ref[...] = sums_ref[...]

    @pl.when(step < units)
    def _():
        blocks, _ = spans(length)
        groups = pairs // GROUP
        row, group = before * last + step // groups, step % groups
        at_rows = pl.ds(pl.multiple_of(row * length, length), length)
        lanes_of = [slice(p * LANES, (p + 1) * LANES) for p in range(GROUP)]

        def turn_back(values, rows):
            return values * cos_ref[rows, :] - pair_swap(values) * sin_ref[rows, :]

        def first(p):
            grads = split_heads(g_ref[:, lanes_of[p]])
            return [
                dot_nt(v_ref[span, lanes_of[p]], stack_heads(grads, own)) for own, span, _ in blocks
            ]

        def second(p, grad_probs):
            made = []
            for (own, span, at), pair in zip(blocks, grad_probs):
                heads = []
                for h in range(2):
                    columns = slice(h * LANES, (h + 1) * LANES)
                    probs = prob_ref[0, p, at, columns].astype(F32)
                    inner = jnp.sum(probs * pair[:, columns], axis=0, keepdims=True)
                    heads.append((probs * (pair[:, columns] - inner)).astype(BF16))
                made.append(jnp.concatenate(heads, axis=1))
            return made

        def third(p, grad_scores):
            lanes = lanes_of[p]
            queries, grads = split_heads(q_ref[:, lanes]), split_heads(g_ref[:, lanes])
            k_t = k_ref[:, lanes].T
            acc_k[p] = jnp.zeros_like(acc_k[p])
            acc_v[p] = jnp.zeros_like(acc_v[p])
            turned_parts = []
            for (own, span, at), low in zip(blocks, grad_scores):
                acc_k[p, span, :] += dot_nn(low, stack_heads(queries, own))
                acc_v[p, span, :] += dot_nn(prob_ref[0, p, at, :], stack_heads(grads, own))
                product = dot_nn(k_t[:, span], low)
                both = jnp.concatenate([product[:HEAD, :LANES], product[HEAD:, LANES:]], axis=0)
                turned_parts.append(both.T)
            return turned_parts

        def fourth(p, turned_parts):
            gq = jnp.concatenate(
                [
                    turn_back(part * 0.125, own).astype(BF16)
                    for (own, _, _), part in zip(blocks, turned_parts)
                ],
                axis=0,
            )
            gk = turn_back(acc_k[p], slice(0, length)).astype(BF16)
            gv = acc_v[p].astype(BF16)
            pair = group * GROUP + p
            at_lanes = pl.ds(pl.multiple_of(pair * LANES, LANES), LANES)
            for i, grad in enumerate((gq, gk, gv)):
                at_grad = pl.ds(pl.multiple_of((i * pairs + pair) * LANES, LANES), LANES)
                grads_all[at_rows, at_grad] = grad
                line = SUM_QKV + i
                small_ref[line : line + 1, at_lanes] += jnp.sum(
                    grad.astype(F32), axis=0, keepdims=True
                )

        grad_probs = first(0)
        waiting = None
        for p in range(GROUP):
            grad_scores = second(p, grad_probs)
            if p + 1 < GROUP:
                grad_probs = first(p + 1)
            turned_parts = third(p, grad_scores)
            if waiting is not None:
                fourth(*waiting)
            waiting = (p, turned_parts)
        fourth(*waiting)

    if not last:

        @pl.when(step == units - 1)
        def _():
            hand_on.start()
            hand_on.wait()

        return

    @pl.when(step == units)
    def _():
        for load in loads:
            load.wait()
        hand_on.start()

    @pl.when(step >= units)
    def _():
        sending = step == units
        height = send_ref.shape[1]
        core = jnp.where(sending, 1 - where[1], where[1])
        left = [
            turned[pl.ds(pl.multiple_of((2 * half + core) * height, 16), height), :]
            for half in (1 - where[0], where[0])
        ]
        value = dot_nn(jnp.concatenate(left, axis=0), grads_all[...]).astype(BF16)
        put_blocks(
            send_ref, keep_ref, sending, (0, 1), slice(0, 3 * width), (value[:height], value[height:])
        )
        for slot, half in enumerate((1 - where[0], where[0])):
            pack_vectors(small_ref, packed, half)
            vectors = jnp.where(core == 0, packed[...], 0.0).astype(BF16)
            put_blocks(
                send_ref, keep_ref, sending, (slot,), slice(3 * width, 3 * width + LANES), (vectors,)
            )

    @pl.when(step == units + 1)
    def _():
        hand_on.wait()


def attend_back(where, q, k, v, grad_context, probs, cosine, sine, turned, sums, row, made=None):
    tokens, width = q.shape
    total, pairs, depth = probs.shape[:3]
    length = tokens // total
    last = row == total - 1
    rows = 1 if last else total - 1
    units = rows * pairs // GROUP
    height = width // 4
    here = tokens if last else rows * length

    def at(s):
        s = jnp.minimum(s, units - 1)
        return row + s // (pairs // GROUP), s % (pairs // GROUP)

    head = pl.BlockSpec((length, GROUP * LANES), lambda s, *_: at(s))
    table = pl.BlockSpec((length, LANES), lambda s, *_: (at(s)[0], 0))
    shape = jax.ShapeDtypeStruct
    out_specs = [whole(*sums.shape)]
    out_shape = [shape(sums.shape, F32)]
    scratch = [pltpu.VMEM((GROUP, length, LANES), F32)] * 2
    scratch += [pltpu.VMEM((here, 3 * width), BF16)]
    extra = ()
    if last:
        extra = (turned,) if made is None else (turned, made)
        out_specs += [
            send_spec(1, height, 3 * width + LANES, units),
            keep_spec(1, height, 3 * width + LANES, units),
        ]
        out_shape += [shape((2, height, 3 * width + LANES), BF16)] * 2
        scratch += [pltpu.VMEM((width, tokens), BF16), pltpu.VMEM((height, LANES), F32)]
    return pl.pallas_call(
        functools.partial(attend_back_kernel, rows, row, last),
        grid_spec=pltpu.PrefetchScalarGridSpec(
            num_scalar_prefetch=1,
            grid=(units + 2 * last,),
            in_specs=[head] * 4
            + [
                pl.BlockSpec((1, GROUP, depth, 2 * LANES), lambda s, *_: at(s) + (0, 0)),
                table,
                table,
                whole(*sums.shape),
            ]
            + [ANY] * len(extra),
            out_specs=out_specs + [ANY],
            scratch_shapes=scratch + [pltpu.SemaphoreType.DMA((3,))],
        ),
        out_shape=out_shape + [shape((here, 3 * width), BF16)],
        compiler_params=params(60),
        cost_estimate=LIGHT,
        name="attend_back",
    )(where, q, k, v, grad_context, probs, cosine, sine, sums, *extra)


def norm_parts(values):
    mean = jnp.mean(values, axis=-1, keepdims=True)
    center = values - mean
    spread = jnp.mean(center * center, axis=-1, keepdims=True)
    scale = lax.rsqrt(spread + EPSILON)
    return center * scale, scale


def norm_back(grads, gain, normal, scale):
    inner = grads * gain
    return scale * (
        inner
        - jnp.mean(inner, axis=-1, keepdims=True)
        - normal * jnp.mean(inner * normal, axis=-1, keepdims=True)
    )


def gelu_parts(values):
    share = 0.5 + 0.5 * lax.erf(values * 0.7071067811865476)
    return share, jnp.exp(values * values * -0.5) * 0.3989422804014327


def down_copies(down, rows, wd, sems):
    scale = wd.shape[0] // wd.shape[1]
    pieces = list(down[:1]) + cut_pieces(down[1:])
    starts = [rows[i] * scale for i in range(len(pieces))]
    return piece_copies(pieces, starts, wd, 0, sems, 0)


def feed_up_kernel(count, rows, ctx_ref, x_ref, vec, bu, *refs):
    own, pieces = refs[:2], refs[2 : 2 + count]
    normal_ref, scale_ref, act_ref, slope_ref, joined, lows, sems = refs[2 + count :]
    width = x_ref.shape[1]
    step, last = pl.program_id(0), pl.num_programs(0) - 1

    def norm_stage():
        bo, g1, s1 = (vec[i : i + 1, :] for i in range(3))
        attended = dot_nn(ctx_ref[...], joined[:, :width]) + bo
        normal, scale = norm_parts(x_ref[...].astype(F32) + attended)
        normal = normal.astype(BF16)
        normal_ref[...] = normal
        scale_ref[...] = scale
        lows[pl.ds(step % 2, 1)] = (normal.astype(F32) * g1 + s1).astype(BF16)[None]

    def wide_stage(between):
        low = lows[pl.ds((step + 1) % 2, 1)][0]
        chunks = list(range(0, bu.shape[1], CHUNK))

        def product(c):
            return dot_nn(low, joined[:, width + c : width + c + CHUNK])

        ahead = product(0)
        for n, c in enumerate(chunks):
            hidden = ahead + bu[:, c : c + CHUNK]
            if n + 1 < len(chunks):
                ahead = product(chunks[n + 1])
            share, density = gelu_parts(hidden)
            act_ref[:, c : c + CHUNK] = (hidden * share).astype(BF16)
            slope_ref[:, c : c + CHUNK] = (share + hidden * density).astype(BF16)
            if n == 1:
                between()

    @pl.when(step == 0)
    def _():
        sooner, later = joined_copies(own, pieces, rows, joined, sems, width)
        for copy in sooner + later:
            copy.start()
        for copy in sooner:
            copy.wait()
        norm_stage()
        for copy in later:
            copy.wait()

    @pl.when((step > 0) & (step < last))
    def _():
        wide_stage(norm_stage)

    @pl.when(step == last)
    def _():
        wide_stage(lambda: None)


def feed_up(ctx, x, joined, vec, bu):
    own, pieces, rows = joined
    count = len(pieces)
    tokens, width = x.shape
    hidden = bu.shape[1]
    steps = tokens // TILE

    def now(columns):
        return pl.BlockSpec((TILE, columns), lambda s: (jnp.minimum(s, steps - 1), 0))

    def late(columns):
        return pl.BlockSpec((TILE, columns), lambda s: (jnp.maximum(s - 1, 0), 0))

    shape = jax.ShapeDtypeStruct
    return pl.pallas_call(
        functools.partial(feed_up_kernel, count),
        grid=(steps + 1,),
        in_specs=[SMEM, now(width), now(width), whole(*vec.shape), whole(*bu.shape)]
        + [ANY] * (2 + count),
        out_specs=[now(width), now(1), late(hidden), late(hidden)],
        out_shape=[
            shape((tokens, width), BF16),
            shape((tokens, 1), F32),
            shape((tokens, hidden), BF16),
            shape((tokens, hidden), BF16),
        ],
        scratch_shapes=[
            pltpu.VMEM((width, width + hidden), BF16),
            pltpu.VMEM((2, TILE, width), BF16),
            pltpu.SemaphoreType.DMA((SPLITS * (2 + 4 * count),)),
        ],
        compiler_params=params(60),
        cost_estimate=LIGHT,
        name="feed_up",
    )(rows, ctx, x, vec, bu, *own, *pieces)


def feed_down_kernel(count, steps, where, rows, normal_ref, cot_ref, vec, act_any, *refs):
    down = refs[:count]
    small_ref, send_ref, keep_ref, res_any, gd_any = refs[count : count + 5]
    wd, act, products, res, grads_all, sems, sems_act, sems_out = refs[count + 5 :]
    step = pl.program_id(0)
    tile = cot_ref.shape[0]

    def rows_at(i):
        return pl.ds(pl.multiple_of(i * tile, tile), tile)

    def stores(i):
        span = rows_at(i)
        return [
            pltpu.make_async_copy(s.at[span, :], d.at[span, :], sems_out.at[j * steps + i])
            for j, (s, d) in enumerate(((res, res_any), (grads_all, gd_any)))
        ]

    def load(i):
        span = rows_at(i)
        return pltpu.make_async_copy(act_any.at[span, :], act.at[span, :], sems_act.at[i])

    def product_stage():
        load(step).wait()
        products[pl.ds(step % 2, 1)] = dot_nn(act[rows_at(step), :], wd[...])[None]

    def norm_stage():
        span = rows_at(step - 1)
        g1, s1, bd, g2, s2 = (vec[j : j + 1, :] for j in range(1, 6))
        normed = normal_ref[...].astype(F32) * g1 + s1
        product = products[pl.ds((step + 1) % 2, 1)][0]
        normal2, scale2 = norm_parts(normed + (product + bd))
        res[span, :] = normal2 * g2 + s2
        cot = cot_ref[...].astype(F32)
        low = norm_back(cot, g2, normal2, scale2).astype(BF16)
        grads_all[span, :] = low
        for j, value in enumerate((cot * normal2, cot, low.astype(F32))):
            line = SUM_FFN + j
            small_ref[line : line + 1, :] += jnp.sum(value, axis=0, keepdims=True)
        for copy in stores(step - 1):
            copy.start()

    @pl.when(step == 0)
    def _():
        small_ref[...] = jnp.zeros_like(small_ref)
        copies = down_copies(down, rows, wd, sems)
        for copy in [load(0)] + copies + [load(j) for j in range(1, steps)]:
            copy.start()
        for copy in copies:
            copy.wait()
        product_stage()

    @pl.when((step > 0) & (step < steps))
    def _():
        product_stage()
        norm_stage()

    @pl.when(step == steps)
    def _():
        norm_stage()

    @pl.when(step > steps)
    def _():
        product_step = step - steps - 1
        height = send_ref.shape[1]
        sending = product_step < 2
        core = jnp.where(sending, 1 - where[1], where[1])
        half = jnp.where(product_step % 2 == 0, 1 - where[0], where[0])
        at_left = pl.ds(pl.multiple_of((2 * half + core) * height, LANES), height)
        value = dot_tn(act[:, at_left], grads_all[...]).astype(BF16)
        put_blocks(send_ref, keep_ref, sending, (0,), slice(None), (value,))

    @pl.when(step == steps + 4)
    def _():
        for i in range(steps):
            for copy in stores(i):
                copy.wait()


def feed_down(where, act, normal, cot, down, rows, vec):
    count = len(down)
    tokens, width = cot.shape
    wide = act.shape[1]
    steps = tokens // TILE
    height = wide // 4
    late = pl.BlockSpec((TILE, width), lambda s, *_: (jnp.clip(s - 1, 0, steps - 1), 0))
    shape = jax.ShapeDtypeStruct
    return pl.pallas_call(
        functools.partial(feed_down_kernel, count, steps),
        grid_spec=pltpu.PrefetchScalarGridSpec(
            num_scalar_prefetch=1,
            grid=(steps + 5,),
            in_specs=[SMEM, late, late, whole(*vec.shape)] + [ANY] * (1 + count),
            out_specs=[whole(SUM_ROWS, width)]
            + [send_spec(2, height, width, steps + 1), keep_spec(2, height, width, steps + 1)]
            + [ANY] * 2,
            scratch_shapes=[
                pltpu.VMEM((wide, width), BF16),
                pltpu.VMEM((tokens, wide), BF16),
                pltpu.VMEM((2, TILE, width), F32),
                pltpu.VMEM((tokens, width), F32),
                pltpu.VMEM((tokens, width), BF16),
                pltpu.SemaphoreType.DMA((SPLITS * (2 * count + 1),)),
                pltpu.SemaphoreType.DMA((steps,)),
                pltpu.SemaphoreType.DMA((2 * steps,)),
            ],
        ),
        out_shape=[shape((SUM_ROWS, width), F32)]
        + [shape((2, height, width), BF16)] * 2
        + [shape((tokens, width), F32), shape((tokens, width), BF16)],
        compiler_params=params(60),
        cost_estimate=LIGHT,
        name="feed_down",
    )(where, rows, normal, cot, vec, act, *down)


def feed_back_kernel(
    count, steps, where, rows, gd_ref, slope_ref, normal_ref, scale_ref, vec, sums_ref, ctx_any,
    *refs,
):
    own, pieces = refs[:2], refs[2 : 2 + count]
    down = refs[2 + count : 3 + 2 * count]
    small_ref, send_ref, keep_ref, ga_any, gc_any = refs[3 + 2 * count : 8 + 2 * count]
    (
        joined, wd, low, ctx, hidden_all, attended_all, grad_sums, gc, wide,
        sems, sems_down, sem_ctx, sems_out,
    ) = refs[8 + 2 * count :]
    tile, width = gd_ref.shape
    hidden = wide.shape[1]
    step = pl.program_id(0)
    load_ctx = pltpu.make_async_copy(ctx_any, ctx, sem_ctx.at[0])

    def rows_at(i):
        return pl.ds(pl.multiple_of(i * tile, tile), tile)

    def stores(i):
        span = rows_at(i)
        return [
            pltpu.make_async_copy(s.at[span, :], d.at[span, :], sems_out.at[j * steps + i])
            for j, (s, d) in enumerate(((attended_all, ga_any), (gc, gc_any)))
        ]

    def norm_stage():
        span = rows_at(step - 1)
        grad_normed = grad_sums[pl.ds((step + 1) % 2, 1)][0]
        normal = normal_ref[...].astype(F32)
        low[span, :] = (normal * vec[1:2, :] + vec[2:3, :]).astype(BF16)
        rounded = norm_back(grad_normed, vec[1:2, :], normal, scale_ref[...]).astype(BF16)
        attended_all[span, :] = rounded
        for j, value in enumerate((grad_normed * normal, grad_normed, rounded.astype(F32))):
            line = SUM_ATTN + j
            small_ref[line : line + 1, :] += jnp.sum(value, axis=0, keepdims=True)
        gc[span, :] = dot_nt(rounded, joined[:, :width]).astype(BF16)

    def wide_stage(waiting, between):
        span = rows_at(step)
        chunks = list(range(0, hidden, CHUNK))

        def product(c):
            return dot_nt(gd_ref[...], wd[c : c + CHUNK, :])

        ahead = product(0)
        for copy in waiting:
            copy.wait()
        total = gd_ref[...].astype(F32)
        for n, c in enumerate(chunks):
            grad_active = ahead
            if n + 1 < len(chunks):
                ahead = product(chunks[n + 1])
            rounded = (grad_active * slope_ref[:, c : c + CHUNK].astype(F32)).astype(BF16)
            hidden_all[span, c : c + CHUNK] = rounded
            wide[0:1, c : c + CHUNK] += jnp.sum(rounded.astype(F32), axis=0, keepdims=True)
            total = total + dot_nt(rounded, joined[:, width + c : width + c + CHUNK])
            if n == 1:
                between()
        grad_sums[pl.ds(step % 2, 1)] = total[None]

    @pl.when(step == 0)
    def _():
        copies = down_copies(down, rows, wd, sems_down)
        later = joined_copies(own, pieces, rows, joined, sems)
        for copy in copies + later + [load_ctx]:
            copy.start()
        small_ref[...] = sums_ref[...]
        wide[...] = jnp.zeros_like(wide)
        for copy in copies:
            copy.wait()
        wide_stage(later, lambda: None)

    @pl.when((step > 0) & (step < steps))
    def _():
        wide_stage([], norm_stage)

    @pl.when(step == steps)
    def _():
        norm_stage()
        for j in range(hidden // width):
            line = SUM_UP + j
            small_ref[line : line + 1, :] = wide[0:1, j * width : (j + 1) * width]
        load_ctx.wait()

    @pl.when((step > 0) & (step <= steps))
    def _():
        for copy in stores(step - 1):
            copy.start()

    @pl.when(step > steps)
    def _():
        sending = step == steps + 1
        core = jnp.where(sending, 1 - where[1], where[1])
        height, cut = width // 2, hidden // 2
        at_wide = pl.ds(pl.multiple_of(core * cut, LANES), cut)
        at_narrow = pl.ds(pl.multiple_of(core * height, LANES), height)
        slots = (jnp.where(where[0] == 0, 1, 0), jnp.where(where[0] == 0, 0, 1))
        value = dot_tn(low[...], hidden_all[:, at_wide]).astype(BF16)
        put_blocks(
            send_ref, keep_ref, sending, slots, slice(0, cut), (value[:height], value[height:])
        )
        value = dot_tn(ctx[...], attended_all[:, at_narrow]).astype(BF16)
        put_blocks(
            send_ref, keep_ref, sending, slots, slice(cut, cut + height),
            (value[:height], value[height:]),
        )

    @pl.when(step == steps + 2)
    def _():
        for i in range(steps):
            for copy in stores(i):
                copy.wait()


def feed_back(where, gd, slope, normal, scale, joined, down, vec, context, sums):
    own, pieces, rows = joined
    count = len(pieces)
    tokens, width = gd.shape
    wide = slope.shape[1]
    steps = tokens // TILE
    total = (wide + width) // 2

    def now(columns):
        return pl.BlockSpec((TILE, columns), lambda s, *_: (jnp.minimum(s, steps - 1), 0))

    def late(columns):
        return pl.BlockSpec((TILE, columns), lambda s, *_: (jnp.clip(s - 1, 0, steps - 1), 0))

    shape = jax.ShapeDtypeStruct
    return pl.pallas_call(
        functools.partial(feed_back_kernel, count, steps),
        grid_spec=pltpu.PrefetchScalarGridSpec(
            num_scalar_prefetch=1,
            grid=(steps + 3,),
            in_specs=[SMEM, now(width), now(wide), late(width), late(1)]
            + [whole(*vec.shape), whole(*sums.shape)]
            + [ANY] * (4 + 2 * count),
            out_specs=[whole(*sums.shape)]
            + [send_spec(1, width // 2, total, steps + 1)]
            + [keep_spec(1, width // 2, total, steps + 1)]
            + [ANY] * 2,
            scratch_shapes=[
                pltpu.VMEM((width, width + wide), BF16),
                pltpu.VMEM((wide, width), BF16),
                pltpu.VMEM((tokens, width), BF16),
                pltpu.VMEM((tokens, width), BF16),
                pltpu.VMEM((tokens, wide), BF16),
                pltpu.VMEM((tokens, width), BF16),
                pltpu.VMEM((2, TILE, width), F32),
                pltpu.VMEM((tokens, width), BF16),
                pltpu.VMEM((8, wide), F32),
                pltpu.SemaphoreType.DMA((SPLITS * (2 + 2 * count),)),
                pltpu.SemaphoreType.DMA((SPLITS * (1 + 2 * count),)),
                pltpu.SemaphoreType.DMA((1,)),
                pltpu.SemaphoreType.DMA((2 * steps,)),
            ],
        ),
        out_shape=[shape(sums.shape, F32)]
        + [shape((2, width // 2, total), BF16)] * 2
        + [shape((tokens, width), BF16)] * 2,
        compiler_params=params(60),
        cost_estimate=LIGHT,
        name="feed_back",
    )(where, rows, gd, slope, normal, scale, vec, sums, context, *own, *pieces, *down)


def inputs_back_kernel(count, rows, ga_ref, grads, *refs):
    own, pieces = refs[:3], refs[3 : 3 + count]
    out_ref, full, sems = refs[3 + count :]

    @pl.when(pl.program_id(0) == 0)
    def _():
        fetch_joined(own, pieces, rows, full, sems)

    out_ref[...] = ga_ref[...].astype(F32) + dot_nt(grads[...], full[...])


def inputs_back(grads, ga, weights):
    own, pieces, rows = weights
    tokens, width = ga.shape
    tile = pl.BlockSpec((TILE, width), lambda t: (t, 0))
    return pl.pallas_call(
        functools.partial(inputs_back_kernel, len(pieces)),
        grid=(tokens // TILE,),
        in_specs=[SMEM, tile, pl.BlockSpec((TILE, 3 * width), lambda t: (t, 0))]
        + [ANY] * (3 + len(pieces)),
        out_specs=tile,
        out_shape=jax.ShapeDtypeStruct((tokens, width), F32),
        scratch_shapes=[
            pltpu.VMEM((width, 3 * width), BF16),
            pltpu.SemaphoreType.DMA((SPLITS * (3 + 2 * len(pieces)),)),
        ],
        compiler_params=params(60),
        cost_estimate=LIGHT,
        name="inputs_back",
    )(rows, ga, grads, *own, *pieces)


CORE, NEAR_Y, NEAR_Z, FAR_Z = 1, 2, 4, 8


def after(value, *others):
    return lax.optimization_barrier((value,) + others)[0]


def swap_dp(values, bit):
    size = lax.axis_size("dp")
    return lax.ppermute(values, "dp", [(i, i ^ bit) for i in range(size)])


def swap_fsdp(values):
    return lax.ppermute(values, "fsdp", [(0, 1), (1, 0)])


def swap_both(values):
    size = lax.axis_size("dp")
    pairs = [(2 * i + h, 2 * (i ^ NEAR_Y) + 1 - h) for i in range(size) for h in range(2)]
    return lax.ppermute(values, ("dp", "fsdp"), pairs)


def rows_of(values, start, count):
    return lax.dynamic_slice_in_dim(values, start, count, axis=0)


def own_part(shards, place):
    half, core, y, z = place
    height = shards[0].shape[0]
    count = height // 8
    starts = (2 * y + core) * count, height // 2 + (2 * z + core) * count
    return jnp.concatenate(
        [jnp.concatenate([rows_of(s, start, count) for s in shards], axis=1) for start in starts],
        axis=0,
    )


def far_parts(first):
    count = first.shape[0] // 2
    return swap_dp(first[:count], NEAR_Y), swap_dp(first[count:], NEAR_Z)


def all_parts(first, far):
    here = (first,) + far
    return here + tuple(swap_dp(part, CORE) for part in here)


def piece_rows(height, place):
    half, core, y, z = place
    count = height // 8
    base = (1 - half) * height
    rows = [half * height]
    for c in (core, 1 - core):
        rows += [
            base + (2 * y + c) * count,
            base + height // 2 + (2 * z + c) * count,
            base + (2 * (1 - y) + c) * count,
            base + height // 2 + (2 * (1 - z) + c) * count,
        ]
    return jnp.stack(rows).astype(jnp.int32)


class Part:
    def __init__(self, terms, place, columns=None):
        self.bits = {0: 1, 1: place[2], 2: place[3]}
        self.swaps = {
            0: swap_fsdp,
            1: lambda v: swap_dp(v, NEAR_Y),
            2: lambda v: swap_dp(v, NEAR_Z),
            3: lambda v: swap_dp(v, FAR_Z),
        }
        self.terms = [t.reshape(2, 2, 2, t.shape[1] // 4, t.shape[2]) for t in terms]
        self.views = [(columns, ())] * len(terms)
        self.flight, self.joined = [], None

    def total(self, *picks):
        value = None
        for term, (columns, before) in zip(self.terms, self.views):
            if columns is not None:
                term = term[..., columns[0] : columns[1]]
            for axis, index in before + picks:
                term = lax.dynamic_slice_in_dim(term, index, 1, axis)
            term = term.astype(F32)
            value = term if value is None else value + term
        return value.astype(BF16)

    def cut(self, *picks):
        self.views = [(columns, before + picks) for columns, before in self.views]

    def halve(self, axis):
        bit = self.bits[axis]
        self.flight, self.route = [self.total((axis, 1 - bit))], [self.swaps[axis]]
        self.cut((axis, bit))

    def both(self):
        bit = self.bits[1]
        self.flight = [
            self.total((0, 0), (1, bit)),
            self.total((0, 1), (1, 1 - bit)),
            self.total((0, 0), (1, 1 - bit)),
        ]
        self.route = [self.swaps[0], self.swaps[1], swap_both]
        self.cut((0, 1), (1, bit))

    def merge(self, *others):
        value = jnp.concatenate([part.total() for part in (self,) + others], axis=-1)
        self.terms, self.views = [value], [(None, ())]

    def split(self, cut):
        other = copy.copy(self)
        end = self.terms[0].shape[-1]
        self.views = [((0, cut), before) for _, before in self.views]
        other.views = [((cut, end), before) for _, before in other.views]
        return other

    def send_whole(self, swap, reshape=None):
        value = self.terms[0]
        if len(self.terms) > 1 or self.views[0][0] is not None:
            value = self.total()
        if reshape:
            value = value.reshape(-1, value.shape[-1])
        self.flight, self.route = [value], [lambda v: (v, swap(v))]
        self.terms, self.views = [], []

    def far(self):
        self.send_whole(self.swaps[3])

    def join(self, axis):
        self.send_whole(self.swaps[axis])
        self.joined = axis

    def finish(self):
        self.send_whole(lambda v: swap_dp(v, CORE), True)

    def land(self):
        for sent, route in zip(self.flight, self.route):
            got = route(sent)
            self.terms += list(got) if isinstance(got, tuple) else [got]
        self.views = self.views + [(None, ())] * (len(self.terms) - len(self.views))
        self.flight = []

    def settle(self):
        if self.joined is None:
            return
        mine, other = self.terms
        axis, self.joined = self.joined, None
        value = jnp.where(
            self.bits[axis] == 0,
            jnp.concatenate([mine, other], axis=axis),
            jnp.concatenate([other, mine], axis=axis),
        )
        self.terms, self.views = [value], [(None, ())]


def fence(parts, *arrays):
    counts = [(len(p.terms), len(p.flight)) for p in parts]
    flat = [a for p in parts for a in p.terms + p.flight] + list(arrays)
    flat = list(lax.optimization_barrier(tuple(flat)))
    for part, (terms, flight) in zip(parts, counts):
        part.terms, flat = flat[:terms], flat[terms:]
        part.flight, flat = flat[:flight], flat[flight:]
    return flat


def widen(mine, other, core, axis):
    low = jnp.where(core == 0, mine, other).astype(F32)
    high = jnp.where(core == 0, other, mine).astype(F32)
    return jnp.concatenate([low, high], axis=axis)


def gather_all(values):
    return lax.all_gather(values, "fsdp", axis=0, tiled=True)


def sum_plain(send, keep, by_rows):
    blocks = [[keep[1], send[1]], [keep[0], send[0]]]
    axis = 0 if by_rows else 1
    value = jnp.concatenate([jnp.concatenate(pair, axis=axis) for pair in blocks], axis=0)
    own = lax.psum_scatter(value, "fsdp", scatter_dimension=0, tiled=True)
    return lax.psum(own, "dp").astype(F32)


def local(
    inputs, segment_ids, cotangent, w_query, b_query, w_key, b_key, w_value, b_value,
    w_output, b_output, gain_attn, bias_attn, w_up, b_up, w_down, b_down, gain_ffn, bias_ffn,
):
    rows, length = segment_ids.shape
    width = inputs.shape[1]
    shards = lax.axis_size("fsdp")
    paired = shards == 2 and lax.axis_size("dp") == 16
    half = lax.axis_index("fsdp")
    dp = lax.axis_index("dp")
    place = (half, dp % 2, dp // 2 % 2, dp // 4 % 2)
    core = place[1]
    vectors = (b_query, b_key, b_value, b_output, gain_attn, bias_attn, b_down, gain_ffn, bias_ffn)
    height = w_query.shape[0]
    cosine, sine, turned = rotary_tables(segment_ids, inputs)
    if paired:
        where = jnp.stack([half, core]).astype(jnp.int32)
        part_qkv = own_part((w_query, w_key, w_value), place)
        part_up = own_part((w_output, w_up), place)
        part_down = own_part((w_down,), place)
        here_qkv = after(swap_fsdp(part_qkv), cosine)
        lines = jnp.concatenate(vectors + (b_up,)).reshape(-1, height)
        other = swap_fsdp(after(lines, part_qkv))
        here_up = swap_fsdp(after(part_up, here_qkv))
        at = piece_rows(height, place)
        joined_qkv = ((w_query, w_key, w_value), all_parts(here_qkv, far_parts(here_qkv)), at)
        lines = jnp.where(half == 0, jnp.stack([lines, other]), jnp.stack([other, lines]))
    else:
        where = jnp.zeros((2,), jnp.int32)
        at = jnp.zeros((1,), jnp.int32)
        joined_qkv = (tuple(gather_all(w) for w in (w_query, w_key, w_value)), (), at)
        joined_up = ((gather_all(w_output), gather_all(w_up)), (), at)
        down = (gather_all(w_down),)
        lines = jnp.concatenate(vectors + (b_up,)).reshape(-1, height)
        lines = lax.all_gather(lines, "fsdp", axis=0)
    lines = lines.astype(F32)
    vec = jnp.swapaxes(lines[:, :9], 0, 1).reshape(9, width)
    bias_up = lines[:, 9:].reshape(1, -1)

    q, k, v = project(inputs, joined_qkv, vec[:3], cosine, sine)
    vec = vec[3:]
    if paired:
        q, here_up, part_down, vec, bias_up = lax.optimization_barrier(
            (q, here_up, part_down, vec, bias_up)
        )
        here_down = swap_fsdp(part_down)
        far_up = far_parts(here_up)
    context, probs = attend(q, k, v, segment_ids)
    if paired:
        context, probs, here_up, here_down, far_up = lax.optimization_barrier(
            (context, probs, here_up, here_down, far_up)
        )
        joined_up = ((w_output, w_up), all_parts(here_up, far_up), at)
        far_down = far_parts(here_down)
    normal, scale, act, slope = feed_up(context, inputs, joined_up, vec, bias_up)
    if paired:
        act, slope, here_down, far_down = lax.optimization_barrier(
            (act, slope, here_down, far_down)
        )
        down = (w_down,) + all_parts(here_down, far_down)
    sums, send, keep, result, grad_down = feed_down(
        where, act, normal, cotangent, down, at, vec
    )
    sent = [(send, keep)]
    if paired:
        sum_d = Part([keep, swap_dp(send, CORE)], place)
        sum_d.both()
        (grad_down,) = fence([sum_d], grad_down)
    outs = feed_back(
        where, grad_down, slope, normal, scale, joined_up, down, vec, context, sums
    )
    sent.append(outs[1:3])
    if paired:
        sum_d.land()
        outs = fence([sum_d], *outs)
    sums, send, keep, grad_attended, grad_context = outs
    if paired:
        sum_d.merge()
        sum_u = Part([keep, swap_dp(send, CORE)], place)
        sum_d.halve(2)
        sum_u.both()
        parts = [sum_d, sum_u]
        (grad_context,) = fence(parts, grad_context)
    tables = (probs, cosine, sine, turned)
    made = None
    if rows > 1:
        sums, made = attend_back(where, q, k, v, grad_context, *tables, sums, 0)
        if paired:
            sum_d.land()
            sums, made, grad_context = fence([sum_d], sums, made, grad_context)
            sum_d.far()
            sums, grad_context = fence([sum_d], sums, grad_context)
    outs = attend_back(where, q, k, v, grad_context, *tables, sums, rows - 1, made)
    sent.append(outs[1:3])
    if paired:
        for p in parts:
            p.land()
        outs = fence(parts, *outs)
    sums, send, keep, grads = outs
    if paired:
        sum_q = Part([keep, swap_dp(send, CORE)], place)
        sum_u.merge()
        sum_d.join(2) if rows > 1 else sum_d.far()
        sum_u.halve(2)
        sum_q.both()
        parts = [sum_d, sum_u, sum_q]
        (grad_attended,) = fence(parts, grad_attended)
    grad_inputs = inputs_back(grads, grad_attended, joined_qkv)
    if paired:
        for p in parts:
            p.land()
        (grad_inputs,) = fence(parts, grad_inputs)
        last = grad_inputs

        def step(part, name, *axis):
            nonlocal last
            (last,) = fence([part], last)
            part.settle()
            getattr(part, name)(*axis)
            (last,) = fence([part], last)
            last = part.flight[0]
            part.land()

        if rows == 1:
            step(sum_d, "join", 2)
        step(sum_u, "far")
        sum_q.merge()
        step(sum_q, "halve", 2)
        step(sum_d, "join", 1)
        step(sum_q, "far")
        cut_u, cut_q = ((p.terms[0].shape[-1] // 2 + 64) // LANES * LANES for p in (sum_u, sum_q))
        (last,) = fence([sum_u], last)
        sum_v = sum_u.split(cut_u)
        step(sum_u, "join", 2)
        step(sum_v, "join", 1)
        step(sum_d, "finish")
        gwd = widen(*sum_d.terms, core, 0)
        (last,) = fence([sum_q], last)
        sum_r = sum_q.split(cut_q)
        step(sum_q, "join", 2)
        step(sum_r, "join", 1)
        step(sum_u, "join", 1)
        step(sum_v, "join", 2)
        (gwd,) = fence([sum_q, sum_r], gwd)
        step(sum_q, "join", 1)
        step(sum_r, "join", 2)
        for part in (sum_u, sum_v):
            part.settle()
            part.finish()
        fence([sum_u, sum_v, sum_q, sum_r])
        sum_u.land()
        sum_v.land()
        for part in (sum_q, sum_r):
            part.settle()
            part.finish()
            part.land()
    else:
        sums = lax.psum(sums, ("dp", "fsdp"))

    wide = b_up.shape[0] * shards
    if paired:
        mine, other = (
            jnp.concatenate([a, b], axis=1) for a, b in zip(sum_u.terms, sum_v.terms)
        )
        cut = wide // 2
        gwu = widen(mine[:, :cut], other[:, :cut], core, 1)
        gwo = widen(mine[:, cut:], other[:, cut:], core, 1)
        mine, other = (
            jnp.concatenate([a, b], axis=1) for a, b in zip(sum_q.terms, sum_r.terms)
        )
        gwq, gwk, gwv = (
            widen(*(end[:, i * width : (i + 1) * width] for end in (mine, other)), core, 0)
            for i in range(3)
        )
        count = height // LANES
        packed = jnp.where(core == 0, mine[:, 3 * width :], other[:, 3 * width :])
        packed = packed[: len(LINES) * count + wide // 2 // LANES].astype(F32)
        vectors = [packed[i * count : (i + 1) * count].reshape(-1) for i in range(len(LINES))]
        gbu = packed[len(LINES) * count :].reshape(-1)
        ggf, gbf, gbd, gga, gba, gbo, gbq, gbk, gbv = vectors
    else:

        def own(line, count=1):
            start = line * width + half * (count * width // shards)
            return lax.dynamic_slice_in_dim(
                sums.reshape(-1), start, count * width // shards, axis=0
            )

        ggf, gbf, gbd, gga, gba, gbo, gbq, gbk, gbv = (own(line) for line in LINES)
        gbu = own(SUM_UP, wide // width)
        gwd = sum_plain(*sent[0], True)
        both = sum_plain(*sent[1], False).reshape(height, 2, -1)
        cut = wide // 2
        gwu = both[..., :cut].reshape(height, -1)
        gwo = both[..., cut:].reshape(height, -1)
        both = sum_plain(*sent[2], True)
        gwq, gwk, gwv = (both[:, i * width : (i + 1) * width] for i in range(3))
    return (
        result, grad_inputs, gwq, gbq, gwk, gbk, gwv, gbv, gwo, gbo, gga, gba,
        gwu, gbu, gwd, gbd, ggf, gbf,
    )


def solution(mesh):
    tokens, matrix, vector = P(("dp", "fsdp"), None), P("fsdp", None), P("fsdp")
    weights = (
        matrix, vector, matrix, vector, matrix, vector, matrix, vector, vector, vector,
        matrix, vector, matrix, vector, vector, vector,
    )
    return jax.shard_map(
        local,
        mesh=mesh,
        in_specs=(tokens,) * 3 + weights,
        out_specs=(tokens,) * 2 + weights,
        check_vma=False,
    )
```

```python
import copy
import functools
import jax
import jax.numpy as jnp
from jax import lax
from jax.experimental import pallas as pl
from jax.experimental.pallas import tpu as pltpu
from jax.sharding import PartitionSpec as P

HEAD = 64
GROUP = 3
EPSILON = 1e-06
LANES = 128
TILE = 256
CHUNK = 512
MASKED = -1e30
SUM_FFN, SUM_ATTN, SUM_UP, SUM_QKV, SUM_ROWS = 0, 3, 6, 10, 16
F32 = jnp.float32
BF16 = jnp.bfloat16


def params(mebibytes):
    return pltpu.CompilerParams(vmem_limit_bytes=mebibytes * 1024 * 1024)


LIGHT = pl.CostEstimate(flops=1000, bytes_accessed=1000, transcendentals=0)


def dot_nn(left, right):
    return lax.dot_general(left, right, (((1,), (0,)), ((), ())), preferred_element_type=F32)


def dot_nt(left, right):
    return lax.dot_general(left, right, (((1,), (1,)), ((), ())), preferred_element_type=F32)


def dot_tn(left, right):
    return lax.dot_general(left, right, (((0,), (0,)), ((), ())), preferred_element_type=F32)


def whole(*shape):
    return pl.BlockSpec(shape, lambda *_: (0,) * len(shape))


SPLITS = 4


def piece_copies(pieces, starts, full, column, sems, first):
    copies = []
    assert len(pieces) == len(starts)
    for i, (piece, start) in enumerate(zip(pieces, starts)):
        height, width = piece.shape
        splits = SPLITS if height * width >= 500_000 and height % (16 * SPLITS) == 0 else 1
        count = height // splits
        for j in range(splits):
            row = pl.multiple_of(start + j * count, 16)
            copies.append(
                pltpu.make_async_copy(
                    piece.at[pl.ds(j * count, count), :],
                    full.at[pl.ds(row, count), column : column + width],
                    sems.at[SPLITS * (first + i) + j],
                )
            )
    return copies


def cut_pieces(pieces):
    cut = []
    for i, piece in enumerate(pieces):
        count = piece.shape[0] // 2
        cut += [piece.at[:count, :], piece.at[count:, :]] if i % 3 == 0 else [piece]
    return cut


def joined_copies(own, pieces, rows, full, sems, cut=None):
    pieces = cut_pieces(pieces)
    shards, column = [], 0
    for i, shard in enumerate(own):
        shards.append(piece_copies([shard], [rows[0]], full, column, sems, i))
        column += shard.shape[1]
    starts = [rows[1 + i] for i in range(len(pieces))]
    first = len(own)
    if cut is None:
        return sum(shards, []) + piece_copies(pieces, starts, full, 0, sems, first)
    left = [piece.at[:, :cut] for piece in pieces]
    right = [piece.at[:, cut:] for piece in pieces]
    return (
        shards[0] + piece_copies(left, starts, full, 0, sems, first),
        sum(shards[1:], []) + piece_copies(right, starts, full, cut, sems, first + len(pieces)),
    )


def fetch_joined(own, pieces, rows, full, sems):
    copies = joined_copies(own, pieces, rows, full, sems)
    for copy in copies:
        copy.start()
    for copy in copies:
        copy.wait()


ANY = pl.BlockSpec(memory_space=pl.ANY)
SMEM = pl.BlockSpec(memory_space=pltpu.SMEM)


def tables_kernel(seg_row, seg_col, x_ref, cos_ref, sin_ref, turned_ref):
    length = seg_row.shape[-1]
    key = lax.broadcasted_iota(jnp.int32, (length, length), 1)
    query = lax.broadcasted_iota(jnp.int32, (length, length), 0)
    earlier = (seg_col[...] == seg_row[0]) & (key < query)
    place = jnp.sum(earlier.astype(F32), axis=1, keepdims=True)
    lane = lax.broadcasted_iota(jnp.int32, (1, LANES), 1)
    paired = (lane % HEAD // 2 * 2).astype(F32)
    freqs = jnp.exp(-jnp.log(F32(10000.0)) * paired / HEAD)
    angle = place * freqs
    cos_ref[...] = jnp.cos(angle)
    sine = jnp.sin(angle)
    sin_ref[...] = jnp.where(lane % 2 == 0, -sine, sine)
    turned_ref[...] = x_ref[...].T


def rotary_tables(segments, x):
    rows, length = segments.shape
    width = x.shape[1]
    return pl.pallas_call(
        tables_kernel,
        grid=(rows,),
        in_specs=[
            pl.BlockSpec((1, 1, length), lambda r: (r, 0, 0)),
            pl.BlockSpec((length, 1), lambda r: (r, 0)),
            pl.BlockSpec((length, width), lambda r: (r, 0)),
        ],
        out_specs=[pl.BlockSpec((length, LANES), lambda r: (r, 0))] * 2
        + [pl.BlockSpec((width, length), lambda r: (0, r))],
        out_shape=[jax.ShapeDtypeStruct((rows * length, LANES), F32)] * 2
        + [jax.ShapeDtypeStruct((width, rows * length), BF16)],
        compiler_params=params(60),
        cost_estimate=LIGHT,
        name="rotary_tables",
    )(segments.reshape(rows, 1, length), segments.reshape(rows * length, 1), x)


def pair_swap(values):
    even = lax.broadcasted_iota(jnp.int32, values.shape, 1) % 2 == 0
    return jnp.where(
        even, pltpu.roll(values, LANES - 1, axis=1), pltpu.roll(values, 1, axis=1)
    )


def project_kernel(count, rows, x_ref, bias, cos_ref, sin_ref, *refs):
    own, pieces = refs[:3], refs[3 : 3 + count]
    q_ref, k_ref, v_ref, full, sems = refs[3 + count :]
    width = x_ref.shape[1]

    @pl.when(pl.program_id(0) == 0)
    def _():
        fetch_joined(own, pieces, rows, full, sems)

    x = x_ref[...]
    cosine, sine = cos_ref[...], sin_ref[...]
    step = 2 * LANES
    for i, out in enumerate((q_ref, k_ref, v_ref)):
        for c in range(0, width, step):
            lin = dot_nn(x, full[:, i * width + c : i * width + c + step])
            lin = lin + bias[i : i + 1, c : c + step]
            if i < 2:
                parts = []
                for d in range(0, step, LANES):
                    part = lin[:, d : d + LANES]
                    part = part * cosine + pair_swap(part) * sine
                    parts.append(part)
                lin = jnp.concatenate(parts, axis=1)
            if i == 0:
                out[:, c : c + step] = (lin.astype(BF16).astype(F32) * 0.125).astype(BF16)
            else:
                out[:, c : c + step] = lin.astype(BF16)


def project(x, weights, bias, cosine, sine):
    own, pieces, rows = weights
    tokens, width = x.shape
    tile = pl.BlockSpec((TILE, width), lambda t: (t, 0))
    table = pl.BlockSpec((TILE, LANES), lambda t: (t, 0))
    return pl.pallas_call(
        functools.partial(project_kernel, len(pieces)),
        grid=(tokens // TILE,),
        in_specs=[SMEM, tile, whole(*bias.shape), table, table] + [ANY] * (3 + len(pieces)),
        out_specs=[tile] * 3,
        out_shape=[jax.ShapeDtypeStruct((tokens, width), BF16)] * 3,
        scratch_shapes=[
            pltpu.VMEM((width, 3 * width), BF16),
            pltpu.SemaphoreType.DMA((SPLITS * (3 + 2 * len(pieces)),)),
        ],
        compiler_params=params(60),
        cost_estimate=LIGHT,
        name="project",
    )(rows, x, bias, cosine, sine, *own, *pieces)


def spans(length):
    found, offset = [], 0
    for first in range(0, length, LANES):
        low, high = max(first - LANES, 0), min(first + 2 * LANES, length)
        found.append((slice(first, first + LANES), slice(low, high), slice(offset, offset + high - low)))
        offset += high - low
    return found, offset


def split_heads(values):
    lane = lax.broadcasted_iota(jnp.int32, (1, LANES), 1)
    return [jnp.where(lane // HEAD == h, values, jnp.zeros_like(values)) for h in range(2)]


def stack_heads(heads, rows):
    return jnp.concatenate([head[rows, :] for head in heads], axis=0)


def merge_heads(stacked):
    lane = lax.broadcasted_iota(jnp.int32, (1, LANES), 1)
    half = stacked.shape[0] // 2
    return jnp.where(lane < HEAD, stacked[:half], stacked[half:])


def attend_kernel(q_ref, k_ref, v_ref, seg_row, seg_col, ctx_ref, prob_ref, bias):
    blocks, _ = spans(q_ref.shape[0])

    @pl.when(pl.program_id(1) == 0)
    def _():
        for own, span, at in blocks:
            bias[at, :] = jnp.where(seg_col[span, :] == seg_row[0, :, own], 0.0, MASKED)

    pairs = [slice(p * LANES, (p + 1) * LANES) for p in range(GROUP)]
    units = [(p, lanes) + block for p, lanes in enumerate(pairs) for block in blocks]
    queries = [split_heads(q_ref[:, lanes]) for lanes in pairs]

    def product(unit):
        p, lanes, own, span, _ = unit
        return dot_nt(k_ref[span, lanes], stack_heads(queries[p], own))

    def soften(unit, scores):
        at = unit[-1]
        heads = []
        for h in range(2):
            masked = scores[:, h * LANES : (h + 1) * LANES] + bias[at, :]
            peak = jnp.max(masked, axis=0, keepdims=True)
            expo = jnp.exp(masked - peak)
            total = jnp.sum(expo, axis=0, keepdims=True)
            heads.append((expo * (1.0 / total)).astype(BF16))
        return jnp.concatenate(heads, axis=1)

    def finish(unit, probs):
        p, lanes, own, span, at = unit
        prob_ref[0, p, at, :] = probs
        ctx_ref[own, lanes] = merge_heads(dot_tn(probs, v_ref[span, lanes])).astype(BF16)

    count = len(blocks)
    scores = [product(unit) for unit in units[:count]]
    waiting = []
    for p in range(GROUP):
        now = units[p * count : (p + 1) * count]
        probs = [soften(unit, value) for unit, value in zip(now, scores)]
        scores = [product(unit) for unit in units[(p + 1) * count : (p + 2) * count]]
        for unit, value in waiting:
            finish(unit, value)
        waiting = list(zip(now, probs))
    for unit, value in waiting:
        finish(unit, value)


def attend(q, k, v, segments):
    rows, length = segments.shape
    tokens, width = q.shape
    pairs = width // LANES
    wide = GROUP * LANES
    _, depth = spans(length)
    head = pl.BlockSpec((length, wide), lambda r, p: (r, p))
    return pl.pallas_call(
        attend_kernel,
        grid=(rows, pairs // GROUP),
        in_specs=[head] * 3
        + [
            pl.BlockSpec((1, 1, length), lambda r, p: (r, 0, 0)),
            pl.BlockSpec((length, 1), lambda r, p: (r, 0)),
        ],
        out_specs=[
            head,
            pl.BlockSpec((1, GROUP, depth, 2 * LANES), lambda r, p: (r, p, 0, 0)),
        ],
        out_shape=[
            jax.ShapeDtypeStruct((tokens, width), BF16),
            jax.ShapeDtypeStruct((rows, pairs, depth, 2 * LANES), BF16),
        ],
        scratch_shapes=[pltpu.VMEM((depth, LANES), F32)],
        compiler_params=params(60),
        cost_estimate=LIGHT,
        name="attend",
    )(q, k, v, segments.reshape(rows, 1, length), segments.reshape(tokens, 1))


def send_spec(steps, height, width, first):
    return pl.BlockSpec(
        (2 // steps, height, width), lambda s, *_: (jnp.clip(s - first, 0, steps - 1), 0, 0)
    )


def keep_spec(steps, height, width, first):
    return pl.BlockSpec(
        (2 // steps, height, width), lambda s, *_: (jnp.clip(s - first - steps, 0, steps - 1), 0, 0)
    )


def put_blocks(send_ref, keep_ref, sending, slots, columns, values):
    @pl.when(sending)
    def _():
        for slot, value in zip(slots, values):
            send_ref[slot, :, columns] = value

    @pl.when(jnp.logical_not(sending))
    def _():
        for slot, value in zip(slots, values):
            keep_ref[slot, :, columns] = value


LINES = (SUM_FFN, SUM_FFN + 1, SUM_FFN + 2, SUM_ATTN, SUM_ATTN + 1, SUM_ATTN + 2) + (
    SUM_QKV, SUM_QKV + 1, SUM_QKV + 2,
)


def pack_vectors(small_ref, packed, half):
    width = small_ref.shape[1]
    part = width // 2 // LANES
    packed[...] = jnp.zeros_like(packed)
    for i, line in enumerate(LINES):
        for j in range(part):
            lanes = pl.ds(pl.multiple_of(half * (width // 2) + j * LANES, LANES), LANES)
            packed[i * part + j : i * part + j + 1, :] = small_ref[line : line + 1, lanes]
    base, count = len(LINES) * part, width // LANES
    lines = (SUM_QKV - SUM_UP) // 2
    for i in range(lines):
        for j in range(count):
            row = base + i * count + j
            lanes = slice(j * LANES, (j + 1) * LANES)
            low, high = (small_ref[SUM_UP + n : SUM_UP + n + 1, lanes] for n in (i, lines + i))
            packed[row : row + 1, :] = jnp.where(half == 0, low, high)


def attend_back_kernel(
    rows, before, last, where, q_ref, k_ref, v_ref, g_ref, prob_ref, cos_ref, sin_ref, sums_ref,
    *refs,
):
    if last:
        (
            turned_any, *made_any, small_ref, send_ref, keep_ref, out_any,
            acc_k, acc_v, grads_all, turned, packed, sems,
        ) = refs
    else:
        small_ref, out_any, acc_k, acc_v, grads_all, sems = refs
    step = pl.program_id(0)
    length, width = q_ref.shape[0], small_ref.shape[1]
    pairs = width // LANES
    units = rows * pairs // GROUP
    hand_on = pltpu.make_async_copy(grads_all, out_any, sems.at[0])
    loads = []
    if last:
        loads.append(pltpu.make_async_copy(turned_any, turned, sems.at[1]))
        if before:
            target = grads_all.at[pl.ds(0, before * length), :]
            loads.append(pltpu.make_async_copy(made_any[0], target, sems.at[2]))

    @pl.when(step == 0)
    def _():
        for load in loads:
            load.start()
        small_ref[...] = sums_ref[...]

    @pl.when(step < units)
    def _():
        blocks, _ = spans(length)
        groups = pairs // GROUP
        row, group = before * last + step // groups, step % groups
        at_rows = pl.ds(pl.multiple_of(row * length, length), length)
        lanes_of = [slice(p * LANES, (p + 1) * LANES) for p in range(GROUP)]

        def turn_back(values, rows):
            return values * cos_ref[rows, :] - pair_swap(values) * sin_ref[rows, :]

        def first(p):
            grads = split_heads(g_ref[:, lanes_of[p]])
            return [
                dot_nt(v_ref[span, lanes_of[p]], stack_heads(grads, own)) for own, span, _ in blocks
            ]

        def second(p, grad_probs):
            made = []
            for (own, span, at), pair in zip(blocks, grad_probs):
                heads = []
                for h in range(2):
                    columns = slice(h * LANES, (h + 1) * LANES)
                    probs = prob_ref[0, p, at, columns].astype(F32)
                    inner = jnp.sum(probs * pair[:, columns], axis=0, keepdims=True)
                    heads.append((probs * (pair[:, columns] - inner)).astype(BF16))
                made.append(jnp.concatenate(heads, axis=1))
            return made

        def third(p, grad_scores):
            lanes = lanes_of[p]
            queries, grads = split_heads(q_ref[:, lanes]), split_heads(g_ref[:, lanes])
            k_t = k_ref[:, lanes].T
            acc_k[p] = jnp.zeros_like(acc_k[p])
            acc_v[p] = jnp.zeros_like(acc_v[p])
            turned_parts = []
            for (own, span, at), low in zip(blocks, grad_scores):
                acc_k[p, span, :] += dot_nn(low, stack_heads(queries, own))
                acc_v[p, span, :] += dot_nn(prob_ref[0, p, at, :], stack_heads(grads, own))
                product = dot_nn(k_t[:, span], low)
                both = jnp.concatenate([product[:HEAD, :LANES], product[HEAD:, LANES:]], axis=0)
                turned_parts.append(both.T)
            return turned_parts

        def fourth(p, turned_parts):
            gq = jnp.concatenate(
                [
                    turn_back(part * 0.125, own).astype(BF16)
                    for (own, _, _), part in zip(blocks, turned_parts)
                ],
                axis=0,
            )
            gk = turn_back(acc_k[p], slice(0, length)).astype(BF16)
            gv = acc_v[p].astype(BF16)
            pair = group * GROUP + p
            at_lanes = pl.ds(pl.multiple_of(pair * LANES, LANES), LANES)
            for i, grad in enumerate((gq, gk, gv)):
                at_grad = pl.ds(pl.multiple_of((i * pairs + pair) * LANES, LANES), LANES)
                grads_all[at_rows, at_grad] = grad
                line = SUM_QKV + i
                small_ref[line : line + 1, at_lanes] += jnp.sum(
                    grad.astype(F32), axis=0, keepdims=True
                )

        grad_probs = first(0)
        waiting = None
        for p in range(GROUP):
            grad_scores = second(p, grad_probs)
            if p + 1 < GROUP:
                grad_probs = first(p + 1)
            turned_parts = third(p, grad_scores)
            if waiting is not None:
                fourth(*waiting)
            waiting = (p, turned_parts)
        fourth(*waiting)

    if not last:

        @pl.when(step == units - 1)
        def _():
            hand_on.start()
            hand_on.wait()

        return

    @pl.when(step == units)
    def _():
        for load in loads:
            load.wait()
        hand_on.start()

    @pl.when(step >= units)
    def _():
        sending = step == units
        height = send_ref.shape[1]
        core = jnp.where(sending, 1 - where[1], where[1])
        left = [
            turned[pl.ds(pl.multiple_of((2 * half + core) * height, 16), height), :]
            for half in (1 - where[0], where[0])
        ]
        value = dot_nn(jnp.concatenate(left, axis=0), grads_all[...]).astype(BF16)
        put_blocks(
            send_ref, keep_ref, sending, (0, 1), slice(0, 3 * width), (value[:height], value[height:])
        )
        for slot, half in enumerate((1 - where[0], where[0])):
            pack_vectors(small_ref, packed, half)
            vectors = jnp.where(core == 0, packed[...], 0.0).astype(BF16)
            put_blocks(
                send_ref, keep_ref, sending, (slot,), slice(3 * width, 3 * width + LANES), (vectors,)
            )

    @pl.when(step == units + 1)
    def _():
        hand_on.wait()


def attend_back(where, q, k, v, grad_context, probs, cosine, sine, turned, sums, row, made=None):
    tokens, width = q.shape
    total, pairs, depth = probs.shape[:3]
    length = tokens // total
    last = row == total - 1
    rows = 1 if last else total - 1
    units = rows * pairs // GROUP
    height = width // 4
    here = tokens if last else rows * length

    def at(s):
        s = jnp.minimum(s, units - 1)
        return row + s // (pairs // GROUP), s % (pairs // GROUP)

    head = pl.BlockSpec((length, GROUP * LANES), lambda s, *_: at(s))
    table = pl.BlockSpec((length, LANES), lambda s, *_: (at(s)[0], 0))
    shape = jax.ShapeDtypeStruct
    out_specs = [whole(*sums.shape)]
    out_shape = [shape(sums.shape, F32)]
    scratch = [pltpu.VMEM((GROUP, length, LANES), F32)] * 2
    scratch += [pltpu.VMEM((here, 3 * width), BF16)]
    extra = ()
    if last:
        extra = (turned,) if made is None else (turned, made)
        out_specs += [
            send_spec(1, height, 3 * width + LANES, units),
            keep_spec(1, height, 3 * width + LANES, units),
        ]
        out_shape += [shape((2, height, 3 * width + LANES), BF16)] * 2
        scratch += [pltpu.VMEM((width, tokens), BF16), pltpu.VMEM((height, LANES), F32)]
    return pl.pallas_call(
        functools.partial(attend_back_kernel, rows, row, last),
        grid_spec=pltpu.PrefetchScalarGridSpec(
            num_scalar_prefetch=1,
            grid=(units + 2 * last,),
            in_specs=[head] * 4
            + [
                pl.BlockSpec((1, GROUP, depth, 2 * LANES), lambda s, *_: at(s) + (0, 0)),
                table,
                table,
                whole(*sums.shape),
            ]
            + [ANY] * len(extra),
            out_specs=out_specs + [ANY],
            scratch_shapes=scratch + [pltpu.SemaphoreType.DMA((3,))],
        ),
        out_shape=out_shape + [shape((here, 3 * width), BF16)],
        compiler_params=params(60),
        cost_estimate=LIGHT,
        name="attend_back",
    )(where, q, k, v, grad_context, probs, cosine, sine, sums, *extra)


def norm_parts(values):
    mean = jnp.mean(values, axis=-1, keepdims=True)
    center = values - mean
    spread = jnp.mean(center * center, axis=-1, keepdims=True)
    scale = lax.rsqrt(spread + EPSILON)
    return center * scale, scale


def norm_back(grads, gain, normal, scale):
    inner = grads * gain
    return scale * (
        inner
        - jnp.mean(inner, axis=-1, keepdims=True)
        - normal * jnp.mean(inner * normal, axis=-1, keepdims=True)
    )


def gelu_parts(values):
    share = 0.5 + 0.5 * lax.erf(values * 0.7071067811865476)
    return share, jnp.exp(values * values * -0.5) * 0.3989422804014327


def down_copies(down, rows, wd, sems):
    scale = wd.shape[0] // wd.shape[1]
    pieces = list(down[:1]) + cut_pieces(down[1:])
    starts = [rows[i] * scale for i in range(len(pieces))]
    return piece_copies(pieces, starts, wd, 0, sems, 0)


def feed_up_kernel(count, rows, ctx_ref, x_ref, vec, bu, *refs):
    own, pieces = refs[:2], refs[2 : 2 + count]
    normal_ref, scale_ref, act_ref, slope_ref, joined, lows, sems = refs[2 + count :]
    width = x_ref.shape[1]
    step, last = pl.program_id(0), pl.num_programs(0) - 1

    def norm_stage():
        bo, g1, s1 = (vec[i : i + 1, :] for i in range(3))
        attended = dot_nn(ctx_ref[...], joined[:, :width]) + bo
        normal, scale = norm_parts(x_ref[...].astype(F32) + attended)
        normal = normal.astype(BF16)
        normal_ref[...] = normal
        scale_ref[...] = scale
        lows[pl.ds(step % 2, 1)] = (normal.astype(F32) * g1 + s1).astype(BF16)[None]

    def wide_stage(between):
        low = lows[pl.ds((step + 1) % 2, 1)][0]
        chunks = list(range(0, bu.shape[1], CHUNK))

        def product(c):
            return dot_nn(low, joined[:, width + c : width + c + CHUNK])

        ahead = product(0)
        for n, c in enumerate(chunks):
            hidden = ahead + bu[:, c : c + CHUNK]
            if n + 1 < len(chunks):
                ahead = product(chunks[n + 1])
            share, density = gelu_parts(hidden)
            act_ref[:, c : c + CHUNK] = (hidden * share).astype(BF16)
            slope_ref[:, c : c + CHUNK] = (share + hidden * density).astype(BF16)
            if n == 1:
                between()

    @pl.when(step == 0)
    def _():
        sooner, later = joined_copies(own, pieces, rows, joined, sems, width)
        for copy in sooner + later:
            copy.start()
        for copy in sooner:
            copy.wait()
        norm_stage()
        for copy in later:
            copy.wait()

    @pl.when((step > 0) & (step < last))
    def _():
        wide_stage(norm_stage)

    @pl.when(step == last)
    def _():
        wide_stage(lambda: None)


def feed_up(ctx, x, joined, vec, bu):
    own, pieces, rows = joined
    count = len(pieces)
    tokens, width = x.shape
    hidden = bu.shape[1]
    steps = tokens // TILE

    def now(columns):
        return pl.BlockSpec((TILE, columns), lambda s: (jnp.minimum(s, steps - 1), 0))

    def late(columns):
        return pl.BlockSpec((TILE, columns), lambda s: (jnp.maximum(s - 1, 0), 0))

    shape = jax.ShapeDtypeStruct
    return pl.pallas_call(
        functools.partial(feed_up_kernel, count),
        grid=(steps + 1,),
        in_specs=[SMEM, now(width), now(width), whole(*vec.shape), whole(*bu.shape)]
        + [ANY] * (2 + count),
        out_specs=[now(width), now(1), late(hidden), late(hidden)],
        out_shape=[
            shape((tokens, width), BF16),
            shape((tokens, 1), F32),
            shape((tokens, hidden), BF16),
            shape((tokens, hidden), BF16),
        ],
        scratch_shapes=[
            pltpu.VMEM((width, width + hidden), BF16),
            pltpu.VMEM((2, TILE, width), BF16),
            pltpu.SemaphoreType.DMA((SPLITS * (2 + 4 * count),)),
        ],
        compiler_params=params(60),
        cost_estimate=LIGHT,
        name="feed_up",
    )(rows, ctx, x, vec, bu, *own, *pieces)


def feed_down_kernel(count, steps, where, rows, normal_ref, cot_ref, vec, act_any, *refs):
    down = refs[:count]
    small_ref, send_ref, keep_ref, res_any, gd_any = refs[count : count + 5]
    wd, act, products, res, grads_all, sems, sems_act, sems_out = refs[count + 5 :]
    step = pl.program_id(0)
    tile = cot_ref.shape[0]

    def rows_at(i):
        return pl.ds(pl.multiple_of(i * tile, tile), tile)

    def stores(i):
        span = rows_at(i)
        return [
            pltpu.make_async_copy(s.at[span, :], d.at[span, :], sems_out.at[j * steps + i])
            for j, (s, d) in enumerate(((res, res_any), (grads_all, gd_any)))
        ]

    def load(i):
        span = rows_at(i)
        return pltpu.make_async_copy(act_any.at[span, :], act.at[span, :], sems_act.at[i])

    def product_stage():
        load(step).wait()
        products[pl.ds(step % 2, 1)] = dot_nn(act[rows_at(step), :], wd[...])[None]

    def norm_stage():
        span = rows_at(step - 1)
        g1, s1, bd, g2, s2 = (vec[j : j + 1, :] for j in range(1, 6))
        normed = normal_ref[...].astype(F32) * g1 + s1
        product = products[pl.ds((step + 1) % 2, 1)][0]
        normal2, scale2 = norm_parts(normed + (product + bd))
        res[span, :] = normal2 * g2 + s2
        cot = cot_ref[...].astype(F32)
        low = norm_back(cot, g2, normal2, scale2).astype(BF16)
        grads_all[span, :] = low
        for j, value in enumerate((cot * normal2, cot, low.astype(F32))):
            line = SUM_FFN + j
            small_ref[line : line + 1, :] += jnp.sum(value, axis=0, keepdims=True)
        for copy in stores(step - 1):
            copy.start()

    @pl.when(step == 0)
    def _():
        small_ref[...] = jnp.zeros_like(small_ref)
        copies = down_copies(down, rows, wd, sems)
        for copy in [load(0)] + copies + [load(j) for j in range(1, steps)]:
            copy.start()
        for copy in copies:
            copy.wait()
        product_stage()

    @pl.when((step > 0) & (step < steps))
    def _():
        product_stage()
        norm_stage()

    @pl.when(step == steps)
    def _():
        norm_stage()

    @pl.when(step > steps)
    def _():
        product_step = step - steps - 1
        height = send_ref.shape[1]
        sending = product_step < 2
        core = jnp.where(sending, 1 - where[1], where[1])
        half = jnp.where(product_step % 2 == 0, 1 - where[0], where[0])
        at_left = pl.ds(pl.multiple_of((2 * half + core) * height, LANES), height)
        value = dot_tn(act[:, at_left], grads_all[...]).astype(BF16)
        put_blocks(send_ref, keep_ref, sending, (0,), slice(None), (value,))

    @pl.when(step == steps + 4)
    def _():
        for i in range(steps):
            for copy in stores(i):
                copy.wait()


def feed_down(where, act, normal, cot, down, rows, vec):
    count = len(down)
    tokens, width = cot.shape
    wide = act.shape[1]
    steps = tokens // TILE
    height = wide // 4
    late = pl.BlockSpec((TILE, width), lambda s, *_: (jnp.clip(s - 1, 0, steps - 1), 0))
    shape = jax.ShapeDtypeStruct
    return pl.pallas_call(
        functools.partial(feed_down_kernel, count, steps),
        grid_spec=pltpu.PrefetchScalarGridSpec(
            num_scalar_prefetch=1,
            grid=(steps + 5,),
            in_specs=[SMEM, late, late, whole(*vec.shape)] + [ANY] * (1 + count),
            out_specs=[whole(SUM_ROWS, width)]
            + [send_spec(2, height, width, steps + 1), keep_spec(2, height, width, steps + 1)]
            + [ANY] * 2,
            scratch_shapes=[
                pltpu.VMEM((wide, width), BF16),
                pltpu.VMEM((tokens, wide), BF16),
                pltpu.VMEM((2, TILE, width), F32),
                pltpu.VMEM((tokens, width), F32),
                pltpu.VMEM((tokens, width), BF16),
                pltpu.SemaphoreType.DMA((SPLITS * (2 * count + 1),)),
                pltpu.SemaphoreType.DMA((steps,)),
                pltpu.SemaphoreType.DMA((2 * steps,)),
            ],
        ),
        out_shape=[shape((SUM_ROWS, width), F32)]
        + [shape((2, height, width), BF16)] * 2
        + [shape((tokens, width), F32), shape((tokens, width), BF16)],
        compiler_params=params(60),
        cost_estimate=LIGHT,
        name="feed_down",
    )(where, rows, normal, cot, vec, act, *down)


def feed_back_kernel(
    count, steps, where, rows, gd_ref, slope_ref, normal_ref, scale_ref, vec, sums_ref, ctx_any,
    *refs,
):
    own, pieces = refs[:2], refs[2 : 2 + count]
    down = refs[2 + count : 3 + 2 * count]
    small_ref, send_ref, keep_ref, ga_any, gc_any = refs[3 + 2 * count : 8 + 2 * count]
    (
        joined, wd, low, ctx, hidden_all, attended_all, grad_sums, gc, wide,
        sems, sems_down, sem_ctx, sems_out,
    ) = refs[8 + 2 * count :]
    tile, width = gd_ref.shape
    hidden = wide.shape[1]
    step = pl.program_id(0)
    load_ctx = pltpu.make_async_copy(ctx_any, ctx, sem_ctx.at[0])

    def rows_at(i):
        return pl.ds(pl.multiple_of(i * tile, tile), tile)

    def stores(i):
        span = rows_at(i)
        return [
            pltpu.make_async_copy(s.at[span, :], d.at[span, :], sems_out.at[j * steps + i])
            for j, (s, d) in enumerate(((attended_all, ga_any), (gc, gc_any)))
        ]

    def norm_stage():
        span = rows_at(step - 1)
        grad_normed = grad_sums[pl.ds((step + 1) % 2, 1)][0]
        normal = normal_ref[...].astype(F32)
        low[span, :] = (normal * vec[1:2, :] + vec[2:3, :]).astype(BF16)
        rounded = norm_back(grad_normed, vec[1:2, :], normal, scale_ref[...]).astype(BF16)
        attended_all[span, :] = rounded
        for j, value in enumerate((grad_normed * normal, grad_normed, rounded.astype(F32))):
            line = SUM_ATTN + j
            small_ref[line : line + 1, :] += jnp.sum(value, axis=0, keepdims=True)
        gc[span, :] = dot_nt(rounded, joined[:, :width]).astype(BF16)

    def wide_stage(waiting, between):
        span = rows_at(step)
        chunks = list(range(0, hidden, CHUNK))

        def product(c):
            return dot_nt(gd_ref[...], wd[c : c + CHUNK, :])

        ahead = product(0)
        for copy in waiting:
            copy.wait()
        total = gd_ref[...].astype(F32)
        for n, c in enumerate(chunks):
            grad_active = ahead
            if n + 1 < len(chunks):
                ahead = product(chunks[n + 1])
            rounded = (grad_active * slope_ref[:, c : c + CHUNK].astype(F32)).astype(BF16)
            hidden_all[span, c : c + CHUNK] = rounded
            wide[0:1, c : c + CHUNK] += jnp.sum(rounded.astype(F32), axis=0, keepdims=True)
            total = total + dot_nt(rounded, joined[:, width + c : width + c + CHUNK])
            if n == 1:
                between()
        grad_sums[pl.ds(step % 2, 1)] = total[None]

    @pl.when(step == 0)
    def _():
        copies = down_copies(down, rows, wd, sems_down)
        later = joined_copies(own, pieces, rows, joined, sems)
        for copy in copies + later + [load_ctx]:
            copy.start()
        small_ref[...] = sums_ref[...]
        wide[...] = jnp.zeros_like(wide)
        for copy in copies:
            copy.wait()
        wide_stage(later, lambda: None)

    @pl.when((step > 0) & (step < steps))
    def _():
        wide_stage([], norm_stage)

    @pl.when(step == steps)
    def _():
        norm_stage()
        for j in range(hidden // width):
            line = SUM_UP + j
            small_ref[line : line + 1, :] = wide[0:1, j * width : (j + 1) * width]
        load_ctx.wait()

    @pl.when((step > 0) & (step <= steps))
    def _():
        for copy in stores(step - 1):
            copy.start()

    @pl.when(step > steps)
    def _():
        sending = step == steps + 1
        core = jnp.where(sending, 1 - where[1], where[1])
        height, cut = width // 2, hidden // 2
        at_wide = pl.ds(pl.multiple_of(core * cut, LANES), cut)
        at_narrow = pl.ds(pl.multiple_of(core * height, LANES), height)
        slots = (jnp.where(where[0] == 0, 1, 0), jnp.where(where[0] == 0, 0, 1))
        value = dot_tn(low[...], hidden_all[:, at_wide]).astype(BF16)
        put_blocks(
            send_ref, keep_ref, sending, slots, slice(0, cut), (value[:height], value[height:])
        )
        value = dot_tn(ctx[...], attended_all[:, at_narrow]).astype(BF16)
        put_blocks(
            send_ref, keep_ref, sending, slots, slice(cut, cut + height),
            (value[:height], value[height:]),
        )

    @pl.when(step == steps + 2)
    def _():
        for i in range(steps):
            for copy in stores(i):
                copy.wait()


def feed_back(where, gd, slope, normal, scale, joined, down, vec, context, sums):
    own, pieces, rows = joined
    count = len(pieces)
    tokens, width = gd.shape
    wide = slope.shape[1]
    steps = tokens // TILE
    total = (wide + width) // 2

    def now(columns):
        return pl.BlockSpec((TILE, columns), lambda s, *_: (jnp.minimum(s, steps - 1), 0))

    def late(columns):
        return pl.BlockSpec((TILE, columns), lambda s, *_: (jnp.clip(s - 1, 0, steps - 1), 0))

    shape = jax.ShapeDtypeStruct
    return pl.pallas_call(
        functools.partial(feed_back_kernel, count, steps),
        grid_spec=pltpu.PrefetchScalarGridSpec(
            num_scalar_prefetch=1,
            grid=(steps + 3,),
            in_specs=[SMEM, now(width), now(wide), late(width), late(1)]
            + [whole(*vec.shape), whole(*sums.shape)]
            + [ANY] * (4 + 2 * count),
            out_specs=[whole(*sums.shape)]
            + [send_spec(1, width // 2, total, steps + 1)]
            + [keep_spec(1, width // 2, total, steps + 1)]
            + [ANY] * 2,
            scratch_shapes=[
                pltpu.VMEM((width, width + wide), BF16),
                pltpu.VMEM((wide, width), BF16),
                pltpu.VMEM((tokens, width), BF16),
                pltpu.VMEM((tokens, width), BF16),
                pltpu.VMEM((tokens, wide), BF16),
                pltpu.VMEM((tokens, width), BF16),
                pltpu.VMEM((2, TILE, width), F32),
                pltpu.VMEM((tokens, width), BF16),
                pltpu.VMEM((8, wide), F32),
                pltpu.SemaphoreType.DMA((SPLITS * (2 + 2 * count),)),
                pltpu.SemaphoreType.DMA((SPLITS * (1 + 2 * count),)),
                pltpu.SemaphoreType.DMA((1,)),
                pltpu.SemaphoreType.DMA((2 * steps,)),
            ],
        ),
        out_shape=[shape(sums.shape, F32)]
        + [shape((2, width // 2, total), BF16)] * 2
        + [shape((tokens, width), BF16)] * 2,
        compiler_params=params(60),
        cost_estimate=LIGHT,
        name="feed_back",
    )(where, rows, gd, slope, normal, scale, vec, sums, context, *own, *pieces, *down)


def inputs_back_kernel(count, rows, ga_ref, grads, *refs):
    own, pieces = refs[:3], refs[3 : 3 + count]
    out_ref, full, sems = refs[3 + count :]

    @pl.when(pl.program_id(0) == 0)
    def _():
        fetch_joined(own, pieces, rows, full, sems)

    out_ref[...] = ga_ref[...].astype(F32) + dot_nt(grads[...], full[...])


def inputs_back(grads, ga, weights):
    own, pieces, rows = weights
    tokens, width = ga.shape
    tile = pl.BlockSpec((TILE, width), lambda t: (t, 0))
    return pl.pallas_call(
        functools.partial(inputs_back_kernel, len(pieces)),
        grid=(tokens // TILE,),
        in_specs=[SMEM, tile, pl.BlockSpec((TILE, 3 * width), lambda t: (t, 0))]
        + [ANY] * (3 + len(pieces)),
        out_specs=tile,
        out_shape=jax.ShapeDtypeStruct((tokens, width), F32),
        scratch_shapes=[
            pltpu.VMEM((width, 3 * width), BF16),
            pltpu.SemaphoreType.DMA((SPLITS * (3 + 2 * len(pieces)),)),
        ],
        compiler_params=params(60),
        cost_estimate=LIGHT,
        name="inputs_back",
    )(rows, ga, grads, *own, *pieces)


CORE, NEAR_Y, NEAR_Z, FAR_Z = 1, 2, 4, 8


def after(value, *others):
    return lax.optimization_barrier((value,) + others)[0]


def swap_dp(values, bit):
    size = lax.axis_size("dp")
    return lax.ppermute(values, "dp", [(i, i ^ bit) for i in range(size)])


def swap_fsdp(values):
    return lax.ppermute(values, "fsdp", [(0, 1), (1, 0)])


def swap_both(values):
    size = lax.axis_size("dp")
    pairs = [(2 * i + h, 2 * (i ^ NEAR_Y) + 1 - h) for i in range(size) for h in range(2)]
    return lax.ppermute(values, ("dp", "fsdp"), pairs)


def rows_of(values, start, count):
    return lax.dynamic_slice_in_dim(values, start, count, axis=0)


def own_part(shards, place):
    half, core, y, z = place
    height = shards[0].shape[0]
    count = height // 8
    starts = (2 * y + core) * count, height // 2 + (2 * z + core) * count
    return jnp.concatenate(
        [jnp.concatenate([rows_of(s, start, count) for s in shards], axis=1) for start in starts],
        axis=0,
    )


def far_parts(first):
    count = first.shape[0] // 2
    return swap_dp(first[:count], NEAR_Y), swap_dp(first[count:], NEAR_Z)


def all_parts(first, far):
    here = (first,) + far
    return here + tuple(swap_dp(part, CORE) for part in here)


def piece_rows(height, place):
    half, core, y, z = place
    count = height // 8
    base = (1 - half) * height
    rows = [half * height]
    for c in (core, 1 - core):
        rows += [
            base + (2 * y + c) * count,
            base + height // 2 + (2 * z + c) * count,
            base + (2 * (1 - y) + c) * count,
            base + height // 2 + (2 * (1 - z) + c) * count,
        ]
    return jnp.stack(rows).astype(jnp.int32)


class Part:
    def __init__(self, terms, place, columns=None):
        self.bits = {0: 1, 1: place[2], 2: place[3]}
        self.swaps = {
            0: swap_fsdp,
            1: lambda v: swap_dp(v, NEAR_Y),
            2: lambda v: swap_dp(v, NEAR_Z),
            3: lambda v: swap_dp(v, FAR_Z),
        }
        self.terms = [t.reshape(2, 2, 2, t.shape[1] // 4, t.shape[2]) for t in terms]
        self.views = [(columns, ())] * len(terms)
        self.flight, self.joined = [], None

    def total(self, *picks):
        value = None
        for term, (columns, before) in zip(self.terms, self.views):
            if columns is not None:
                term = term[..., columns[0] : columns[1]]
            for axis, index in before + picks:
                term = lax.dynamic_slice_in_dim(term, index, 1, axis)
            term = term.astype(F32)
            value = term if value is None else value + term
        return value.astype(BF16)

    def cut(self, *picks):
        self.views = [(columns, before + picks) for columns, before in self.views]

    def halve(self, axis):
        bit = self.bits[axis]
        self.flight, self.route = [self.total((axis, 1 - bit))], [self.swaps[axis]]
        self.cut((axis, bit))

    def both(self):
        bit = self.bits[1]
        self.flight = [
            self.total((0, 0), (1, bit)),
            self.total((0, 1), (1, 1 - bit)),
            self.total((0, 0), (1, 1 - bit)),
        ]
        self.route = [self.swaps[0], self.swaps[1], swap_both]
        self.cut((0, 1), (1, bit))

    def merge(self, *others):
        value = jnp.concatenate([part.total() for part in (self,) + others], axis=-1)
        self.terms, self.views = [value], [(None, ())]

    def split(self, cut):
        other = copy.copy(self)
        end = self.terms[0].shape[-1]
        self.views = [((0, cut), before) for _, before in self.views]
        other.views = [((cut, end), before) for _, before in other.views]
        return other

    def send_whole(self, swap, reshape=None):
        value = self.terms[0]
        if len(self.terms) > 1 or self.views[0][0] is not None:
            value = self.total()
        if reshape:
            value = value.reshape(-1, value.shape[-1])
        self.flight, self.route = [value], [lambda v: (v, swap(v))]
        self.terms, self.views = [], []

    def far(self):
        self.send_whole(self.swaps[3])

    def join(self, axis):
        self.send_whole(self.swaps[axis])
        self.joined = axis

    def finish(self):
        self.send_whole(lambda v: swap_dp(v, CORE), True)

    def land(self):
        for sent, route in zip(self.flight, self.route):
            got = route(sent)
            self.terms += list(got) if isinstance(got, tuple) else [got]
        self.views = self.views + [(None, ())] * (len(self.terms) - len(self.views))
        self.flight = []

    def settle(self):
        if self.joined is None:
            return
        mine, other = self.terms
        axis, self.joined = self.joined, None
        value = jnp.where(
            self.bits[axis] == 0,
            jnp.concatenate([mine, other], axis=axis),
            jnp.concatenate([other, mine], axis=axis),
        )
        self.terms, self.views = [value], [(None, ())]


def fence(parts, *arrays):
    counts = [(len(p.terms), len(p.flight)) for p in parts]
    flat = [a for p in parts for a in p.terms + p.flight] + list(arrays)
    flat = list(lax.optimization_barrier(tuple(flat)))
    for part, (terms, flight) in zip(parts, counts):
        part.terms, flat = flat[:terms], flat[terms:]
        part.flight, flat = flat[:flight], flat[flight:]
    return flat


def widen(mine, other, core, axis):
    low = jnp.where(core == 0, mine, other).astype(F32)
    high = jnp.where(core == 0, other, mine).astype(F32)
    return jnp.concatenate([low, high], axis=axis)


def gather_all(values):
    return lax.all_gather(values, "fsdp", axis=0, tiled=True)


def sum_plain(send, keep, by_rows):
    blocks = [[keep[1], send[1]], [keep[0], send[0]]]
    axis = 0 if by_rows else 1
    value = jnp.concatenate([jnp.concatenate(pair, axis=axis) for pair in blocks], axis=0)
    own = lax.psum_scatter(value, "fsdp", scatter_dimension=0, tiled=True)
    return lax.psum(own, "dp").astype(F32)


def local(
    inputs, segment_ids, cotangent, w_query, b_query, w_key, b_key, w_value, b_value,
    w_output, b_output, gain_attn, bias_attn, w_up, b_up, w_down, b_down, gain_ffn, bias_ffn,
):
    rows, length = segment_ids.shape
    width = inputs.shape[1]
    shards = lax.axis_size("fsdp")
    paired = shards == 2 and lax.axis_size("dp") == 16
    half = lax.axis_index("fsdp")
    dp = lax.axis_index("dp")
    place = (half, dp % 2, dp // 2 % 2, dp // 4 % 2)
    core = place[1]
    vectors = (b_query, b_key, b_value, b_output, gain_attn, bias_attn, b_down, gain_ffn, bias_ffn)
    height = w_query.shape[0]
    if paired:
        where = jnp.stack([half, core]).astype(jnp.int32)
        part_qkv = own_part((w_query, w_key, w_value), place)
        part_up = own_part((w_output, w_up), place)
        here_qkv = swap_fsdp(part_qkv)
        part_down = own_part((after(w_down, here_qkv),), place)
        cosine, sine, turned = rotary_tables(segment_ids, after(inputs, here_qkv))
        lines = jnp.concatenate(vectors + (b_up,)).reshape(-1, height)
        other = swap_fsdp(after(lines, part_qkv))
        here_up = swap_fsdp(after(part_up, part_qkv))
        at = piece_rows(height, place)
        joined_qkv = ((w_query, w_key, w_value), all_parts(here_qkv, far_parts(here_qkv)), at)
        lines = jnp.where(half == 0, jnp.stack([lines, other]), jnp.stack([other, lines]))
    else:
        cosine, sine, turned = rotary_tables(segment_ids, inputs)
        where = jnp.zeros((2,), jnp.int32)
        at = jnp.zeros((1,), jnp.int32)
        joined_qkv = (tuple(gather_all(w) for w in (w_query, w_key, w_value)), (), at)
        joined_up = ((gather_all(w_output), gather_all(w_up)), (), at)
        down = (gather_all(w_down),)
        lines = jnp.concatenate(vectors + (b_up,)).reshape(-1, height)
        lines = lax.all_gather(lines, "fsdp", axis=0)
    lines = lines.astype(F32)
    vec = jnp.swapaxes(lines[:, :9], 0, 1).reshape(9, width)
    bias_up = lines[:, 9:].reshape(1, -1)

    q, k, v = project(inputs, joined_qkv, vec[:3], cosine, sine)
    vec = vec[3:]
    if paired:
        q, here_up, part_down, vec, bias_up = lax.optimization_barrier(
            (q, here_up, part_down, vec, bias_up)
        )
        here_down = swap_fsdp(part_down)
        far_up = far_parts(here_up)
    context, probs = attend(q, k, v, segment_ids)
    if paired:
        context, probs, here_up, here_down, far_up = lax.optimization_barrier(
            (context, probs, here_up, here_down, far_up)
        )
        joined_up = ((w_output, w_up), all_parts(here_up, far_up), at)
        far_down = far_parts(here_down)
    normal, scale, act, slope = feed_up(context, inputs, joined_up, vec, bias_up)
    if paired:
        act, slope, here_down, far_down = lax.optimization_barrier(
            (act, slope, here_down, far_down)
        )
        down = (w_down,) + all_parts(here_down, far_down)
    sums, send, keep, result, grad_down = feed_down(
        where, act, normal, cotangent, down, at, vec
    )
    sent = [(send, keep)]
    if paired:
        sum_d = Part([keep, swap_dp(send, CORE)], place)
        sum_d.both()
        (grad_down,) = fence([sum_d], grad_down)
    outs = feed_back(
        where, grad_down, slope, normal, scale, joined_up, down, vec, context, sums
    )
    sent.append(outs[1:3])
    if paired:
        sum_d.land()
        outs = fence([sum_d], *outs)
    sums, send, keep, grad_attended, grad_context = outs
    if paired:
        sum_d.merge()
        sum_u = Part([keep, swap_dp(send, CORE)], place)
        sum_d.halve(2)
        sum_u.both()
        parts = [sum_d, sum_u]
        (grad_context,) = fence(parts, grad_context)
    tables = (probs, cosine, sine, turned)
    made = None
    if rows > 1:
        sums, made = attend_back(where, q, k, v, grad_context, *tables, sums, 0)
        if paired:
            sum_d.land()
            sums, made, grad_context = fence([sum_d], sums, made, grad_context)
            sum_d.far()
            sums, grad_context = fence([sum_d], sums, grad_context)
    outs = attend_back(where, q, k, v, grad_context, *tables, sums, rows - 1, made)
    sent.append(outs[1:3])
    if paired:
        for p in parts:
            p.land()
        outs = fence(parts, *outs)
    sums, send, keep, grads = outs
    if paired:
        sum_q = Part([keep, swap_dp(send, CORE)], place)
        sum_u.merge()
        sum_d.join(2) if rows > 1 else sum_d.far()
        sum_u.halve(2)
        sum_q.both()
        parts = [sum_d, sum_u, sum_q]
        (grad_attended,) = fence(parts, grad_attended)
    grad_inputs = inputs_back(grads, grad_attended, joined_qkv)
    if paired:
        for p in parts:
            p.land()
        (grad_inputs,) = fence(parts, grad_inputs)
        last = grad_inputs

        def step(part, name, *axis):
            nonlocal last
            (last,) = fence([part], last)
            part.settle()
            getattr(part, name)(*axis)
            (last,) = fence([part], last)
            last = part.flight[0]
            part.land()

        if rows == 1:
            step(sum_d, "join", 2)
        step(sum_u, "far")
        sum_q.merge()
        step(sum_q, "halve", 2)
        step(sum_d, "join", 1)
        step(sum_q, "far")
        cut_u, cut_q = ((p.terms[0].shape[-1] // 2 + 64) // LANES * LANES for p in (sum_u, sum_q))
        (last,) = fence([sum_u], last)
        sum_v = sum_u.split(cut_u)
        step(sum_u, "join", 2)
        step(sum_v, "join", 1)
        step(sum_d, "finish")
        gwd = widen(*sum_d.terms, core, 0)
        (last,) = fence([sum_q], last)
        sum_r = sum_q.split(cut_q)
        step(sum_q, "join", 2)
        step(sum_r, "join", 1)
        step(sum_u, "join", 1)
        step(sum_v, "join", 2)
        (gwd,) = fence([sum_q, sum_r], gwd)
        step(sum_q, "join", 1)
        step(sum_r, "join", 2)
        for part in (sum_u, sum_v):
            part.settle()
            part.finish()
        fence([sum_u, sum_v, sum_q, sum_r])
        sum_u.land()
        sum_v.land()
        for part in (sum_q, sum_r):
            part.settle()
            part.finish()
            part.land()
    else:
        sums = lax.psum(sums, ("dp", "fsdp"))

    wide = b_up.shape[0] * shards
    if paired:
        mine, other = (
            jnp.concatenate([a, b], axis=1) for a, b in zip(sum_u.terms, sum_v.terms)
        )
        cut = wide // 2
        gwu = widen(mine[:, :cut], other[:, :cut], core, 1)
        gwo = widen(mine[:, cut:], other[:, cut:], core, 1)
        mine, other = (
            jnp.concatenate([a, b], axis=1) for a, b in zip(sum_q.terms, sum_r.terms)
        )
        gwq, gwk, gwv = (
            widen(*(end[:, i * width : (i + 1) * width] for end in (mine, other)), core, 0)
            for i in range(3)
        )
        count = height // LANES
        packed = jnp.where(core == 0, mine[:, 3 * width :], other[:, 3 * width :])
        packed = packed[: len(LINES) * count + wide // 2 // LANES].astype(F32)
        vectors = [packed[i * count : (i + 1) * count].reshape(-1) for i in range(len(LINES))]
        gbu = packed[len(LINES) * count :].reshape(-1)
        ggf, gbf, gbd, gga, gba, gbo, gbq, gbk, gbv = vectors
    else:

        def own(line, count=1):
            start = line * width + half * (count * width // shards)
            return lax.dynamic_slice_in_dim(
                sums.reshape(-1), start, count * width // shards, axis=0
            )

        ggf, gbf, gbd, gga, gba, gbo, gbq, gbk, gbv = (own(line) for line in LINES)
        gbu = own(SUM_UP, wide // width)
        gwd = sum_plain(*sent[0], True)
        both = sum_plain(*sent[1], False).reshape(height, 2, -1)
        cut = wide // 2
        gwu = both[..., :cut].reshape(height, -1)
        gwo = both[..., cut:].reshape(height, -1)
        both = sum_plain(*sent[2], True)
        gwq, gwk, gwv = (both[:, i * width : (i + 1) * width] for i in range(3))
    return (
        result, grad_inputs, gwq, gbq, gwk, gbk, gwv, gbv, gwo, gbo, gga, gba,
        gwu, gbu, gwd, gbd, ggf, gbf,
    )


def solution(mesh):
    tokens, matrix, vector = P(("dp", "fsdp"), None), P("fsdp", None), P("fsdp")
    weights = (
        matrix, vector, matrix, vector, matrix, vector, matrix, vector, vector, vector,
        matrix, vector, matrix, vector, vector, vector,
    )
    return jax.shard_map(
        local,
        mesh=mesh,
        in_specs=(tokens,) * 3 + weights,
        out_specs=(tokens,) * 2 + weights,
        check_vma=False,
    )
```

```python
import copy
import functools
import jax
import jax.numpy as jnp
from jax import lax
from jax.experimental import pallas as pl
from jax.experimental.pallas import tpu as pltpu
from jax.sharding import PartitionSpec as P

HEAD = 64
GROUP = 3
EPSILON = 1e-06
LANES = 128
TILE = 256
CHUNK = 512
MASKED = -1e30
SUM_FFN, SUM_ATTN, SUM_UP, SUM_QKV, SUM_ROWS = 0, 3, 6, 10, 16
F32 = jnp.float32
BF16 = jnp.bfloat16


def params(mebibytes):
    return pltpu.CompilerParams(vmem_limit_bytes=mebibytes * 1024 * 1024)


LIGHT = pl.CostEstimate(flops=1000, bytes_accessed=1000, transcendentals=0)


def dot_nn(left, right):
    return lax.dot_general(left, right, (((1,), (0,)), ((), ())), preferred_element_type=F32)


def dot_nt(left, right):
    return lax.dot_general(left, right, (((1,), (1,)), ((), ())), preferred_element_type=F32)


def dot_tn(left, right):
    return lax.dot_general(left, right, (((0,), (0,)), ((), ())), preferred_element_type=F32)


def whole(*shape):
    return pl.BlockSpec(shape, lambda *_: (0,) * len(shape))


SPLITS = 4


def piece_copies(pieces, starts, full, column, sems, first):
    copies = []
    assert len(pieces) == len(starts)
    for i, (piece, start) in enumerate(zip(pieces, starts)):
        height, width = piece.shape
        splits = SPLITS if height * width >= 500_000 and height % (16 * SPLITS) == 0 else 1
        count = height // splits
        for j in range(splits):
            row = pl.multiple_of(start + j * count, 16)
            copies.append(
                pltpu.make_async_copy(
                    piece.at[pl.ds(j * count, count), :],
                    full.at[pl.ds(row, count), column : column + width],
                    sems.at[SPLITS * (first + i) + j],
                )
            )
    return copies


def cut_pieces(pieces):
    cut = []
    for i, piece in enumerate(pieces):
        count = piece.shape[0] // 2
        cut += [piece.at[:count, :], piece.at[count:, :]] if i % 3 == 0 else [piece]
    return cut


def joined_copies(own, pieces, rows, full, sems, cut=None):
    pieces = cut_pieces(pieces)
    shards, column = [], 0
    for i, shard in enumerate(own):
        shards.append(piece_copies([shard], [rows[0]], full, column, sems, i))
        column += shard.shape[1]
    starts = [rows[1 + i] for i in range(len(pieces))]
    first = len(own)
    if cut is None:
        return sum(shards, []) + piece_copies(pieces, starts, full, 0, sems, first)
    left = [piece.at[:, :cut] for piece in pieces]
    right = [piece.at[:, cut:] for piece in pieces]
    return (
        shards[0] + piece_copies(left, starts, full, 0, sems, first),
        sum(shards[1:], []) + piece_copies(right, starts, full, cut, sems, first + len(pieces)),
    )


def fetch_joined(own, pieces, rows, full, sems):
    copies = joined_copies(own, pieces, rows, full, sems)
    for copy in copies:
        copy.start()
    for copy in copies:
        copy.wait()


ANY = pl.BlockSpec(memory_space=pl.ANY)
SMEM = pl.BlockSpec(memory_space=pltpu.SMEM)


def tables_kernel(seg_row, seg_col, x_ref, cos_ref, sin_ref, turned_ref):
    length = seg_row.shape[-1]
    key = lax.broadcasted_iota(jnp.int32, (length, length), 1)
    query = lax.broadcasted_iota(jnp.int32, (length, length), 0)
    earlier = (seg_col[...] == seg_row[0]) & (key < query)
    place = jnp.sum(earlier.astype(F32), axis=1, keepdims=True)
    lane = lax.broadcasted_iota(jnp.int32, (1, LANES), 1)
    paired = (lane % HEAD // 2 * 2).astype(F32)
    freqs = jnp.exp(-jnp.log(F32(10000.0)) * paired / HEAD)
    angle = place * freqs
    cos_ref[...] = jnp.cos(angle)
    sine = jnp.sin(angle)
    sin_ref[...] = jnp.where(lane % 2 == 0, -sine, sine)
    turned_ref[...] = x_ref[...].T


def rotary_tables(segments, x):
    rows, length = segments.shape
    width = x.shape[1]
    return pl.pallas_call(
        tables_kernel,
        grid=(rows,),
        in_specs=[
            pl.BlockSpec((1, 1, length), lambda r: (r, 0, 0)),
            pl.BlockSpec((length, 1), lambda r: (r, 0)),
            pl.BlockSpec((length, width), lambda r: (r, 0)),
        ],
        out_specs=[pl.BlockSpec((length, LANES), lambda r: (r, 0))] * 2
        + [pl.BlockSpec((width, length), lambda r: (0, r))],
        out_shape=[jax.ShapeDtypeStruct((rows * length, LANES), F32)] * 2
        + [jax.ShapeDtypeStruct((width, rows * length), BF16)],
        compiler_params=params(60),
        cost_estimate=LIGHT,
        name="rotary_tables",
    )(segments.reshape(rows, 1, length), segments.reshape(rows * length, 1), x)


def pair_swap(values):
    even = lax.broadcasted_iota(jnp.int32, values.shape, 1) % 2 == 0
    return jnp.where(
        even, pltpu.roll(values, LANES - 1, axis=1), pltpu.roll(values, 1, axis=1)
    )


def project_kernel(count, rows, x_ref, bias, cos_ref, sin_ref, *refs):
    own, pieces = refs[:3], refs[3 : 3 + count]
    q_ref, k_ref, v_ref, full, sems = refs[3 + count :]
    width = x_ref.shape[1]

    @pl.when(pl.program_id(0) == 0)
    def _():
        fetch_joined(own, pieces, rows, full, sems)

    x = x_ref[...]
    cosine, sine = cos_ref[...], sin_ref[...]
    step = 2 * LANES
    for i, out in enumerate((q_ref, k_ref, v_ref)):
        for c in range(0, width, step):
            lin = dot_nn(x, full[:, i * width + c : i * width + c + step])
            lin = lin + bias[i : i + 1, c : c + step]
            if i < 2:
                parts = []
                for d in range(0, step, LANES):
                    part = lin[:, d : d + LANES]
                    part = part * cosine + pair_swap(part) * sine
                    parts.append(part)
                lin = jnp.concatenate(parts, axis=1)
            if i == 0:
                out[:, c : c + step] = (lin.astype(BF16).astype(F32) * 0.125).astype(BF16)
            else:
                out[:, c : c + step] = lin.astype(BF16)


def project(x, weights, bias, cosine, sine):
    own, pieces, rows = weights
    tokens, width = x.shape
    tile = pl.BlockSpec((TILE, width), lambda t: (t, 0))
    table = pl.BlockSpec((TILE, LANES), lambda t: (t, 0))
    return pl.pallas_call(
        functools.partial(project_kernel, len(pieces)),
        grid=(tokens // TILE,),
        in_specs=[SMEM, tile, whole(*bias.shape), table, table] + [ANY] * (3 + len(pieces)),
        out_specs=[tile] * 3,
        out_shape=[jax.ShapeDtypeStruct((tokens, width), BF16)] * 3,
        scratch_shapes=[
            pltpu.VMEM((width, 3 * width), BF16),
            pltpu.SemaphoreType.DMA((SPLITS * (3 + 2 * len(pieces)),)),
        ],
        compiler_params=params(60),
        cost_estimate=LIGHT,
        name="project",
    )(rows, x, bias, cosine, sine, *own, *pieces)


def spans(length):
    found, offset = [], 0
    for first in range(0, length, LANES):
        low, high = max(first - LANES, 0), min(first + 2 * LANES, length)
        found.append((slice(first, first + LANES), slice(low, high), slice(offset, offset + high - low)))
        offset += high - low
    return found, offset


def split_heads(values):
    lane = lax.broadcasted_iota(jnp.int32, (1, LANES), 1)
    return [jnp.where(lane // HEAD == h, values, jnp.zeros_like(values)) for h in range(2)]


def stack_heads(heads, rows):
    return jnp.concatenate([head[rows, :] for head in heads], axis=0)


def merge_heads(stacked):
    lane = lax.broadcasted_iota(jnp.int32, (1, LANES), 1)
    half = stacked.shape[0] // 2
    return jnp.where(lane < HEAD, stacked[:half], stacked[half:])


def attend_kernel(q_ref, k_ref, v_ref, seg_row, seg_col, ctx_ref, prob_ref, bias):
    blocks, _ = spans(q_ref.shape[0])

    @pl.when(pl.program_id(1) == 0)
    def _():
        for own, span, at in blocks:
            bias[at, :] = jnp.where(seg_col[span, :] == seg_row[0, :, own], 0.0, MASKED)

    pairs = [slice(p * LANES, (p + 1) * LANES) for p in range(GROUP)]
    units = [(p, lanes) + block for p, lanes in enumerate(pairs) for block in blocks]
    queries = [split_heads(q_ref[:, lanes]) for lanes in pairs]

    def product(unit):
        p, lanes, own, span, _ = unit
        return dot_nt(k_ref[span, lanes], stack_heads(queries[p], own))

    def soften(unit, scores):
        at = unit[-1]
        heads = []
        for h in range(2):
            masked = scores[:, h * LANES : (h + 1) * LANES] + bias[at, :]
            peak = jnp.max(masked, axis=0, keepdims=True)
            expo = jnp.exp(masked - peak)
            total = jnp.sum(expo, axis=0, keepdims=True)
            heads.append((expo * (1.0 / total)).astype(BF16))
        return jnp.concatenate(heads, axis=1)

    def finish(unit, probs):
        p, lanes, own, span, at = unit
        prob_ref[0, p, at, :] = probs
        ctx_ref[own, lanes] = merge_heads(dot_tn(probs, v_ref[span, lanes])).astype(BF16)

    count = len(blocks)
    scores = [product(unit) for unit in units[:count]]
    waiting = []
    for p in range(GROUP):
        now = units[p * count : (p + 1) * count]
        probs = [soften(unit, value) for unit, value in zip(now, scores)]
        scores = [product(unit) for unit in units[(p + 1) * count : (p + 2) * count]]
        for unit, value in waiting:
            finish(unit, value)
        waiting = list(zip(now, probs))
    for unit, value in waiting:
        finish(unit, value)


def attend(q, k, v, segments):
    rows, length = segments.shape
    tokens, width = q.shape
    pairs = width // LANES
    wide = GROUP * LANES
    _, depth = spans(length)
    head = pl.BlockSpec((length, wide), lambda r, p: (r, p))
    return pl.pallas_call(
        attend_kernel,
        grid=(rows, pairs // GROUP),
        in_specs=[head] * 3
        + [
            pl.BlockSpec((1, 1, length), lambda r, p: (r, 0, 0)),
            pl.BlockSpec((length, 1), lambda r, p: (r, 0)),
        ],
        out_specs=[
            head,
            pl.BlockSpec((1, GROUP, depth, 2 * LANES), lambda r, p: (r, p, 0, 0)),
        ],
        out_shape=[
            jax.ShapeDtypeStruct((tokens, width), BF16),
            jax.ShapeDtypeStruct((rows, pairs, depth, 2 * LANES), BF16),
        ],
        scratch_shapes=[pltpu.VMEM((depth, LANES), F32)],
        compiler_params=params(60),
        cost_estimate=LIGHT,
        name="attend",
    )(q, k, v, segments.reshape(rows, 1, length), segments.reshape(tokens, 1))


def send_spec(steps, height, width, first):
    return pl.BlockSpec(
        (2 // steps, height, width), lambda s, *_: (jnp.clip(s - first, 0, steps - 1), 0, 0)
    )


def keep_spec(steps, height, width, first):
    return pl.BlockSpec(
        (2 // steps, height, width), lambda s, *_: (jnp.clip(s - first - steps, 0, steps - 1), 0, 0)
    )


def put_blocks(send_ref, keep_ref, sending, slots, columns, values):
    @pl.when(sending)
    def _():
        for slot, value in zip(slots, values):
            send_ref[slot, :, columns] = value

    @pl.when(jnp.logical_not(sending))
    def _():
        for slot, value in zip(slots, values):
            keep_ref[slot, :, columns] = value


LINES = (SUM_FFN, SUM_FFN + 1, SUM_FFN + 2, SUM_ATTN, SUM_ATTN + 1, SUM_ATTN + 2) + (
    SUM_QKV, SUM_QKV + 1, SUM_QKV + 2,
)


def pack_vectors(small_ref, packed, half):
    width = small_ref.shape[1]
    part = width // 2 // LANES
    packed[...] = jnp.zeros_like(packed)
    for i, line in enumerate(LINES):
        for j in range(part):
            lanes = pl.ds(pl.multiple_of(half * (width // 2) + j * LANES, LANES), LANES)
            packed[i * part + j : i * part + j + 1, :] = small_ref[line : line + 1, lanes]
    base, count = len(LINES) * part, width // LANES
    lines = (SUM_QKV - SUM_UP) // 2
    for i in range(lines):
        for j in range(count):
            row = base + i * count + j
            lanes = slice(j * LANES, (j + 1) * LANES)
            low, high = (small_ref[SUM_UP + n : SUM_UP + n + 1, lanes] for n in (i, lines + i))
            packed[row : row + 1, :] = jnp.where(half == 0, low, high)


def attend_back_kernel(
    rows, before, last, where, q_ref, k_ref, v_ref, g_ref, prob_ref, cos_ref, sin_ref, sums_ref,
    *refs,
):
    if last:
        (
            turned_any, *made_any, small_ref, send_ref, keep_ref, out_any,
            acc_k, acc_v, grads_all, turned, packed, sems,
        ) = refs
    else:
        small_ref, out_any, acc_k, acc_v, grads_all, sems = refs
    step = pl.program_id(0)
    length, width = q_ref.shape[0], small_ref.shape[1]
    pairs = width // LANES
    units = rows * pairs // GROUP
    hand_on = pltpu.make_async_copy(grads_all, out_any, sems.at[0])
    loads = []
    if last:
        loads.append(pltpu.make_async_copy(turned_any, turned, sems.at[1]))
        if before:
            target = grads_all.at[pl.ds(0, before * length), :]
            loads.append(pltpu.make_async_copy(made_any[0], target, sems.at[2]))

    @pl.when(step == 0)
    def _():
        for load in loads:
            load.start()
        small_ref[...] = sums_ref[...]

    @pl.when(step < units)
    def _():
        blocks, _ = spans(length)
        groups = pairs // GROUP
        row, group = before * last + step // groups, step % groups
        at_rows = pl.ds(pl.multiple_of(row * length, length), length)
        lanes_of = [slice(p * LANES, (p + 1) * LANES) for p in range(GROUP)]

        def turn_back(values, rows):
            return values * cos_ref[rows, :] - pair_swap(values) * sin_ref[rows, :]

        def first(p):
            grads = split_heads(g_ref[:, lanes_of[p]])
            return [
                dot_nt(v_ref[span, lanes_of[p]], stack_heads(grads, own)) for own, span, _ in blocks
            ]

        def second(p, grad_probs):
            made = []
            for (own, span, at), pair in zip(blocks, grad_probs):
                heads = []
                for h in range(2):
                    columns = slice(h * LANES, (h + 1) * LANES)
                    probs = prob_ref[0, p, at, columns].astype(F32)
                    inner = jnp.sum(probs * pair[:, columns], axis=0, keepdims=True)
                    heads.append((probs * (pair[:, columns] - inner)).astype(BF16))
                made.append(jnp.concatenate(heads, axis=1))
            return made

        def third(p, grad_scores):
            lanes = lanes_of[p]
            queries, grads = split_heads(q_ref[:, lanes]), split_heads(g_ref[:, lanes])
            k_t = k_ref[:, lanes].T
            acc_k[p] = jnp.zeros_like(acc_k[p])
            acc_v[p] = jnp.zeros_like(acc_v[p])
            turned_parts = []
            for (own, span, at), low in zip(blocks, grad_scores):
                acc_k[p, span, :] += dot_nn(low, stack_heads(queries, own))
                acc_v[p, span, :] += dot_nn(prob_ref[0, p, at, :], stack_heads(grads, own))
                product = dot_nn(k_t[:, span], low)
                both = jnp.concatenate([product[:HEAD, :LANES], product[HEAD:, LANES:]], axis=0)
                turned_parts.append(both.T)
            return turned_parts

        def fourth(p, turned_parts):
            gq = jnp.concatenate(
                [
                    turn_back(part * 0.125, own).astype(BF16)
                    for (own, _, _), part in zip(blocks, turned_parts)
                ],
                axis=0,
            )
            gk = turn_back(acc_k[p], slice(0, length)).astype(BF16)
            gv = acc_v[p].astype(BF16)
            pair = group * GROUP + p
            at_lanes = pl.ds(pl.multiple_of(pair * LANES, LANES), LANES)
            for i, grad in enumerate((gq, gk, gv)):
                at_grad = pl.ds(pl.multiple_of((i * pairs + pair) * LANES, LANES), LANES)
                grads_all[at_rows, at_grad] = grad
                line = SUM_QKV + i
                small_ref[line : line + 1, at_lanes] += jnp.sum(
                    grad.astype(F32), axis=0, keepdims=True
                )

        grad_probs = first(0)
        waiting = None
        for p in range(GROUP):
            grad_scores = second(p, grad_probs)
            if p + 1 < GROUP:
                grad_probs = first(p + 1)
            turned_parts = third(p, grad_scores)
            if waiting is not None:
                fourth(*waiting)
            waiting = (p, turned_parts)
        fourth(*waiting)

    if not last:

        @pl.when(step == units - 1)
        def _():
            hand_on.start()
            hand_on.wait()

        return

    @pl.when(step == units)
    def _():
        for load in loads:
            load.wait()
        hand_on.start()

    @pl.when(step >= units)
    def _():
        sending = step == units
        height = send_ref.shape[1]
        core = jnp.where(sending, 1 - where[1], where[1])
        left = [
            turned[pl.ds(pl.multiple_of((2 * half + core) * height, 16), height), :]
            for half in (1 - where[0], where[0])
        ]
        value = dot_nn(jnp.concatenate(left, axis=0), grads_all[...]).astype(BF16)
        put_blocks(
            send_ref, keep_ref, sending, (0, 1), slice(0, 3 * width), (value[:height], value[height:])
        )
        for slot, half in enumerate((1 - where[0], where[0])):
            pack_vectors(small_ref, packed, half)
            vectors = jnp.where(core == 0, packed[...], 0.0).astype(BF16)
            put_blocks(
                send_ref, keep_ref, sending, (slot,), slice(3 * width, 3 * width + LANES), (vectors,)
            )

    @pl.when(step == units + 1)
    def _():
        hand_on.wait()


def attend_back(where, q, k, v, grad_context, probs, cosine, sine, turned, sums, row, made=None):
    tokens, width = q.shape
    total, pairs, depth = probs.shape[:3]
    length = tokens // total
    last = row == total - 1
    rows = 1 if last else total - 1
    units = rows * pairs // GROUP
    height = width // 4
    here = tokens if last else rows * length

    def at(s):
        s = jnp.minimum(s, units - 1)
        return row + s // (pairs // GROUP), s % (pairs // GROUP)

    head = pl.BlockSpec((length, GROUP * LANES), lambda s, *_: at(s))
    table = pl.BlockSpec((length, LANES), lambda s, *_: (at(s)[0], 0))
    shape = jax.ShapeDtypeStruct
    out_specs = [whole(*sums.shape)]
    out_shape = [shape(sums.shape, F32)]
    scratch = [pltpu.VMEM((GROUP, length, LANES), F32)] * 2
    scratch += [pltpu.VMEM((here, 3 * width), BF16)]
    extra = ()
    if last:
        extra = (turned,) if made is None else (turned, made)
        out_specs += [
            send_spec(1, height, 3 * width + LANES, units),
            keep_spec(1, height, 3 * width + LANES, units),
        ]
        out_shape += [shape((2, height, 3 * width + LANES), BF16)] * 2
        scratch += [pltpu.VMEM((width, tokens), BF16), pltpu.VMEM((height, LANES), F32)]
    return pl.pallas_call(
        functools.partial(attend_back_kernel, rows, row, last),
        grid_spec=pltpu.PrefetchScalarGridSpec(
            num_scalar_prefetch=1,
            grid=(units + 2 * last,),
            in_specs=[head] * 4
            + [
                pl.BlockSpec((1, GROUP, depth, 2 * LANES), lambda s, *_: at(s) + (0, 0)),
                table,
                table,
                whole(*sums.shape),
            ]
            + [ANY] * len(extra),
            out_specs=out_specs + [ANY],
            scratch_shapes=scratch + [pltpu.SemaphoreType.DMA((3,))],
        ),
        out_shape=out_shape + [shape((here, 3 * width), BF16)],
        compiler_params=params(60),
        cost_estimate=LIGHT,
        name="attend_back",
    )(where, q, k, v, grad_context, probs, cosine, sine, sums, *extra)


def norm_parts(values):
    mean = jnp.mean(values, axis=-1, keepdims=True)
    center = values - mean
    spread = jnp.mean(center * center, axis=-1, keepdims=True)
    scale = lax.rsqrt(spread + EPSILON)
    return center * scale, scale


def norm_back(grads, gain, normal, scale):
    inner = grads * gain
    return scale * (
        inner
        - jnp.mean(inner, axis=-1, keepdims=True)
        - normal * jnp.mean(inner * normal, axis=-1, keepdims=True)
    )


def gelu_parts(values):
    share = 0.5 + 0.5 * lax.erf(values * 0.7071067811865476)
    return share, jnp.exp(values * values * -0.5) * 0.3989422804014327


def down_copies(down, rows, wd, sems):
    scale = wd.shape[0] // wd.shape[1]
    pieces = list(down[:1]) + cut_pieces(down[1:])
    starts = [rows[i] * scale for i in range(len(pieces))]
    return piece_copies(pieces, starts, wd, 0, sems, 0)


def feed_up_kernel(count, rows, ctx_ref, x_ref, vec, bu, *refs):
    own, pieces = refs[:2], refs[2 : 2 + count]
    normal_ref, scale_ref, act_ref, slope_ref, joined, lows, sems = refs[2 + count :]
    width = x_ref.shape[1]
    step, last = pl.program_id(0), pl.num_programs(0) - 1

    def norm_stage():
        bo, g1, s1 = (vec[i : i + 1, :] for i in range(3))
        attended = dot_nn(ctx_ref[...], joined[:, :width]) + bo
        normal, scale = norm_parts(x_ref[...].astype(F32) + attended)
        normal = normal.astype(BF16)
        normal_ref[...] = normal
        scale_ref[...] = scale
        lows[pl.ds(step % 2, 1)] = (normal.astype(F32) * g1 + s1).astype(BF16)[None]

    def wide_stage(between):
        low = lows[pl.ds((step + 1) % 2, 1)][0]
        chunks = list(range(0, bu.shape[1], CHUNK))

        def product(c):
            return dot_nn(low, joined[:, width + c : width + c + CHUNK])

        ahead = product(0)
        for n, c in enumerate(chunks):
            hidden = ahead + bu[:, c : c + CHUNK]
            if n + 1 < len(chunks):
                ahead = product(chunks[n + 1])
            share, density = gelu_parts(hidden)
            act_ref[:, c : c + CHUNK] = (hidden * share).astype(BF16)
            slope_ref[:, c : c + CHUNK] = (share + hidden * density).astype(BF16)
            if n == 1:
                between()

    @pl.when(step == 0)
    def _():
        sooner, later = joined_copies(own, pieces, rows, joined, sems, width)
        for copy in sooner + later:
            copy.start()
        for copy in sooner:
            copy.wait()
        norm_stage()
        for copy in later:
            copy.wait()

    @pl.when((step > 0) & (step < last))
    def _():
        wide_stage(norm_stage)

    @pl.when(step == last)
    def _():
        wide_stage(lambda: None)


def feed_up(ctx, x, joined, vec, bu):
    own, pieces, rows = joined
    count = len(pieces)
    tokens, width = x.shape
    hidden = bu.shape[1]
    steps = tokens // TILE

    def now(columns):
        return pl.BlockSpec((TILE, columns), lambda s: (jnp.minimum(s, steps - 1), 0))

    def late(columns):
        return pl.BlockSpec((TILE, columns), lambda s: (jnp.maximum(s - 1, 0), 0))

    shape = jax.ShapeDtypeStruct
    return pl.pallas_call(
        functools.partial(feed_up_kernel, count),
        grid=(steps + 1,),
        in_specs=[SMEM, now(width), now(width), whole(*vec.shape), whole(*bu.shape)]
        + [ANY] * (2 + count),
        out_specs=[now(width), now(1), late(hidden), late(hidden)],
        out_shape=[
            shape((tokens, width), BF16),
            shape((tokens, 1), F32),
            shape((tokens, hidden), BF16),
            shape((tokens, hidden), BF16),
        ],
        scratch_shapes=[
            pltpu.VMEM((width, width + hidden), BF16),
            pltpu.VMEM((2, TILE, width), BF16),
            pltpu.SemaphoreType.DMA((SPLITS * (2 + 4 * count),)),
        ],
        compiler_params=params(60),
        cost_estimate=LIGHT,
        name="feed_up",
    )(rows, ctx, x, vec, bu, *own, *pieces)


def feed_down_kernel(count, steps, where, rows, normal_ref, cot_ref, vec, act_any, *refs):
    down = refs[:count]
    small_ref, send_ref, keep_ref, res_any, gd_any = refs[count : count + 5]
    wd, act, products, res, grads_all, sems, sems_act, sems_out = refs[count + 5 :]
    step = pl.program_id(0)
    tile = cot_ref.shape[0]

    def rows_at(i):
        return pl.ds(pl.multiple_of(i * tile, tile), tile)

    def stores(i):
        span = rows_at(i)
        return [
            pltpu.make_async_copy(s.at[span, :], d.at[span, :], sems_out.at[j * steps + i])
            for j, (s, d) in enumerate(((res, res_any), (grads_all, gd_any)))
        ]

    def load(i):
        span = rows_at(i)
        return pltpu.make_async_copy(act_any.at[span, :], act.at[span, :], sems_act.at[i])

    def product_stage():
        load(step).wait()
        products[pl.ds(step % 2, 1)] = dot_nn(act[rows_at(step), :], wd[...])[None]

    def norm_stage():
        span = rows_at(step - 1)
        g1, s1, bd, g2, s2 = (vec[j : j + 1, :] for j in range(1, 6))
        normed = normal_ref[...].astype(F32) * g1 + s1
        product = products[pl.ds((step + 1) % 2, 1)][0]
        normal2, scale2 = norm_parts(normed + (product + bd))
        res[span, :] = normal2 * g2 + s2
        cot = cot_ref[...].astype(F32)
        low = norm_back(cot, g2, normal2, scale2).astype(BF16)
        grads_all[span, :] = low
        for j, value in enumerate((cot * normal2, cot, low.astype(F32))):
            line = SUM_FFN + j
            small_ref[line : line + 1, :] += jnp.sum(value, axis=0, keepdims=True)
        for copy in stores(step - 1):
            copy.start()

    @pl.when(step == 0)
    def _():
        small_ref[...] = jnp.zeros_like(small_ref)
        copies = down_copies(down, rows, wd, sems)
        for copy in [load(0)] + copies + [load(j) for j in range(1, steps)]:
            copy.start()
        for copy in copies:
            copy.wait()
        product_stage()

    @pl.when((step > 0) & (step < steps))
    def _():
        product_stage()
        norm_stage()

    @pl.when(step == steps)
    def _():
        norm_stage()

    @pl.when(step > steps)
    def _():
        product_step = step - steps - 1
        height = send_ref.shape[1]
        sending = product_step < 2
        core = jnp.where(sending, 1 - where[1], where[1])
        half = jnp.where(product_step % 2 == 0, 1 - where[0], where[0])
        at_left = pl.ds(pl.multiple_of((2 * half + core) * height, LANES), height)
        value = dot_tn(act[:, at_left], grads_all[...]).astype(BF16)
        put_blocks(send_ref, keep_ref, sending, (0,), slice(None), (value,))

    @pl.when(step == steps + 4)
    def _():
        for i in range(steps):
            for copy in stores(i):
                copy.wait()


def feed_down(where, act, normal, cot, down, rows, vec):
    count = len(down)
    tokens, width = cot.shape
    wide = act.shape[1]
    tile = 2 * TILE
    steps = tokens // tile
    height = wide // 4
    late = pl.BlockSpec((tile, width), lambda s, *_: (jnp.clip(s - 1, 0, steps - 1), 0))
    shape = jax.ShapeDtypeStruct
    return pl.pallas_call(
        functools.partial(feed_down_kernel, count, steps),
        grid_spec=pltpu.PrefetchScalarGridSpec(
            num_scalar_prefetch=1,
            grid=(steps + 5,),
            in_specs=[SMEM, late, late, whole(*vec.shape)] + [ANY] * (1 + count),
            out_specs=[whole(SUM_ROWS, width)]
            + [send_spec(2, height, width, steps + 1), keep_spec(2, height, width, steps + 1)]
            + [ANY] * 2,
            scratch_shapes=[
                pltpu.VMEM((wide, width), BF16),
                pltpu.VMEM((tokens, wide), BF16),
                pltpu.VMEM((2, tile, width), F32),
                pltpu.VMEM((tokens, width), F32),
                pltpu.VMEM((tokens, width), BF16),
                pltpu.SemaphoreType.DMA((SPLITS * (2 * count + 1),)),
                pltpu.SemaphoreType.DMA((steps,)),
                pltpu.SemaphoreType.DMA((2 * steps,)),
            ],
        ),
        out_shape=[shape((SUM_ROWS, width), F32)]
        + [shape((2, height, width), BF16)] * 2
        + [shape((tokens, width), F32), shape((tokens, width), BF16)],
        compiler_params=params(60),
        cost_estimate=LIGHT,
        name="feed_down",
    )(where, rows, normal, cot, vec, act, *down)


def feed_back_kernel(
    count, steps, where, rows, gd_ref, slope_ref, normal_ref, scale_ref, vec, sums_ref, ctx_any,
    *refs,
):
    own, pieces = refs[:2], refs[2 : 2 + count]
    down = refs[2 + count : 3 + 2 * count]
    small_ref, send_ref, keep_ref, ga_any, gc_any = refs[3 + 2 * count : 8 + 2 * count]
    (
        joined, wd, low, ctx, hidden_all, attended_all, grad_sums, gc, wide,
        sems, sems_down, sem_ctx, sems_out,
    ) = refs[8 + 2 * count :]
    tile, width = gd_ref.shape
    hidden = wide.shape[1]
    step = pl.program_id(0)
    load_ctx = pltpu.make_async_copy(ctx_any, ctx, sem_ctx.at[0])

    def rows_at(i):
        return pl.ds(pl.multiple_of(i * tile, tile), tile)

    def stores(i):
        span = rows_at(i)
        return [
            pltpu.make_async_copy(s.at[span, :], d.at[span, :], sems_out.at[j * steps + i])
            for j, (s, d) in enumerate(((attended_all, ga_any), (gc, gc_any)))
        ]

    def norm_stage():
        span = rows_at(step - 1)
        grad_normed = grad_sums[pl.ds((step + 1) % 2, 1)][0]
        normal = normal_ref[...].astype(F32)
        low[span, :] = (normal * vec[1:2, :] + vec[2:3, :]).astype(BF16)
        rounded = norm_back(grad_normed, vec[1:2, :], normal, scale_ref[...]).astype(BF16)
        attended_all[span, :] = rounded
        for j, value in enumerate((grad_normed * normal, grad_normed, rounded.astype(F32))):
            line = SUM_ATTN + j
            small_ref[line : line + 1, :] += jnp.sum(value, axis=0, keepdims=True)
        gc[span, :] = dot_nt(rounded, joined[:, :width]).astype(BF16)

    def wide_stage(waiting, between):
        span = rows_at(step)
        chunks = list(range(0, hidden, CHUNK))

        def product(c):
            return dot_nt(gd_ref[...], wd[c : c + CHUNK, :])

        ahead = product(0)
        for copy in waiting:
            copy.wait()
        total = gd_ref[...].astype(F32)
        for n, c in enumerate(chunks):
            grad_active = ahead
            if n + 1 < len(chunks):
                ahead = product(chunks[n + 1])
            rounded = (grad_active * slope_ref[:, c : c + CHUNK].astype(F32)).astype(BF16)
            hidden_all[span, c : c + CHUNK] = rounded
            wide[0:1, c : c + CHUNK] += jnp.sum(rounded.astype(F32), axis=0, keepdims=True)
            total = total + dot_nt(rounded, joined[:, width + c : width + c + CHUNK])
            if n == 1:
                between()
        grad_sums[pl.ds(step % 2, 1)] = total[None]

    @pl.when(step == 0)
    def _():
        copies = down_copies(down, rows, wd, sems_down)
        later = joined_copies(own, pieces, rows, joined, sems)
        for copy in copies + later + [load_ctx]:
            copy.start()
        small_ref[...] = sums_ref[...]
        wide[...] = jnp.zeros_like(wide)
        for copy in copies:
            copy.wait()
        wide_stage(later, lambda: None)

    @pl.when((step > 0) & (step < steps))
    def _():
        wide_stage([], norm_stage)

    @pl.when(step == steps)
    def _():
        norm_stage()
        for j in range(hidden // width):
            line = SUM_UP + j
            small_ref[line : line + 1, :] = wide[0:1, j * width : (j + 1) * width]
        load_ctx.wait()

    @pl.when((step > 0) & (step <= steps))
    def _():
        for copy in stores(step - 1):
            copy.start()

    @pl.when(step > steps)
    def _():
        sending = step == steps + 1
        core = jnp.where(sending, 1 - where[1], where[1])
        height, cut = width // 2, hidden // 2
        at_wide = pl.ds(pl.multiple_of(core * cut, LANES), cut)
        at_narrow = pl.ds(pl.multiple_of(core * height, LANES), height)
        slots = (jnp.where(where[0] == 0, 1, 0), jnp.where(where[0] == 0, 0, 1))
        value = dot_tn(low[...], hidden_all[:, at_wide]).astype(BF16)
        put_blocks(
            send_ref, keep_ref, sending, slots, slice(0, cut), (value[:height], value[height:])
        )
        value = dot_tn(ctx[...], attended_all[:, at_narrow]).astype(BF16)
        put_blocks(
            send_ref, keep_ref, sending, slots, slice(cut, cut + height),
            (value[:height], value[height:]),
        )

    @pl.when(step == steps + 2)
    def _():
        for i in range(steps):
            for copy in stores(i):
                copy.wait()


def feed_back(where, gd, slope, normal, scale, joined, down, vec, context, sums):
    own, pieces, rows = joined
    count = len(pieces)
    tokens, width = gd.shape
    wide = slope.shape[1]
    steps = tokens // TILE
    total = (wide + width) // 2

    def now(columns):
        return pl.BlockSpec((TILE, columns), lambda s, *_: (jnp.minimum(s, steps - 1), 0))

    def late(columns):
        return pl.BlockSpec((TILE, columns), lambda s, *_: (jnp.clip(s - 1, 0, steps - 1), 0))

    shape = jax.ShapeDtypeStruct
    return pl.pallas_call(
        functools.partial(feed_back_kernel, count, steps),
        grid_spec=pltpu.PrefetchScalarGridSpec(
            num_scalar_prefetch=1,
            grid=(steps + 3,),
            in_specs=[SMEM, now(width), now(wide), late(width), late(1)]
            + [whole(*vec.shape), whole(*sums.shape)]
            + [ANY] * (4 + 2 * count),
            out_specs=[whole(*sums.shape)]
            + [send_spec(1, width // 2, total, steps + 1)]
            + [keep_spec(1, width // 2, total, steps + 1)]
            + [ANY] * 2,
            scratch_shapes=[
                pltpu.VMEM((width, width + wide), BF16),
                pltpu.VMEM((wide, width), BF16),
                pltpu.VMEM((tokens, width), BF16),
                pltpu.VMEM((tokens, width), BF16),
                pltpu.VMEM((tokens, wide), BF16),
                pltpu.VMEM((tokens, width), BF16),
                pltpu.VMEM((2, TILE, width), F32),
                pltpu.VMEM((tokens, width), BF16),
                pltpu.VMEM((8, wide), F32),
                pltpu.SemaphoreType.DMA((SPLITS * (2 + 2 * count),)),
                pltpu.SemaphoreType.DMA((SPLITS * (1 + 2 * count),)),
                pltpu.SemaphoreType.DMA((1,)),
                pltpu.SemaphoreType.DMA((2 * steps,)),
            ],
        ),
        out_shape=[shape(sums.shape, F32)]
        + [shape((2, width // 2, total), BF16)] * 2
        + [shape((tokens, width), BF16)] * 2,
        compiler_params=params(60),
        cost_estimate=LIGHT,
        name="feed_back",
    )(where, rows, gd, slope, normal, scale, vec, sums, context, *own, *pieces, *down)


def inputs_back_kernel(count, rows, ga_ref, grads, *refs):
    own, pieces = refs[:3], refs[3 : 3 + count]
    out_ref, full, sems = refs[3 + count :]

    @pl.when(pl.program_id(0) == 0)
    def _():
        fetch_joined(own, pieces, rows, full, sems)

    out_ref[...] = ga_ref[...].astype(F32) + dot_nt(grads[...], full[...])


def inputs_back(grads, ga, weights):
    own, pieces, rows = weights
    tokens, width = ga.shape
    tile = pl.BlockSpec((TILE, width), lambda t: (t, 0))
    return pl.pallas_call(
        functools.partial(inputs_back_kernel, len(pieces)),
        grid=(tokens // TILE,),
        in_specs=[SMEM, tile, pl.BlockSpec((TILE, 3 * width), lambda t: (t, 0))]
        + [ANY] * (3 + len(pieces)),
        out_specs=tile,
        out_shape=jax.ShapeDtypeStruct((tokens, width), F32),
        scratch_shapes=[
            pltpu.VMEM((width, 3 * width), BF16),
            pltpu.SemaphoreType.DMA((SPLITS * (3 + 2 * len(pieces)),)),
        ],
        compiler_params=params(60),
        cost_estimate=LIGHT,
        name="inputs_back",
    )(rows, ga, grads, *own, *pieces)


CORE, NEAR_Y, NEAR_Z, FAR_Z = 1, 2, 4, 8


def after(value, *others):
    return lax.optimization_barrier((value,) + others)[0]


def swap_dp(values, bit):
    size = lax.axis_size("dp")
    return lax.ppermute(values, "dp", [(i, i ^ bit) for i in range(size)])


def swap_fsdp(values):
    return lax.ppermute(values, "fsdp", [(0, 1), (1, 0)])


def swap_both(values):
    size = lax.axis_size("dp")
    pairs = [(2 * i + h, 2 * (i ^ NEAR_Y) + 1 - h) for i in range(size) for h in range(2)]
    return lax.ppermute(values, ("dp", "fsdp"), pairs)


def rows_of(values, start, count):
    return lax.dynamic_slice_in_dim(values, start, count, axis=0)


def own_part(shards, place):
    half, core, y, z = place
    height = shards[0].shape[0]
    count = height // 8
    starts = (2 * y + core) * count, height // 2 + (2 * z + core) * count
    return jnp.concatenate(
        [jnp.concatenate([rows_of(s, start, count) for s in shards], axis=1) for start in starts],
        axis=0,
    )


def far_parts(first):
    count = first.shape[0] // 2
    return swap_dp(first[:count], NEAR_Y), swap_dp(first[count:], NEAR_Z)


def all_parts(first, far):
    here = (first,) + far
    return here + tuple(swap_dp(part, CORE) for part in here)


def piece_rows(height, place):
    half, core, y, z = place
    count = height // 8
    base = (1 - half) * height
    rows = [half * height]
    for c in (core, 1 - core):
        rows += [
            base + (2 * y + c) * count,
            base + height // 2 + (2 * z + c) * count,
            base + (2 * (1 - y) + c) * count,
            base + height // 2 + (2 * (1 - z) + c) * count,
        ]
    return jnp.stack(rows).astype(jnp.int32)


class Part:
    def __init__(self, terms, place, columns=None):
        self.bits = {0: 1, 1: place[2], 2: place[3]}
        self.swaps = {
            0: swap_fsdp,
            1: lambda v: swap_dp(v, NEAR_Y),
            2: lambda v: swap_dp(v, NEAR_Z),
            3: lambda v: swap_dp(v, FAR_Z),
        }
        self.terms = [t.reshape(2, 2, 2, t.shape[1] // 4, t.shape[2]) for t in terms]
        self.views = [(columns, ())] * len(terms)
        self.flight, self.joined = [], None

    def total(self, *picks):
        value = None
        for term, (columns, before) in zip(self.terms, self.views):
            if columns is not None:
                term = term[..., columns[0] : columns[1]]
            for axis, index in before + picks:
                term = lax.dynamic_slice_in_dim(term, index, 1, axis)
            term = term.astype(F32)
            value = term if value is None else value + term
        return value.astype(BF16)

    def cut(self, *picks):
        self.views = [(columns, before + picks) for columns, before in self.views]

    def halve(self, axis):
        bit = self.bits[axis]
        self.flight, self.route = [self.total((axis, 1 - bit))], [self.swaps[axis]]
        self.cut((axis, bit))

    def both(self):
        bit = self.bits[1]
        self.flight = [
            self.total((0, 0), (1, bit)),
            self.total((0, 1), (1, 1 - bit)),
            self.total((0, 0), (1, 1 - bit)),
        ]
        self.route = [self.swaps[0], self.swaps[1], swap_both]
        self.cut((0, 1), (1, bit))

    def merge(self, *others):
        value = jnp.concatenate([part.total() for part in (self,) + others], axis=-1)
        self.terms, self.views = [value], [(None, ())]

    def split(self, cut):
        other = copy.copy(self)
        end = self.terms[0].shape[-1]
        self.views = [((0, cut), before) for _, before in self.views]
        other.views = [((cut, end), before) for _, before in other.views]
        return other

    def send_whole(self, swap, reshape=None):
        value = self.terms[0]
        if len(self.terms) > 1 or self.views[0][0] is not None:
            value = self.total()
        if reshape:
            value = value.reshape(-1, value.shape[-1])
        self.flight, self.route = [value], [lambda v: (v, swap(v))]
        self.terms, self.views = [], []

    def far(self):
        self.send_whole(self.swaps[3])

    def join(self, axis):
        self.send_whole(self.swaps[axis])
        self.joined = axis

    def finish(self):
        self.send_whole(lambda v: swap_dp(v, CORE), True)

    def land(self):
        for sent, route in zip(self.flight, self.route):
            got = route(sent)
            self.terms += list(got) if isinstance(got, tuple) else [got]
        self.views = self.views + [(None, ())] * (len(self.terms) - len(self.views))
        self.flight = []

    def settle(self):
        if self.joined is None:
            return
        mine, other = self.terms
        axis, self.joined = self.joined, None
        value = jnp.where(
            self.bits[axis] == 0,
            jnp.concatenate([mine, other], axis=axis),
            jnp.concatenate([other, mine], axis=axis),
        )
        self.terms, self.views = [value], [(None, ())]


def fence(parts, *arrays):
    counts = [(len(p.terms), len(p.flight)) for p in parts]
    flat = [a for p in parts for a in p.terms + p.flight] + list(arrays)
    flat = list(lax.optimization_barrier(tuple(flat)))
    for part, (terms, flight) in zip(parts, counts):
        part.terms, flat = flat[:terms], flat[terms:]
        part.flight, flat = flat[:flight], flat[flight:]
    return flat


def widen(mine, other, core, axis):
    low = jnp.where(core == 0, mine, other).astype(F32)
    high = jnp.where(core == 0, other, mine).astype(F32)
    return jnp.concatenate([low, high], axis=axis)


def gather_all(values):
    return lax.all_gather(values, "fsdp", axis=0, tiled=True)


def sum_plain(send, keep, by_rows):
    blocks = [[keep[1], send[1]], [keep[0], send[0]]]
    axis = 0 if by_rows else 1
    value = jnp.concatenate([jnp.concatenate(pair, axis=axis) for pair in blocks], axis=0)
    own = lax.psum_scatter(value, "fsdp", scatter_dimension=0, tiled=True)
    return lax.psum(own, "dp").astype(F32)


def local(
    inputs, segment_ids, cotangent, w_query, b_query, w_key, b_key, w_value, b_value,
    w_output, b_output, gain_attn, bias_attn, w_up, b_up, w_down, b_down, gain_ffn, bias_ffn,
):
    rows, length = segment_ids.shape
    width = inputs.shape[1]
    shards = lax.axis_size("fsdp")
    paired = shards == 2 and lax.axis_size("dp") == 16
    half = lax.axis_index("fsdp")
    dp = lax.axis_index("dp")
    place = (half, dp % 2, dp // 2 % 2, dp // 4 % 2)
    core = place[1]
    vectors = (b_query, b_key, b_value, b_output, gain_attn, bias_attn, b_down, gain_ffn, bias_ffn)
    height = w_query.shape[0]
    cosine, sine, turned = rotary_tables(segment_ids, inputs)
    if paired:
        where = jnp.stack([half, core]).astype(jnp.int32)
        part_qkv = own_part((w_query, w_key, w_value), place)
        part_up = own_part((w_output, w_up), place)
        here_qkv = swap_fsdp(part_qkv)
        part_down = own_part((after(w_down, here_qkv),), place)
        lines = jnp.concatenate(vectors + (b_up,)).reshape(-1, height)
        other = swap_fsdp(after(lines, part_qkv))
        here_up = swap_fsdp(after(part_up, part_qkv))
        at = piece_rows(height, place)
        joined_qkv = ((w_query, w_key, w_value), all_parts(here_qkv, far_parts(here_qkv)), at)
        lines = jnp.where(half == 0, jnp.stack([lines, other]), jnp.stack([other, lines]))
    else:
        where = jnp.zeros((2,), jnp.int32)
        at = jnp.zeros((1,), jnp.int32)
        joined_qkv = (tuple(gather_all(w) for w in (w_query, w_key, w_value)), (), at)
        joined_up = ((gather_all(w_output), gather_all(w_up)), (), at)
        down = (gather_all(w_down),)
        lines = jnp.concatenate(vectors + (b_up,)).reshape(-1, height)
        lines = lax.all_gather(lines, "fsdp", axis=0)
    lines = lines.astype(F32)
    vec = jnp.swapaxes(lines[:, :9], 0, 1).reshape(9, width)
    bias_up = lines[:, 9:].reshape(1, -1)

    q, k, v = project(inputs, joined_qkv, vec[:3], cosine, sine)
    vec = vec[3:]
    if paired:
        q, here_up, part_down, vec, bias_up = lax.optimization_barrier(
            (q, here_up, part_down, vec, bias_up)
        )
        here_down = swap_fsdp(part_down)
        far_up = far_parts(here_up)
    context, probs = attend(q, k, v, segment_ids)
    if paired:
        context, probs, here_up, here_down, far_up = lax.optimization_barrier(
            (context, probs, here_up, here_down, far_up)
        )
        joined_up = ((w_output, w_up), all_parts(here_up, far_up), at)
        far_down = far_parts(here_down)
    normal, scale, act, slope = feed_up(context, inputs, joined_up, vec, bias_up)
    if paired:
        act, slope, here_down, far_down = lax.optimization_barrier(
            (act, slope, here_down, far_down)
        )
        down = (w_down,) + all_parts(here_down, far_down)
    sums, send, keep, result, grad_down = feed_down(
        where, act, normal, cotangent, down, at, vec
    )
    sent = [(send, keep)]
    if paired:
        sum_d = Part([keep, swap_dp(send, CORE)], place)
        sum_d.both()
        (grad_down,) = fence([sum_d], grad_down)
    outs = feed_back(
        where, grad_down, slope, normal, scale, joined_up, down, vec, context, sums
    )
    sent.append(outs[1:3])
    if paired:
        sum_d.land()
        outs = fence([sum_d], *outs)
    sums, send, keep, grad_attended, grad_context = outs
    if paired:
        sum_d.merge()
        sum_u = Part([keep, swap_dp(send, CORE)], place)
        sum_d.halve(2)
        sum_u.both()
        parts = [sum_d, sum_u]
        (grad_context,) = fence(parts, grad_context)
    tables = (probs, cosine, sine, turned)
    made = None
    if rows > 1:
        sums, made = attend_back(where, q, k, v, grad_context, *tables, sums, 0)
        if paired:
            sum_d.land()
            sums, made, grad_context = fence([sum_d], sums, made, grad_context)
            sum_d.far()
            sums, grad_context = fence([sum_d], sums, grad_context)
    outs = attend_back(where, q, k, v, grad_context, *tables, sums, rows - 1, made)
    sent.append(outs[1:3])
    if paired:
        for p in parts:
            p.land()
        outs = fence(parts, *outs)
    sums, send, keep, grads = outs
    if paired:
        sum_q = Part([keep, swap_dp(send, CORE)], place)
        sum_u.merge()
        sum_d.join(2) if rows > 1 else sum_d.far()
        sum_u.halve(2)
        sum_q.both()
        parts = [sum_d, sum_u, sum_q]
        (grad_attended,) = fence(parts, grad_attended)
    grad_inputs = inputs_back(grads, grad_attended, joined_qkv)
    if paired:
        for p in parts:
            p.land()
        (grad_inputs,) = fence(parts, grad_inputs)
        last = grad_inputs

        def step(part, name, *axis):
            nonlocal last
            (last,) = fence([part], last)
            part.settle()
            getattr(part, name)(*axis)
            (last,) = fence([part], last)
            last = part.flight[0]
            part.land()

        if rows == 1:
            step(sum_d, "join", 2)
        step(sum_u, "far")
        sum_q.merge()
        step(sum_q, "halve", 2)
        step(sum_d, "join", 1)
        step(sum_q, "far")
        cut_u, cut_q = ((p.terms[0].shape[-1] // 2 + 64) // LANES * LANES for p in (sum_u, sum_q))
        (last,) = fence([sum_u], last)
        sum_v = sum_u.split(cut_u)
        step(sum_u, "join", 2)
        step(sum_v, "join", 1)
        step(sum_d, "finish")
        gwd = widen(*sum_d.terms, core, 0)
        (last,) = fence([sum_q], last)
        sum_r = sum_q.split(cut_q)
        step(sum_q, "join", 2)
        step(sum_r, "join", 1)
        step(sum_u, "join", 1)
        step(sum_v, "join", 2)
        (gwd,) = fence([sum_q, sum_r], gwd)
        step(sum_q, "join", 1)
        step(sum_r, "join", 2)
        for part in (sum_u, sum_v):
            part.settle()
            part.finish()
        fence([sum_u, sum_v, sum_q, sum_r])
        sum_u.land()
        sum_v.land()
        for part in (sum_q, sum_r):
            part.settle()
            part.finish()
            part.land()
    else:
        sums = lax.psum(sums, ("dp", "fsdp"))

    wide = b_up.shape[0] * shards
    if paired:
        mine, other = (
            jnp.concatenate([a, b], axis=1) for a, b in zip(sum_u.terms, sum_v.terms)
        )
        cut = wide // 2
        gwu = widen(mine[:, :cut], other[:, :cut], core, 1)
        gwo = widen(mine[:, cut:], other[:, cut:], core, 1)
        mine, other = (
            jnp.concatenate([a, b], axis=1) for a, b in zip(sum_q.terms, sum_r.terms)
        )
        gwq, gwk, gwv = (
            widen(*(end[:, i * width : (i + 1) * width] for end in (mine, other)), core, 0)
            for i in range(3)
        )
        count = height // LANES
        packed = jnp.where(core == 0, mine[:, 3 * width :], other[:, 3 * width :])
        packed = packed[: len(LINES) * count + wide // 2 // LANES].astype(F32)
        vectors = [packed[i * count : (i + 1) * count].reshape(-1) for i in range(len(LINES))]
        gbu = packed[len(LINES) * count :].reshape(-1)
        ggf, gbf, gbd, gga, gba, gbo, gbq, gbk, gbv = vectors
    else:

        def own(line, count=1):
            start = line * width + half * (count * width // shards)
            return lax.dynamic_slice_in_dim(
                sums.reshape(-1), start, count * width // shards, axis=0
            )

        ggf, gbf, gbd, gga, gba, gbo, gbq, gbk, gbv = (own(line) for line in LINES)
        gbu = own(SUM_UP, wide // width)
        gwd = sum_plain(*sent[0], True)
        both = sum_plain(*sent[1], False).reshape(height, 2, -1)
        cut = wide // 2
        gwu = both[..., :cut].reshape(height, -1)
        gwo = both[..., cut:].reshape(height, -1)
        both = sum_plain(*sent[2], True)
        gwq, gwk, gwv = (both[:, i * width : (i + 1) * width] for i in range(3))
    return (
        result, grad_inputs, gwq, gbq, gwk, gbk, gwv, gbv, gwo, gbo, gga, gba,
        gwu, gbu, gwd, gbd, ggf, gbf,
    )


def solution(mesh):
    tokens, matrix, vector = P(("dp", "fsdp"), None), P("fsdp", None), P("fsdp")
    weights = (
        matrix, vector, matrix, vector, matrix, vector, matrix, vector, vector, vector,
        matrix, vector, matrix, vector, vector, vector,
    )
    return jax.shard_map(
        local,
        mesh=mesh,
        in_specs=(tokens,) * 3 + weights,
        out_specs=(tokens,) * 2 + weights,
        check_vma=False,
    )
```

```python
import copy
import functools
import jax
import jax.numpy as jnp
from jax import lax
from jax.experimental import pallas as pl
from jax.experimental.pallas import tpu as pltpu
from jax.sharding import PartitionSpec as P

HEAD = 64
GROUP = 3
EPSILON = 1e-06
LANES = 128
TILE = 256
CHUNK = 512
MASKED = -1e30
SUM_FFN, SUM_ATTN, SUM_UP, SUM_QKV, SUM_ROWS = 0, 3, 6, 10, 16
F32 = jnp.float32
BF16 = jnp.bfloat16


def params(mebibytes):
    return pltpu.CompilerParams(vmem_limit_bytes=mebibytes * 1024 * 1024)


LIGHT = pl.CostEstimate(flops=1000, bytes_accessed=1000, transcendentals=0)


def dot_nn(left, right):
    return lax.dot_general(left, right, (((1,), (0,)), ((), ())), preferred_element_type=F32)


def dot_nt(left, right):
    return lax.dot_general(left, right, (((1,), (1,)), ((), ())), preferred_element_type=F32)


def dot_tn(left, right):
    return lax.dot_general(left, right, (((0,), (0,)), ((), ())), preferred_element_type=F32)


def whole(*shape):
    return pl.BlockSpec(shape, lambda *_: (0,) * len(shape))


SPLITS = 4


def piece_copies(pieces, starts, full, column, sems, first):
    copies = []
    assert len(pieces) == len(starts)
    for i, (piece, start) in enumerate(zip(pieces, starts)):
        height, width = piece.shape
        splits = SPLITS if height * width >= 500_000 and height % (16 * SPLITS) == 0 else 1
        count = height // splits
        for j in range(splits):
            row = pl.multiple_of(start + j * count, 16)
            copies.append(
                pltpu.make_async_copy(
                    piece.at[pl.ds(j * count, count), :],
                    full.at[pl.ds(row, count), column : column + width],
                    sems.at[SPLITS * (first + i) + j],
                )
            )
    return copies


def cut_pieces(pieces):
    cut = []
    for i, piece in enumerate(pieces):
        count = piece.shape[0] // 2
        cut += [piece.at[:count, :], piece.at[count:, :]] if i % 3 == 0 else [piece]
    return cut


def joined_copies(own, pieces, rows, full, sems, cut=None):
    pieces = cut_pieces(pieces)
    shards, column = [], 0
    for i, shard in enumerate(own):
        shards.append(piece_copies([shard], [rows[0]], full, column, sems, i))
        column += shard.shape[1]
    starts = [rows[1 + i] for i in range(len(pieces))]
    first = len(own)
    if cut is None:
        return sum(shards, []) + piece_copies(pieces, starts, full, 0, sems, first)
    left = [piece.at[:, :cut] for piece in pieces]
    right = [piece.at[:, cut:] for piece in pieces]
    return (
        shards[0] + piece_copies(left, starts, full, 0, sems, first),
        sum(shards[1:], []) + piece_copies(right, starts, full, cut, sems, first + len(pieces)),
    )


def fetch_joined(own, pieces, rows, full, sems):
    copies = joined_copies(own, pieces, rows, full, sems)
    for copy in copies:
        copy.start()
    for copy in copies:
        copy.wait()


ANY = pl.BlockSpec(memory_space=pl.ANY)
SMEM = pl.BlockSpec(memory_space=pltpu.SMEM)


def tables_kernel(seg_row, seg_col, x_ref, cos_ref, sin_ref, turned_ref):
    length = seg_row.shape[-1]
    key = lax.broadcasted_iota(jnp.int32, (length, length), 1)
    query = lax.broadcasted_iota(jnp.int32, (length, length), 0)
    earlier = (seg_col[...] == seg_row[0]) & (key < query)
    place = jnp.sum(earlier.astype(F32), axis=1, keepdims=True)
    lane = lax.broadcasted_iota(jnp.int32, (1, LANES), 1)
    paired = (lane % HEAD // 2 * 2).astype(F32)
    freqs = jnp.exp(-jnp.log(F32(10000.0)) * paired / HEAD)
    angle = place * freqs
    cos_ref[...] = jnp.cos(angle)
    sine = jnp.sin(angle)
    sin_ref[...] = jnp.where(lane % 2 == 0, -sine, sine)
    turned_ref[...] = x_ref[...].T


def rotary_tables(segments, x):
    rows, length = segments.shape
    width = x.shape[1]
    return pl.pallas_call(
        tables_kernel,
        grid=(rows,),
        in_specs=[
            pl.BlockSpec((1, 1, length), lambda r: (r, 0, 0)),
            pl.BlockSpec((length, 1), lambda r: (r, 0)),
            pl.BlockSpec((length, width), lambda r: (r, 0)),
        ],
        out_specs=[pl.BlockSpec((length, LANES), lambda r: (r, 0))] * 2
        + [pl.BlockSpec((width, length), lambda r: (0, r))],
        out_shape=[jax.ShapeDtypeStruct((rows * length, LANES), F32)] * 2
        + [jax.ShapeDtypeStruct((width, rows * length), BF16)],
        compiler_params=params(60),
        cost_estimate=LIGHT,
        name="rotary_tables",
    )(segments.reshape(rows, 1, length), segments.reshape(rows * length, 1), x)


def pair_swap(values):
    even = lax.broadcasted_iota(jnp.int32, values.shape, 1) % 2 == 0
    return jnp.where(
        even, pltpu.roll(values, LANES - 1, axis=1), pltpu.roll(values, 1, axis=1)
    )


def project_kernel(count, rows, x_ref, bias, cos_ref, sin_ref, *refs):
    own, pieces = refs[:3], refs[3 : 3 + count]
    q_ref, k_ref, v_ref, full, sems = refs[3 + count :]
    width = x_ref.shape[1]

    @pl.when(pl.program_id(0) == 0)
    def _():
        fetch_joined(own, pieces, rows, full, sems)

    x = x_ref[...]
    cosine, sine = cos_ref[...], sin_ref[...]
    step = 2 * LANES
    for i, out in enumerate((q_ref, k_ref, v_ref)):
        for c in range(0, width, step):
            lin = dot_nn(x, full[:, i * width + c : i * width + c + step])
            lin = lin + bias[i : i + 1, c : c + step]
            if i < 2:
                parts = []
                for d in range(0, step, LANES):
                    part = lin[:, d : d + LANES]
                    part = part * cosine + pair_swap(part) * sine
                    parts.append(part)
                lin = jnp.concatenate(parts, axis=1)
            if i == 0:
                out[:, c : c + step] = (lin.astype(BF16).astype(F32) * 0.125).astype(BF16)
            else:
                out[:, c : c + step] = lin.astype(BF16)


def project(x, weights, bias, cosine, sine):
    own, pieces, rows = weights
    tokens, width = x.shape
    tile = pl.BlockSpec((TILE, width), lambda t: (t, 0))
    table = pl.BlockSpec((TILE, LANES), lambda t: (t, 0))
    return pl.pallas_call(
        functools.partial(project_kernel, len(pieces)),
        grid=(tokens // TILE,),
        in_specs=[SMEM, tile, whole(*bias.shape), table, table] + [ANY] * (3 + len(pieces)),
        out_specs=[tile] * 3,
        out_shape=[jax.ShapeDtypeStruct((tokens, width), BF16)] * 3,
        scratch_shapes=[
            pltpu.VMEM((width, 3 * width), BF16),
            pltpu.SemaphoreType.DMA((SPLITS * (3 + 2 * len(pieces)),)),
        ],
        compiler_params=params(60),
        cost_estimate=LIGHT,
        name="project",
    )(rows, x, bias, cosine, sine, *own, *pieces)


def spans(length):
    found, offset = [], 0
    for first in range(0, length, LANES):
        low, high = max(first - LANES, 0), min(first + 2 * LANES, length)
        found.append((slice(first, first + LANES), slice(low, high), slice(offset, offset + high - low)))
        offset += high - low
    return found, offset


def split_heads(values):
    lane = lax.broadcasted_iota(jnp.int32, (1, LANES), 1)
    return [jnp.where(lane // HEAD == h, values, jnp.zeros_like(values)) for h in range(2)]


def stack_heads(heads, rows):
    return jnp.concatenate([head[rows, :] for head in heads], axis=0)


def merge_heads(stacked):
    lane = lax.broadcasted_iota(jnp.int32, (1, LANES), 1)
    half = stacked.shape[0] // 2
    return jnp.where(lane < HEAD, stacked[:half], stacked[half:])


def attend_kernel(q_ref, k_ref, v_ref, seg_row, seg_col, ctx_ref, prob_ref, bias):
    blocks, _ = spans(q_ref.shape[0])

    @pl.when(pl.program_id(1) == 0)
    def _():
        for own, span, at in blocks:
            bias[at, :] = jnp.where(seg_col[span, :] == seg_row[0, :, own], 0.0, MASKED)

    pairs = [slice(p * LANES, (p + 1) * LANES) for p in range(GROUP)]
    units = [(p, lanes) + block for p, lanes in enumerate(pairs) for block in blocks]
    queries = [split_heads(q_ref[:, lanes]) for lanes in pairs]

    def product(unit):
        p, lanes, own, span, _ = unit
        return dot_nt(k_ref[span, lanes], stack_heads(queries[p], own))

    def soften(unit, scores):
        at = unit[-1]
        heads = []
        for h in range(2):
            masked = scores[:, h * LANES : (h + 1) * LANES] + bias[at, :]
            peak = jnp.max(masked, axis=0, keepdims=True)
            expo = jnp.exp(masked - peak)
            total = jnp.sum(expo, axis=0, keepdims=True)
            heads.append((expo * (1.0 / total)).astype(BF16))
        return jnp.concatenate(heads, axis=1)

    def finish(unit, probs):
        p, lanes, own, span, at = unit
        prob_ref[0, p, at, :] = probs
        ctx_ref[own, lanes] = merge_heads(dot_tn(probs, v_ref[span, lanes])).astype(BF16)

    count = len(blocks)
    scores = [product(unit) for unit in units[:count]]
    waiting = []
    for p in range(GROUP):
        now = units[p * count : (p + 1) * count]
        probs = [soften(unit, value) for unit, value in zip(now, scores)]
        scores = [product(unit) for unit in units[(p + 1) * count : (p + 2) * count]]
        for unit, value in waiting:
            finish(unit, value)
        waiting = list(zip(now, probs))
    for unit, value in waiting:
        finish(unit, value)


def attend(q, k, v, segments):
    rows, length = segments.shape
    tokens, width = q.shape
    pairs = width // LANES
    wide = GROUP * LANES
    _, depth = spans(length)
    head = pl.BlockSpec((length, wide), lambda r, p: (r, p))
    return pl.pallas_call(
        attend_kernel,
        grid=(rows, pairs // GROUP),
        in_specs=[head] * 3
        + [
            pl.BlockSpec((1, 1, length), lambda r, p: (r, 0, 0)),
            pl.BlockSpec((length, 1), lambda r, p: (r, 0)),
        ],
        out_specs=[
            head,
            pl.BlockSpec((1, GROUP, depth, 2 * LANES), lambda r, p: (r, p, 0, 0)),
        ],
        out_shape=[
            jax.ShapeDtypeStruct((tokens, width), BF16),
            jax.ShapeDtypeStruct((rows, pairs, depth, 2 * LANES), BF16),
        ],
        scratch_shapes=[pltpu.VMEM((depth, LANES), F32)],
        compiler_params=params(60),
        cost_estimate=LIGHT,
        name="attend",
    )(q, k, v, segments.reshape(rows, 1, length), segments.reshape(tokens, 1))


def send_spec(steps, height, width, first):
    return pl.BlockSpec(
        (2 // steps, height, width), lambda s, *_: (jnp.clip(s - first, 0, steps - 1), 0, 0)
    )


def keep_spec(steps, height, width, first):
    return pl.BlockSpec(
        (2 // steps, height, width), lambda s, *_: (jnp.clip(s - first - steps, 0, steps - 1), 0, 0)
    )


def put_blocks(send_ref, keep_ref, sending, slots, columns, values):
    @pl.when(sending)
    def _():
        for slot, value in zip(slots, values):
            send_ref[slot, :, columns] = value

    @pl.when(jnp.logical_not(sending))
    def _():
        for slot, value in zip(slots, values):
            keep_ref[slot, :, columns] = value


LINES = (SUM_FFN, SUM_FFN + 1, SUM_FFN + 2, SUM_ATTN, SUM_ATTN + 1, SUM_ATTN + 2) + (
    SUM_QKV, SUM_QKV + 1, SUM_QKV + 2,
)


def pack_vectors(small_ref, packed, half):
    width = small_ref.shape[1]
    part = width // 2 // LANES
    packed[...] = jnp.zeros_like(packed)
    for i, line in enumerate(LINES):
        for j in range(part):
            lanes = pl.ds(pl.multiple_of(half * (width // 2) + j * LANES, LANES), LANES)
            packed[i * part + j : i * part + j + 1, :] = small_ref[line : line + 1, lanes]
    base, count = len(LINES) * part, width // LANES
    lines = (SUM_QKV - SUM_UP) // 2
    for i in range(lines):
        for j in range(count):
            row = base + i * count + j
            lanes = slice(j * LANES, (j + 1) * LANES)
            low, high = (small_ref[SUM_UP + n : SUM_UP + n + 1, lanes] for n in (i, lines + i))
            packed[row : row + 1, :] = jnp.where(half == 0, low, high)


def attend_back_kernel(
    rows, before, last, where, q_ref, k_ref, v_ref, g_ref, prob_ref, cos_ref, sin_ref, sums_ref,
    *refs,
):
    if last:
        (
            turned_any, *made_any, small_ref, send_ref, keep_ref, out_any,
            acc_k, acc_v, grads_all, turned, packed, sems,
        ) = refs
    else:
        small_ref, out_any, acc_k, acc_v, grads_all, sems = refs
    step = pl.program_id(0)
    length, width = q_ref.shape[0], small_ref.shape[1]
    pairs = width // LANES
    units = rows * pairs // GROUP
    hand_on = pltpu.make_async_copy(grads_all, out_any, sems.at[0])
    loads = []
    if last:
        loads.append(pltpu.make_async_copy(turned_any, turned, sems.at[1]))
        if before:
            target = grads_all.at[pl.ds(0, before * length), :]
            loads.append(pltpu.make_async_copy(made_any[0], target, sems.at[2]))

    @pl.when(step == 0)
    def _():
        for load in loads:
            load.start()
        small_ref[...] = sums_ref[...]

    @pl.when(step < units)
    def _():
        blocks, _ = spans(length)
        groups = pairs // GROUP
        row, group = before * last + step // groups, step % groups
        at_rows = pl.ds(pl.multiple_of(row * length, length), length)
        lanes_of = [slice(p * LANES, (p + 1) * LANES) for p in range(GROUP)]

        def turn_back(values, rows):
            return values * cos_ref[rows, :] - pair_swap(values) * sin_ref[rows, :]

        def first(p):
            grads = split_heads(g_ref[:, lanes_of[p]])
            return [
                dot_nt(v_ref[span, lanes_of[p]], stack_heads(grads, own)) for own, span, _ in blocks
            ]

        def second(p, grad_probs):
            made = []
            for (own, span, at), pair in zip(blocks, grad_probs):
                heads = []
                for h in range(2):
                    columns = slice(h * LANES, (h + 1) * LANES)
                    probs = prob_ref[0, p, at, columns].astype(F32)
                    inner = jnp.sum(probs * pair[:, columns], axis=0, keepdims=True)
                    heads.append((probs * (pair[:, columns] - inner)).astype(BF16))
                made.append(jnp.concatenate(heads, axis=1))
            return made

        def third(p, grad_scores):
            lanes = lanes_of[p]
            queries, grads = split_heads(q_ref[:, lanes]), split_heads(g_ref[:, lanes])
            k_t = k_ref[:, lanes].T
            acc_k[p] = jnp.zeros_like(acc_k[p])
            acc_v[p] = jnp.zeros_like(acc_v[p])
            turned_parts = []
            for (own, span, at), low in zip(blocks, grad_scores):
                acc_k[p, span, :] += dot_nn(low, stack_heads(queries, own))
                acc_v[p, span, :] += dot_nn(prob_ref[0, p, at, :], stack_heads(grads, own))
                product = dot_nn(k_t[:, span], low)
                both = jnp.concatenate([product[:HEAD, :LANES], product[HEAD:, LANES:]], axis=0)
                turned_parts.append(both.T)
            return turned_parts

        def fourth(p, turned_parts):
            gq = jnp.concatenate(
                [
                    turn_back(part * 0.125, own).astype(BF16)
                    for (own, _, _), part in zip(blocks, turned_parts)
                ],
                axis=0,
            )
            gk = turn_back(acc_k[p], slice(0, length)).astype(BF16)
            gv = acc_v[p].astype(BF16)
            pair = group * GROUP + p
            at_lanes = pl.ds(pl.multiple_of(pair * LANES, LANES), LANES)
            for i, grad in enumerate((gq, gk, gv)):
                at_grad = pl.ds(pl.multiple_of((i * pairs + pair) * LANES, LANES), LANES)
                grads_all[at_rows, at_grad] = grad
                line = SUM_QKV + i
                small_ref[line : line + 1, at_lanes] += jnp.sum(
                    grad.astype(F32), axis=0, keepdims=True
                )

        grad_probs = first(0)
        waiting = None
        for p in range(GROUP):
            grad_scores = second(p, grad_probs)
            if p + 1 < GROUP:
                grad_probs = first(p + 1)
            turned_parts = third(p, grad_scores)
            if waiting is not None:
                fourth(*waiting)
            waiting = (p, turned_parts)
        fourth(*waiting)

    if not last:

        @pl.when(step == units - 1)
        def _():
            hand_on.start()
            hand_on.wait()

        return

    @pl.when(step == units)
    def _():
        for load in loads:
            load.wait()
        hand_on.start()

    @pl.when(step >= units)
    def _():
        sending = step == units
        height = send_ref.shape[1]
        core = jnp.where(sending, 1 - where[1], where[1])
        left = [
            turned[pl.ds(pl.multiple_of((2 * half + core) * height, 16), height), :]
            for half in (1 - where[0], where[0])
        ]
        value = dot_nn(jnp.concatenate(left, axis=0), grads_all[...]).astype(BF16)
        put_blocks(
            send_ref, keep_ref, sending, (0, 1), slice(0, 3 * width), (value[:height], value[height:])
        )
        for slot, half in enumerate((1 - where[0], where[0])):
            pack_vectors(small_ref, packed, half)
            vectors = jnp.where(core == 0, packed[...], 0.0).astype(BF16)
            put_blocks(
                send_ref, keep_ref, sending, (slot,), slice(3 * width, 3 * width + LANES), (vectors,)
            )

    @pl.when(step == units + 1)
    def _():
        hand_on.wait()


def attend_back(where, q, k, v, grad_context, probs, cosine, sine, turned, sums, row, made=None):
    tokens, width = q.shape
    total, pairs, depth = probs.shape[:3]
    length = tokens // total
    last = row == total - 1
    rows = 1 if last else total - 1
    units = rows * pairs // GROUP
    height = width // 4
    here = tokens if last else rows * length

    def at(s):
        s = jnp.minimum(s, units - 1)
        return row + s // (pairs // GROUP), s % (pairs // GROUP)

    head = pl.BlockSpec((length, GROUP * LANES), lambda s, *_: at(s))
    table = pl.BlockSpec((length, LANES), lambda s, *_: (at(s)[0], 0))
    shape = jax.ShapeDtypeStruct
    out_specs = [whole(*sums.shape)]
    out_shape = [shape(sums.shape, F32)]
    scratch = [pltpu.VMEM((GROUP, length, LANES), F32)] * 2
    scratch += [pltpu.VMEM((here, 3 * width), BF16)]
    extra = ()
    if last:
        extra = (turned,) if made is None else (turned, made)
        out_specs += [
            send_spec(1, height, 3 * width + LANES, units),
            keep_spec(1, height, 3 * width + LANES, units),
        ]
        out_shape += [shape((2, height, 3 * width + LANES), BF16)] * 2
        scratch += [pltpu.VMEM((width, tokens), BF16), pltpu.VMEM((height, LANES), F32)]
    return pl.pallas_call(
        functools.partial(attend_back_kernel, rows, row, last),
        grid_spec=pltpu.PrefetchScalarGridSpec(
            num_scalar_prefetch=1,
            grid=(units + 2 * last,),
            in_specs=[head] * 4
            + [
                pl.BlockSpec((1, GROUP, depth, 2 * LANES), lambda s, *_: at(s) + (0, 0)),
                table,
                table,
                whole(*sums.shape),
            ]
            + [ANY] * len(extra),
            out_specs=out_specs + [ANY],
            scratch_shapes=scratch + [pltpu.SemaphoreType.DMA((3,))],
        ),
        out_shape=out_shape + [shape((here, 3 * width), BF16)],
        compiler_params=params(60),
        cost_estimate=LIGHT,
        name="attend_back",
    )(where, q, k, v, grad_context, probs, cosine, sine, sums, *extra)


def norm_parts(values):
    mean = jnp.mean(values, axis=-1, keepdims=True)
    center = values - mean
    spread = jnp.mean(center * center, axis=-1, keepdims=True)
    scale = lax.rsqrt(spread + EPSILON)
    return center * scale, scale


def norm_back(grads, gain, normal, scale):
    inner = grads * gain
    return scale * (
        inner
        - jnp.mean(inner, axis=-1, keepdims=True)
        - normal * jnp.mean(inner * normal, axis=-1, keepdims=True)
    )


def gelu_parts(values):
    share = 0.5 + 0.5 * lax.erf(values * 0.7071067811865476)
    return share, jnp.exp(values * values * -0.5) * 0.3989422804014327


def down_copies(down, rows, wd, sems):
    scale = wd.shape[0] // wd.shape[1]
    pieces = list(down[:1]) + cut_pieces(down[1:])
    starts = [rows[i] * scale for i in range(len(pieces))]
    return piece_copies(pieces, starts, wd, 0, sems, 0)


def feed_up_kernel(count, rows, ctx_ref, x_ref, vec, bu, *refs):
    own, pieces = refs[:2], refs[2 : 2 + count]
    normal_ref, scale_ref, act_ref, slope_ref, joined, lows, sems = refs[2 + count :]
    width = x_ref.shape[1]
    step, last = pl.program_id(0), pl.num_programs(0) - 1

    def norm_stage():
        bo, g1, s1 = (vec[i : i + 1, :] for i in range(3))
        attended = dot_nn(ctx_ref[...], joined[:, :width]) + bo
        normal, scale = norm_parts(x_ref[...].astype(F32) + attended)
        normal = normal.astype(BF16)
        normal_ref[...] = normal
        scale_ref[...] = scale
        lows[pl.ds(step % 2, 1)] = (normal.astype(F32) * g1 + s1).astype(BF16)[None]

    def wide_stage(between):
        low = lows[pl.ds((step + 1) % 2, 1)][0]
        chunks = list(range(0, bu.shape[1], CHUNK))

        def product(c):
            return dot_nn(low, joined[:, width + c : width + c + CHUNK])

        ahead = product(0)
        for n, c in enumerate(chunks):
            hidden = ahead + bu[:, c : c + CHUNK]
            if n + 1 < len(chunks):
                ahead = product(chunks[n + 1])
            share, density = gelu_parts(hidden)
            act_ref[:, c : c + CHUNK] = (hidden * share).astype(BF16)
            slope_ref[:, c : c + CHUNK] = (share + hidden * density).astype(BF16)
            if n == 1:
                between()

    @pl.when(step == 0)
    def _():
        sooner, later = joined_copies(own, pieces, rows, joined, sems, width)
        for copy in sooner + later:
            copy.start()
        for copy in sooner:
            copy.wait()
        norm_stage()
        for copy in later:
            copy.wait()

    @pl.when((step > 0) & (step < last))
    def _():
        wide_stage(norm_stage)

    @pl.when(step == last)
    def _():
        wide_stage(lambda: None)


def feed_up(ctx, x, joined, vec, bu):
    own, pieces, rows = joined
    count = len(pieces)
    tokens, width = x.shape
    hidden = bu.shape[1]
    steps = tokens // TILE

    def now(columns):
        return pl.BlockSpec((TILE, columns), lambda s: (jnp.minimum(s, steps - 1), 0))

    def late(columns):
        return pl.BlockSpec((TILE, columns), lambda s: (jnp.maximum(s - 1, 0), 0))

    shape = jax.ShapeDtypeStruct
    return pl.pallas_call(
        functools.partial(feed_up_kernel, count),
        grid=(steps + 1,),
        in_specs=[SMEM, now(width), now(width), whole(*vec.shape), whole(*bu.shape)]
        + [ANY] * (2 + count),
        out_specs=[now(width), now(1), late(hidden), late(hidden)],
        out_shape=[
            shape((tokens, width), BF16),
            shape((tokens, 1), F32),
            shape((tokens, hidden), BF16),
            shape((tokens, hidden), BF16),
        ],
        scratch_shapes=[
            pltpu.VMEM((width, width + hidden), BF16),
            pltpu.VMEM((2, TILE, width), BF16),
            pltpu.SemaphoreType.DMA((SPLITS * (2 + 4 * count),)),
        ],
        compiler_params=params(60),
        cost_estimate=LIGHT,
        name="feed_up",
    )(rows, ctx, x, vec, bu, *own, *pieces)


def feed_down_kernel(count, steps, where, rows, normal_ref, cot_ref, vec, act_any, *refs):
    down = refs[:count]
    small_ref, send_ref, keep_ref, res_any, gd_any = refs[count : count + 5]
    wd, act, products, res, grads_all, sems, sems_act, sems_out = refs[count + 5 :]
    step = pl.program_id(0)
    tile = cot_ref.shape[0]

    def rows_at(i):
        return pl.ds(pl.multiple_of(i * tile, tile), tile)

    def stores(i):
        span = rows_at(i)
        return [
            pltpu.make_async_copy(s.at[span, :], d.at[span, :], sems_out.at[j * steps + i])
            for j, (s, d) in enumerate(((res, res_any), (grads_all, gd_any)))
        ]

    def load(i):
        span = rows_at(i)
        return pltpu.make_async_copy(act_any.at[span, :], act.at[span, :], sems_act.at[i])

    def product_stage():
        load(step).wait()
        products[pl.ds(step % 2, 1)] = dot_nn(act[rows_at(step), :], wd[...])[None]

    def norm_stage():
        span = rows_at(step - 1)
        g1, s1, bd, g2, s2 = (vec[j : j + 1, :] for j in range(1, 6))
        normed = normal_ref[...].astype(F32) * g1 + s1
        product = products[pl.ds((step + 1) % 2, 1)][0]
        normal2, scale2 = norm_parts(normed + (product + bd))
        res[span, :] = normal2 * g2 + s2
        cot = cot_ref[...].astype(F32)
        low = norm_back(cot, g2, normal2, scale2).astype(BF16)
        grads_all[span, :] = low
        for j, value in enumerate((cot * normal2, cot, low.astype(F32))):
            line = SUM_FFN + j
            small_ref[line : line + 1, :] += jnp.sum(value, axis=0, keepdims=True)
        for copy in stores(step - 1):
            copy.start()

    @pl.when(step == 0)
    def _():
        small_ref[...] = jnp.zeros_like(small_ref)
        copies = down_copies(down, rows, wd, sems)
        for copy in [load(0)] + copies + [load(j) for j in range(1, steps)]:
            copy.start()
        for copy in copies:
            copy.wait()
        product_stage()

    @pl.when((step > 0) & (step < steps))
    def _():
        product_stage()
        norm_stage()

    @pl.when(step == steps)
    def _():
        norm_stage()

    @pl.when(step > steps)
    def _():
        product_step = step - steps - 1
        height = send_ref.shape[1]
        sending = product_step < 2
        core = jnp.where(sending, 1 - where[1], where[1])
        half = jnp.where(product_step % 2 == 0, 1 - where[0], where[0])
        at_left = pl.ds(pl.multiple_of((2 * half + core) * height, LANES), height)
        value = dot_tn(act[:, at_left], grads_all[...]).astype(BF16)
        put_blocks(send_ref, keep_ref, sending, (0,), slice(None), (value,))

    @pl.when(step == steps + 4)
    def _():
        for i in range(steps):
            for copy in stores(i):
                copy.wait()


def feed_down(where, act, normal, cot, down, rows, vec):
    count = len(down)
    tokens, width = cot.shape
    wide = act.shape[1]
    tile = 2 * TILE
    steps = tokens // tile
    height = wide // 4
    late = pl.BlockSpec((tile, width), lambda s, *_: (jnp.clip(s - 1, 0, steps - 1), 0))
    shape = jax.ShapeDtypeStruct
    return pl.pallas_call(
        functools.partial(feed_down_kernel, count, steps),
        grid_spec=pltpu.PrefetchScalarGridSpec(
            num_scalar_prefetch=1,
            grid=(steps + 5,),
            in_specs=[SMEM, late, late, whole(*vec.shape)] + [ANY] * (1 + count),
            out_specs=[whole(SUM_ROWS, width)]
            + [send_spec(2, height, width, steps + 1), keep_spec(2, height, width, steps + 1)]
            + [ANY] * 2,
            scratch_shapes=[
                pltpu.VMEM((wide, width), BF16),
                pltpu.VMEM((tokens, wide), BF16),
                pltpu.VMEM((2, tile, width), F32),
                pltpu.VMEM((tokens, width), F32),
                pltpu.VMEM((tokens, width), BF16),
                pltpu.SemaphoreType.DMA((SPLITS * (2 * count + 1),)),
                pltpu.SemaphoreType.DMA((steps,)),
                pltpu.SemaphoreType.DMA((2 * steps,)),
            ],
        ),
        out_shape=[shape((SUM_ROWS, width), F32)]
        + [shape((2, height, width), BF16)] * 2
        + [shape((tokens, width), F32), shape((tokens, width), BF16)],
        compiler_params=params(60),
        cost_estimate=LIGHT,
        name="feed_down",
    )(where, rows, normal, cot, vec, act, *down)


def feed_back_kernel(
    count, steps, where, rows, gd_ref, slope_ref, normal_ref, scale_ref, vec, sums_ref, ctx_any,
    *refs,
):
    own, pieces = refs[:2], refs[2 : 2 + count]
    down = refs[2 + count : 3 + 2 * count]
    small_ref, send_ref, keep_ref, ga_any, gc_any = refs[3 + 2 * count : 8 + 2 * count]
    (
        joined, wd, low, ctx, hidden_all, attended_all, grad_sums, gc, wide,
        sems, sems_down, sem_ctx, sems_out,
    ) = refs[8 + 2 * count :]
    tile, width = gd_ref.shape
    hidden = wide.shape[1]
    step = pl.program_id(0)
    load_ctx = pltpu.make_async_copy(ctx_any, ctx, sem_ctx.at[0])

    def rows_at(i):
        return pl.ds(pl.multiple_of(i * tile, tile), tile)

    def stores(i):
        span = rows_at(i)
        return [
            pltpu.make_async_copy(s.at[span, :], d.at[span, :], sems_out.at[j * steps + i])
            for j, (s, d) in enumerate(((attended_all, ga_any), (gc, gc_any)))
        ]

    def norm_stage():
        span = rows_at(step - 1)
        grad_normed = grad_sums[pl.ds((step + 1) % 2, 1)][0]
        normal = normal_ref[...].astype(F32)
        low[span, :] = (normal * vec[1:2, :] + vec[2:3, :]).astype(BF16)
        rounded = norm_back(grad_normed, vec[1:2, :], normal, scale_ref[...]).astype(BF16)
        attended_all[span, :] = rounded
        for j, value in enumerate((grad_normed * normal, grad_normed, rounded.astype(F32))):
            line = SUM_ATTN + j
            small_ref[line : line + 1, :] += jnp.sum(value, axis=0, keepdims=True)
        gc[span, :] = dot_nt(rounded, joined[:, :width]).astype(BF16)

    def wide_stage(waiting, between):
        span = rows_at(step)
        chunks = list(range(0, hidden, CHUNK))

        def product(c):
            return dot_nt(gd_ref[...], wd[c : c + CHUNK, :])

        ahead = product(0)
        for copy in waiting:
            copy.wait()
        total = gd_ref[...].astype(F32)
        for n, c in enumerate(chunks):
            grad_active = ahead
            if n + 1 < len(chunks):
                ahead = product(chunks[n + 1])
            rounded = (grad_active * slope_ref[:, c : c + CHUNK].astype(F32)).astype(BF16)
            hidden_all[span, c : c + CHUNK] = rounded
            wide[0:1, c : c + CHUNK] += jnp.sum(rounded.astype(F32), axis=0, keepdims=True)
            total = total + dot_nt(rounded, joined[:, width + c : width + c + CHUNK])
            if n == 1:
                between()
        grad_sums[pl.ds(step % 2, 1)] = total[None]

    @pl.when(step == 0)
    def _():
        copies = down_copies(down, rows, wd, sems_down)
        later = joined_copies(own, pieces, rows, joined, sems)
        for copy in copies + later + [load_ctx]:
            copy.start()
        small_ref[...] = sums_ref[...]
        wide[...] = jnp.zeros_like(wide)
        for copy in copies:
            copy.wait()
        wide_stage(later, lambda: None)

    @pl.when((step > 0) & (step < steps))
    def _():
        wide_stage([], norm_stage)

    @pl.when(step == steps)
    def _():
        norm_stage()
        for j in range(hidden // width):
            line = SUM_UP + j
            small_ref[line : line + 1, :] = wide[0:1, j * width : (j + 1) * width]
        load_ctx.wait()

    @pl.when((step > 0) & (step <= steps))
    def _():
        for copy in stores(step - 1):
            copy.start()

    @pl.when(step > steps)
    def _():
        sending = step == steps + 1
        core = jnp.where(sending, 1 - where[1], where[1])
        height, cut = width // 2, hidden // 2
        at_wide = pl.ds(pl.multiple_of(core * cut, LANES), cut)
        at_narrow = pl.ds(pl.multiple_of(core * height, LANES), height)
        slots = (jnp.where(where[0] == 0, 1, 0), jnp.where(where[0] == 0, 0, 1))
        value = dot_tn(low[...], hidden_all[:, at_wide]).astype(BF16)
        put_blocks(
            send_ref, keep_ref, sending, slots, slice(0, cut), (value[:height], value[height:])
        )
        value = dot_tn(ctx[...], attended_all[:, at_narrow]).astype(BF16)
        put_blocks(
            send_ref, keep_ref, sending, slots, slice(cut, cut + height),
            (value[:height], value[height:]),
        )

    @pl.when(step == steps + 2)
    def _():
        for i in range(steps):
            for copy in stores(i):
                copy.wait()


def feed_back(where, gd, slope, normal, scale, joined, down, vec, context, sums):
    own, pieces, rows = joined
    count = len(pieces)
    tokens, width = gd.shape
    wide = slope.shape[1]
    steps = tokens // TILE
    total = (wide + width) // 2

    def now(columns):
        return pl.BlockSpec((TILE, columns), lambda s, *_: (jnp.minimum(s, steps - 1), 0))

    def late(columns):
        return pl.BlockSpec((TILE, columns), lambda s, *_: (jnp.clip(s - 1, 0, steps - 1), 0))

    shape = jax.ShapeDtypeStruct
    return pl.pallas_call(
        functools.partial(feed_back_kernel, count, steps),
        grid_spec=pltpu.PrefetchScalarGridSpec(
            num_scalar_prefetch=1,
            grid=(steps + 3,),
            in_specs=[SMEM, now(width), now(wide), late(width), late(1)]
            + [whole(*vec.shape), whole(*sums.shape)]
            + [ANY] * (4 + 2 * count),
            out_specs=[whole(*sums.shape)]
            + [send_spec(1, width // 2, total, steps + 1)]
            + [keep_spec(1, width // 2, total, steps + 1)]
            + [ANY] * 2,
            scratch_shapes=[
                pltpu.VMEM((width, width + wide), BF16),
                pltpu.VMEM((wide, width), BF16),
                pltpu.VMEM((tokens, width), BF16),
                pltpu.VMEM((tokens, width), BF16),
                pltpu.VMEM((tokens, wide), BF16),
                pltpu.VMEM((tokens, width), BF16),
                pltpu.VMEM((2, TILE, width), F32),
                pltpu.VMEM((tokens, width), BF16),
                pltpu.VMEM((8, wide), F32),
                pltpu.SemaphoreType.DMA((SPLITS * (2 + 2 * count),)),
                pltpu.SemaphoreType.DMA((SPLITS * (1 + 2 * count),)),
                pltpu.SemaphoreType.DMA((1,)),
                pltpu.SemaphoreType.DMA((2 * steps,)),
            ],
        ),
        out_shape=[shape(sums.shape, F32)]
        + [shape((2, width // 2, total), BF16)] * 2
        + [shape((tokens, width), BF16)] * 2,
        compiler_params=params(60),
        cost_estimate=LIGHT,
        name="feed_back",
    )(where, rows, gd, slope, normal, scale, vec, sums, context, *own, *pieces, *down)


def inputs_back_kernel(count, rows, ga_ref, grads, *refs):
    own, pieces = refs[:3], refs[3 : 3 + count]
    out_ref, full, sems = refs[3 + count :]

    @pl.when(pl.program_id(0) == 0)
    def _():
        fetch_joined(own, pieces, rows, full, sems)

    out_ref[...] = ga_ref[...].astype(F32) + dot_nt(grads[...], full[...])


def inputs_back(grads, ga, weights):
    own, pieces, rows = weights
    tokens, width = ga.shape
    tile = pl.BlockSpec((TILE, width), lambda t: (t, 0))
    return pl.pallas_call(
        functools.partial(inputs_back_kernel, len(pieces)),
        grid=(tokens // TILE,),
        in_specs=[SMEM, tile, pl.BlockSpec((TILE, 3 * width), lambda t: (t, 0))]
        + [ANY] * (3 + len(pieces)),
        out_specs=tile,
        out_shape=jax.ShapeDtypeStruct((tokens, width), F32),
        scratch_shapes=[
            pltpu.VMEM((width, 3 * width), BF16),
            pltpu.SemaphoreType.DMA((SPLITS * (3 + 2 * len(pieces)),)),
        ],
        compiler_params=params(60),
        cost_estimate=LIGHT,
        name="inputs_back",
    )(rows, ga, grads, *own, *pieces)


CORE, NEAR_Y, NEAR_Z, FAR_Z = 1, 2, 4, 8


def after(value, *others):
    return lax.optimization_barrier((value,) + others)[0]


def swap_dp(values, bit):
    size = lax.axis_size("dp")
    return lax.ppermute(values, "dp", [(i, i ^ bit) for i in range(size)])


def swap_fsdp(values):
    return lax.ppermute(values, "fsdp", [(0, 1), (1, 0)])


def swap_both(values):
    size = lax.axis_size("dp")
    pairs = [(2 * i + h, 2 * (i ^ NEAR_Y) + 1 - h) for i in range(size) for h in range(2)]
    return lax.ppermute(values, ("dp", "fsdp"), pairs)


def rows_of(values, start, count):
    return lax.dynamic_slice_in_dim(values, start, count, axis=0)


def own_part(shards, place):
    half, core, y, z = place
    height = shards[0].shape[0]
    count = height // 8
    starts = (2 * y + core) * count, height // 2 + (2 * z + core) * count
    return jnp.concatenate(
        [jnp.concatenate([rows_of(s, start, count) for s in shards], axis=1) for start in starts],
        axis=0,
    )


def far_parts(first):
    count = first.shape[0] // 2
    return swap_dp(first[:count], NEAR_Y), swap_dp(first[count:], NEAR_Z)


def all_parts(first, far):
    here = (first,) + far
    return here + tuple(swap_dp(part, CORE) for part in here)


def piece_rows(height, place):
    half, core, y, z = place
    count = height // 8
    base = (1 - half) * height
    rows = [half * height]
    for c in (core, 1 - core):
        rows += [
            base + (2 * y + c) * count,
            base + height // 2 + (2 * z + c) * count,
            base + (2 * (1 - y) + c) * count,
            base + height // 2 + (2 * (1 - z) + c) * count,
        ]
    return jnp.stack(rows).astype(jnp.int32)


class Part:
    def __init__(self, terms, place, columns=None):
        self.bits = {0: 1, 1: place[2], 2: place[3]}
        self.swaps = {
            0: swap_fsdp,
            1: lambda v: swap_dp(v, NEAR_Y),
            2: lambda v: swap_dp(v, NEAR_Z),
            3: lambda v: swap_dp(v, FAR_Z),
        }
        self.terms = [t.reshape(2, 2, 2, t.shape[1] // 4, t.shape[2]) for t in terms]
        self.views = [(columns, ())] * len(terms)
        self.flight, self.joined = [], None

    def total(self, *picks):
        value = None
        for term, (columns, before) in zip(self.terms, self.views):
            if columns is not None:
                term = term[..., columns[0] : columns[1]]
            for axis, index in before + picks:
                term = lax.dynamic_slice_in_dim(term, index, 1, axis)
            term = term.astype(F32)
            value = term if value is None else value + term
        return value.astype(BF16)

    def cut(self, *picks):
        self.views = [(columns, before + picks) for columns, before in self.views]

    def halve(self, axis):
        bit = self.bits[axis]
        self.flight, self.route = [self.total((axis, 1 - bit))], [self.swaps[axis]]
        self.cut((axis, bit))

    def both(self):
        bit = self.bits[1]
        self.flight = [
            self.total((0, 0), (1, bit)),
            self.total((0, 1), (1, 1 - bit)),
            self.total((0, 0), (1, 1 - bit)),
        ]
        self.route = [self.swaps[0], self.swaps[1], swap_both]
        self.cut((0, 1), (1, bit))

    def merge(self, *others):
        value = jnp.concatenate([part.total() for part in (self,) + others], axis=-1)
        self.terms, self.views = [value], [(None, ())]

    def split(self, cut):
        other = copy.copy(self)
        end = self.terms[0].shape[-1]
        self.views = [((0, cut), before) for _, before in self.views]
        other.views = [((cut, end), before) for _, before in other.views]
        return other

    def send_whole(self, swap, reshape=None):
        value = self.terms[0]
        if len(self.terms) > 1 or self.views[0][0] is not None:
            value = self.total()
        if reshape:
            value = value.reshape(-1, value.shape[-1])
        self.flight, self.route = [value], [lambda v: (v, swap(v))]
        self.terms, self.views = [], []

    def far(self):
        self.send_whole(self.swaps[3])

    def join(self, axis):
        self.send_whole(self.swaps[axis])
        self.joined = axis

    def finish(self):
        self.send_whole(lambda v: swap_dp(v, CORE), True)

    def land(self):
        for sent, route in zip(self.flight, self.route):
            got = route(sent)
            self.terms += list(got) if isinstance(got, tuple) else [got]
        self.views = self.views + [(None, ())] * (len(self.terms) - len(self.views))
        self.flight = []

    def settle(self):
        if self.joined is None:
            return
        mine, other = self.terms
        axis, self.joined = self.joined, None
        value = jnp.where(
            self.bits[axis] == 0,
            jnp.concatenate([mine, other], axis=axis),
            jnp.concatenate([other, mine], axis=axis),
        )
        self.terms, self.views = [value], [(None, ())]


def fence(parts, *arrays):
    counts = [(len(p.terms), len(p.flight)) for p in parts]
    flat = [a for p in parts for a in p.terms + p.flight] + list(arrays)
    flat = list(lax.optimization_barrier(tuple(flat)))
    for part, (terms, flight) in zip(parts, counts):
        part.terms, flat = flat[:terms], flat[terms:]
        part.flight, flat = flat[:flight], flat[flight:]
    return flat


def widen(mine, other, core, axis):
    low = jnp.where(core == 0, mine, other).astype(F32)
    high = jnp.where(core == 0, other, mine).astype(F32)
    return jnp.concatenate([low, high], axis=axis)


def gather_all(values):
    return lax.all_gather(values, "fsdp", axis=0, tiled=True)


def sum_plain(send, keep, by_rows):
    blocks = [[keep[1], send[1]], [keep[0], send[0]]]
    axis = 0 if by_rows else 1
    value = jnp.concatenate([jnp.concatenate(pair, axis=axis) for pair in blocks], axis=0)
    own = lax.psum_scatter(value, "fsdp", scatter_dimension=0, tiled=True)
    return lax.psum(own, "dp").astype(F32)


def local(
    inputs, segment_ids, cotangent, w_query, b_query, w_key, b_key, w_value, b_value,
    w_output, b_output, gain_attn, bias_attn, w_up, b_up, w_down, b_down, gain_ffn, bias_ffn,
):
    rows, length = segment_ids.shape
    width = inputs.shape[1]
    shards = lax.axis_size("fsdp")
    paired = shards == 2 and lax.axis_size("dp") == 16
    half = lax.axis_index("fsdp")
    dp = lax.axis_index("dp")
    place = (half, dp % 2, dp // 2 % 2, dp // 4 % 2)
    core = place[1]
    vectors = (b_query, b_key, b_value, b_output, gain_attn, bias_attn, b_down, gain_ffn, bias_ffn)
    height = w_query.shape[0]
    cosine, sine, turned = rotary_tables(segment_ids, inputs)
    if paired:
        where = jnp.stack([half, core]).astype(jnp.int32)
        part_qkv = own_part((w_query, w_key, w_value), place)
        part_up = own_part((w_output, w_up), place)
        here_qkv = swap_fsdp(part_qkv)
        part_down = own_part((after(w_down, here_qkv),), place)
        lines = jnp.concatenate(vectors + (b_up,)).reshape(-1, height)
        other = swap_fsdp(after(lines, part_qkv))
        here_up = swap_fsdp(after(part_up, part_qkv))
        at = piece_rows(height, place)
        joined_qkv = ((w_query, w_key, w_value), all_parts(here_qkv, far_parts(here_qkv)), at)
        lines = jnp.where(half == 0, jnp.stack([lines, other]), jnp.stack([other, lines]))
    else:
        where = jnp.zeros((2,), jnp.int32)
        at = jnp.zeros((1,), jnp.int32)
        joined_qkv = (tuple(gather_all(w) for w in (w_query, w_key, w_value)), (), at)
        joined_up = ((gather_all(w_output), gather_all(w_up)), (), at)
        down = (gather_all(w_down),)
        lines = jnp.concatenate(vectors + (b_up,)).reshape(-1, height)
        lines = lax.all_gather(lines, "fsdp", axis=0)
    lines = lines.astype(F32)
    vec = jnp.swapaxes(lines[:, :9], 0, 1).reshape(9, width)
    bias_up = lines[:, 9:].reshape(1, -1)

    q, k, v = project(inputs, joined_qkv, vec[:3], cosine, sine)
    vec = vec[3:]
    if paired:
        q, here_up, part_down, vec, bias_up = lax.optimization_barrier(
            (q, here_up, part_down, vec, bias_up)
        )
        here_down = swap_fsdp(part_down)
        far_up = far_parts(here_up)
    context, probs = attend(q, k, v, segment_ids)
    if paired:
        context, probs, here_up, here_down, far_up = lax.optimization_barrier(
            (context, probs, here_up, here_down, far_up)
        )
        joined_up = ((w_output, w_up), all_parts(here_up, far_up), at)
        far_down = far_parts(here_down)
    normal, scale, act, slope = feed_up(context, inputs, joined_up, vec, bias_up)
    if paired:
        act, slope, here_down, far_down = lax.optimization_barrier(
            (act, slope, here_down, far_down)
        )
        down = (w_down,) + all_parts(here_down, far_down)
    sums, send, keep, result, grad_down = feed_down(
        where, act, normal, cotangent, down, at, vec
    )
    sent = [(send, keep)]
    if paired:
        sum_d = Part([keep, swap_dp(send, CORE)], place)
        sum_d.both()
        (grad_down,) = fence([sum_d], grad_down)
    outs = feed_back(
        where, grad_down, slope, normal, scale, joined_up, down, vec, context, sums
    )
    sent.append(outs[1:3])
    if paired:
        sum_d.land()
        outs = fence([sum_d], *outs)
    sums, send, keep, grad_attended, grad_context = outs
    if paired:
        sum_d.merge()
        sum_u = Part([keep, swap_dp(send, CORE)], place)
        sum_d.halve(2)
        sum_u.both()
        parts = [sum_d, sum_u]
        (grad_context,) = fence(parts, grad_context)
    tables = (probs, cosine, sine, turned)
    made = None
    if rows > 1:
        sums, made = attend_back(where, q, k, v, grad_context, *tables, sums, 0)
        if paired:
            sum_d.land()
            sums, made, grad_context = fence([sum_d], sums, made, grad_context)
            sum_d.far()
            sums, grad_context = fence([sum_d], sums, grad_context)
    outs = attend_back(where, q, k, v, grad_context, *tables, sums, rows - 1, made)
    sent.append(outs[1:3])
    if paired:
        for p in parts:
            p.land()
        outs = fence(parts, *outs)
    sums, send, keep, grads = outs
    if paired:
        sum_q = Part([keep, swap_dp(send, CORE)], place)
        sum_u.merge()
        sum_d.join(2) if rows > 1 else sum_d.far()
        sum_u.halve(2)
        sum_q.both()
        parts = [sum_d, sum_u, sum_q]
        (grad_attended,) = fence(parts, grad_attended)
    grad_inputs = inputs_back(grads, grad_attended, joined_qkv)
    if paired:
        for p in parts:
            p.land()
        (grad_inputs,) = fence(parts, grad_inputs)
        last = grad_inputs

        def step(part, name, *axis):
            nonlocal last
            (last,) = fence([part], last)
            part.settle()
            getattr(part, name)(*axis)
            (last,) = fence([part], last)
            last = part.flight[0]
            part.land()

        if rows == 1:
            step(sum_d, "join", 2)
        step(sum_u, "far")
        sum_q.merge()
        step(sum_q, "halve", 2)
        step(sum_d, "join", 1)
        sum_q.terms = [after(term, sum_u.terms[-1]) for term in sum_q.terms]
        step(sum_q, "far")
        cut_u, cut_q = ((p.terms[0].shape[-1] // 2 + 64) // LANES * LANES for p in (sum_u, sum_q))
        (last,) = fence([sum_u], last)
        sum_v = sum_u.split(cut_u)
        step(sum_u, "join", 2)
        step(sum_v, "join", 1)
        step(sum_d, "finish")
        gwd = widen(*sum_d.terms, core, 0)
        (last,) = fence([sum_q], last)
        sum_r = sum_q.split(cut_q)
        step(sum_q, "join", 2)
        step(sum_r, "join", 1)
        step(sum_u, "join", 1)
        step(sum_v, "join", 2)
        step(sum_q, "join", 1)
        step(sum_r, "join", 2)
        for part in (sum_u, sum_v):
            part.settle()
            part.finish()
        (gwd,) = fence([sum_u, sum_v, sum_q, sum_r], gwd)
        sum_u.land()
        sum_v.land()
        for part in (sum_q, sum_r):
            part.settle()
            part.finish()
            part.land()
    else:
        sums = lax.psum(sums, ("dp", "fsdp"))

    wide = b_up.shape[0] * shards
    if paired:
        mine, other = (
            jnp.concatenate([a, b], axis=1) for a, b in zip(sum_u.terms, sum_v.terms)
        )
        cut = wide // 2
        gwu = widen(mine[:, :cut], other[:, :cut], core, 1)
        gwo = widen(mine[:, cut:], other[:, cut:], core, 1)
        mine, other = (
            jnp.concatenate([a, b], axis=1) for a, b in zip(sum_q.terms, sum_r.terms)
        )
        gwq, gwk, gwv = (
            widen(*(end[:, i * width : (i + 1) * width] for end in (mine, other)), core, 0)
            for i in range(3)
        )
        count = height // LANES
        packed = jnp.where(core == 0, mine[:, 3 * width :], other[:, 3 * width :])
        packed = packed[: len(LINES) * count + wide // 2 // LANES].astype(F32)
        vectors = [packed[i * count : (i + 1) * count].reshape(-1) for i in range(len(LINES))]
        gbu = packed[len(LINES) * count :].reshape(-1)
        ggf, gbf, gbd, gga, gba, gbo, gbq, gbk, gbv = vectors
    else:

        def own(line, count=1):
            start = line * width + half * (count * width // shards)
            return lax.dynamic_slice_in_dim(
                sums.reshape(-1), start, count * width // shards, axis=0
            )

        ggf, gbf, gbd, gga, gba, gbo, gbq, gbk, gbv = (own(line) for line in LINES)
        gbu = own(SUM_UP, wide // width)
        gwd = sum_plain(*sent[0], True)
        both = sum_plain(*sent[1], False).reshape(height, 2, -1)
        cut = wide // 2
        gwu = both[..., :cut].reshape(height, -1)
        gwo = both[..., cut:].reshape(height, -1)
        both = sum_plain(*sent[2], True)
        gwq, gwk, gwv = (both[:, i * width : (i + 1) * width] for i in range(3))
    return (
        result, grad_inputs, gwq, gbq, gwk, gbk, gwv, gbv, gwo, gbo, gga, gba,
        gwu, gbu, gwd, gbd, ggf, gbf,
    )


def solution(mesh):
    tokens, matrix, vector = P(("dp", "fsdp"), None), P("fsdp", None), P("fsdp")
    weights = (
        matrix, vector, matrix, vector, matrix, vector, matrix, vector, vector, vector,
        matrix, vector, matrix, vector, vector, vector,
    )
    return jax.shard_map(
        local,
        mesh=mesh,
        in_specs=(tokens,) * 3 + weights,
        out_specs=(tokens,) * 2 + weights,
        check_vma=False,
    )
```

```python
import copy
import functools
import jax
import jax.numpy as jnp
from jax import lax
from jax.experimental import pallas as pl
from jax.experimental.pallas import tpu as pltpu
from jax.sharding import PartitionSpec as P

HEAD = 64
GROUP = 3
EPSILON = 1e-06
LANES = 128
TILE = 256
CHUNK = 512
MASKED = -1e30
SUM_FFN, SUM_ATTN, SUM_UP, SUM_QKV, SUM_ROWS = 0, 3, 6, 10, 16
F32 = jnp.float32
BF16 = jnp.bfloat16


def params(mebibytes):
    return pltpu.CompilerParams(vmem_limit_bytes=mebibytes * 1024 * 1024)


LIGHT = pl.CostEstimate(flops=1000, bytes_accessed=1000, transcendentals=0)


def dot_nn(left, right):
    return lax.dot_general(left, right, (((1,), (0,)), ((), ())), preferred_element_type=F32)


def dot_nt(left, right):
    return lax.dot_general(left, right, (((1,), (1,)), ((), ())), preferred_element_type=F32)


def dot_tn(left, right):
    return lax.dot_general(left, right, (((0,), (0,)), ((), ())), preferred_element_type=F32)


def whole(*shape):
    return pl.BlockSpec(shape, lambda *_: (0,) * len(shape))


SPLITS = 4


def piece_copies(pieces, starts, full, column, sems, first):
    copies = []
    assert len(pieces) == len(starts)
    for i, (piece, start) in enumerate(zip(pieces, starts)):
        height, width = piece.shape
        splits = SPLITS if height * width >= 500_000 and height % (16 * SPLITS) == 0 else 1
        count = height // splits
        for j in range(splits):
            row = pl.multiple_of(start + j * count, 16)
            copies.append(
                pltpu.make_async_copy(
                    piece.at[pl.ds(j * count, count), :],
                    full.at[pl.ds(row, count), column : column + width],
                    sems.at[SPLITS * (first + i) + j],
                )
            )
    return copies


def cut_pieces(pieces):
    cut = []
    for i, piece in enumerate(pieces):
        count = piece.shape[0] // 2
        cut += [piece.at[:count, :], piece.at[count:, :]] if i % 3 == 0 else [piece]
    return cut


def joined_copies(own, pieces, rows, full, sems, cut=None):
    pieces = cut_pieces(pieces)
    shards, column = [], 0
    for i, shard in enumerate(own):
        shards.append(piece_copies([shard], [rows[0]], full, column, sems, i))
        column += shard.shape[1]
    starts = [rows[1 + i] for i in range(len(pieces))]
    first = len(own)
    if cut is None:
        return sum(shards, []) + piece_copies(pieces, starts, full, 0, sems, first)
    left = [piece.at[:, :cut] for piece in pieces]
    right = [piece.at[:, cut:] for piece in pieces]
    return (
        shards[0] + piece_copies(left, starts, full, 0, sems, first),
        sum(shards[1:], []) + piece_copies(right, starts, full, cut, sems, first + len(pieces)),
    )


def fetch_joined(own, pieces, rows, full, sems):
    copies = joined_copies(own, pieces, rows, full, sems)
    for copy in copies:
        copy.start()
    for copy in copies:
        copy.wait()


ANY = pl.BlockSpec(memory_space=pl.ANY)
SMEM = pl.BlockSpec(memory_space=pltpu.SMEM)


def tables_kernel(seg_row, seg_col, x_ref, cos_ref, sin_ref, turned_ref):
    length = seg_row.shape[-1]
    key = lax.broadcasted_iota(jnp.int32, (length, length), 1)
    query = lax.broadcasted_iota(jnp.int32, (length, length), 0)
    earlier = (seg_col[...] == seg_row[0]) & (key < query)
    place = jnp.sum(earlier.astype(F32), axis=1, keepdims=True)
    lane = lax.broadcasted_iota(jnp.int32, (1, LANES), 1)
    paired = (lane % HEAD // 2 * 2).astype(F32)
    freqs = jnp.exp(-jnp.log(F32(10000.0)) * paired / HEAD)
    angle = place * freqs
    cos_ref[...] = jnp.cos(angle)
    sine = jnp.sin(angle)
    sin_ref[...] = jnp.where(lane % 2 == 0, -sine, sine)
    turned_ref[...] = x_ref[...].T


def rotary_tables(segments, x):
    rows, length = segments.shape
    width = x.shape[1]
    return pl.pallas_call(
        tables_kernel,
        grid=(rows,),
        in_specs=[
            pl.BlockSpec((1, 1, length), lambda r: (r, 0, 0)),
            pl.BlockSpec((length, 1), lambda r: (r, 0)),
            pl.BlockSpec((length, width), lambda r: (r, 0)),
        ],
        out_specs=[pl.BlockSpec((length, LANES), lambda r: (r, 0))] * 2
        + [pl.BlockSpec((width, length), lambda r: (0, r))],
        out_shape=[jax.ShapeDtypeStruct((rows * length, LANES), F32)] * 2
        + [jax.ShapeDtypeStruct((width, rows * length), BF16)],
        compiler_params=params(60),
        cost_estimate=LIGHT,
        name="rotary_tables",
    )(segments.reshape(rows, 1, length), segments.reshape(rows * length, 1), x)


def pair_swap(values):
    even = lax.broadcasted_iota(jnp.int32, values.shape, 1) % 2 == 0
    return jnp.where(
        even, pltpu.roll(values, LANES - 1, axis=1), pltpu.roll(values, 1, axis=1)
    )


def project_kernel(count, rows, x_ref, bias, cos_ref, sin_ref, *refs):
    own, pieces = refs[:3], refs[3 : 3 + count]
    q_ref, k_ref, v_ref, full, sems = refs[3 + count :]
    width = x_ref.shape[1]

    @pl.when(pl.program_id(0) == 0)
    def _():
        fetch_joined(own, pieces, rows, full, sems)

    x = x_ref[...]
    cosine, sine = cos_ref[...], sin_ref[...]
    step = 2 * LANES
    for i, out in enumerate((q_ref, k_ref, v_ref)):
        for c in range(0, width, step):
            lin = dot_nn(x, full[:, i * width + c : i * width + c + step])
            lin = lin + bias[i : i + 1, c : c + step]
            if i < 2:
                parts = []
                for d in range(0, step, LANES):
                    part = lin[:, d : d + LANES]
                    part = part * cosine + pair_swap(part) * sine
                    parts.append(part)
                lin = jnp.concatenate(parts, axis=1)
            if i == 0:
                out[:, c : c + step] = (lin.astype(BF16).astype(F32) * 0.125).astype(BF16)
            else:
                out[:, c : c + step] = lin.astype(BF16)


def project(x, weights, bias, cosine, sine):
    own, pieces, rows = weights
    tokens, width = x.shape
    tile = pl.BlockSpec((TILE, width), lambda t: (t, 0))
    table = pl.BlockSpec((TILE, LANES), lambda t: (t, 0))
    return pl.pallas_call(
        functools.partial(project_kernel, len(pieces)),
        grid=(tokens // TILE,),
        in_specs=[SMEM, tile, whole(*bias.shape), table, table] + [ANY] * (3 + len(pieces)),
        out_specs=[tile] * 3,
        out_shape=[jax.ShapeDtypeStruct((tokens, width), BF16)] * 3,
        scratch_shapes=[
            pltpu.VMEM((width, 3 * width), BF16),
            pltpu.SemaphoreType.DMA((SPLITS * (3 + 2 * len(pieces)),)),
        ],
        compiler_params=params(60),
        cost_estimate=LIGHT,
        name="project",
    )(rows, x, bias, cosine, sine, *own, *pieces)


def spans(length):
    found, offset = [], 0
    for first in range(0, length, LANES):
        low, high = max(first - LANES, 0), min(first + 2 * LANES, length)
        found.append((slice(first, first + LANES), slice(low, high), slice(offset, offset + high - low)))
        offset += high - low
    return found, offset


def split_heads(values):
    lane = lax.broadcasted_iota(jnp.int32, (1, LANES), 1)
    return [jnp.where(lane // HEAD == h, values, jnp.zeros_like(values)) for h in range(2)]


def stack_heads(heads, rows):
    return jnp.concatenate([head[rows, :] for head in heads], axis=0)


def merge_heads(stacked):
    lane = lax.broadcasted_iota(jnp.int32, (1, LANES), 1)
    half = stacked.shape[0] // 2
    return jnp.where(lane < HEAD, stacked[:half], stacked[half:])


def attend_kernel(q_ref, k_ref, v_ref, seg_row, seg_col, ctx_ref, prob_ref, bias):
    blocks, _ = spans(q_ref.shape[0])

    @pl.when(pl.program_id(1) == 0)
    def _():
        for own, span, at in blocks:
            bias[at, :] = jnp.where(seg_col[span, :] == seg_row[0, :, own], 0.0, MASKED)

    pairs = [slice(p * LANES, (p + 1) * LANES) for p in range(GROUP)]
    units = [(p, lanes) + block for p, lanes in enumerate(pairs) for block in blocks]
    queries = [split_heads(q_ref[:, lanes]) for lanes in pairs]

    def product(unit):
        p, lanes, own, span, _ = unit
        return dot_nt(k_ref[span, lanes], stack_heads(queries[p], own))

    def soften(unit, scores):
        at = unit[-1]
        heads = []
        for h in range(2):
            masked = scores[:, h * LANES : (h + 1) * LANES] + bias[at, :]
            peak = jnp.max(masked, axis=0, keepdims=True)
            expo = jnp.exp(masked - peak)
            total = jnp.sum(expo, axis=0, keepdims=True)
            heads.append((expo * (1.0 / total)).astype(BF16))
        return jnp.concatenate(heads, axis=1)

    def finish(unit, probs):
        p, lanes, own, span, at = unit
        prob_ref[0, p, at, :] = probs
        ctx_ref[own, lanes] = merge_heads(dot_tn(probs, v_ref[span, lanes])).astype(BF16)

    count = len(blocks)
    scores = [product(unit) for unit in units[:count]]
    waiting = []
    for p in range(GROUP):
        now = units[p * count : (p + 1) * count]
        probs = [soften(unit, value) for unit, value in zip(now, scores)]
        scores = [product(unit) for unit in units[(p + 1) * count : (p + 2) * count]]
        for unit, value in waiting:
            finish(unit, value)
        waiting = list(zip(now, probs))
    for unit, value in waiting:
        finish(unit, value)


def attend(q, k, v, segments):
    rows, length = segments.shape
    tokens, width = q.shape
    pairs = width // LANES
    wide = GROUP * LANES
    _, depth = spans(length)
    head = pl.BlockSpec((length, wide), lambda r, p: (r, p))
    return pl.pallas_call(
        attend_kernel,
        grid=(rows, pairs // GROUP),
        in_specs=[head] * 3
        + [
            pl.BlockSpec((1, 1, length), lambda r, p: (r, 0, 0)),
            pl.BlockSpec((length, 1), lambda r, p: (r, 0)),
        ],
        out_specs=[
            head,
            pl.BlockSpec((1, GROUP, depth, 2 * LANES), lambda r, p: (r, p, 0, 0)),
        ],
        out_shape=[
            jax.ShapeDtypeStruct((tokens, width), BF16),
            jax.ShapeDtypeStruct((rows, pairs, depth, 2 * LANES), BF16),
        ],
        scratch_shapes=[pltpu.VMEM((depth, LANES), F32)],
        compiler_params=params(60),
        cost_estimate=LIGHT,
        name="attend",
    )(q, k, v, segments.reshape(rows, 1, length), segments.reshape(tokens, 1))


def send_spec(steps, height, width, first):
    return pl.BlockSpec(
        (2 // steps, height, width), lambda s, *_: (jnp.clip(s - first, 0, steps - 1), 0, 0)
    )


def keep_spec(steps, height, width, first):
    return pl.BlockSpec(
        (2 // steps, height, width), lambda s, *_: (jnp.clip(s - first - steps, 0, steps - 1), 0, 0)
    )


def put_blocks(send_ref, keep_ref, sending, slots, columns, values):
    @pl.when(sending)
    def _():
        for slot, value in zip(slots, values):
            send_ref[slot, :, columns] = value

    @pl.when(jnp.logical_not(sending))
    def _():
        for slot, value in zip(slots, values):
            keep_ref[slot, :, columns] = value


LINES = (SUM_FFN, SUM_FFN + 1, SUM_FFN + 2, SUM_ATTN, SUM_ATTN + 1, SUM_ATTN + 2) + (
    SUM_QKV, SUM_QKV + 1, SUM_QKV + 2,
)


def pack_vectors(small_ref, packed, half):
    width = small_ref.shape[1]
    part = width // 2 // LANES
    packed[...] = jnp.zeros_like(packed)
    for i, line in enumerate(LINES):
        for j in range(part):
            lanes = pl.ds(pl.multiple_of(half * (width // 2) + j * LANES, LANES), LANES)
            packed[i * part + j : i * part + j + 1, :] = small_ref[line : line + 1, lanes]
    base, count = len(LINES) * part, width // LANES
    lines = (SUM_QKV - SUM_UP) // 2
    for i in range(lines):
        for j in range(count):
            row = base + i * count + j
            lanes = slice(j * LANES, (j + 1) * LANES)
            low, high = (small_ref[SUM_UP + n : SUM_UP + n + 1, lanes] for n in (i, lines + i))
            packed[row : row + 1, :] = jnp.where(half == 0, low, high)


def attend_back_kernel(
    rows, before, last, where, q_ref, k_ref, v_ref, g_ref, prob_ref, cos_ref, sin_ref, sums_ref,
    *refs,
):
    if last:
        (
            turned_any, *made_any, small_ref, send_ref, keep_ref, out_any,
            acc_k, acc_v, grads_all, turned, packed, sems,
        ) = refs
    else:
        small_ref, out_any, acc_k, acc_v, grads_all, sems = refs
    step = pl.program_id(0)
    length, width = q_ref.shape[0], small_ref.shape[1]
    pairs = width // LANES
    units = rows * pairs // GROUP
    hand_on = pltpu.make_async_copy(grads_all, out_any, sems.at[0])
    loads = []
    if last:
        loads.append(pltpu.make_async_copy(turned_any, turned, sems.at[1]))
        if before:
            target = grads_all.at[pl.ds(0, before * length), :]
            loads.append(pltpu.make_async_copy(made_any[0], target, sems.at[2]))

    @pl.when(step == 0)
    def _():
        for load in loads:
            load.start()
        small_ref[...] = sums_ref[...]

    @pl.when(step < units)
    def _():
        blocks, _ = spans(length)
        groups = pairs // GROUP
        row, group = before * last + step // groups, step % groups
        at_rows = pl.ds(pl.multiple_of(row * length, length), length)
        lanes_of = [slice(p * LANES, (p + 1) * LANES) for p in range(GROUP)]

        def turn_back(values, rows):
            return values * cos_ref[rows, :] - pair_swap(values) * sin_ref[rows, :]

        def first(p):
            grads = split_heads(g_ref[:, lanes_of[p]])
            return [
                dot_nt(v_ref[span, lanes_of[p]], stack_heads(grads, own)) for own, span, _ in blocks
            ]

        def second(p, grad_probs):
            made = []
            for (own, span, at), pair in zip(blocks, grad_probs):
                heads = []
                for h in range(2):
                    columns = slice(h * LANES, (h + 1) * LANES)
                    probs = prob_ref[0, p, at, columns].astype(F32)
                    inner = jnp.sum(probs * pair[:, columns], axis=0, keepdims=True)
                    heads.append((probs * (pair[:, columns] - inner)).astype(BF16))
                made.append(jnp.concatenate(heads, axis=1))
            return made

        def third(p, grad_scores):
            lanes = lanes_of[p]
            queries, grads = split_heads(q_ref[:, lanes]), split_heads(g_ref[:, lanes])
            k_t = k_ref[:, lanes].T
            acc_k[p] = jnp.zeros_like(acc_k[p])
            acc_v[p] = jnp.zeros_like(acc_v[p])
            turned_parts = []
            for (own, span, at), low in zip(blocks, grad_scores):
                acc_k[p, span, :] += dot_nn(low, stack_heads(queries, own))
                acc_v[p, span, :] += dot_nn(prob_ref[0, p, at, :], stack_heads(grads, own))
                product = dot_nn(k_t[:, span], low)
                both = jnp.concatenate([product[:HEAD, :LANES], product[HEAD:, LANES:]], axis=0)
                turned_parts.append(both.T)
            return turned_parts

        def fourth(p, turned_parts):
            gq = jnp.concatenate(
                [
                    turn_back(part * 0.125, own).astype(BF16)
                    for (own, _, _), part in zip(blocks, turned_parts)
                ],
                axis=0,
            )
            gk = turn_back(acc_k[p], slice(0, length)).astype(BF16)
            gv = acc_v[p].astype(BF16)
            pair = group * GROUP + p
            at_lanes = pl.ds(pl.multiple_of(pair * LANES, LANES), LANES)
            for i, grad in enumerate((gq, gk, gv)):
                at_grad = pl.ds(pl.multiple_of((i * pairs + pair) * LANES, LANES), LANES)
                grads_all[at_rows, at_grad] = grad
                line = SUM_QKV + i
                small_ref[line : line + 1, at_lanes] += jnp.sum(
                    grad.astype(F32), axis=0, keepdims=True
                )

        grad_probs = first(0)
        waiting = None
        for p in range(GROUP):
            grad_scores = second(p, grad_probs)
            if p + 1 < GROUP:
                grad_probs = first(p + 1)
            turned_parts = third(p, grad_scores)
            if waiting is not None:
                fourth(*waiting)
            waiting = (p, turned_parts)
        fourth(*waiting)

    if not last:

        @pl.when(step == units - 1)
        def _():
            hand_on.start()
            hand_on.wait()

        return

    @pl.when(step == units)
    def _():
        for load in loads:
            load.wait()
        hand_on.start()

    @pl.when(step >= units)
    def _():
        sending = step == units
        height = send_ref.shape[1]
        core = jnp.where(sending, 1 - where[1], where[1])
        left = [
            turned[pl.ds(pl.multiple_of((2 * half + core) * height, 16), height), :]
            for half in (1 - where[0], where[0])
        ]
        value = dot_nn(jnp.concatenate(left, axis=0), grads_all[...]).astype(BF16)
        put_blocks(
            send_ref, keep_ref, sending, (0, 1), slice(0, 3 * width), (value[:height], value[height:])
        )
        for slot, half in enumerate((1 - where[0], where[0])):
            pack_vectors(small_ref, packed, half)
            vectors = jnp.where(core == 0, packed[...], 0.0).astype(BF16)
            put_blocks(
                send_ref, keep_ref, sending, (slot,), slice(3 * width, 3 * width + LANES), (vectors,)
            )

    @pl.when(step == units + 1)
    def _():
        hand_on.wait()


def attend_back(where, q, k, v, grad_context, probs, cosine, sine, turned, sums, row, made=None):
    tokens, width = q.shape
    total, pairs, depth = probs.shape[:3]
    length = tokens // total
    last = row == total - 1
    rows = 1 if last else total - 1
    units = rows * pairs // GROUP
    height = width // 4
    here = tokens if last else rows * length

    def at(s):
        s = jnp.minimum(s, units - 1)
        return row + s // (pairs // GROUP), s % (pairs // GROUP)

    head = pl.BlockSpec((length, GROUP * LANES), lambda s, *_: at(s))
    table = pl.BlockSpec((length, LANES), lambda s, *_: (at(s)[0], 0))
    shape = jax.ShapeDtypeStruct
    out_specs = [whole(*sums.shape)]
    out_shape = [shape(sums.shape, F32)]
    scratch = [pltpu.VMEM((GROUP, length, LANES), F32)] * 2
    scratch += [pltpu.VMEM((here, 3 * width), BF16)]
    extra = ()
    if last:
        extra = (turned,) if made is None else (turned, made)
        out_specs += [
            send_spec(1, height, 3 * width + LANES, units),
            keep_spec(1, height, 3 * width + LANES, units),
        ]
        out_shape += [shape((2, height, 3 * width + LANES), BF16)] * 2
        scratch += [pltpu.VMEM((width, tokens), BF16), pltpu.VMEM((height, LANES), F32)]
    return pl.pallas_call(
        functools.partial(attend_back_kernel, rows, row, last),
        grid_spec=pltpu.PrefetchScalarGridSpec(
            num_scalar_prefetch=1,
            grid=(units + 2 * last,),
            in_specs=[head] * 4
            + [
                pl.BlockSpec((1, GROUP, depth, 2 * LANES), lambda s, *_: at(s) + (0, 0)),
                table,
                table,
                whole(*sums.shape),
            ]
            + [ANY] * len(extra),
            out_specs=out_specs + [ANY],
            scratch_shapes=scratch + [pltpu.SemaphoreType.DMA((3,))],
        ),
        out_shape=out_shape + [shape((here, 3 * width), BF16)],
        compiler_params=params(60),
        cost_estimate=LIGHT,
        name="attend_back",
    )(where, q, k, v, grad_context, probs, cosine, sine, sums, *extra)


def norm_parts(values):
    mean = jnp.mean(values, axis=-1, keepdims=True)
    center = values - mean
    spread = jnp.mean(center * center, axis=-1, keepdims=True)
    scale = lax.rsqrt(spread + EPSILON)
    return center * scale, scale


def norm_back(grads, gain, normal, scale):
    inner = grads * gain
    return scale * (
        inner
        - jnp.mean(inner, axis=-1, keepdims=True)
        - normal * jnp.mean(inner * normal, axis=-1, keepdims=True)
    )


def gelu_parts(values):
    share = 0.5 + 0.5 * lax.erf(values * 0.7071067811865476)
    return share, jnp.exp(values * values * -0.5) * 0.3989422804014327


def down_copies(down, rows, wd, sems):
    scale = wd.shape[0] // wd.shape[1]
    pieces = list(down[:1]) + cut_pieces(down[1:])
    starts = [rows[i] * scale for i in range(len(pieces))]
    return piece_copies(pieces, starts, wd, 0, sems, 0)


def feed_up_kernel(count, rows, ctx_ref, x_ref, vec, bu, *refs):
    own, pieces = refs[:2], refs[2 : 2 + count]
    normal_ref, scale_ref, act_ref, slope_ref, joined, lows, sems = refs[2 + count :]
    width = x_ref.shape[1]
    step, last = pl.program_id(0), pl.num_programs(0) - 1

    def norm_stage():
        bo, g1, s1 = (vec[i : i + 1, :] for i in range(3))
        attended = dot_nn(ctx_ref[...], joined[:, :width]) + bo
        normal, scale = norm_parts(x_ref[...].astype(F32) + attended)
        normal = normal.astype(BF16)
        normal_ref[...] = normal
        scale_ref[...] = scale
        lows[pl.ds(step % 2, 1)] = (normal.astype(F32) * g1 + s1).astype(BF16)[None]

    def wide_stage(between):
        low = lows[pl.ds((step + 1) % 2, 1)][0]
        chunks = list(range(0, bu.shape[1], CHUNK))

        def product(c):
            return dot_nn(low, joined[:, width + c : width + c + CHUNK])

        ahead = product(0)
        for n, c in enumerate(chunks):
            hidden = ahead + bu[:, c : c + CHUNK]
            if n + 1 < len(chunks):
                ahead = product(chunks[n + 1])
            share, density = gelu_parts(hidden)
            act_ref[:, c : c + CHUNK] = (hidden * share).astype(BF16)
            slope_ref[:, c : c + CHUNK] = (share + hidden * density).astype(BF16)
            if n == 1:
                between()

    @pl.when(step == 0)
    def _():
        sooner, later = joined_copies(own, pieces, rows, joined, sems, width)
        for copy in sooner + later:
            copy.start()
        for copy in sooner:
            copy.wait()
        norm_stage()
        for copy in later:
            copy.wait()

    @pl.when((step > 0) & (step < last))
    def _():
        wide_stage(norm_stage)

    @pl.when(step == last)
    def _():
        wide_stage(lambda: None)


def feed_up(ctx, x, joined, vec, bu):
    own, pieces, rows = joined
    count = len(pieces)
    tokens, width = x.shape
    hidden = bu.shape[1]
    steps = tokens // TILE

    def now(columns):
        return pl.BlockSpec((TILE, columns), lambda s: (jnp.minimum(s, steps - 1), 0))

    def late(columns):
        return pl.BlockSpec((TILE, columns), lambda s: (jnp.maximum(s - 1, 0), 0))

    shape = jax.ShapeDtypeStruct
    return pl.pallas_call(
        functools.partial(feed_up_kernel, count),
        grid=(steps + 1,),
        in_specs=[SMEM, now(width), now(width), whole(*vec.shape), whole(*bu.shape)]
        + [ANY] * (2 + count),
        out_specs=[now(width), now(1), late(hidden), late(hidden)],
        out_shape=[
            shape((tokens, width), BF16),
            shape((tokens, 1), F32),
            shape((tokens, hidden), BF16),
            shape((tokens, hidden), BF16),
        ],
        scratch_shapes=[
            pltpu.VMEM((width, width + hidden), BF16),
            pltpu.VMEM((2, TILE, width), BF16),
            pltpu.SemaphoreType.DMA((SPLITS * (2 + 4 * count),)),
        ],
        compiler_params=params(60),
        cost_estimate=LIGHT,
        name="feed_up",
    )(rows, ctx, x, vec, bu, *own, *pieces)


def feed_down_kernel(count, steps, where, rows, normal_ref, cot_ref, vec, act_any, *refs):
    down = refs[:count]
    small_ref, send_ref, keep_ref, res_any, gd_any = refs[count : count + 5]
    wd, act, products, res, grads_all, sems, sems_act, sems_out = refs[count + 5 :]
    step = pl.program_id(0)
    tile = cot_ref.shape[0]

    def rows_at(i):
        return pl.ds(pl.multiple_of(i * tile, tile), tile)

    def stores(i):
        span = rows_at(i)
        return [
            pltpu.make_async_copy(s.at[span, :], d.at[span, :], sems_out.at[j * steps + i])
            for j, (s, d) in enumerate(((res, res_any), (grads_all, gd_any)))
        ]

    def load(i):
        span = rows_at(i)
        return pltpu.make_async_copy(act_any.at[span, :], act.at[span, :], sems_act.at[i])

    def product_stage():
        load(step).wait()
        products[pl.ds(step % 2, 1)] = dot_nn(act[rows_at(step), :], wd[...])[None]

    def norm_stage():
        span = rows_at(step - 1)
        g1, s1, bd, g2, s2 = (vec[j : j + 1, :] for j in range(1, 6))
        normed = normal_ref[...].astype(F32) * g1 + s1
        product = products[pl.ds((step + 1) % 2, 1)][0]
        normal2, scale2 = norm_parts(normed + (product + bd))
        res[span, :] = normal2 * g2 + s2
        cot = cot_ref[...].astype(F32)
        low = norm_back(cot, g2, normal2, scale2).astype(BF16)
        grads_all[span, :] = low
        for j, value in enumerate((cot * normal2, cot, low.astype(F32))):
            line = SUM_FFN + j
            small_ref[line : line + 1, :] += jnp.sum(value, axis=0, keepdims=True)
        for copy in stores(step - 1):
            copy.start()

    @pl.when(step == 0)
    def _():
        small_ref[...] = jnp.zeros_like(small_ref)
        copies = down_copies(down, rows, wd, sems)
        for copy in [load(0)] + copies + [load(j) for j in range(1, steps)]:
            copy.start()
        for copy in copies:
            copy.wait()
        product_stage()

    @pl.when((step > 0) & (step < steps))
    def _():
        product_stage()
        norm_stage()

    @pl.when(step == steps)
    def _():
        norm_stage()

    @pl.when(step > steps)
    def _():
        product_step = step - steps - 1
        height = send_ref.shape[1]
        sending = product_step < 2
        core = jnp.where(sending, 1 - where[1], where[1])
        half = jnp.where(product_step % 2 == 0, 1 - where[0], where[0])
        at_left = pl.ds(pl.multiple_of((2 * half + core) * height, LANES), height)
        value = dot_tn(act[:, at_left], grads_all[...]).astype(BF16)
        put_blocks(send_ref, keep_ref, sending, (0,), slice(None), (value,))

    @pl.when(step == steps + 4)
    def _():
        for i in range(steps):
            for copy in stores(i):
                copy.wait()


def feed_down(where, act, normal, cot, down, rows, vec):
    count = len(down)
    tokens, width = cot.shape
    wide = act.shape[1]
    tile = 2 * TILE
    steps = tokens // tile
    height = wide // 4
    late = pl.BlockSpec((tile, width), lambda s, *_: (jnp.clip(s - 1, 0, steps - 1), 0))
    shape = jax.ShapeDtypeStruct
    return pl.pallas_call(
        functools.partial(feed_down_kernel, count, steps),
        grid_spec=pltpu.PrefetchScalarGridSpec(
            num_scalar_prefetch=1,
            grid=(steps + 5,),
            in_specs=[SMEM, late, late, whole(*vec.shape)] + [ANY] * (1 + count),
            out_specs=[whole(SUM_ROWS, width)]
            + [send_spec(2, height, width, steps + 1), keep_spec(2, height, width, steps + 1)]
            + [ANY] * 2,
            scratch_shapes=[
                pltpu.VMEM((wide, width), BF16),
                pltpu.VMEM((tokens, wide), BF16),
                pltpu.VMEM((2, tile, width), F32),
                pltpu.VMEM((tokens, width), F32),
                pltpu.VMEM((tokens, width), BF16),
                pltpu.SemaphoreType.DMA((SPLITS * (2 * count + 1),)),
                pltpu.SemaphoreType.DMA((steps,)),
                pltpu.SemaphoreType.DMA((2 * steps,)),
            ],
        ),
        out_shape=[shape((SUM_ROWS, width), F32)]
        + [shape((2, height, width), BF16)] * 2
        + [shape((tokens, width), F32), shape((tokens, width), BF16)],
        compiler_params=params(60),
        cost_estimate=LIGHT,
        name="feed_down",
    )(where, rows, normal, cot, vec, act, *down)


def feed_back_kernel(
    count, steps, where, rows, gd_ref, slope_ref, normal_ref, scale_ref, vec, sums_ref, ctx_any,
    *refs,
):
    own, pieces = refs[:2], refs[2 : 2 + count]
    down = refs[2 + count : 3 + 2 * count]
    small_ref, send_ref, keep_ref, ga_any, gc_any = refs[3 + 2 * count : 8 + 2 * count]
    (
        joined, wd, low, ctx, hidden_all, attended_all, grad_sums, gc, wide,
        sems, sems_down, sem_ctx, sems_out,
    ) = refs[8 + 2 * count :]
    tile, width = gd_ref.shape
    hidden = wide.shape[1]
    step = pl.program_id(0)
    load_ctx = pltpu.make_async_copy(ctx_any, ctx, sem_ctx.at[0])

    def rows_at(i):
        return pl.ds(pl.multiple_of(i * tile, tile), tile)

    def stores(i):
        span = rows_at(i)
        return [
            pltpu.make_async_copy(s.at[span, :], d.at[span, :], sems_out.at[j * steps + i])
            for j, (s, d) in enumerate(((attended_all, ga_any), (gc, gc_any)))
        ]

    def norm_stage():
        span = rows_at(step - 1)
        grad_normed = grad_sums[pl.ds((step + 1) % 2, 1)][0]
        normal = normal_ref[...].astype(F32)
        low[span, :] = (normal * vec[1:2, :] + vec[2:3, :]).astype(BF16)
        rounded = norm_back(grad_normed, vec[1:2, :], normal, scale_ref[...]).astype(BF16)
        attended_all[span, :] = rounded
        for j, value in enumerate((grad_normed * normal, grad_normed, rounded.astype(F32))):
            line = SUM_ATTN + j
            small_ref[line : line + 1, :] += jnp.sum(value, axis=0, keepdims=True)
        gc[span, :] = dot_nt(rounded, joined[:, :width]).astype(BF16)

    def wide_stage(waiting, between):
        span = rows_at(step)
        chunks = list(range(0, hidden, CHUNK))

        def product(c):
            return dot_nt(gd_ref[...], wd[c : c + CHUNK, :])

        ahead = product(0)
        for copy in waiting:
            copy.wait()
        total = gd_ref[...].astype(F32)
        for n, c in enumerate(chunks):
            grad_active = ahead
            if n + 1 < len(chunks):
                ahead = product(chunks[n + 1])
            rounded = (grad_active * slope_ref[:, c : c + CHUNK].astype(F32)).astype(BF16)
            hidden_all[span, c : c + CHUNK] = rounded
            wide[0:1, c : c + CHUNK] += jnp.sum(rounded.astype(F32), axis=0, keepdims=True)
            total = total + dot_nt(rounded, joined[:, width + c : width + c + CHUNK])
            if n == 1:
                between()
        grad_sums[pl.ds(step % 2, 1)] = total[None]

    @pl.when(step == 0)
    def _():
        copies = down_copies(down, rows, wd, sems_down)
        later = joined_copies(own, pieces, rows, joined, sems)
        for copy in copies + later + [load_ctx]:
            copy.start()
        small_ref[...] = sums_ref[...]
        wide[...] = jnp.zeros_like(wide)
        for copy in copies:
            copy.wait()
        wide_stage(later, lambda: None)

    @pl.when((step > 0) & (step < steps))
    def _():
        wide_stage([], norm_stage)

    @pl.when(step == steps)
    def _():
        norm_stage()
        for j in range(hidden // width):
            line = SUM_UP + j
            small_ref[line : line + 1, :] = wide[0:1, j * width : (j + 1) * width]
        load_ctx.wait()

    @pl.when((step > 0) & (step <= steps))
    def _():
        for copy in stores(step - 1):
            copy.start()

    @pl.when(step > steps)
    def _():
        sending = step == steps + 1
        core = jnp.where(sending, 1 - where[1], where[1])
        height, cut = width // 2, hidden // 2
        at_wide = pl.ds(pl.multiple_of(core * cut, LANES), cut)
        at_narrow = pl.ds(pl.multiple_of(core * height, LANES), height)
        slots = (jnp.where(where[0] == 0, 1, 0), jnp.where(where[0] == 0, 0, 1))
        value = dot_tn(low[...], hidden_all[:, at_wide]).astype(BF16)
        put_blocks(
            send_ref, keep_ref, sending, slots, slice(0, cut), (value[:height], value[height:])
        )
        value = dot_tn(ctx[...], attended_all[:, at_narrow]).astype(BF16)
        put_blocks(
            send_ref, keep_ref, sending, slots, slice(cut, cut + height),
            (value[:height], value[height:]),
        )

    @pl.when(step == steps + 2)
    def _():
        for i in range(steps):
            for copy in stores(i):
                copy.wait()


def feed_back(where, gd, slope, normal, scale, joined, down, vec, context, sums):
    own, pieces, rows = joined
    count = len(pieces)
    tokens, width = gd.shape
    wide = slope.shape[1]
    steps = tokens // TILE
    total = (wide + width) // 2

    def now(columns):
        return pl.BlockSpec((TILE, columns), lambda s, *_: (jnp.minimum(s, steps - 1), 0))

    def late(columns):
        return pl.BlockSpec((TILE, columns), lambda s, *_: (jnp.clip(s - 1, 0, steps - 1), 0))

    shape = jax.ShapeDtypeStruct
    return pl.pallas_call(
        functools.partial(feed_back_kernel, count, steps),
        grid_spec=pltpu.PrefetchScalarGridSpec(
            num_scalar_prefetch=1,
            grid=(steps + 3,),
            in_specs=[SMEM, now(width), now(wide), late(width), late(1)]
            + [whole(*vec.shape), whole(*sums.shape)]
            + [ANY] * (4 + 2 * count),
            out_specs=[whole(*sums.shape)]
            + [send_spec(1, width // 2, total, steps + 1)]
            + [keep_spec(1, width // 2, total, steps + 1)]
            + [ANY] * 2,
            scratch_shapes=[
                pltpu.VMEM((width, width + wide), BF16),
                pltpu.VMEM((wide, width), BF16),
                pltpu.VMEM((tokens, width), BF16),
                pltpu.VMEM((tokens, width), BF16),
                pltpu.VMEM((tokens, wide), BF16),
                pltpu.VMEM((tokens, width), BF16),
                pltpu.VMEM((2, TILE, width), F32),
                pltpu.VMEM((tokens, width), BF16),
                pltpu.VMEM((8, wide), F32),
                pltpu.SemaphoreType.DMA((SPLITS * (2 + 2 * count),)),
                pltpu.SemaphoreType.DMA((SPLITS * (1 + 2 * count),)),
                pltpu.SemaphoreType.DMA((1,)),
                pltpu.SemaphoreType.DMA((2 * steps,)),
            ],
        ),
        out_shape=[shape(sums.shape, F32)]
        + [shape((2, width // 2, total), BF16)] * 2
        + [shape((tokens, width), BF16)] * 2,
        compiler_params=params(60),
        cost_estimate=LIGHT,
        name="feed_back",
    )(where, rows, gd, slope, normal, scale, vec, sums, context, *own, *pieces, *down)


def inputs_back_kernel(count, rows, ga_ref, grads, *refs):
    own, pieces = refs[:3], refs[3 : 3 + count]
    out_ref, full, sems = refs[3 + count :]

    @pl.when(pl.program_id(0) == 0)
    def _():
        fetch_joined(own, pieces, rows, full, sems)

    out_ref[...] = ga_ref[...].astype(F32) + dot_nt(grads[...], full[...])


def inputs_back(grads, ga, weights):
    own, pieces, rows = weights
    tokens, width = ga.shape
    tile = pl.BlockSpec((TILE, width), lambda t: (t, 0))
    return pl.pallas_call(
        functools.partial(inputs_back_kernel, len(pieces)),
        grid=(tokens // TILE,),
        in_specs=[SMEM, tile, pl.BlockSpec((TILE, 3 * width), lambda t: (t, 0))]
        + [ANY] * (3 + len(pieces)),
        out_specs=tile,
        out_shape=jax.ShapeDtypeStruct((tokens, width), F32),
        scratch_shapes=[
            pltpu.VMEM((width, 3 * width), BF16),
            pltpu.SemaphoreType.DMA((SPLITS * (3 + 2 * len(pieces)),)),
        ],
        compiler_params=params(60),
        cost_estimate=LIGHT,
        name="inputs_back",
    )(rows, ga, grads, *own, *pieces)


CORE, NEAR_Y, NEAR_Z, FAR_Z = 1, 2, 4, 8


def after(value, *others):
    return lax.optimization_barrier((value,) + others)[0]


def swap_dp(values, bit):
    size = lax.axis_size("dp")
    return lax.ppermute(values, "dp", [(i, i ^ bit) for i in range(size)])


def swap_fsdp(values):
    return lax.ppermute(values, "fsdp", [(0, 1), (1, 0)])


def swap_both(values):
    size = lax.axis_size("dp")
    pairs = [(2 * i + h, 2 * (i ^ NEAR_Y) + 1 - h) for i in range(size) for h in range(2)]
    return lax.ppermute(values, ("dp", "fsdp"), pairs)


def rows_of(values, start, count):
    return lax.dynamic_slice_in_dim(values, start, count, axis=0)


def own_part(shards, place):
    half, core, y, z = place
    height = shards[0].shape[0]
    count = height // 8
    starts = (2 * y + core) * count, height // 2 + (2 * z + core) * count
    return jnp.concatenate(
        [jnp.concatenate([rows_of(s, start, count) for s in shards], axis=1) for start in starts],
        axis=0,
    )


def far_parts(first):
    count = first.shape[0] // 2
    return swap_dp(first[:count], NEAR_Y), swap_dp(first[count:], NEAR_Z)


def all_parts(first, far):
    here = (first,) + far
    return here + tuple(swap_dp(part, CORE) for part in here)


def piece_rows(height, place):
    half, core, y, z = place
    count = height // 8
    base = (1 - half) * height
    rows = [half * height]
    for c in (core, 1 - core):
        rows += [
            base + (2 * y + c) * count,
            base + height // 2 + (2 * z + c) * count,
            base + (2 * (1 - y) + c) * count,
            base + height // 2 + (2 * (1 - z) + c) * count,
        ]
    return jnp.stack(rows).astype(jnp.int32)


class Part:
    def __init__(self, terms, place, columns=None):
        self.bits = {0: 1, 1: place[2], 2: place[3]}
        self.swaps = {
            0: swap_fsdp,
            1: lambda v: swap_dp(v, NEAR_Y),
            2: lambda v: swap_dp(v, NEAR_Z),
            3: lambda v: swap_dp(v, FAR_Z),
        }
        self.terms = [t.reshape(2, 2, 2, t.shape[1] // 4, t.shape[2]) for t in terms]
        self.views = [(columns, ())] * len(terms)
        self.flight, self.joined = [], None

    def total(self, *picks):
        value = None
        for term, (columns, before) in zip(self.terms, self.views):
            if columns is not None:
                term = term[..., columns[0] : columns[1]]
            for axis, index in before + picks:
                term = lax.dynamic_slice_in_dim(term, index, 1, axis)
            term = term.astype(F32)
            value = term if value is None else value + term
        return value.astype(BF16)

    def cut(self, *picks):
        self.views = [(columns, before + picks) for columns, before in self.views]

    def halve(self, axis):
        bit = self.bits[axis]
        self.flight, self.route = [self.total((axis, 1 - bit))], [self.swaps[axis]]
        self.cut((axis, bit))

    def both(self):
        bit = self.bits[1]
        self.flight = [
            self.total((0, 0), (1, bit)),
            self.total((0, 1), (1, 1 - bit)),
            self.total((0, 0), (1, 1 - bit)),
        ]
        self.route = [self.swaps[0], self.swaps[1], swap_both]
        self.cut((0, 1), (1, bit))

    def merge(self, *others):
        value = jnp.concatenate([part.total() for part in (self,) + others], axis=-1)
        self.terms, self.views = [value], [(None, ())]

    def split(self, cut):
        other = copy.copy(self)
        end = self.terms[0].shape[-1]
        self.views = [((0, cut), before) for _, before in self.views]
        other.views = [((cut, end), before) for _, before in other.views]
        return other

    def send_whole(self, swap, reshape=None):
        value = self.terms[0]
        if len(self.terms) > 1 or self.views[0][0] is not None:
            value = self.total()
        if reshape:
            value = value.reshape(-1, value.shape[-1])
        self.flight, self.route = [value], [lambda v: (v, swap(v))]
        self.terms, self.views = [], []

    def far(self):
        self.send_whole(self.swaps[3])

    def join(self, axis):
        self.send_whole(self.swaps[axis])
        self.joined = axis

    def finish(self):
        self.send_whole(lambda v: swap_dp(v, CORE), True)

    def land(self):
        for sent, route in zip(self.flight, self.route):
            got = route(sent)
            self.terms += list(got) if isinstance(got, tuple) else [got]
        self.views = self.views + [(None, ())] * (len(self.terms) - len(self.views))
        self.flight = []

    def settle(self):
        if self.joined is None:
            return
        mine, other = self.terms
        axis, self.joined = self.joined, None
        value = jnp.where(
            self.bits[axis] == 0,
            jnp.concatenate([mine, other], axis=axis),
            jnp.concatenate([other, mine], axis=axis),
        )
        self.terms, self.views = [value], [(None, ())]


def fence(parts, *arrays):
    counts = [(len(p.terms), len(p.flight)) for p in parts]
    flat = [a for p in parts for a in p.terms + p.flight] + list(arrays)
    flat = list(lax.optimization_barrier(tuple(flat)))
    for part, (terms, flight) in zip(parts, counts):
        part.terms, flat = flat[:terms], flat[terms:]
        part.flight, flat = flat[:flight], flat[flight:]
    return flat


def widen(mine, other, core, axis):
    low = jnp.where(core == 0, mine, other).astype(F32)
    high = jnp.where(core == 0, other, mine).astype(F32)
    return jnp.concatenate([low, high], axis=axis)


def gather_all(values):
    return lax.all_gather(values, "fsdp", axis=0, tiled=True)


def sum_plain(send, keep, by_rows):
    blocks = [[keep[1], send[1]], [keep[0], send[0]]]
    axis = 0 if by_rows else 1
    value = jnp.concatenate([jnp.concatenate(pair, axis=axis) for pair in blocks], axis=0)
    own = lax.psum_scatter(value, "fsdp", scatter_dimension=0, tiled=True)
    return lax.psum(own, "dp").astype(F32)


def local(
    inputs, segment_ids, cotangent, w_query, b_query, w_key, b_key, w_value, b_value,
    w_output, b_output, gain_attn, bias_attn, w_up, b_up, w_down, b_down, gain_ffn, bias_ffn,
):
    rows, length = segment_ids.shape
    width = inputs.shape[1]
    shards = lax.axis_size("fsdp")
    paired = shards == 2 and lax.axis_size("dp") == 16
    half = lax.axis_index("fsdp")
    dp = lax.axis_index("dp")
    place = (half, dp % 2, dp // 2 % 2, dp // 4 % 2)
    core = place[1]
    vectors = (b_query, b_key, b_value, b_output, gain_attn, bias_attn, b_down, gain_ffn, bias_ffn)
    height = w_query.shape[0]
    cosine, sine, turned = rotary_tables(segment_ids, inputs)
    if paired:
        where = jnp.stack([half, core]).astype(jnp.int32)
        part_qkv = own_part((w_query, w_key, w_value), place)
        part_up = own_part((w_output, w_up), place)
        here_qkv = swap_fsdp(part_qkv)
        part_down = own_part((after(w_down, here_qkv),), place)
        lines = jnp.concatenate(vectors + (b_up,)).reshape(-1, height)
        other = swap_fsdp(after(lines, part_qkv))
        here_up = swap_fsdp(after(part_up, part_qkv))
        at = piece_rows(height, place)
        joined_qkv = ((w_query, w_key, w_value), all_parts(here_qkv, far_parts(here_qkv)), at)
        lines = jnp.where(half == 0, jnp.stack([lines, other]), jnp.stack([other, lines]))
    else:
        where = jnp.zeros((2,), jnp.int32)
        at = jnp.zeros((1,), jnp.int32)
        joined_qkv = (tuple(gather_all(w) for w in (w_query, w_key, w_value)), (), at)
        joined_up = ((gather_all(w_output), gather_all(w_up)), (), at)
        down = (gather_all(w_down),)
        lines = jnp.concatenate(vectors + (b_up,)).reshape(-1, height)
        lines = lax.all_gather(lines, "fsdp", axis=0)
    lines = lines.astype(F32)
    vec = jnp.swapaxes(lines[:, :9], 0, 1).reshape(9, width)
    bias_up = lines[:, 9:].reshape(1, -1)

    q, k, v = project(inputs, joined_qkv, vec[:3], cosine, sine)
    vec = vec[3:]
    if paired:
        q, here_up, part_down, vec, bias_up = lax.optimization_barrier(
            (q, here_up, part_down, vec, bias_up)
        )
        here_down = swap_fsdp(part_down)
        far_up = far_parts(here_up)
    context, probs = attend(q, k, v, segment_ids)
    if paired:
        context, probs, here_up, here_down, far_up = lax.optimization_barrier(
            (context, probs, here_up, here_down, far_up)
        )
        joined_up = ((w_output, w_up), all_parts(here_up, far_up), at)
        far_down = far_parts(here_down)
    normal, scale, act, slope = feed_up(context, inputs, joined_up, vec, bias_up)
    if paired:
        act, slope, here_down, far_down = lax.optimization_barrier(
            (act, slope, here_down, far_down)
        )
        down = (w_down,) + all_parts(here_down, far_down)
    sums, send, keep, result, grad_down = feed_down(
        where, act, normal, cotangent, down, at, vec
    )
    sent = [(send, keep)]
    if paired:
        sum_d = Part([keep, swap_dp(send, CORE)], place)
        sum_d.both()
        (grad_down,) = fence([sum_d], grad_down)
    outs = feed_back(
        where, grad_down, slope, normal, scale, joined_up, down, vec, context, sums
    )
    sent.append(outs[1:3])
    if paired:
        sum_d.land()
        outs = fence([sum_d], *outs)
    sums, send, keep, grad_attended, grad_context = outs
    if paired:
        sum_d.merge()
        sum_u = Part([keep, swap_dp(send, CORE)], place)
        sum_d.halve(2)
        sum_u.both()
        parts = [sum_d, sum_u]
        (grad_context,) = fence(parts, grad_context)
    tables = (probs, cosine, sine, turned)
    made = None
    if rows > 1:
        sums, made = attend_back(where, q, k, v, grad_context, *tables, sums, 0)
        if paired:
            sum_d.land()
            sums, made, grad_context = fence([sum_d], sums, made, grad_context)
            sum_d.far()
            sums, grad_context = fence([sum_d], sums, grad_context)
    outs = attend_back(where, q, k, v, grad_context, *tables, sums, rows - 1, made)
    sent.append(outs[1:3])
    if paired:
        for p in parts:
            p.land()
        outs = fence(parts, *outs)
    sums, send, keep, grads = outs
    if paired:
        sum_q = Part([keep, swap_dp(send, CORE)], place)
        sum_u.merge()
        sum_d.join(2) if rows > 1 else sum_d.far()
        sum_u.halve(2)
        sum_q.both()
        parts = [sum_d, sum_u, sum_q]
        (grad_attended,) = fence(parts, grad_attended)
    grad_inputs = inputs_back(grads, grad_attended, joined_qkv)
    if paired:
        for p in parts:
            p.land()
        (grad_inputs,) = fence(parts, grad_inputs)
        last = grad_inputs

        def step(part, name, *axis):
            nonlocal last
            (last,) = fence([part], last)
            part.settle()
            getattr(part, name)(*axis)
            (last,) = fence([part], last)
            last = part.flight[0]
            part.land()

        if rows == 1:
            step(sum_d, "join", 2)
        step(sum_u, "far")
        sum_q.merge()
        step(sum_q, "halve", 2)
        step(sum_d, "join", 1)
        sum_q.terms = [after(term, sum_u.terms[-1]) for term in sum_q.terms]
        step(sum_q, "far")
        cut_u, cut_q = ((p.terms[0].shape[-1] // 2 + 64) // LANES * LANES for p in (sum_u, sum_q))
        (last,) = fence([sum_u], last)
        sum_v = sum_u.split(cut_u)
        step(sum_u, "join", 2)
        step(sum_v, "join", 1)
        step(sum_d, "finish")
        gwd = widen(*sum_d.terms, core, 0)
        (last,) = fence([sum_q], last)
        sum_r = sum_q.split(cut_q)
        step(sum_q, "join", 2)
        step(sum_r, "join", 1)
        step(sum_u, "join", 1)
        step(sum_v, "join", 2)
        step(sum_q, "join", 1)
        step(sum_r, "join", 2)
        for part in (sum_u, sum_v):
            part.terms = [after(term, gwd) for term in part.terms]
            part.settle()
            part.finish()
        fence([sum_u, sum_v, sum_q, sum_r])
        sum_u.land()
        sum_v.land()
        for part in (sum_q, sum_r):
            part.settle()
            part.finish()
            part.land()
    else:
        sums = lax.psum(sums, ("dp", "fsdp"))

    wide = b_up.shape[0] * shards
    if paired:
        mine, other = (
            jnp.concatenate([a, b], axis=1) for a, b in zip(sum_u.terms, sum_v.terms)
        )
        cut = wide // 2
        gwu = widen(mine[:, :cut], other[:, :cut], core, 1)
        gwo = widen(mine[:, cut:], other[:, cut:], core, 1)
        mine, other = (
            jnp.concatenate([a, b], axis=1) for a, b in zip(sum_q.terms, sum_r.terms)
        )
        gwq, gwk, gwv = (
            widen(*(end[:, i * width : (i + 1) * width] for end in (mine, other)), core, 0)
            for i in range(3)
        )
        count = height // LANES
        packed = jnp.where(core == 0, mine[:, 3 * width :], other[:, 3 * width :])
        packed = packed[: len(LINES) * count + wide // 2 // LANES].astype(F32)
        vectors = [packed[i * count : (i + 1) * count].reshape(-1) for i in range(len(LINES))]
        gbu = packed[len(LINES) * count :].reshape(-1)
        ggf, gbf, gbd, gga, gba, gbo, gbq, gbk, gbv = vectors
    else:

        def own(line, count=1):
            start = line * width + half * (count * width // shards)
            return lax.dynamic_slice_in_dim(
                sums.reshape(-1), start, count * width // shards, axis=0
            )

        ggf, gbf, gbd, gga, gba, gbo, gbq, gbk, gbv = (own(line) for line in LINES)
        gbu = own(SUM_UP, wide // width)
        gwd = sum_plain(*sent[0], True)
        both = sum_plain(*sent[1], False).reshape(height, 2, -1)
        cut = wide // 2
        gwu = both[..., :cut].reshape(height, -1)
        gwo = both[..., cut:].reshape(height, -1)
        both = sum_plain(*sent[2], True)
        gwq, gwk, gwv = (both[:, i * width : (i + 1) * width] for i in range(3))
    return (
        result, grad_inputs, gwq, gbq, gwk, gbk, gwv, gbv, gwo, gbo, gga, gba,
        gwu, gbu, gwd, gbd, ggf, gbf,
    )


def solution(mesh):
    tokens, matrix, vector = P(("dp", "fsdp"), None), P("fsdp", None), P("fsdp")
    weights = (
        matrix, vector, matrix, vector, matrix, vector, matrix, vector, vector, vector,
        matrix, vector, matrix, vector, vector, vector,
    )
    return jax.shard_map(
        local,
        mesh=mesh,
        in_specs=(tokens,) * 3 + weights,
        out_specs=(tokens,) * 2 + weights,
        check_vma=False,
    )
```
